32 devices in a mesh: wide: 16 (over z, x, core), tensor: 2 (over y).
Axes of the slice: x: 2, y: 2, z: 4, core: 2. Of those that a mesh axis runs over, the one named last changes fastest.
Arguments:
- images: bfloat16 [18464, 1024], P('wide', 'tensor'), may hold values from -6 to 6
- first_gain: bfloat16 [2, 1024], replicated, may hold values from 0.5 to 1.5
- first_shift: bfloat16 [2, 1024], replicated, may hold values from -3 to 3
- query_weight: bfloat16 [2, 1024, 1024], P(None, 'wide', 'tensor'), may hold values from -0.1875 to 0.1875
- key_weight: bfloat16 [2, 1024, 1024], P(None, 'wide', 'tensor'), may hold values from -0.1875 to 0.1875
- value_weight: bfloat16 [2, 1024, 1024], P(None, 'wide', 'tensor'), may hold values from -0.1875 to 0.1875
- query_bias: bfloat16 [2, 1024], P(None, 'tensor'), may hold values from -3 to 3
- value_bias: bfloat16 [2, 1024], P(None, 'tensor'), may hold values from -3 to 3
- out_weight: bfloat16 [2, 1024, 1024], P(None, 'tensor', 'wide'), may hold values from -3 to 3
- out_bias: bfloat16 [2, 1024], P(None, 'tensor'), may hold values from -2 to 2
- second_gain: bfloat16 [2, 1024], replicated, may hold values from 0.5 to 1.5
- second_shift: bfloat16 [2, 1024], replicated, may hold values from -3 to 3
- up_weight: bfloat16 [2, 1024, 4096], P(None, 'wide', 'tensor'), may hold values from -0.1875 to 0.1875
- up_bias: bfloat16 [2, 4096], P(None, 'tensor'), may hold values from -3 to 3
- down_weight: bfloat16 [2, 4096, 1024], P(None, 'tensor', 'wide'), may hold values from -0.09375 to 0.09375
- down_bias: bfloat16 [2, 1024], P(None, 'tensor'), may hold values from -2 to 2
- cotangent: bfloat16 [18464, 1024], P('wide', 'tensor'), may hold values from -6 to 6
Outputs:
- activations: bfloat16 [18464, 1024], P('wide', 'tensor')
- input_gradient: float32 [18464, 1024], P('wide', 'tensor')
- query_weight_gradient: float32 [2, 1024, 1024], P(None, 'wide', 'tensor')
- key_weight_gradient: float32 [2, 1024, 1024], P(None, 'wide', 'tensor')
- value_weight_gradient: float32 [2, 1024, 1024], P(None, 'wide', 'tensor')
- out_weight_gradient: float32 [2, 1024, 1024], P(None, 'tensor', 'wide')
- up_weight_gradient: float32 [2, 1024, 4096], P(None, 'wide', 'tensor')
- down_weight_gradient: float32 [2, 4096, 1024], P(None, 'tensor', 'wide')
- query_bias_gradient: float32 [2, 1024], replicated
- value_bias_gradient: float32 [2, 1024], replicated
- out_bias_gradient: float32 [2, 1024], replicated
- up_bias_gradient: float32 [2, 4096], replicated
- down_bias_gradient: float32 [2, 1024], replicated
- first_gain_gradient: float32 [2, 1024], replicated
- first_shift_gradient: float32 [2, 1024], replicated
- second_gain_gradient: float32 [2, 1024], replicated
- second_shift_gradient: float32 [2, 1024], replicated
The draws below stay inside these ranges and needn't reach their ends.
All inputs are finite; a program needn't handle non-finite values.
Results may differ from the reference program's by a relative error of at most 0.018.
Values may be sent and summed in bfloat16 or wider, within the bound.
A program may use at most 320 MiB of HBM per device.

```python
import math
import jax
import jax.numpy as jnp
from jax import lax

HEADS = 16
HEAD_DIM = 64
FF = 4096
SEQ = 577
LAYERS = 2
D = 1024
IMAGES = 32
TOKENS = 18464


def block_levels(own_key, extent, pieces, smallest, high):
    level = 1.0
    for axis_at, shards_of in pieces:
        heights = jax.random.uniform(jax.random.fold_in(jax.random.fold_in(own_key, 6), axis_at), (shards_of,), jnp.float32, smallest / len(pieces), high / len(pieces))
        level = level * jnp.repeat(jnp.exp(heights), extent[axis_at] // shards_of).reshape((-1,) + (1,) * (len(extent) - 1 - axis_at))
    return level


def gaussian(stream_key, dims, width, reach, shards=(), kind=jnp.bfloat16):
    entries = jax.random.normal(stream_key, dims, jnp.float32) * width
    if len(shards) > 0:
        entries = block_levels(stream_key, dims, shards, -0.22, 0.18) * entries
    return jnp.clip(entries, min=-reach, max=reach).astype(kind)


def setup_inputs(seed: int = 0) -> dict:
    key_list = jax.random.split(jax.random.key(seed), 18)
    return {
        "images": gaussian(key_list[0], (TOKENS, D), 1.0, 6.0, ((0, 16), (1, 2))),
        "first_gain": jnp.clip(1.0 + 0.1 * jax.random.normal(key_list[1], (LAYERS, D), jnp.float32), 0.5, 1.5).astype(jnp.bfloat16),
        "first_shift": gaussian(key_list[2], (LAYERS, D), 0.5, 3.0),
        "query_weight": gaussian(key_list[3], (LAYERS, D, D), D ** -0.5, 0.1875, ((1, 16), (2, 2))),
        "key_weight": gaussian(key_list[4], (LAYERS, D, D), D ** -0.5, 0.1875, ((1, 16), (2, 2))),
        "value_weight": gaussian(key_list[5], (LAYERS, D, D), D ** -0.5, 0.1875, ((1, 16), (2, 2))),
        "query_bias": gaussian(key_list[6], (LAYERS, D), 0.5, 3.0, ((1, 2),)),
        "value_bias": gaussian(key_list[7], (LAYERS, D), 0.5, 3.0, ((1, 2),)),
        "out_weight": gaussian(key_list[8], (LAYERS, D, D), 4 ** -0.5, 3.0, ((1, 2), (2, 16))),
        "out_bias": gaussian(key_list[9], (LAYERS, D), 0.3, 2.0, ((1, 2),)),
        "second_gain": jnp.clip(1.0 + 0.1 * jax.random.normal(key_list[10], (LAYERS, D), jnp.float32), 0.5, 1.5).astype(jnp.bfloat16),
        "second_shift": gaussian(key_list[11], (LAYERS, D), 0.5, 3.0),
        "up_weight": gaussian(key_list[12], (LAYERS, D, FF), D ** -0.5, 0.1875, ((1, 16), (2, 2))),
        "up_bias": gaussian(key_list[13], (LAYERS, FF), 0.5, 3.0, ((1, 2),)),
        "down_weight": gaussian(key_list[14], (LAYERS, FF, D), FF ** -0.5, 0.09375, ((1, 2), (2, 16))),
        "down_bias": gaussian(key_list[15], (LAYERS, D), 0.3, 2.0, ((1, 2),)),
        "cotangent": gaussian(key_list[16], (TOKENS, D), 1.0, 6.0, ((0, 16), (1, 2))),
    }


@jax.custom_vjp
def low(v):
    return lax.optimization_barrier(v.astype(jnp.bfloat16)).astype(jnp.float32)

@jax.custom_vjp
def low_back(v):
    return v

def low_keep(v):
    return (low(v), None)

def low_pass(kept, grad):
    return (grad,)

def back_keep(v):
    return (v, None)

def back_low(kept, grad):
    return (low(grad),)
low.defvjp(low_keep, low_pass)
low_back.defvjp(back_keep, back_low)
norm_eps = 1e-06

def matmul_high(left, right):
    return jnp.dot(left, right, precision=lax.Precision.HIGHEST)

def layer_norm(values, gain, shift):
    row_mean = lax.optimization_barrier(jnp.mean(values, axis=-1, keepdims=True))
    variance = lax.optimization_barrier(jnp.mean(values * values, axis=-1, keepdims=True)) - row_mean * row_mean
    return (values - row_mean) * lax.rsqrt(variance + norm_eps) * gain + shift

def attention(queries, keys_proj, values_proj):
    image_count = queries.shape[0] // SEQ
    shape_four = (image_count, SEQ, HEADS, HEAD_DIM)
    query_four = queries.reshape(shape_four)
    key_four = keys_proj.reshape(shape_four)
    value_four = values_proj.reshape(shape_four)
    scores = low_back(jnp.einsum('iqhd,ikhd->ihqk', query_four, key_four, precision=lax.Precision.HIGHEST) * HEAD_DIM ** (-0.5))
    softmax_weights = jax.nn.softmax(scores, axis=-1)
    mixed_heads = jnp.einsum('ihqk,ikhd->iqhd', low(softmax_weights), value_four, precision=lax.Precision.HIGHEST)
    return mixed_heads.reshape(queries.shape[0], HEADS * HEAD_DIM)

def run_group(tokens, params):
    first_gain, first_shift, query_weight, key_weight, value_weight, query_bias, value_bias, out_weight, out_bias, second_gain, second_shift, up_weight, up_bias, down_weight, down_bias = params
    stream = tokens
    for layer_idx in range(LAYERS):
        normed = low(layer_norm(stream, first_gain[layer_idx], first_shift[layer_idx]))
        queries = low(low_back(matmul_high(normed, query_weight[layer_idx]) + query_bias[layer_idx]))
        keys_proj = low(low_back(matmul_high(normed, key_weight[layer_idx])))
        values_proj = low(low_back(matmul_high(normed, value_weight[layer_idx]) + value_bias[layer_idx]))
        mixed_heads = low(low_back(attention(queries, keys_proj, values_proj)))
        stream = stream + low_back(matmul_high(mixed_heads, out_weight[layer_idx])) + out_bias[layer_idx]
        normed_two = low(layer_norm(stream, second_gain[layer_idx], second_shift[layer_idx]))
        hidden_pre = low_back(matmul_high(normed_two, up_weight[layer_idx]) + up_bias[layer_idx])
        hidden = low(jax.nn.gelu(hidden_pre, approximate=False))
        stream = stream + low_back(matmul_high(hidden, down_weight[layer_idx])) + down_bias[layer_idx]
    return stream

def reference(images, first_gain, first_shift, query_weight, key_weight, value_weight, query_bias, value_bias, out_weight, out_bias, second_gain, second_shift, up_weight, up_bias, down_weight, down_bias, cotangent):
    params = tuple((argument.astype(jnp.float32) for argument in (first_gain, first_shift, query_weight, key_weight, value_weight, query_bias, value_bias, out_weight, out_bias, second_gain, second_shift, up_weight, up_bias, down_weight, down_bias)))
    start_stream = images.astype(jnp.float32)
    group_images = math.gcd(IMAGES, 4)
    group_rows = group_images * SEQ
    group_count = IMAGES // group_images
    run_checked = jax.checkpoint(run_group)

    def forward(stream_in, weights):
        grouped = stream_in.reshape(group_count, group_rows, stream_in.shape[1])

        def group_step(state_carry, group_block):
            return (state_carry, run_checked(group_block, weights))
        unused, result = lax.scan(group_step, None, grouped)
        return result.reshape(stream_in.shape)
    outputs, pullback = jax.vjp(forward, start_stream, params)
    input_gradient, gradients = pullback(cotangent.astype(jnp.float32))
    return (outputs.astype(jnp.bfloat16), input_gradient, gradients[2], gradients[3], gradients[4], gradients[7], gradients[11], gradients[13], gradients[5], gradients[6], gradients[8], gradients[12], gradients[14], gradients[0], gradients[1], gradients[9], gradients[10])
```

```python
import jax
import jax.numpy as jnp
from jax import lax
from jax.experimental import pallas as pl
from jax.experimental.pallas import tpu as pltpu
from jax.sharding import PartitionSpec as P

HEAD_DIM = 64
SEQ = 577
MICRO = 2


norm_eps = 1e-06


def row_totals(first_terms, second_terms):
    return lax.psum((first_terms, second_terms), "tensor")


def full_rows(share_low):
    return lax.all_gather(share_low, "tensor", axis=1, tiled=True)


def feature_total(partial_sums):
    return lax.psum_scatter(
        partial_sums.astype(jnp.bfloat16), "tensor", scatter_dimension=1, tiled=True
    ).astype(jnp.float32)


def fetch_weights(query_block, key_block, value_block, out_block, up_block, down_block):
    return (
        lax.all_gather(query_block, "wide", axis=0, tiled=True),
        lax.all_gather(key_block, "wide", axis=0, tiled=True),
        lax.all_gather(value_block, "wide", axis=0, tiled=True),
        lax.all_gather(out_block, "wide", axis=1, tiled=True),
        lax.all_gather(up_block, "wide", axis=0, tiled=True),
        lax.all_gather(down_block, "wide", axis=1, tiled=True),
    )


def settle_grads(query_piece, key_piece, value_piece, out_piece, up_piece, down_piece):
    return (
        lax.psum_scatter(
            query_piece.astype(jnp.bfloat16), "wide", scatter_dimension=0, tiled=True
        ).astype(jnp.float32),
        lax.psum_scatter(
            key_piece.astype(jnp.bfloat16), "wide", scatter_dimension=0, tiled=True
        ).astype(jnp.float32),
        lax.psum_scatter(
            value_piece.astype(jnp.bfloat16), "wide", scatter_dimension=0, tiled=True
        ).astype(jnp.float32),
        lax.psum_scatter(
            out_piece.astype(jnp.bfloat16), "wide", scatter_dimension=1, tiled=True
        ).astype(jnp.float32),
        lax.psum_scatter(
            up_piece.astype(jnp.bfloat16), "wide", scatter_dimension=0, tiled=True
        ).astype(jnp.float32),
        lax.psum_scatter(
            down_piece.astype(jnp.bfloat16), "wide", scatter_dimension=1, tiled=True
        ).astype(jnp.float32),
    )


def add_terms(earlier, latest):
    if earlier is None:
        return latest
    return jax.tree.map(jnp.add, earlier, latest)


def norm_forward(stream, gain, shift, full_width):
    first_terms, second_terms = row_totals(
        jnp.sum(stream, axis=1), jnp.sum(stream * stream, axis=1)
    )
    row_mean = first_terms / full_width
    inverse_std = lax.rsqrt(second_terms / full_width - row_mean * row_mean + norm_eps)
    centred = (stream - row_mean[:, None]) * inverse_std[:, None]
    return (centred * gain + shift, centred, inverse_std)


def norm_backward(upstream, centred, inverse_std, gain, full_width):
    scaled = upstream * gain
    first_terms, second_terms = row_totals(
        jnp.sum(scaled, axis=1), jnp.sum(scaled * centred, axis=1)
    )
    return inverse_std[:, None] * (
        scaled - first_terms[:, None] / full_width - centred * (second_terms[:, None] / full_width)
    )


def attention_forward(queries, keys_here, values_here, image_count, heads_here):
    score_scale = HEAD_DIM ** (-0.5)
    shape_four = (image_count, SEQ, heads_here, HEAD_DIM)
    query_four = queries.reshape(shape_four)
    key_four = keys_here.reshape(shape_four)
    value_four = values_here.reshape(shape_four)
    scores = (
        jnp.einsum("iqhd,ikhd->ihqk", query_four, key_four, preferred_element_type=jnp.float32)
        * score_scale
    )
    row_peak = jnp.max(scores, axis=-1, keepdims=True)
    exponent = jnp.exp(scores - row_peak)
    row_total = jnp.sum(exponent, axis=-1, keepdims=True)
    weights_soft = (exponent / row_total).astype(jnp.bfloat16)
    mixed_heads = jnp.einsum(
        "ihqk,ikhd->iqhd", weights_soft, value_four, preferred_element_type=jnp.float32
    )
    log_total = row_peak[..., 0] + jnp.log(row_total[..., 0])
    return (mixed_heads.reshape(queries.shape).astype(jnp.bfloat16), log_total)


def attention_backward(
    queries, keys_here, values_here, log_total, mixed_grad, image_count, heads_here
):
    score_scale = HEAD_DIM ** (-0.5)
    shape_four = (image_count, SEQ, heads_here, HEAD_DIM)
    query_four = queries.reshape(shape_four)
    key_four = keys_here.reshape(shape_four)
    value_four = values_here.reshape(shape_four)
    grad_four = mixed_grad.reshape(shape_four)
    scores = (
        jnp.einsum("iqhd,ikhd->ihqk", query_four, key_four, preferred_element_type=jnp.float32)
        * score_scale
    )
    weights_soft = jnp.exp(scores - log_total[..., None])
    weight_grad = jnp.einsum(
        "iqhd,ikhd->ihqk", grad_four, value_four, preferred_element_type=jnp.float32
    )
    row_delta = jnp.sum(weight_grad * weights_soft, axis=-1, keepdims=True)
    score_grad = (weights_soft * (weight_grad - row_delta)).astype(jnp.bfloat16)
    query_grad = (
        jnp.einsum("ihqk,ikhd->iqhd", score_grad, key_four, preferred_element_type=jnp.float32)
        * score_scale
    )
    key_grad = (
        jnp.einsum("ihqk,iqhd->ikhd", score_grad, query_four, preferred_element_type=jnp.float32)
        * score_scale
    )
    value_grad = jnp.einsum(
        "ihqk,iqhd->ikhd",
        weights_soft.astype(jnp.bfloat16),
        grad_four,
        preferred_element_type=jnp.float32,
    )
    flat_shape = queries.shape
    return (
        query_grad.reshape(flat_shape),
        key_grad.reshape(flat_shape),
        value_grad.reshape(flat_shape),
    )


def gelu_slope(values):
    normal_cdf = 0.5 * (1.0 + lax.erf(values * 0.7071067811865476))
    return normal_cdf + values * jnp.exp(-0.5 * values * values) * 0.3989422804014327


def body(
    images,
    first_gain,
    first_shift,
    query_weight,
    key_weight,
    value_weight,
    query_bias,
    value_bias,
    out_weight,
    out_bias,
    second_gain,
    second_shift,
    up_weight,
    up_bias,
    down_weight,
    down_bias,
    cotangent,
):
    layer_count = query_weight.shape[0]
    feature_block = images.shape[1]
    tensor_count = lax.axis_size("tensor")
    full_width = feature_block * tensor_count
    heads_here = feature_block // HEAD_DIM
    tensor_place = lax.axis_index("tensor")
    micro_rows = images.shape[0] // MICRO
    image_count = micro_rows // SEQ

    def gain_share(param_table, layer_idx):
        return lax.dynamic_slice_in_dim(
            param_table[layer_idx], tensor_place * feature_block, feature_block
        )

    def layer_weights(layer_idx):
        return fetch_weights(
            query_weight[layer_idx],
            key_weight[layer_idx],
            value_weight[layer_idx],
            out_weight[layer_idx],
            up_weight[layer_idx],
            down_weight[layer_idx],
        )

    weight_sums = [None] * layer_count
    small_sums = [None] * layer_count
    activation_parts = []
    gradient_parts = []
    for micro_idx in range(MICRO):
        row_start = micro_idx * micro_rows
        stream = images[row_start : row_start + micro_rows].astype(jnp.float32)
        saved_state = []
        for layer_idx in range(layer_count):
            query_full, key_full, value_full, out_full, up_full, down_full = layer_weights(
                layer_idx
            )
            normed, centred_one, inverse_one = norm_forward(
                stream,
                gain_share(first_gain, layer_idx),
                gain_share(first_shift, layer_idx),
                full_width,
            )
            normed_full = full_rows(normed.astype(jnp.bfloat16))
            joined_weight = jnp.concatenate((query_full, key_full, value_full), axis=1)
            projected = jnp.dot(normed_full, joined_weight, preferred_element_type=jnp.float32)
            queries = (projected[:, :feature_block] + query_bias[layer_idx]).astype(jnp.bfloat16)
            keys_here = projected[:, feature_block : 2 * feature_block].astype(jnp.bfloat16)
            values_here = (projected[:, 2 * feature_block :] + value_bias[layer_idx]).astype(
                jnp.bfloat16
            )
            mixed_heads, log_total = attention_forward(
                queries, keys_here, values_here, image_count, heads_here
            )
            attention_sum = feature_total(
                jnp.dot(mixed_heads, out_full, preferred_element_type=jnp.float32)
            )
            after_attention = stream + attention_sum + out_bias[layer_idx]
            normed_two, centred_two, inverse_two = norm_forward(
                after_attention,
                gain_share(second_gain, layer_idx),
                gain_share(second_shift, layer_idx),
                full_width,
            )
            normed_two_full = full_rows(normed_two.astype(jnp.bfloat16))
            hidden_pre = (
                jnp.dot(normed_two_full, up_full, preferred_element_type=jnp.float32)
                + up_bias[layer_idx]
            )
            hidden = jax.nn.gelu(hidden_pre, approximate=False).astype(jnp.bfloat16)
            feedforward_sum = feature_total(
                jnp.dot(hidden, down_full, preferred_element_type=jnp.float32)
            )
            saved_state.append(
                (
                    centred_one,
                    inverse_one,
                    normed_full,
                    queries,
                    keys_here,
                    values_here,
                    mixed_heads,
                    log_total,
                    centred_two,
                    inverse_two,
                    normed_two_full,
                    hidden_pre,
                    hidden,
                )
            )
            stream = after_attention + feedforward_sum + down_bias[layer_idx]
        activation_parts.append(stream.astype(jnp.bfloat16))
        upstream = cotangent[row_start : row_start + micro_rows].astype(jnp.float32)
        for layer_idx in reversed(range(layer_count)):
            query_full, key_full, value_full, out_full, up_full, down_full = layer_weights(
                layer_idx
            )
            (
                centred_one,
                inverse_one,
                normed_full,
                queries,
                keys_here,
                values_here,
                mixed_heads,
                log_total,
                centred_two,
                inverse_two,
                normed_two_full,
                hidden_pre,
                hidden,
            ) = saved_state[layer_idx]
            down_bias_term = jnp.sum(upstream, axis=0)
            upstream_full = full_rows(upstream.astype(jnp.bfloat16))
            down_term = jnp.einsum(
                "rc,rd->cd", hidden, upstream_full, preferred_element_type=jnp.float32
            )
            hidden_grad = jnp.einsum(
                "rd,cd->rc", upstream_full, down_full, preferred_element_type=jnp.float32
            )
            pre_grad = (hidden_grad * gelu_slope(hidden_pre)).astype(jnp.bfloat16)
            up_bias_term = jnp.sum(pre_grad.astype(jnp.float32), axis=0)
            up_term = jnp.einsum(
                "rd,rc->dc", normed_two_full, pre_grad, preferred_element_type=jnp.float32
            )
            normed_two_grad = feature_total(
                jnp.einsum("rc,dc->rd", pre_grad, up_full, preferred_element_type=jnp.float32)
            )
            second_gain_term = jnp.sum(normed_two_grad * centred_two, axis=0)
            second_shift_term = jnp.sum(normed_two_grad, axis=0)
            upstream = upstream + norm_backward(
                normed_two_grad,
                centred_two,
                inverse_two,
                gain_share(second_gain, layer_idx),
                full_width,
            )
            out_bias_term = jnp.sum(upstream, axis=0)
            upstream_full = full_rows(upstream.astype(jnp.bfloat16))
            out_term = jnp.einsum(
                "rc,rd->cd", mixed_heads, upstream_full, preferred_element_type=jnp.float32
            )
            mixed_grad = jnp.einsum(
                "rd,cd->rc", upstream_full, out_full, preferred_element_type=jnp.float32
            ).astype(jnp.bfloat16)
            query_grad, key_grad, value_grad = attention_backward(
                queries, keys_here, values_here, log_total, mixed_grad, image_count, heads_here
            )
            joined_grad = jnp.concatenate((query_grad, key_grad, value_grad), axis=1).astype(
                jnp.bfloat16
            )
            joined_float = joined_grad.astype(jnp.float32)
            query_bias_term = jnp.sum(joined_float[:, :feature_block], axis=0)
            value_bias_term = jnp.sum(joined_float[:, 2 * feature_block :], axis=0)
            joined_term = jnp.einsum(
                "rd,rc->dc", normed_full, joined_grad, preferred_element_type=jnp.float32
            )
            joined_weight = jnp.concatenate((query_full, key_full, value_full), axis=1)
            normed_grad = feature_total(
                jnp.einsum(
                    "rc,dc->rd", joined_grad, joined_weight, preferred_element_type=jnp.float32
                )
            )
            first_gain_term = jnp.sum(normed_grad * centred_one, axis=0)
            first_shift_term = jnp.sum(normed_grad, axis=0)
            upstream = upstream + norm_backward(
                normed_grad, centred_one, inverse_one, gain_share(first_gain, layer_idx), full_width
            )
            query_term = joined_term[:, :feature_block]
            key_term = joined_term[:, feature_block : 2 * feature_block]
            value_term = joined_term[:, 2 * feature_block :]
            weight_sums[layer_idx] = add_terms(
                weight_sums[layer_idx],
                settle_grads(query_term, key_term, value_term, out_term, up_term, down_term),
            )
            small_sums[layer_idx] = add_terms(
                small_sums[layer_idx],
                (
                    query_bias_term,
                    value_bias_term,
                    out_bias_term,
                    up_bias_term,
                    down_bias_term,
                    first_gain_term,
                    first_shift_term,
                    second_gain_term,
                    second_shift_term,
                ),
            )
        gradient_parts.append(upstream)
    share_sets = []
    for layer_idx in range(layer_count):
        share_sets.append(weight_sums[layer_idx])
    weight_outputs = [
        jnp.stack([share_sets[layer_idx][entry_idx] for layer_idx in range(layer_count)])
        for entry_idx in range(6)
    ]
    small_stack = [
        jnp.stack([small_sums[layer_idx][entry_idx] for layer_idx in range(layer_count)])
        for entry_idx in range(9)
    ]
    widened = [
        lax.dynamic_update_slice_in_dim(
            jnp.zeros((layer_count, share_piece.shape[1] * tensor_count), jnp.float32),
            share_piece,
            tensor_place * share_piece.shape[1],
            1,
        )
        for share_piece in small_stack
    ]
    totals = lax.psum(
        (
            widened[0],
            widened[1],
            widened[2],
            widened[3],
            widened[4],
            widened[5],
            widened[6],
            widened[7],
            widened[8],
        ),
        ("wide", "tensor"),
    )
    activations = jnp.concatenate(activation_parts, axis=0)
    input_gradient = jnp.concatenate(gradient_parts, axis=0)
    return (
        activations,
        input_gradient,
        weight_outputs[0],
        weight_outputs[1],
        weight_outputs[2],
        weight_outputs[3],
        weight_outputs[4],
        weight_outputs[5],
        totals[0],
        totals[1],
        totals[2],
        totals[3],
        totals[4],
        totals[5],
        totals[6],
        totals[7],
        totals[8],
    )


MESH_IDS = pl.DeviceIdType.MESH
LOW = jnp.bfloat16
BLOCK = 64


def place():
    wide = lax.axis_index("wide")
    return (
        lax.div(wide, 4),
        lax.rem(lax.div(wide, 2), 2),
        lax.rem(wide, 2),
        lax.axis_index("tensor"),
    )


def neighbours():
    z, x, c, y = place()

    def at(z, x, c, y):
        return (z * 4 + x * 2 + c, y)

    return {
        "core": at(z, x, 1 - c, y),
        "x": at(z, 1 - x, c, y),
        "y": at(z, x, c, 1 - y),
        "z1": at(z + 1 - 2 * lax.rem(z, 2), x, c, y),
        "z2": at(lax.rem(z + 2, 4), x, c, y),
    }


LINKS = ("core", "x", "y", "z1", "z2")


def greet(partners):
    barrier = pltpu.get_barrier_semaphore()
    for link in LINKS:
        pl.semaphore_signal(barrier, inc=1, device_id=partners[link], device_id_type=MESH_IDS)
    pl.semaphore_wait(barrier, len(LINKS))


def gather_stages(z, x, c, y, width):
    share = width * 7 // 16
    part_a, part_b, part_c = pl.ds(0, share), pl.ds(share, share), pl.ds(2 * share, width - 2 * share)
    part_ab = pl.ds(0, 2 * share)
    all_rows = pl.ds(0, BLOCK)
    pair = pl.ds(lax.div(z, 2) * 2, 2)
    every_z, every_x, every_t = pl.ds(0, 4), pl.ds(0, 2), pl.ds(0, 2)
    far_x, far_y = 1 - x, 1 - y
    return (
        (
            ("z1", (y, z, x, c, all_rows, part_ab)),
            ("x", (y, z, x, c, all_rows, part_c)),
        ),
        (
            ("z2", (y, pair, x, c, all_rows, part_ab)),
            ("y", (y, z, every_x, c, all_rows, part_c)),
        ),
        (
            ("x", (y, every_z, x, c, all_rows, part_a)),
            ("y", (y, every_z, x, c, all_rows, part_b)),
            ("z1", (every_t, z, every_x, c, all_rows, part_c)),
            ("core", (y, every_z, x, c, all_rows, part_ab)),
        ),
        (
            ("y", (y, every_z, every_x, c, all_rows, part_a)),
            ("x", (every_t, every_z, x, c, all_rows, part_b)),
            ("z2", (every_t, pair, every_x, c, all_rows, part_c)),
            ("core", (y, every_z, far_x, c, all_rows, part_a)),
            ("core", (far_y, every_z, x, c, all_rows, part_b)),
        ),
        (
            ("core", (far_y, every_z, every_x, c, all_rows, part_a)),
            ("core", (every_t, every_z, far_x, c, all_rows, part_b)),
            ("core", (every_t, every_z, every_x, c, all_rows, part_c)),
        ),
    )


def gather_kernel(count, shard_ref, *rest):
    whole_refs = rest[:count]
    send_sem, recv_sem, local_sem = rest[count:]
    z, x, c, y = place()
    partners = neighbours()
    width = shard_ref.shape[2]
    stages = gather_stages(z, x, c, y, width)
    own = []
    for chunk in range(count):
        copy = pltpu.make_async_copy(
            shard_ref.at[chunk], whole_refs[chunk].at[y, z, x, c], local_sem.at[chunk]
        )
        copy.start()
        own.append(copy)
    greet(partners)
    flying = {}
    for tick in range(count + len(stages)):
        for stage_idx in range(len(stages), -1, -1):
            chunk = tick - stage_idx
            if chunk < 0 or chunk >= count:
                continue
            if stage_idx == 0:
                own[chunk].wait()
            for copy in flying.get((chunk, stage_idx - 1), ()):
                copy.wait_recv()
            if stage_idx == len(stages):
                continue
            started = []
            base = sum(len(stage) for stage in stages[:stage_idx])
            for entry, (link, index) in enumerate(stages[stage_idx]):
                copy = pltpu.make_async_remote_copy(
                    src_ref=whole_refs[chunk].at[index],
                    dst_ref=whole_refs[chunk].at[index],
                    send_sem=send_sem.at[chunk, base + entry],
                    recv_sem=recv_sem.at[chunk, base + entry],
                    device_id=partners[link],
                    device_id_type=MESH_IDS,
                )
                copy.start()
                started.append(copy)
            flying[(chunk, stage_idx)] = started
    for started in flying.values():
        for copy in started:
            copy.wait_send()


def gather_weights(shards):
    count, _, width = shards.shape
    copies = 16
    return pl.pallas_call(
        lambda *refs: gather_kernel(count, *refs),
        out_shape=[jax.ShapeDtypeStruct((2, 4, 2, 2, BLOCK, width), LOW)] * count,
        in_specs=[pl.BlockSpec(memory_space=pl.ANY)],
        out_specs=[pl.BlockSpec(memory_space=pl.ANY)] * count,
        scratch_shapes=[
            pltpu.SemaphoreType.DMA((count, copies)),
            pltpu.SemaphoreType.DMA((count, copies)),
            pltpu.SemaphoreType.DMA((count,)),
        ],
        compiler_params=pltpu.CompilerParams(collective_id=0, has_side_effects=True),
        name="gather_weights",
    )(shards)


def swap_tensor(block):
    return lax.ppermute(block, "tensor", [(0, 1), (1, 0)])


def in_order(own, other, y, axis):
    first = jnp.where(y == 0, own, other)
    second = jnp.where(y == 0, other, own)
    return jnp.concatenate((first, second), axis=axis)


def whole_norm(stream, gain, shift):
    row_mean = jnp.mean(stream, axis=1, keepdims=True)
    square_mean = jnp.mean(stream * stream, axis=1, keepdims=True)
    inverse_std = lax.rsqrt(square_mean - row_mean * row_mean + norm_eps)
    centred = (stream - row_mean) * inverse_std
    return (centred * gain + shift).astype(LOW), centred, inverse_std


def whole_norm_backward(upstream, centred, inverse_std, gain):
    scaled = upstream * gain
    return inverse_std * (
        scaled
        - jnp.mean(scaled, axis=1, keepdims=True)
        - centred * jnp.mean(scaled * centred, axis=1, keepdims=True)
    )


def dot_rows(left, right):
    return lax.dot_general(
        left, right, (((1,), (0,)), ((), ())), preferred_element_type=jnp.float32
    )


def dot_cols(left, right):
    return lax.dot_general(
        left, right, (((1,), (1,)), ((), ())), preferred_element_type=jnp.float32
    )


def dot_tokens(left, right):
    return lax.dot_general(
        left, right, (((0,), (0,)), ((), ())), preferred_element_type=jnp.float32
    )


def image_body(
    images,
    first_gain,
    first_shift,
    query_weight,
    key_weight,
    value_weight,
    query_bias,
    value_bias,
    out_weight,
    out_bias,
    second_gain,
    second_shift,
    up_weight,
    up_bias,
    down_weight,
    down_bias,
    cotangent,
):
    layers = query_weight.shape[0]
    half = images.shape[1]
    hidden_half = up_weight.shape[2]
    y = lax.axis_index("tensor")
    far = 1 - y

    out_turned = jnp.swapaxes(out_weight, 1, 2)
    down_turned = jnp.swapaxes(down_weight, 1, 2)
    mixed = jnp.concatenate((query_weight, key_weight, value_weight, out_turned), axis=2)
    shards = jnp.stack(
        [block[layer] for layer in range(layers) for block in (mixed, up_weight, down_turned)]
    )
    gathered = gather_weights(shards)
    gathered = [part.reshape(2, -1, part.shape[-1]) for part in gathered]

    tokens = jnp.stack((images.reshape(2, SEQ, half), cotangent.reshape(2, SEQ, half)))
    tokens = jnp.swapaxes(tokens, 0, 1)
    near_tokens = lax.dynamic_index_in_dim(tokens, y, 0, keepdims=False)
    far_tokens = swap_tensor(lax.dynamic_index_in_dim(tokens, far, 0, keepdims=False))
    tokens = in_order(near_tokens, far_tokens, y, 2)
    biases = jnp.concatenate((query_bias, value_bias, out_bias, down_bias, up_bias), axis=1)
    both = in_order(biases[None], swap_tensor(biases)[None], y, 0)

    def whole_bias(start, size, layer):
        return both[:, layer, start : start + size].reshape(1, -1).astype(jnp.float32)

    def row(table, layer):
        return table[layer][None].astype(jnp.float32)

    stream = tokens[0].astype(jnp.float32)
    saved = []
    for layer in range(layers):
        mixed_w, up_w, down_w = gathered[3 * layer : 3 * layer + 3]
        normed, centred, inverse = whole_norm(
            stream, row(first_gain, layer), row(first_shift, layer)
        )
        projected = [dot_rows(normed, mixed_w[t][:, : 3 * half]) for t in range(2)]
        queries = jnp.concatenate([p[:, :half] for p in projected], axis=1)
        keys_here = jnp.concatenate([p[:, half : 2 * half] for p in projected], axis=1)
        values_here = jnp.concatenate([p[:, 2 * half :] for p in projected], axis=1)
        queries = (queries + whole_bias(0, half, layer)).astype(LOW)
        keys_here = keys_here.astype(LOW)
        values_here = (values_here + whole_bias(half, half, layer)).astype(LOW)
        heads, log_total = attention_forward(
            queries, keys_here, values_here, 1, 2 * half // HEAD_DIM
        )
        attended = dot_cols(heads[:, :half], mixed_w[0][:, 3 * half :]) + dot_cols(
            heads[:, half:], mixed_w[1][:, 3 * half :]
        )
        middle = stream + attended + whole_bias(2 * half, half, layer)
        normed_two, centred_two, inverse_two = whole_norm(
            middle, row(second_gain, layer), row(second_shift, layer)
        )
        before = [dot_rows(normed_two, up_w[t]) for t in range(2)]
        before = [
            before[t] + both[t, layer, 4 * half :][None].astype(jnp.float32) for t in range(2)
        ]
        hidden = [jax.nn.gelu(b, approximate=False).astype(LOW) for b in before]
        fed = dot_cols(hidden[0], down_w[0]) + dot_cols(hidden[1], down_w[1])
        saved.append(
            (
                normed,
                centred,
                inverse,
                queries,
                keys_here,
                values_here,
                heads,
                log_total,
                normed_two,
                centred_two,
                inverse_two,
                before,
                hidden,
            )
        )
        stream = middle + fed + whole_bias(3 * half, half, layer)
    activations = stream.astype(LOW)

    upstream = tokens[1].astype(jnp.float32)
    small = [None] * layers
    owned = [None] * layers
    for layer in reversed(range(layers)):
        mixed_w, up_w, down_w = gathered[3 * layer : 3 * layer + 3]
        (
            normed,
            centred,
            inverse,
            queries,
            keys_here,
            values_here,
            heads,
            log_total,
            normed_two,
            centred_two,
            inverse_two,
            before,
            hidden,
        ) = saved[layer]
        down_bias_sum = jnp.sum(upstream, axis=0)
        upstream_low = upstream.astype(LOW)
        hidden_grad = [
            (dot_rows(upstream_low, down_w[t]) * gelu_slope(before[t])).astype(LOW)
            for t in range(2)
        ]
        up_bias_sum = [jnp.sum(g.astype(jnp.float32), axis=0) for g in hidden_grad]
        down_term = [dot_tokens(upstream_low, hidden[t]).astype(LOW) for t in range(2)]
        up_term = [dot_tokens(normed_two, hidden_grad[t]).astype(LOW) for t in range(2)]
        normed_two_grad = dot_cols(hidden_grad[0], up_w[0]) + dot_cols(hidden_grad[1], up_w[1])
        second_gain_sum = jnp.sum(normed_two_grad * centred_two, axis=0)
        second_shift_sum = jnp.sum(normed_two_grad, axis=0)
        upstream = upstream + whole_norm_backward(
            normed_two_grad, centred_two, inverse_two, row(second_gain, layer)
        )
        out_bias_sum = jnp.sum(upstream, axis=0)
        upstream_low = upstream.astype(LOW)
        heads_grad = jnp.concatenate(
            [dot_rows(upstream_low, mixed_w[t][:, 3 * half :]) for t in range(2)], axis=1
        ).astype(LOW)
        query_grad, key_grad, value_grad = attention_backward(
            queries, keys_here, values_here, log_total, heads_grad, 1, 2 * half // HEAD_DIM
        )
        query_grad = query_grad.astype(LOW)
        key_grad = key_grad.astype(LOW)
        value_grad = value_grad.astype(LOW)
        query_bias_sum = jnp.sum(query_grad.astype(jnp.float32), axis=0)
        value_bias_sum = jnp.sum(value_grad.astype(jnp.float32), axis=0)
        mixed_term = []
        normed_grad = 0.0
        for t in range(2):
            cols = slice(t * half, (t + 1) * half)
            joined = jnp.concatenate(
                (query_grad[:, cols], key_grad[:, cols], value_grad[:, cols]), axis=1
            )
            mixed_term.append(
                jnp.concatenate(
                    (
                        dot_tokens(normed, joined).astype(LOW),
                        dot_tokens(upstream_low, heads[:, cols]).astype(LOW),
                    ),
                    axis=1,
                )
            )
            normed_grad = normed_grad + dot_cols(joined, mixed_w[t][:, : 3 * half])
        first_gain_sum = jnp.sum(normed_grad * centred, axis=0)
        first_shift_sum = jnp.sum(normed_grad, axis=0)
        upstream = upstream + whole_norm_backward(
            normed_grad, centred, inverse, row(first_gain, layer)
        )
        small[layer] = jnp.concatenate(
            (
                query_bias_sum,
                value_bias_sum,
                out_bias_sum,
                up_bias_sum[0],
                up_bias_sum[1],
                down_bias_sum,
                first_gain_sum,
                first_shift_sum,
                second_gain_sum,
                second_shift_sum,
            )
        )
        owned[layer] = settle_whole((mixed_term, up_term, down_term))

    totals = lax.psum(jnp.stack(small), ("wide", "tensor"))
    width = 2 * half
    small_outs, at = [], 0
    for size in (width, width, width, 2 * hidden_half, width, width, width, width, width):
        small_outs.append(totals[:, at : at + size])
        at += size
    mixed_own, up_own, down_own = [
        jnp.stack([owned[layer][entry] for layer in range(layers)]) for entry in range(3)
    ]

    def to_owner(rows):
        parts = rows.reshape(SEQ, 2, half)
        near = lax.dynamic_index_in_dim(parts, y, 1, keepdims=False)
        moved = swap_tensor(lax.dynamic_index_in_dim(parts, far, 1, keepdims=False).astype(LOW))
        return in_order(near, moved.astype(near.dtype), y, 0)

    return (
        to_owner(activations),
        to_owner(upstream),
        mixed_own[:, :, :half],
        mixed_own[:, :, half : 2 * half],
        mixed_own[:, :, 2 * half : 3 * half],
        jnp.swapaxes(mixed_own[:, :, 3 * half :], 1, 2),
        up_own,
        jnp.swapaxes(down_own, 1, 2),
        *small_outs,
    )


def settle_whole(terms):
    mixed_term, up_term, down_term = terms
    whole = jnp.concatenate(
        [
            jnp.concatenate([term[t].reshape(16, 1, BLOCK, -1) for t in range(2)], axis=1)
            for term in (mixed_term, up_term, down_term)
        ],
        axis=3,
    )
    width = whole.shape[-1] // 3
    piece = lax.psum_scatter(
        whole.reshape(-1, whole.shape[-1]), ("wide", "tensor"), scatter_dimension=0, tiled=True
    ).astype(jnp.float32)
    return piece[:, :width], piece[:, width : 2 * width], piece[:, 2 * width :]


def solution(mesh):
    in_specs = (
        P("wide", "tensor"),
        P(),
        P(),
        P(None, "wide", "tensor"),
        P(None, "wide", "tensor"),
        P(None, "wide", "tensor"),
        P(None, "tensor"),
        P(None, "tensor"),
        P(None, "tensor", "wide"),
        P(None, "tensor"),
        P(),
        P(),
        P(None, "wide", "tensor"),
        P(None, "tensor"),
        P(None, "tensor", "wide"),
        P(None, "tensor"),
        P("wide", "tensor"),
    )
    out_specs = (
        P("wide", "tensor"),
        P("wide", "tensor"),
        P(None, "wide", "tensor"),
        P(None, "wide", "tensor"),
        P(None, "wide", "tensor"),
        P(None, "tensor", "wide"),
        P(None, "wide", "tensor"),
        P(None, "tensor", "wide"),
        P(),
        P(),
        P(),
        P(),
        P(),
        P(),
        P(),
        P(),
        P(),
    )
    chosen = body
    if mesh.shape["wide"] == 16 and mesh.shape["tensor"] == 2:
        chosen = image_body
    return jax.shard_map(
        chosen, mesh=mesh, in_specs=in_specs, out_specs=out_specs, check_vma=False
    )
```

```python
import jax
import jax.numpy as jnp
from jax import lax
from jax.experimental import pallas as pl
from jax.experimental.pallas import tpu as pltpu
from jax.sharding import PartitionSpec as P

HEAD_DIM = 64
SEQ = 577
MICRO = 2


norm_eps = 1e-06


def row_totals(first_terms, second_terms):
    return lax.psum((first_terms, second_terms), "tensor")


def full_rows(share_low):
    return lax.all_gather(share_low, "tensor", axis=1, tiled=True)


def feature_total(partial_sums):
    return lax.psum_scatter(
        partial_sums.astype(jnp.bfloat16), "tensor", scatter_dimension=1, tiled=True
    ).astype(jnp.float32)


def fetch_weights(query_block, key_block, value_block, out_block, up_block, down_block):
    return (
        lax.all_gather(query_block, "wide", axis=0, tiled=True),
        lax.all_gather(key_block, "wide", axis=0, tiled=True),
        lax.all_gather(value_block, "wide", axis=0, tiled=True),
        lax.all_gather(out_block, "wide", axis=1, tiled=True),
        lax.all_gather(up_block, "wide", axis=0, tiled=True),
        lax.all_gather(down_block, "wide", axis=1, tiled=True),
    )


def settle_grads(query_piece, key_piece, value_piece, out_piece, up_piece, down_piece):
    return (
        lax.psum_scatter(
            query_piece.astype(jnp.bfloat16), "wide", scatter_dimension=0, tiled=True
        ).astype(jnp.float32),
        lax.psum_scatter(
            key_piece.astype(jnp.bfloat16), "wide", scatter_dimension=0, tiled=True
        ).astype(jnp.float32),
        lax.psum_scatter(
            value_piece.astype(jnp.bfloat16), "wide", scatter_dimension=0, tiled=True
        ).astype(jnp.float32),
        lax.psum_scatter(
            out_piece.astype(jnp.bfloat16), "wide", scatter_dimension=1, tiled=True
        ).astype(jnp.float32),
        lax.psum_scatter(
            up_piece.astype(jnp.bfloat16), "wide", scatter_dimension=0, tiled=True
        ).astype(jnp.float32),
        lax.psum_scatter(
            down_piece.astype(jnp.bfloat16), "wide", scatter_dimension=1, tiled=True
        ).astype(jnp.float32),
    )


def add_terms(earlier, latest):
    if earlier is None:
        return latest
    return jax.tree.map(jnp.add, earlier, latest)


def norm_forward(stream, gain, shift, full_width):
    first_terms, second_terms = row_totals(
        jnp.sum(stream, axis=1), jnp.sum(stream * stream, axis=1)
    )
    row_mean = first_terms / full_width
    inverse_std = lax.rsqrt(second_terms / full_width - row_mean * row_mean + norm_eps)
    centred = (stream - row_mean[:, None]) * inverse_std[:, None]
    return (centred * gain + shift, centred, inverse_std)


def norm_backward(upstream, centred, inverse_std, gain, full_width):
    scaled = upstream * gain
    first_terms, second_terms = row_totals(
        jnp.sum(scaled, axis=1), jnp.sum(scaled * centred, axis=1)
    )
    return inverse_std[:, None] * (
        scaled - first_terms[:, None] / full_width - centred * (second_terms[:, None] / full_width)
    )


def attention_forward(queries, keys_here, values_here, image_count, heads_here):
    score_scale = HEAD_DIM ** (-0.5)
    shape_four = (image_count, SEQ, heads_here, HEAD_DIM)
    query_four = queries.reshape(shape_four)
    key_four = keys_here.reshape(shape_four)
    value_four = values_here.reshape(shape_four)
    scores = (
        jnp.einsum("iqhd,ikhd->ihqk", query_four, key_four, preferred_element_type=jnp.float32)
        * score_scale
    )
    row_peak = jnp.max(scores, axis=-1, keepdims=True)
    exponent = jnp.exp(scores - row_peak)
    row_total = jnp.sum(exponent, axis=-1, keepdims=True)
    weights_soft = (exponent / row_total).astype(jnp.bfloat16)
    mixed_heads = jnp.einsum(
        "ihqk,ikhd->iqhd", weights_soft, value_four, preferred_element_type=jnp.float32
    )
    log_total = row_peak[..., 0] + jnp.log(row_total[..., 0])
    return (mixed_heads.reshape(queries.shape).astype(jnp.bfloat16), log_total)


def attention_backward(
    queries, keys_here, values_here, log_total, mixed_grad, image_count, heads_here
):
    score_scale = HEAD_DIM ** (-0.5)
    shape_four = (image_count, SEQ, heads_here, HEAD_DIM)
    query_four = queries.reshape(shape_four)
    key_four = keys_here.reshape(shape_four)
    value_four = values_here.reshape(shape_four)
    grad_four = mixed_grad.reshape(shape_four)
    scores = (
        jnp.einsum("iqhd,ikhd->ihqk", query_four, key_four, preferred_element_type=jnp.float32)
        * score_scale
    )
    weights_soft = jnp.exp(scores - log_total[..., None])
    weight_grad = jnp.einsum(
        "iqhd,ikhd->ihqk", grad_four, value_four, preferred_element_type=jnp.float32
    )
    row_delta = jnp.sum(weight_grad * weights_soft, axis=-1, keepdims=True)
    score_grad = (weights_soft * (weight_grad - row_delta)).astype(jnp.bfloat16)
    query_grad = (
        jnp.einsum("ihqk,ikhd->iqhd", score_grad, key_four, preferred_element_type=jnp.float32)
        * score_scale
    )
    key_grad = (
        jnp.einsum("ihqk,iqhd->ikhd", score_grad, query_four, preferred_element_type=jnp.float32)
        * score_scale
    )
    value_grad = jnp.einsum(
        "ihqk,iqhd->ikhd",
        weights_soft.astype(jnp.bfloat16),
        grad_four,
        preferred_element_type=jnp.float32,
    )
    flat_shape = queries.shape
    return (
        query_grad.reshape(flat_shape),
        key_grad.reshape(flat_shape),
        value_grad.reshape(flat_shape),
    )


def gelu_slope(values):
    normal_cdf = 0.5 * (1.0 + lax.erf(values * 0.7071067811865476))
    return normal_cdf + values * jnp.exp(-0.5 * values * values) * 0.3989422804014327


def body(
    images,
    first_gain,
    first_shift,
    query_weight,
    key_weight,
    value_weight,
    query_bias,
    value_bias,
    out_weight,
    out_bias,
    second_gain,
    second_shift,
    up_weight,
    up_bias,
    down_weight,
    down_bias,
    cotangent,
):
    layer_count = query_weight.shape[0]
    feature_block = images.shape[1]
    tensor_count = lax.axis_size("tensor")
    full_width = feature_block * tensor_count
    heads_here = feature_block // HEAD_DIM
    tensor_place = lax.axis_index("tensor")
    micro_rows = images.shape[0] // MICRO
    image_count = micro_rows // SEQ

    def gain_share(param_table, layer_idx):
        return lax.dynamic_slice_in_dim(
            param_table[layer_idx], tensor_place * feature_block, feature_block
        )

    def layer_weights(layer_idx):
        return fetch_weights(
            query_weight[layer_idx],
            key_weight[layer_idx],
            value_weight[layer_idx],
            out_weight[layer_idx],
            up_weight[layer_idx],
            down_weight[layer_idx],
        )

    weight_sums = [None] * layer_count
    small_sums = [None] * layer_count
    activation_parts = []
    gradient_parts = []
    for micro_idx in range(MICRO):
        row_start = micro_idx * micro_rows
        stream = images[row_start : row_start + micro_rows].astype(jnp.float32)
        saved_state = []
        for layer_idx in range(layer_count):
            query_full, key_full, value_full, out_full, up_full, down_full = layer_weights(
                layer_idx
            )
            normed, centred_one, inverse_one = norm_forward(
                stream,
                gain_share(first_gain, layer_idx),
                gain_share(first_shift, layer_idx),
                full_width,
            )
            normed_full = full_rows(normed.astype(jnp.bfloat16))
            joined_weight = jnp.concatenate((query_full, key_full, value_full), axis=1)
            projected = jnp.dot(normed_full, joined_weight, preferred_element_type=jnp.float32)
            queries = (projected[:, :feature_block] + query_bias[layer_idx]).astype(jnp.bfloat16)
            keys_here = projected[:, feature_block : 2 * feature_block].astype(jnp.bfloat16)
            values_here = (projected[:, 2 * feature_block :] + value_bias[layer_idx]).astype(
                jnp.bfloat16
            )
            mixed_heads, log_total = attention_forward(
                queries, keys_here, values_here, image_count, heads_here
            )
            attention_sum = feature_total(
                jnp.dot(mixed_heads, out_full, preferred_element_type=jnp.float32)
            )
            after_attention = stream + attention_sum + out_bias[layer_idx]
            normed_two, centred_two, inverse_two = norm_forward(
                after_attention,
                gain_share(second_gain, layer_idx),
                gain_share(second_shift, layer_idx),
                full_width,
            )
            normed_two_full = full_rows(normed_two.astype(jnp.bfloat16))
            hidden_pre = (
                jnp.dot(normed_two_full, up_full, preferred_element_type=jnp.float32)
                + up_bias[layer_idx]
            )
            hidden = jax.nn.gelu(hidden_pre, approximate=False).astype(jnp.bfloat16)
            feedforward_sum = feature_total(
                jnp.dot(hidden, down_full, preferred_element_type=jnp.float32)
            )
            saved_state.append(
                (
                    centred_one,
                    inverse_one,
                    normed_full,
                    queries,
                    keys_here,
                    values_here,
                    mixed_heads,
                    log_total,
                    centred_two,
                    inverse_two,
                    normed_two_full,
                    hidden_pre,
                    hidden,
                )
            )
            stream = after_attention + feedforward_sum + down_bias[layer_idx]
        activation_parts.append(stream.astype(jnp.bfloat16))
        upstream = cotangent[row_start : row_start + micro_rows].astype(jnp.float32)
        for layer_idx in reversed(range(layer_count)):
            query_full, key_full, value_full, out_full, up_full, down_full = layer_weights(
                layer_idx
            )
            (
                centred_one,
                inverse_one,
                normed_full,
                queries,
                keys_here,
                values_here,
                mixed_heads,
                log_total,
                centred_two,
                inverse_two,
                normed_two_full,
                hidden_pre,
                hidden,
            ) = saved_state[layer_idx]
            down_bias_term = jnp.sum(upstream, axis=0)
            upstream_full = full_rows(upstream.astype(jnp.bfloat16))
            down_term = jnp.einsum(
                "rc,rd->cd", hidden, upstream_full, preferred_element_type=jnp.float32
            )
            hidden_grad = jnp.einsum(
                "rd,cd->rc", upstream_full, down_full, preferred_element_type=jnp.float32
            )
            pre_grad = (hidden_grad * gelu_slope(hidden_pre)).astype(jnp.bfloat16)
            up_bias_term = jnp.sum(pre_grad.astype(jnp.float32), axis=0)
            up_term = jnp.einsum(
                "rd,rc->dc", normed_two_full, pre_grad, preferred_element_type=jnp.float32
            )
            normed_two_grad = feature_total(
                jnp.einsum("rc,dc->rd", pre_grad, up_full, preferred_element_type=jnp.float32)
            )
            second_gain_term = jnp.sum(normed_two_grad * centred_two, axis=0)
            second_shift_term = jnp.sum(normed_two_grad, axis=0)
            upstream = upstream + norm_backward(
                normed_two_grad,
                centred_two,
                inverse_two,
                gain_share(second_gain, layer_idx),
                full_width,
            )
            out_bias_term = jnp.sum(upstream, axis=0)
            upstream_full = full_rows(upstream.astype(jnp.bfloat16))
            out_term = jnp.einsum(
                "rc,rd->cd", mixed_heads, upstream_full, preferred_element_type=jnp.float32
            )
            mixed_grad = jnp.einsum(
                "rd,cd->rc", upstream_full, out_full, preferred_element_type=jnp.float32
            ).astype(jnp.bfloat16)
            query_grad, key_grad, value_grad = attention_backward(
                queries, keys_here, values_here, log_total, mixed_grad, image_count, heads_here
            )
            joined_grad = jnp.concatenate((query_grad, key_grad, value_grad), axis=1).astype(
                jnp.bfloat16
            )
            joined_float = joined_grad.astype(jnp.float32)
            query_bias_term = jnp.sum(joined_float[:, :feature_block], axis=0)
            value_bias_term = jnp.sum(joined_float[:, 2 * feature_block :], axis=0)
            joined_term = jnp.einsum(
                "rd,rc->dc", normed_full, joined_grad, preferred_element_type=jnp.float32
            )
            joined_weight = jnp.concatenate((query_full, key_full, value_full), axis=1)
            normed_grad = feature_total(
                jnp.einsum(
                    "rc,dc->rd", joined_grad, joined_weight, preferred_element_type=jnp.float32
                )
            )
            first_gain_term = jnp.sum(normed_grad * centred_one, axis=0)
            first_shift_term = jnp.sum(normed_grad, axis=0)
            upstream = upstream + norm_backward(
                normed_grad, centred_one, inverse_one, gain_share(first_gain, layer_idx), full_width
            )
            query_term = joined_term[:, :feature_block]
            key_term = joined_term[:, feature_block : 2 * feature_block]
            value_term = joined_term[:, 2 * feature_block :]
            weight_sums[layer_idx] = add_terms(
                weight_sums[layer_idx],
                settle_grads(query_term, key_term, value_term, out_term, up_term, down_term),
            )
            small_sums[layer_idx] = add_terms(
                small_sums[layer_idx],
                (
                    query_bias_term,
                    value_bias_term,
                    out_bias_term,
                    up_bias_term,
                    down_bias_term,
                    first_gain_term,
                    first_shift_term,
                    second_gain_term,
                    second_shift_term,
                ),
            )
        gradient_parts.append(upstream)
    share_sets = []
    for layer_idx in range(layer_count):
        share_sets.append(weight_sums[layer_idx])
    weight_outputs = [
        jnp.stack([share_sets[layer_idx][entry_idx] for layer_idx in range(layer_count)])
        for entry_idx in range(6)
    ]
    small_stack = [
        jnp.stack([small_sums[layer_idx][entry_idx] for layer_idx in range(layer_count)])
        for entry_idx in range(9)
    ]
    widened = [
        lax.dynamic_update_slice_in_dim(
            jnp.zeros((layer_count, share_piece.shape[1] * tensor_count), jnp.float32),
            share_piece,
            tensor_place * share_piece.shape[1],
            1,
        )
        for share_piece in small_stack
    ]
    totals = lax.psum(
        (
            widened[0],
            widened[1],
            widened[2],
            widened[3],
            widened[4],
            widened[5],
            widened[6],
            widened[7],
            widened[8],
        ),
        ("wide", "tensor"),
    )
    activations = jnp.concatenate(activation_parts, axis=0)
    input_gradient = jnp.concatenate(gradient_parts, axis=0)
    return (
        activations,
        input_gradient,
        weight_outputs[0],
        weight_outputs[1],
        weight_outputs[2],
        weight_outputs[3],
        weight_outputs[4],
        weight_outputs[5],
        totals[0],
        totals[1],
        totals[2],
        totals[3],
        totals[4],
        totals[5],
        totals[6],
        totals[7],
        totals[8],
    )


MESH_IDS = pl.DeviceIdType.MESH
LOW = jnp.bfloat16
BLOCK = 64


def place():
    wide = lax.axis_index("wide")
    return (
        lax.div(wide, 4),
        lax.rem(lax.div(wide, 2), 2),
        lax.rem(wide, 2),
        lax.axis_index("tensor"),
    )


def neighbours():
    z, x, c, y = place()

    def at(z, x, c, y):
        return (z * 4 + x * 2 + c, y)

    return {
        "core": at(z, x, 1 - c, y),
        "x": at(z, 1 - x, c, y),
        "y": at(z, x, c, 1 - y),
        "z1": at(z + 1 - 2 * lax.rem(z, 2), x, c, y),
        "z2": at(lax.rem(z + 2, 4), x, c, y),
    }


LINKS = ("core", "x", "y", "z1", "z2")


def greet(partners):
    barrier = pltpu.get_barrier_semaphore()
    for link in LINKS:
        pl.semaphore_signal(barrier, inc=1, device_id=partners[link], device_id_type=MESH_IDS)
    pl.semaphore_wait(barrier, len(LINKS))


def gather_parts(width):
    last = 256 if width >= 1024 else 0
    share = (width - last) // 2
    return ((0, share), (share, share), (2 * share, last))


def gather_stages(z, x, c, y, width):
    (_, share), _, (last_at, last) = gather_parts(width)

    def cols(t, start, size):
        return pl.ds(pl.multiple_of(t * width + start, 128), size)

    all_rows = pl.ds(0, BLOCK)
    pair = pl.ds(lax.div(z, 2) * 2, 2)
    every_z, every_x = pl.ds(0, 4), pl.ds(0, 2)
    far_x, far_y = 1 - x, 1 - y

    def part_a(t):
        return cols(t, 0, share)

    def part_b(t):
        return cols(t, share, share)

    def part_ab(t):
        return cols(t, 0, 2 * share)

    def part_c(t):
        return cols(t, last_at, last)

    stages = [
        [("z1", (z, x, c, all_rows, part_ab(y)))],
        [("z2", (pair, x, c, all_rows, part_ab(y)))],
        [
            ("x", (every_z, x, c, all_rows, part_a(y))),
            ("y", (every_z, x, c, all_rows, part_b(y))),
            ("core", (every_z, x, c, all_rows, part_ab(y))),
        ],
        [
            ("y", (every_z, every_x, c, all_rows, part_a(y))),
            ("x", (every_z, x, c, all_rows, part_b(0))),
            ("x", (every_z, x, c, all_rows, part_b(1))),
            ("core", (every_z, far_x, c, all_rows, part_a(y))),
            ("core", (every_z, x, c, all_rows, part_b(far_y))),
        ],
        [
            ("core", (every_z, every_x, c, all_rows, part_a(far_y))),
            ("core", (every_z, far_x, c, all_rows, part_b(0))),
            ("core", (every_z, far_x, c, all_rows, part_b(1))),
        ],
    ]
    if last:
        stages[0].append(("x", (z, x, c, all_rows, part_c(y))))
        stages[1].append(("y", (z, every_x, c, all_rows, part_c(y))))
        for t in range(2):
            stages[2].append(("z1", (z, every_x, c, all_rows, part_c(t))))
            stages[3].append(("z2", (pair, every_x, c, all_rows, part_c(t))))
            stages[4].append(("core", (every_z, every_x, c, all_rows, part_c(t))))
    return stages


GATHER_COPIES = 21


def gather_kernel(layers, kinds, *refs):
    shard_refs = refs[:kinds]
    count = layers * kinds
    whole_refs = refs[kinds : kinds + count]
    send_sem, recv_sem, local_sem = refs[kinds + count :]
    z, x, c, y = place()
    partners = neighbours()
    own, plans = [], []
    for chunk in range(count):
        layer, kind = divmod(chunk, kinds)
        width = shard_refs[kind].shape[2]
        plans.append(gather_stages(z, x, c, y, width))
        mine = pl.ds(pl.multiple_of(y * width, 128), width)
        copy = pltpu.make_async_copy(
            shard_refs[kind].at[layer],
            whole_refs[chunk].at[z, x, c, pl.ds(0, BLOCK), mine],
            local_sem.at[chunk],
        )
        copy.start()
        own.append(copy)
    greet(partners)
    depth = len(plans[0])
    flying = {}
    for tick in range(count + depth):
        for stage_idx in range(depth, -1, -1):
            chunk = tick - stage_idx
            if chunk < 0 or chunk >= count:
                continue
            if stage_idx == 0:
                own[chunk].wait()
            for copy in flying.get((chunk, stage_idx - 1), ()):
                copy.wait_recv()
            if stage_idx == depth:
                continue
            started = []
            base = sum(len(stage) for stage in plans[chunk][:stage_idx])
            for entry, (link, index) in enumerate(plans[chunk][stage_idx]):
                copy = pltpu.make_async_remote_copy(
                    src_ref=whole_refs[chunk].at[index],
                    dst_ref=whole_refs[chunk].at[index],
                    send_sem=send_sem.at[chunk, base + entry],
                    recv_sem=recv_sem.at[chunk, base + entry],
                    device_id=partners[link],
                    device_id_type=MESH_IDS,
                )
                copy.start()
                started.append(copy)
            flying[(chunk, stage_idx)] = started
    for started in flying.values():
        for copy in started:
            copy.wait_send()


def gather_weights(shards):
    layers, kinds = shards[0].shape[0], len(shards)
    count = layers * kinds
    whole = pl.pallas_call(
        lambda *refs: gather_kernel(layers, kinds, *refs),
        out_shape=[
            jax.ShapeDtypeStruct((4, 2, 2, BLOCK, 2 * shards[chunk % kinds].shape[2]), LOW)
            for chunk in range(count)
        ],
        in_specs=[pl.BlockSpec(memory_space=pl.ANY)] * kinds,
        out_specs=[pl.BlockSpec(memory_space=pl.ANY)] * count,
        scratch_shapes=[
            pltpu.SemaphoreType.DMA((count, GATHER_COPIES)),
            pltpu.SemaphoreType.DMA((count, GATHER_COPIES)),
            pltpu.SemaphoreType.DMA((count,)),
        ],
        compiler_params=pltpu.CompilerParams(collective_id=0, has_side_effects=True),
        cost_estimate=pl.CostEstimate(
            flops=0, bytes_accessed=600 * 1024 * 1024, transcendentals=0
        ),
        name="gather_weights",
    )(*shards)
    return [
        [whole[layer * kinds + kind].reshape(1024, -1) for kind in range(kinds)]
        for layer in range(layers)
    ]


def dot_rows(left, right):
    return lax.dot_general(
        left, right, (((1,), (0,)), ((), ())), preferred_element_type=jnp.float32
    )


def dot_cols(left, right):
    return lax.dot_general(
        left, right, (((1,), (1,)), ((), ())), preferred_element_type=jnp.float32
    )


def dot_tokens(left, right):
    return lax.dot_general(
        left, right, (((0,), (0,)), ((), ())), preferred_element_type=jnp.float32
    )


PAIR = 2 * HEAD_DIM


def turned_softmax(keys_here, queries):
    scores = dot_cols(keys_here, queries)
    exponent = jnp.exp(scores - jnp.max(scores, axis=0, keepdims=True))
    return exponent * (1.0 / jnp.sum(exponent, axis=0, keepdims=True))


def heads_kernel(query_a, key_a, value_a, query_b, key_b, value_b, mixed_ref):
    step = pl.program_id(0)
    scale = jnp.asarray(HEAD_DIM**-0.5, LOW)
    half_width = mixed_ref.shape[1] // 2
    for t, (query_ref, key_ref, value_ref) in enumerate(
        ((query_a, key_a, value_a), (query_b, key_b, value_b))
    ):
        pieces = []
        for head in range(2):
            cols = slice(head * HEAD_DIM, (head + 1) * HEAD_DIM)
            soft = turned_softmax(key_ref[:, cols], query_ref[:, cols] * scale)
            pieces.append(dot_tokens(soft.astype(LOW), value_ref[:, cols]).astype(LOW))
        at = pl.multiple_of(t * half_width + step * PAIR, PAIR)
        mixed_ref[:, pl.ds(at, PAIR)] = jnp.concatenate(pieces, axis=1)


def projected_specs(blocks):
    def spec(offset):
        return pl.BlockSpec((SEQ, PAIR), lambda step: (0, offset + step))

    return [spec(t * 3 * blocks + part * blocks) for t in range(2) for part in range(3)]


def mix_heads(projected):
    width = projected.shape[1] // 3
    blocks = width // 2 // PAIR
    return pl.pallas_call(
        heads_kernel,
        grid=(blocks,),
        in_specs=projected_specs(blocks),
        out_specs=pl.BlockSpec((SEQ, width), lambda step: (0, 0)),
        out_shape=jax.ShapeDtypeStruct((SEQ, width), LOW),
        compiler_params=pltpu.CompilerParams(vmem_limit_bytes=40 * 1024 * 1024),
        cost_estimate=pl.CostEstimate(
            flops=4 * SEQ * SEQ * width, bytes_accessed=45 * 1024 * 1024, transcendentals=0
        ),
        name="mix_heads",
    )(*[projected] * 6)


def heads_backward_kernel(
    query_a, key_a, value_a, query_b, key_b, value_b, grad_a, grad_b, out_ref
):
    step = pl.program_id(0)
    scale = jnp.asarray(HEAD_DIM**-0.5, LOW)
    part_width = out_ref.shape[1] // 6
    for t, (query_ref, key_ref, value_ref, grad_ref) in enumerate(
        ((query_a, key_a, value_a, grad_a), (query_b, key_b, value_b, grad_b))
    ):
        pieces = ([], [], [])
        for head in range(2):
            cols = slice(head * HEAD_DIM, (head + 1) * HEAD_DIM)
            keys_here, values_here = key_ref[:, cols], value_ref[:, cols]
            grads = grad_ref[:, cols]
            queries = query_ref[:, cols] * scale
            soft = turned_softmax(keys_here, queries)
            soft_grad = dot_cols(values_here, grads)
            delta = jnp.sum(soft_grad * soft, axis=0, keepdims=True)
            score_grad = (soft * (soft_grad - delta)).astype(LOW)
            pieces[0].append((dot_tokens(score_grad, keys_here) * HEAD_DIM**-0.5).astype(LOW))
            pieces[1].append(dot_rows(score_grad, queries).astype(LOW))
            pieces[2].append(dot_rows(soft.astype(LOW), grads).astype(LOW))
        for part in range(3):
            at = pl.multiple_of((t * 3 + part) * part_width + step * PAIR, PAIR)
            out_ref[:, pl.ds(at, PAIR)] = jnp.concatenate(pieces[part], axis=1)


def mix_heads_backward(projected, mixed_grad):
    width = mixed_grad.shape[1]
    blocks = width // 2 // PAIR

    def grad_spec(offset):
        return pl.BlockSpec((SEQ, PAIR), lambda step: (0, offset + step))

    return pl.pallas_call(
        heads_backward_kernel,
        grid=(blocks,),
        in_specs=projected_specs(blocks) + [grad_spec(0), grad_spec(blocks)],
        out_specs=pl.BlockSpec((SEQ, 3 * width), lambda step: (0, 0)),
        out_shape=jax.ShapeDtypeStruct((SEQ, 3 * width), LOW),
        compiler_params=pltpu.CompilerParams(vmem_limit_bytes=48 * 1024 * 1024),
        cost_estimate=pl.CostEstimate(
            flops=10 * SEQ * SEQ * width, bytes_accessed=90 * 1024 * 1024, transcendentals=0
        ),
        name="mix_heads_backward",
    )(*[projected] * 6, mixed_grad, mixed_grad)


def swap_link(block, link):
    if link == "y":
        return lax.ppermute(block, "tensor", [(0, 1), (1, 0)])
    flip = {"core": 1, "x": 2, "z1": 4, "z2": 8}[link]
    return lax.ppermute(block, "wide", [(i, i ^ flip) for i in range(16)])


def pick(block, at, axis):
    return lax.dynamic_index_in_dim(block, at, axis, keepdims=False)


def add_low(left, right):
    return (left.astype(jnp.float32) + right.astype(jnp.float32)).astype(LOW)


def settle(left, right, first_link):
    z, x, c, y = place()
    right = right.reshape(SEQ, 2, 2, -1)
    cols = right.shape[-1]
    if first_link == "y":

        def product(far, core):
            picked = pick(pick(right, 1 - y if far else y, 1), core, 1)
            return dot_tokens(left, picked)

    else:
        left = left.reshape(SEQ, 4, 2, 128)

        def product(far, core):
            rows = pick(left, 1 - x if far else x, 2).reshape(SEQ, 512)
            picked = pick(right, core, 2).reshape(SEQ, 2 * cols)
            return dot_tokens(rows, picked)

    outgoing = [product(far, 1 - c).astype(LOW) for far in (True, False)]
    arrived = [swap_link(block, "core") for block in outgoing]
    far_sum = (product(True, c) + arrived[0].astype(jnp.float32)).astype(LOW)
    near_sum = (product(False, c) + arrived[1].astype(jnp.float32)).astype(LOW)
    kept = add_low(near_sum, swap_link(far_sum, first_link))
    if first_link == "y":
        kept = kept.reshape(4, 2, 128, cols)
        kept = add_low(pick(kept, x, 1), swap_link(pick(kept, 1 - x, 1), "x"))
    else:
        kept = kept.reshape(4, 128, 2, cols)
        kept = add_low(pick(kept, y, 2), swap_link(pick(kept, 1 - y, 2), "y"))
    return kept


def settle_along_z(kept):
    z, x, c, y = place()
    cols = kept.shape[-1]
    kept = kept.reshape(2, 2, 128, cols)
    high, lower = lax.div(z, 2), lax.rem(z, 2)
    kept = add_low(pick(kept, high, 0), swap_link(pick(kept, 1 - high, 0), "z2"))
    kept = add_low(pick(kept, lower, 0), swap_link(pick(kept, 1 - lower, 0), "z1"))
    kept = kept.reshape(2, BLOCK, cols)
    near, other = pick(kept, c, 0), swap_link(pick(kept, 1 - c, 0), "core")
    return in_order(near[None], other[None], c, 0)


def all_total(block):
    for link in ("core", "x", "y", "z1", "z2"):
        block = block + swap_link(block, link)
    return block


def in_order(own, other, index, axis):
    first = jnp.where(index == 0, own, other)
    second = jnp.where(index == 0, other, own)
    return jnp.concatenate((first, second), axis=axis)


def whole_norm(stream, gain, shift):
    row_mean = jnp.mean(stream, axis=1, keepdims=True)
    square_mean = jnp.mean(stream * stream, axis=1, keepdims=True)
    inverse_std = lax.rsqrt(square_mean - row_mean * row_mean + norm_eps)
    centred = (stream - row_mean) * inverse_std
    return (centred * gain + shift).astype(LOW), centred, inverse_std


def whole_norm_backward(upstream, centred, inverse_std, gain):
    scaled = upstream * gain
    return inverse_std * (
        scaled
        - jnp.mean(scaled, axis=1, keepdims=True)
        - centred * jnp.mean(scaled * centred, axis=1, keepdims=True)
    )


def image_body(
    images,
    first_gain,
    first_shift,
    query_weight,
    key_weight,
    value_weight,
    query_bias,
    value_bias,
    out_weight,
    out_bias,
    second_gain,
    second_shift,
    up_weight,
    up_bias,
    down_weight,
    down_bias,
    cotangent,
):
    layers = query_weight.shape[0]
    half = images.shape[1]
    hidden_width = 2 * up_weight.shape[2]
    y = lax.axis_index("tensor")
    far = 1 - y

    whole = gather_weights(
        (
            jnp.concatenate((query_weight, key_weight, value_weight), axis=2),
            jnp.swapaxes(out_weight, 1, 2),
            up_weight,
            jnp.swapaxes(down_weight, 1, 2),
        )
    )

    tokens = jnp.stack((images.reshape(2, SEQ, half), cotangent.reshape(2, SEQ, half)))
    near_tokens = pick(tokens, y, 1)
    far_tokens = swap_link(pick(tokens, far, 1), "y")
    tokens = in_order(near_tokens, far_tokens, y, 2)
    biases = jnp.concatenate(
        (query_bias, jnp.zeros_like(query_bias), value_bias, out_bias, down_bias, up_bias), axis=1
    )
    both = in_order(biases[None], swap_link(biases, "y")[None], y, 0)

    def whole_bias(start, size, layer):
        return both[:, layer, start : start + size].reshape(1, -1).astype(jnp.float32)

    def row(table, layer):
        return table[layer][None].astype(jnp.float32)

    stream = tokens[0].astype(jnp.float32)
    saved = []
    for layer in range(layers):
        project_w, out_w, up_w, down_w = whole[layer]
        normed, centred, inverse = whole_norm(
            stream, row(first_gain, layer), row(first_shift, layer)
        )
        projected = (dot_rows(normed, project_w) + whole_bias(0, 3 * half, layer)).astype(LOW)
        heads = mix_heads(projected)
        middle = stream + dot_cols(heads, out_w) + whole_bias(3 * half, half, layer)
        normed_two, centred_two, inverse_two = whole_norm(
            middle, row(second_gain, layer), row(second_shift, layer)
        )
        before = dot_rows(normed_two, up_w) + whole_bias(5 * half, hidden_width // 2, layer)
        hidden = (before * (0.5 * (1.0 + lax.erf(before * 0.7071067811865476)))).astype(LOW)
        saved.append(
            (
                normed,
                centred,
                inverse,
                projected,
                heads,
                normed_two,
                centred_two,
                inverse_two,
                before,
                hidden,
            )
        )
        stream = middle + dot_cols(hidden, down_w) + whole_bias(4 * half, half, layer)
    activations = stream.astype(LOW)

    upstream = tokens[1].astype(jnp.float32)
    small = [None] * layers
    owned = [None] * layers
    for layer in reversed(range(layers)):
        project_w, out_w, up_w, down_w = whole[layer]
        (
            normed,
            centred,
            inverse,
            projected,
            heads,
            normed_two,
            centred_two,
            inverse_two,
            before,
            hidden,
        ) = saved[layer]
        down_bias_sum = jnp.sum(upstream, axis=0)
        upstream_low = upstream.astype(LOW)
        down_term = settle(upstream_low, hidden, "x")
        hidden_grad = (dot_rows(upstream_low, down_w) * gelu_slope(before)).astype(LOW)
        up_bias_sum = jnp.sum(hidden_grad.astype(jnp.float32), axis=0)
        up_term = settle(normed_two, hidden_grad, "y")
        normed_two_grad = dot_cols(hidden_grad, up_w)
        second_gain_sum = jnp.sum(normed_two_grad * centred_two, axis=0)
        second_shift_sum = jnp.sum(normed_two_grad, axis=0)
        upstream = upstream + whole_norm_backward(
            normed_two_grad, centred_two, inverse_two, row(second_gain, layer)
        )
        out_bias_sum = jnp.sum(upstream, axis=0)
        upstream_low = upstream.astype(LOW)
        out_term = settle(upstream_low, heads, "x")
        heads_grad = dot_rows(upstream_low, out_w).astype(LOW)
        joined = mix_heads_backward(projected, heads_grad)
        joined_sums = jnp.sum(joined.astype(jnp.float32), axis=0).reshape(2, 3, half)
        project_term = settle(normed, joined, "y")
        normed_grad = dot_cols(joined, project_w)
        first_gain_sum = jnp.sum(normed_grad * centred, axis=0)
        first_shift_sum = jnp.sum(normed_grad, axis=0)
        upstream = upstream + whole_norm_backward(
            normed_grad, centred, inverse, row(first_gain, layer)
        )
        small[layer] = all_total(
            jnp.concatenate(
                (
                    joined_sums[:, 0].reshape(-1),
                    joined_sums[:, 2].reshape(-1),
                    out_bias_sum,
                    up_bias_sum,
                    down_bias_sum,
                    first_gain_sum,
                    first_shift_sum,
                    second_gain_sum,
                    second_shift_sum,
                )
            )
        )
        feed_own = settle_along_z(jnp.concatenate((up_term, down_term), axis=2))
        mixed_own = settle_along_z(jnp.concatenate((project_term, out_term), axis=2))
        owned[layer] = (feed_own, mixed_own)

    totals = jnp.stack(small)
    width = 2 * half
    small_outs, at = [], 0
    for size in (width, width, width, hidden_width, width, width, width, width, width):
        small_outs.append(totals[:, at : at + size])
        at += size
    feed_own = jnp.stack([owned[layer][0] for layer in range(layers)])
    mixed_own = jnp.stack([owned[layer][1] for layer in range(layers)])

    def weight_out(pieces, start, size):
        block = jnp.swapaxes(pieces[..., start : start + size].astype(jnp.float32), 1, 2)
        return block.reshape(layers, BLOCK, 2 * size)

    quarter = hidden_width // 4
    project_out = weight_out(mixed_own, 0, 3 * half // 2)
    out_out = weight_out(mixed_own, 3 * half // 2, half // 2)
    up_out = weight_out(feed_own, 0, quarter)
    down_out = weight_out(feed_own, quarter, quarter)

    def to_owner(rows):
        parts = rows.reshape(SEQ, 2, half)
        near = pick(parts, y, 1)
        moved = swap_link(pick(parts, far, 1).astype(LOW), "y")
        return in_order(near, moved.astype(near.dtype), y, 0)

    return (
        to_owner(activations),
        to_owner(upstream),
        project_out[:, :, :half],
        project_out[:, :, half : 2 * half],
        project_out[:, :, 2 * half :],
        jnp.swapaxes(out_out, 1, 2),
        up_out,
        jnp.swapaxes(down_out, 1, 2),
        *small_outs,
    )


def solution(mesh):
    in_specs = (
        P("wide", "tensor"),
        P(),
        P(),
        P(None, "wide", "tensor"),
        P(None, "wide", "tensor"),
        P(None, "wide", "tensor"),
        P(None, "tensor"),
        P(None, "tensor"),
        P(None, "tensor", "wide"),
        P(None, "tensor"),
        P(),
        P(),
        P(None, "wide", "tensor"),
        P(None, "tensor"),
        P(None, "tensor", "wide"),
        P(None, "tensor"),
        P("wide", "tensor"),
    )
    out_specs = (
        P("wide", "tensor"),
        P("wide", "tensor"),
        P(None, "wide", "tensor"),
        P(None, "wide", "tensor"),
        P(None, "wide", "tensor"),
        P(None, "tensor", "wide"),
        P(None, "wide", "tensor"),
        P(None, "tensor", "wide"),
        P(),
        P(),
        P(),
        P(),
        P(),
        P(),
        P(),
        P(),
        P(),
    )
    chosen = body
    if mesh.shape["wide"] == 16 and mesh.shape["tensor"] == 2:
        chosen = image_body
    return jax.shard_map(
        chosen, mesh=mesh, in_specs=in_specs, out_specs=out_specs, check_vma=False
    )
```

```python
import jax
import jax.numpy as jnp
from jax import lax
from jax.experimental import pallas as pl
from jax.experimental.pallas import tpu as pltpu
from jax.sharding import PartitionSpec as P

HEAD_DIM = 64
SEQ = 577
MICRO = 2


norm_eps = 1e-06


def row_totals(first_terms, second_terms):
    return lax.psum((first_terms, second_terms), "tensor")


def full_rows(share_low):
    return lax.all_gather(share_low, "tensor", axis=1, tiled=True)


def feature_total(partial_sums):
    return lax.psum_scatter(
        partial_sums.astype(jnp.bfloat16), "tensor", scatter_dimension=1, tiled=True
    ).astype(jnp.float32)


def fetch_weights(query_block, key_block, value_block, out_block, up_block, down_block):
    return (
        lax.all_gather(query_block, "wide", axis=0, tiled=True),
        lax.all_gather(key_block, "wide", axis=0, tiled=True),
        lax.all_gather(value_block, "wide", axis=0, tiled=True),
        lax.all_gather(out_block, "wide", axis=1, tiled=True),
        lax.all_gather(up_block, "wide", axis=0, tiled=True),
        lax.all_gather(down_block, "wide", axis=1, tiled=True),
    )


def settle_grads(query_piece, key_piece, value_piece, out_piece, up_piece, down_piece):
    return (
        lax.psum_scatter(
            query_piece.astype(jnp.bfloat16), "wide", scatter_dimension=0, tiled=True
        ).astype(jnp.float32),
        lax.psum_scatter(
            key_piece.astype(jnp.bfloat16), "wide", scatter_dimension=0, tiled=True
        ).astype(jnp.float32),
        lax.psum_scatter(
            value_piece.astype(jnp.bfloat16), "wide", scatter_dimension=0, tiled=True
        ).astype(jnp.float32),
        lax.psum_scatter(
            out_piece.astype(jnp.bfloat16), "wide", scatter_dimension=1, tiled=True
        ).astype(jnp.float32),
        lax.psum_scatter(
            up_piece.astype(jnp.bfloat16), "wide", scatter_dimension=0, tiled=True
        ).astype(jnp.float32),
        lax.psum_scatter(
            down_piece.astype(jnp.bfloat16), "wide", scatter_dimension=1, tiled=True
        ).astype(jnp.float32),
    )


def add_terms(earlier, latest):
    if earlier is None:
        return latest
    return jax.tree.map(jnp.add, earlier, latest)


def norm_forward(stream, gain, shift, full_width):
    first_terms, second_terms = row_totals(
        jnp.sum(stream, axis=1), jnp.sum(stream * stream, axis=1)
    )
    row_mean = first_terms / full_width
    inverse_std = lax.rsqrt(second_terms / full_width - row_mean * row_mean + norm_eps)
    centred = (stream - row_mean[:, None]) * inverse_std[:, None]
    return (centred * gain + shift, centred, inverse_std)


def norm_backward(upstream, centred, inverse_std, gain, full_width):
    scaled = upstream * gain
    first_terms, second_terms = row_totals(
        jnp.sum(scaled, axis=1), jnp.sum(scaled * centred, axis=1)
    )
    return inverse_std[:, None] * (
        scaled - first_terms[:, None] / full_width - centred * (second_terms[:, None] / full_width)
    )


def attention_forward(queries, keys_here, values_here, image_count, heads_here):
    score_scale = HEAD_DIM ** (-0.5)
    shape_four = (image_count, SEQ, heads_here, HEAD_DIM)
    query_four = queries.reshape(shape_four)
    key_four = keys_here.reshape(shape_four)
    value_four = values_here.reshape(shape_four)
    scores = (
        jnp.einsum("iqhd,ikhd->ihqk", query_four, key_four, preferred_element_type=jnp.float32)
        * score_scale
    )
    row_peak = jnp.max(scores, axis=-1, keepdims=True)
    exponent = jnp.exp(scores - row_peak)
    row_total = jnp.sum(exponent, axis=-1, keepdims=True)
    weights_soft = (exponent / row_total).astype(jnp.bfloat16)
    mixed_heads = jnp.einsum(
        "ihqk,ikhd->iqhd", weights_soft, value_four, preferred_element_type=jnp.float32
    )
    log_total = row_peak[..., 0] + jnp.log(row_total[..., 0])
    return (mixed_heads.reshape(queries.shape).astype(jnp.bfloat16), log_total)


def attention_backward(
    queries, keys_here, values_here, log_total, mixed_grad, image_count, heads_here
):
    score_scale = HEAD_DIM ** (-0.5)
    shape_four = (image_count, SEQ, heads_here, HEAD_DIM)
    query_four = queries.reshape(shape_four)
    key_four = keys_here.reshape(shape_four)
    value_four = values_here.reshape(shape_four)
    grad_four = mixed_grad.reshape(shape_four)
    scores = (
        jnp.einsum("iqhd,ikhd->ihqk", query_four, key_four, preferred_element_type=jnp.float32)
        * score_scale
    )
    weights_soft = jnp.exp(scores - log_total[..., None])
    weight_grad = jnp.einsum(
        "iqhd,ikhd->ihqk", grad_four, value_four, preferred_element_type=jnp.float32
    )
    row_delta = jnp.sum(weight_grad * weights_soft, axis=-1, keepdims=True)
    score_grad = (weights_soft * (weight_grad - row_delta)).astype(jnp.bfloat16)
    query_grad = (
        jnp.einsum("ihqk,ikhd->iqhd", score_grad, key_four, preferred_element_type=jnp.float32)
        * score_scale
    )
    key_grad = (
        jnp.einsum("ihqk,iqhd->ikhd", score_grad, query_four, preferred_element_type=jnp.float32)
        * score_scale
    )
    value_grad = jnp.einsum(
        "ihqk,iqhd->ikhd",
        weights_soft.astype(jnp.bfloat16),
        grad_four,
        preferred_element_type=jnp.float32,
    )
    flat_shape = queries.shape
    return (
        query_grad.reshape(flat_shape),
        key_grad.reshape(flat_shape),
        value_grad.reshape(flat_shape),
    )


def gelu_slope(values):
    normal_cdf = 0.5 * (1.0 + lax.erf(values * 0.7071067811865476))
    return normal_cdf + values * jnp.exp(-0.5 * values * values) * 0.3989422804014327


def body(
    images,
    first_gain,
    first_shift,
    query_weight,
    key_weight,
    value_weight,
    query_bias,
    value_bias,
    out_weight,
    out_bias,
    second_gain,
    second_shift,
    up_weight,
    up_bias,
    down_weight,
    down_bias,
    cotangent,
):
    layer_count = query_weight.shape[0]
    feature_block = images.shape[1]
    tensor_count = lax.axis_size("tensor")
    full_width = feature_block * tensor_count
    heads_here = feature_block // HEAD_DIM
    tensor_place = lax.axis_index("tensor")
    micro_rows = images.shape[0] // MICRO
    image_count = micro_rows // SEQ

    def gain_share(param_table, layer_idx):
        return lax.dynamic_slice_in_dim(
            param_table[layer_idx], tensor_place * feature_block, feature_block
        )

    def layer_weights(layer_idx):
        return fetch_weights(
            query_weight[layer_idx],
            key_weight[layer_idx],
            value_weight[layer_idx],
            out_weight[layer_idx],
            up_weight[layer_idx],
            down_weight[layer_idx],
        )

    weight_sums = [None] * layer_count
    small_sums = [None] * layer_count
    activation_parts = []
    gradient_parts = []
    for micro_idx in range(MICRO):
        row_start = micro_idx * micro_rows
        stream = images[row_start : row_start + micro_rows].astype(jnp.float32)
        saved_state = []
        for layer_idx in range(layer_count):
            query_full, key_full, value_full, out_full, up_full, down_full = layer_weights(
                layer_idx
            )
            normed, centred_one, inverse_one = norm_forward(
                stream,
                gain_share(first_gain, layer_idx),
                gain_share(first_shift, layer_idx),
                full_width,
            )
            normed_full = full_rows(normed.astype(jnp.bfloat16))
            joined_weight = jnp.concatenate((query_full, key_full, value_full), axis=1)
            projected = jnp.dot(normed_full, joined_weight, preferred_element_type=jnp.float32)
            queries = (projected[:, :feature_block] + query_bias[layer_idx]).astype(jnp.bfloat16)
            keys_here = projected[:, feature_block : 2 * feature_block].astype(jnp.bfloat16)
            values_here = (projected[:, 2 * feature_block :] + value_bias[layer_idx]).astype(
                jnp.bfloat16
            )
            mixed_heads, log_total = attention_forward(
                queries, keys_here, values_here, image_count, heads_here
            )
            attention_sum = feature_total(
                jnp.dot(mixed_heads, out_full, preferred_element_type=jnp.float32)
            )
            after_attention = stream + attention_sum + out_bias[layer_idx]
            normed_two, centred_two, inverse_two = norm_forward(
                after_attention,
                gain_share(second_gain, layer_idx),
                gain_share(second_shift, layer_idx),
                full_width,
            )
            normed_two_full = full_rows(normed_two.astype(jnp.bfloat16))
            hidden_pre = (
                jnp.dot(normed_two_full, up_full, preferred_element_type=jnp.float32)
                + up_bias[layer_idx]
            )
            hidden = jax.nn.gelu(hidden_pre, approximate=False).astype(jnp.bfloat16)
            feedforward_sum = feature_total(
                jnp.dot(hidden, down_full, preferred_element_type=jnp.float32)
            )
            saved_state.append(
                (
                    centred_one,
                    inverse_one,
                    normed_full,
                    queries,
                    keys_here,
                    values_here,
                    mixed_heads,
                    log_total,
                    centred_two,
                    inverse_two,
                    normed_two_full,
                    hidden_pre,
                    hidden,
                )
            )
            stream = after_attention + feedforward_sum + down_bias[layer_idx]
        activation_parts.append(stream.astype(jnp.bfloat16))
        upstream = cotangent[row_start : row_start + micro_rows].astype(jnp.float32)
        for layer_idx in reversed(range(layer_count)):
            query_full, key_full, value_full, out_full, up_full, down_full = layer_weights(
                layer_idx
            )
            (
                centred_one,
                inverse_one,
                normed_full,
                queries,
                keys_here,
                values_here,
                mixed_heads,
                log_total,
                centred_two,
                inverse_two,
                normed_two_full,
                hidden_pre,
                hidden,
            ) = saved_state[layer_idx]
            down_bias_term = jnp.sum(upstream, axis=0)
            upstream_full = full_rows(upstream.astype(jnp.bfloat16))
            down_term = jnp.einsum(
                "rc,rd->cd", hidden, upstream_full, preferred_element_type=jnp.float32
            )
            hidden_grad = jnp.einsum(
                "rd,cd->rc", upstream_full, down_full, preferred_element_type=jnp.float32
            )
            pre_grad = (hidden_grad * gelu_slope(hidden_pre)).astype(jnp.bfloat16)
            up_bias_term = jnp.sum(pre_grad.astype(jnp.float32), axis=0)
            up_term = jnp.einsum(
                "rd,rc->dc", normed_two_full, pre_grad, preferred_element_type=jnp.float32
            )
            normed_two_grad = feature_total(
                jnp.einsum("rc,dc->rd", pre_grad, up_full, preferred_element_type=jnp.float32)
            )
            second_gain_term = jnp.sum(normed_two_grad * centred_two, axis=0)
            second_shift_term = jnp.sum(normed_two_grad, axis=0)
            upstream = upstream + norm_backward(
                normed_two_grad,
                centred_two,
                inverse_two,
                gain_share(second_gain, layer_idx),
                full_width,
            )
            out_bias_term = jnp.sum(upstream, axis=0)
            upstream_full = full_rows(upstream.astype(jnp.bfloat16))
            out_term = jnp.einsum(
                "rc,rd->cd", mixed_heads, upstream_full, preferred_element_type=jnp.float32
            )
            mixed_grad = jnp.einsum(
                "rd,cd->rc", upstream_full, out_full, preferred_element_type=jnp.float32
            ).astype(jnp.bfloat16)
            query_grad, key_grad, value_grad = attention_backward(
                queries, keys_here, values_here, log_total, mixed_grad, image_count, heads_here
            )
            joined_grad = jnp.concatenate((query_grad, key_grad, value_grad), axis=1).astype(
                jnp.bfloat16
            )
            joined_float = joined_grad.astype(jnp.float32)
            query_bias_term = jnp.sum(joined_float[:, :feature_block], axis=0)
            value_bias_term = jnp.sum(joined_float[:, 2 * feature_block :], axis=0)
            joined_term = jnp.einsum(
                "rd,rc->dc", normed_full, joined_grad, preferred_element_type=jnp.float32
            )
            joined_weight = jnp.concatenate((query_full, key_full, value_full), axis=1)
            normed_grad = feature_total(
                jnp.einsum(
                    "rc,dc->rd", joined_grad, joined_weight, preferred_element_type=jnp.float32
                )
            )
            first_gain_term = jnp.sum(normed_grad * centred_one, axis=0)
            first_shift_term = jnp.sum(normed_grad, axis=0)
            upstream = upstream + norm_backward(
                normed_grad, centred_one, inverse_one, gain_share(first_gain, layer_idx), full_width
            )
            query_term = joined_term[:, :feature_block]
            key_term = joined_term[:, feature_block : 2 * feature_block]
            value_term = joined_term[:, 2 * feature_block :]
            weight_sums[layer_idx] = add_terms(
                weight_sums[layer_idx],
                settle_grads(query_term, key_term, value_term, out_term, up_term, down_term),
            )
            small_sums[layer_idx] = add_terms(
                small_sums[layer_idx],
                (
                    query_bias_term,
                    value_bias_term,
                    out_bias_term,
                    up_bias_term,
                    down_bias_term,
                    first_gain_term,
                    first_shift_term,
                    second_gain_term,
                    second_shift_term,
                ),
            )
        gradient_parts.append(upstream)
    share_sets = []
    for layer_idx in range(layer_count):
        share_sets.append(weight_sums[layer_idx])
    weight_outputs = [
        jnp.stack([share_sets[layer_idx][entry_idx] for layer_idx in range(layer_count)])
        for entry_idx in range(6)
    ]
    small_stack = [
        jnp.stack([small_sums[layer_idx][entry_idx] for layer_idx in range(layer_count)])
        for entry_idx in range(9)
    ]
    widened = [
        lax.dynamic_update_slice_in_dim(
            jnp.zeros((layer_count, share_piece.shape[1] * tensor_count), jnp.float32),
            share_piece,
            tensor_place * share_piece.shape[1],
            1,
        )
        for share_piece in small_stack
    ]
    totals = lax.psum(
        (
            widened[0],
            widened[1],
            widened[2],
            widened[3],
            widened[4],
            widened[5],
            widened[6],
            widened[7],
            widened[8],
        ),
        ("wide", "tensor"),
    )
    activations = jnp.concatenate(activation_parts, axis=0)
    input_gradient = jnp.concatenate(gradient_parts, axis=0)
    return (
        activations,
        input_gradient,
        weight_outputs[0],
        weight_outputs[1],
        weight_outputs[2],
        weight_outputs[3],
        weight_outputs[4],
        weight_outputs[5],
        totals[0],
        totals[1],
        totals[2],
        totals[3],
        totals[4],
        totals[5],
        totals[6],
        totals[7],
        totals[8],
    )


MESH_IDS = pl.DeviceIdType.MESH
LOW = jnp.bfloat16
BLOCK = 64
ROWS = -(-SEQ // 16) * 16
DEEP = -(-SEQ // 128) * 128


def place():
    wide = lax.axis_index("wide")
    return (
        lax.div(wide, 4),
        lax.rem(lax.div(wide, 2), 2),
        lax.rem(wide, 2),
        lax.axis_index("tensor"),
    )


def neighbours():
    z, x, c, y = place()

    def at(z, x, c, y):
        return (z * 4 + x * 2 + c, y)

    return {
        "core": at(z, x, 1 - c, y),
        "x": at(z, 1 - x, c, y),
        "y": at(z, x, c, 1 - y),
        "z1": at(z + 1 - 2 * lax.rem(z, 2), x, c, y),
        "z2": at(lax.rem(z + 2, 4), x, c, y),
    }


LINKS = ("core", "x", "y", "z1", "z2")


def greet(partners):
    barrier = pltpu.get_barrier_semaphore()
    for link in LINKS:
        pl.semaphore_signal(barrier, inc=1, device_id=partners[link], device_id_type=MESH_IDS)
    pl.semaphore_wait(barrier, len(LINKS))


def gather_parts(width):
    last = 256 if width >= 1024 else 0
    share = (width - last) // 2
    return ((0, share), (share, share), (2 * share, last))


def gather_stages(z, x, c, y, width):
    (_, share), _, (last_at, last) = gather_parts(width)

    def cols(t, start, size):
        return pl.ds(pl.multiple_of(t * width + start, 128), size)

    all_rows = pl.ds(0, BLOCK)
    pair = pl.ds(lax.div(z, 2) * 2, 2)
    every_z, every_x = pl.ds(0, 4), pl.ds(0, 2)
    far_x, far_y = 1 - x, 1 - y

    def part_a(t):
        return cols(t, 0, share)

    def part_b(t):
        return cols(t, share, share)

    def part_ab(t):
        return cols(t, 0, 2 * share)

    def part_c(t):
        return cols(t, last_at, last)

    stages = [
        [("z1", (z, x, c, all_rows, part_ab(y)))],
        [("z2", (pair, x, c, all_rows, part_ab(y)))],
        [
            ("x", (every_z, x, c, all_rows, part_a(y))),
            ("y", (every_z, x, c, all_rows, part_b(y))),
            ("core", (every_z, x, c, all_rows, part_ab(y))),
        ],
        [
            ("y", (every_z, every_x, c, all_rows, part_a(y))),
            ("x", (every_z, x, c, all_rows, part_b(0))),
            ("x", (every_z, x, c, all_rows, part_b(1))),
            ("core", (every_z, far_x, c, all_rows, part_a(y))),
            ("core", (every_z, x, c, all_rows, part_b(far_y))),
        ],
        [
            ("core", (every_z, every_x, c, all_rows, part_a(far_y))),
            ("core", (every_z, far_x, c, all_rows, part_b(0))),
            ("core", (every_z, far_x, c, all_rows, part_b(1))),
        ],
    ]
    if last:
        stages[0].append(("x", (z, x, c, all_rows, part_c(y))))
        stages[1].append(("y", (z, every_x, c, all_rows, part_c(y))))
        for t in range(2):
            stages[2].append(("z1", (z, every_x, c, all_rows, part_c(t))))
            stages[3].append(("z2", (pair, every_x, c, all_rows, part_c(t))))
            stages[4].append(("core", (every_z, every_x, c, all_rows, part_c(t))))
    return stages


GATHER_COPIES = 21


def gather_kernel(layers, kinds, *refs):
    shard_refs = refs[:kinds]
    count = layers * kinds
    whole_refs = refs[kinds : kinds + count]
    send_sem, recv_sem, local_sem = refs[kinds + count :]
    z, x, c, y = place()
    partners = neighbours()
    own, plans = [], []
    for chunk in range(count):
        layer, kind = divmod(chunk, kinds)
        width = shard_refs[kind].shape[2]
        plans.append(gather_stages(z, x, c, y, width))
        mine = pl.ds(pl.multiple_of(y * width, 128), width)
        copy = pltpu.make_async_copy(
            shard_refs[kind].at[layer],
            whole_refs[chunk].at[z, x, c, pl.ds(0, BLOCK), mine],
            local_sem.at[chunk],
        )
        copy.start()
        own.append(copy)
    greet(partners)
    depth = len(plans[0])
    flying = {}
    for tick in range(count + depth):
        for stage_idx in range(depth, -1, -1):
            chunk = tick - stage_idx
            if chunk < 0 or chunk >= count:
                continue
            if stage_idx == 0:
                own[chunk].wait()
            for copy in flying.get((chunk, stage_idx - 1), ()):
                copy.wait_recv()
            if stage_idx == depth:
                continue
            started = []
            base = sum(len(stage) for stage in plans[chunk][:stage_idx])
            for entry, (link, index) in enumerate(plans[chunk][stage_idx]):
                copy = pltpu.make_async_remote_copy(
                    src_ref=whole_refs[chunk].at[index],
                    dst_ref=whole_refs[chunk].at[index],
                    send_sem=send_sem.at[chunk, base + entry],
                    recv_sem=recv_sem.at[chunk, base + entry],
                    device_id=partners[link],
                    device_id_type=MESH_IDS,
                )
                copy.start()
                started.append(copy)
            flying[(chunk, stage_idx)] = started
    for started in flying.values():
        for copy in started:
            copy.wait_send()


def gather_weights(shards):
    layers, kinds = shards[0].shape[0], len(shards)
    count = layers * kinds
    whole = pl.pallas_call(
        lambda *refs: gather_kernel(layers, kinds, *refs),
        out_shape=[
            jax.ShapeDtypeStruct((4, 2, 2, BLOCK, 2 * shards[chunk % kinds].shape[2]), LOW)
            for chunk in range(count)
        ],
        in_specs=[pl.BlockSpec(memory_space=pl.ANY)] * kinds,
        out_specs=[pl.BlockSpec(memory_space=pl.ANY)] * count,
        scratch_shapes=[
            pltpu.SemaphoreType.DMA((count, GATHER_COPIES)),
            pltpu.SemaphoreType.DMA((count, GATHER_COPIES)),
            pltpu.SemaphoreType.DMA((count,)),
        ],
        compiler_params=pltpu.CompilerParams(collective_id=0, has_side_effects=True),
        cost_estimate=pl.CostEstimate(
            flops=0, bytes_accessed=600 * 1024 * 1024, transcendentals=0
        ),
        name="gather_weights",
    )(*shards)
    return [
        [whole[layer * kinds + kind].reshape(1024, -1) for kind in range(kinds)]
        for layer in range(layers)
    ]


def dot_rows(left, right):
    return lax.dot_general(
        left, right, (((1,), (0,)), ((), ())), preferred_element_type=jnp.float32
    )


def dot_cols(left, right):
    return lax.dot_general(
        left, right, (((1,), (1,)), ((), ())), preferred_element_type=jnp.float32
    )


def dot_tokens(left, right):
    return lax.dot_general(
        left, right, (((0,), (0,)), ((), ())), preferred_element_type=jnp.float32
    )


PAIR = 2 * HEAD_DIM


def turned_softmax(keys_here, queries):
    scores = dot_cols(keys_here, queries)
    exponent = jnp.exp(scores - jnp.max(scores, axis=0, keepdims=True))
    return exponent * (1.0 / jnp.sum(exponent, axis=0, keepdims=True))


def store_rows(ref, at, pieces):
    full = SEQ // 16 * 16
    ref[pl.ds(full, ROWS - full), pl.ds(at, PAIR)] = jnp.zeros((ROWS - full, PAIR), LOW)
    ref[pl.ds(0, SEQ), pl.ds(at, PAIR)] = jnp.concatenate(pieces, axis=1)


def heads_kernel(query_a, key_a, value_a, query_b, key_b, value_b, mixed_ref):
    step = pl.program_id(0)
    scale = jnp.asarray(HEAD_DIM**-0.5, LOW)
    half_width = mixed_ref.shape[1] // 2
    for t, (query_ref, key_ref, value_ref) in enumerate(
        ((query_a, key_a, value_a), (query_b, key_b, value_b))
    ):
        pieces = []
        for head in range(2):
            cols = slice(head * HEAD_DIM, (head + 1) * HEAD_DIM)
            soft = turned_softmax(key_ref[:SEQ, cols], query_ref[:SEQ, cols] * scale)
            pieces.append(dot_tokens(soft.astype(LOW), value_ref[:SEQ, cols]).astype(LOW))
        at = pl.multiple_of(t * half_width + step * PAIR, PAIR)
        store_rows(mixed_ref, at, pieces)


def projected_specs(blocks):
    def spec(offset):
        return pl.BlockSpec((ROWS, PAIR), lambda step: (0, offset + step))

    return [spec(t * 3 * blocks + part * blocks) for t in range(2) for part in range(3)]


def mix_heads(projected):
    width = projected.shape[1] // 3
    blocks = width // 2 // PAIR
    return pl.pallas_call(
        heads_kernel,
        grid=(blocks,),
        in_specs=projected_specs(blocks),
        out_specs=pl.BlockSpec((ROWS, width), lambda step: (0, 0)),
        out_shape=jax.ShapeDtypeStruct((ROWS, width), LOW),
        compiler_params=pltpu.CompilerParams(vmem_limit_bytes=40 * 1024 * 1024),
        cost_estimate=pl.CostEstimate(
            flops=4 * SEQ * SEQ * width, bytes_accessed=45 * 1024 * 1024, transcendentals=0
        ),
        name="mix_heads",
    )(*[projected] * 6)


def heads_backward_kernel(
    query_a, key_a, value_a, query_b, key_b, value_b, grad_a, grad_b, out_ref
):
    step = pl.program_id(0)
    scale = jnp.asarray(HEAD_DIM**-0.5, LOW)
    part_width = out_ref.shape[1] // 6
    for t, (query_ref, key_ref, value_ref, grad_ref) in enumerate(
        ((query_a, key_a, value_a, grad_a), (query_b, key_b, value_b, grad_b))
    ):
        pieces = ([], [], [])
        for head in range(2):
            cols = slice(head * HEAD_DIM, (head + 1) * HEAD_DIM)
            keys_here, values_here = key_ref[:SEQ, cols], value_ref[:SEQ, cols]
            grads = grad_ref[:SEQ, cols]
            queries = query_ref[:SEQ, cols] * scale
            soft = turned_softmax(keys_here, queries)
            soft_grad = dot_cols(values_here, grads)
            delta = jnp.sum(soft_grad * soft, axis=0, keepdims=True)
            score_grad = (soft * (soft_grad - delta)).astype(LOW)
            pieces[0].append((dot_tokens(score_grad, keys_here) * HEAD_DIM**-0.5).astype(LOW))
            pieces[1].append(dot_rows(score_grad, queries).astype(LOW))
            pieces[2].append(dot_rows(soft.astype(LOW), grads).astype(LOW))
        for part in range(3):
            at = pl.multiple_of((t * 3 + part) * part_width + step * PAIR, PAIR)
            store_rows(out_ref, at, pieces[part])


def mix_heads_backward(projected, mixed_grad):
    width = mixed_grad.shape[1]
    blocks = width // 2 // PAIR

    def grad_spec(offset):
        return pl.BlockSpec((ROWS, PAIR), lambda step: (0, offset + step))

    return pl.pallas_call(
        heads_backward_kernel,
        grid=(blocks,),
        in_specs=projected_specs(blocks) + [grad_spec(0), grad_spec(blocks)],
        out_specs=pl.BlockSpec((ROWS, 3 * width), lambda step: (0, 0)),
        out_shape=jax.ShapeDtypeStruct((ROWS, 3 * width), LOW),
        compiler_params=pltpu.CompilerParams(vmem_limit_bytes=48 * 1024 * 1024),
        cost_estimate=pl.CostEstimate(
            flops=10 * SEQ * SEQ * width, bytes_accessed=90 * 1024 * 1024, transcendentals=0
        ),
        name="mix_heads_backward",
    )(*[projected] * 6, mixed_grad, mixed_grad)


def swap_link(block, link):
    if link == "y":
        return lax.ppermute(block, "tensor", [(0, 1), (1, 0)])
    flip = {"core": 1, "x": 2, "z1": 4, "z2": 8}[link]
    return lax.ppermute(block, "wide", [(i, i ^ flip) for i in range(16)])


def pick(block, at, axis):
    return lax.dynamic_index_in_dim(block, at, axis, keepdims=False)


COLS = 256
SETTLE_DEPTH = 6
VAL_SLOTS, ARRIVAL_SLOTS = 6, 3


class Settle:
    def __init__(self, widths, pairs):
        self.widths, self.pairs = widths, pairs

    def scratch(self):
        rows = (4, 2, 2, BLOCK, COLS)
        pairs, vals, slots = len(self.pairs), VAL_SLOTS, ARRIVAL_SLOTS
        sem = pltpu.SemaphoreType.DMA
        return dict(
            left_in=pltpu.VMEM((2, ROWS, 1024), LOW),
            left_turned=pltpu.VMEM((4, 1024, DEEP), LOW),
            right_in=pltpu.VMEM((2, 2, 4, DEEP, COLS), LOW),
            core_out=pltpu.VMEM((2, 2, 2, *rows), LOW),
            core_in=pltpu.VMEM((slots, 2, 2, *rows), LOW),
            val=pltpu.VMEM((vals, 2, 2, *rows), LOW),
            first_a=pltpu.VMEM((slots, *rows), LOW),
            first_b=pltpu.VMEM((slots, 2, 4, 2, BLOCK, COLS), LOW),
            second=pltpu.VMEM((slots, 2, 4, 2, BLOCK, COLS), LOW),
            third=pltpu.VMEM((slots, 2, 2, 2, BLOCK, COLS), LOW),
            fourth=pltpu.VMEM((slots, 2, 2, BLOCK, COLS), LOW),
            fifth=pltpu.VMEM((slots, 2, BLOCK, COLS), LOW),
            send_sem=sem((pairs, 2, SETTLE_DEPTH)),
            recv_sem=sem((pairs, 2, SETTLE_DEPTH)),
            right_sem=sem((pairs, 2, 4)),
            left_sem=sem((len(self.widths),)),
        )

    def bind(self, lefts, rights, outs, refs):
        self.lefts, self.rights, self.outs = lefts, rights, outs
        for name, ref in zip(self.scratch(), refs, strict=True):
            setattr(self, name, ref)
        self.z, self.x, self.c, self.y = place()
        self.partners = neighbours()
        self.copies = {}
        self.left_copies = {}
        self.turned = {}
        self.loaded = []
        tail = ROWS // 128 * 128
        self.left_turned[:, :, pl.ds(tail, DEEP - tail)] = jnp.zeros((4, 1024, DEEP - tail), LOW)
        self.right_in[:, :, :, pl.ds(ROWS, DEEP - ROWS)] = jnp.zeros(
            (2, 2, 4, DEEP - ROWS, COLS), LOW
        )

    def load(self, pair):
        if pair >= len(self.pairs):
            return
        for unit, (matrix, step) in enumerate(self.pairs[pair]):
            if matrix not in self.left_copies:
                copy = pltpu.make_async_copy(
                    self.lefts[matrix],
                    self.left_in.at[len(self.loaded) % 2],
                    self.left_sem.at[len(self.loaded)],
                )
                copy.start()
                self.left_copies[matrix] = (copy, len(self.loaded))
                self.loaded.append(matrix)
            width = self.widths[matrix]
            for t in range(2):
                for core in range(2):
                    at = t * width + core * (width // 2) + step * COLS
                    copy = pltpu.make_async_copy(
                        self.rights[matrix].at[:, pl.ds(at, COLS)],
                        self.right_in.at[pair % 2, unit, 2 * t + core, pl.ds(0, ROWS)],
                        self.right_sem.at[pair, unit, 2 * t + core],
                    )
                    copy.start()
                    self.copies[(pair, unit, "right", 2 * t + core)] = copy

    def wait_load(self, pair):
        for unit, (matrix, _) in enumerate(self.pairs[pair]):
            if matrix not in self.turned:
                copy, at = self.left_copies[matrix]
                copy.wait()
                self.left_turned[at % 4, :, pl.ds(0, ROWS)] = self.left_in[at % 2].T
                self.turned[matrix] = at % 4
            for entry in range(4):
                self.copies.pop((pair, unit, "right", entry)).wait()

    def send(self, pair, unit, stage, source, target, link):
        copy = pltpu.make_async_remote_copy(
            src_ref=source,
            dst_ref=target,
            send_sem=self.send_sem.at[pair, unit, stage],
            recv_sem=self.recv_sem.at[pair, unit, stage],
            device_id=self.partners[link],
            device_id_type=MESH_IDS,
        )
        copy.start()
        self.copies[(pair, unit, stage)] = copy

    def product(self, pair, unit, t, core, z):
        matrix, _ = self.pairs[pair][unit]
        at = pl.multiple_of(z * 256, 256)
        left = self.left_turned[self.turned[matrix], pl.ds(at, 256), :]
        right = self.right_in[pair % 2, unit, 2 * t + core]
        total = dot_rows(left[:, :512], right[:512]) + dot_rows(left[:, 512:], right[512:])
        return total.reshape(2, 2, BLOCK, COLS)

    def stage(self, pair, unit, stage):
        if pair < 0 or pair >= len(self.pairs):
            return
        z, x, c, y = self.z, self.x, self.c, self.y
        slot, arrival = pair % VAL_SLOTS, pair % ARRIVAL_SLOTS
        high, lower = lax.div(z, 2), lax.rem(z, 2)
        near_pair, far_pair = pl.ds(2 * high, 2), pl.ds(2 * (1 - high), 2)
        far_z = z + 1 - 2 * lower
        val = self.val.at[slot, unit]
        if stage == 0:
            out = self.core_out.at[pair % 2, unit]

            @pl.loop(0, 4)
            def _(row):
                for t in range(2):
                    out[t, row] = self.product(pair, unit, t, 1 - c, row).astype(LOW)

            self.send(pair, unit, 0, out, self.core_in.at[arrival, unit], "core")
            return
        self.copies.pop((pair, unit, stage - 1)).wait()
        if stage == 1:
            other = self.core_in.at[arrival, unit]

            @pl.loop(0, 4)
            def _(row):
                for t in range(2):
                    total = self.product(pair, unit, t, c, row)
                    val[t, row] = (total + other[t, row].astype(jnp.float32)).astype(LOW)

            if unit == 0:
                self.send(pair, unit, 1, val.at[1 - y], self.first_a.at[arrival], "y")
            else:
                self.send(pair, unit, 1, val.at[:, :, 1 - x], self.first_b.at[arrival], "x")
        elif stage == 2:
            target = self.second.at[arrival, unit]
            if unit == 0:

                @pl.loop(0, 4)
                def _(row):
                    val[y, row] = val[y, row] + self.first_a[arrival, row]

                self.send(pair, unit, 2, val.at[y, :, 1 - x], target, "x")
            else:

                @pl.loop(0, 4)
                def _(row):
                    for t in range(2):
                        val[t, row, x] = val[t, row, x] + self.first_b[arrival, t, row]

                self.send(pair, unit, 2, val.at[1 - y, :, x], target, "y")
        elif stage == 3:

            @pl.loop(0, 4)
            def _(row):
                val[y, row, x] = val[y, row, x] + self.second[arrival, unit, row]

            target = self.third.at[arrival, unit]
            self.send(pair, unit, 3, val.at[y, far_pair, x], target, "z2")
        elif stage == 4:
            for row in range(2):
                at = 2 * high + row
                val[y, at, x] = val[y, at, x] + self.third[arrival, unit, row]
            target = self.fourth.at[arrival, unit]
            self.send(pair, unit, 4, val.at[y, far_z, x], target, "z1")
        elif stage == 5:
            val[y, z, x] = val[y, z, x] + self.fourth[arrival, unit]
            target = self.fifth.at[arrival, unit]
            self.send(pair, unit, 5, val.at[y, z, x, 1 - c], target, "core")
        else:
            matrix, step = self.pairs[pair][unit]
            out_ref, layer = self.outs[matrix]
            cols = pl.ds(step * COLS, COLS)
            out_ref[layer, c, :, cols] = val[y, z, x, c].astype(jnp.float32)
            out_ref[layer, 1 - c, :, cols] = self.fifth[arrival, unit].astype(jnp.float32)

    def tick(self, pair):
        for stage in range(SETTLE_DEPTH, 0, -1):
            for unit in range(2):
                self.stage(pair - stage, unit, stage)
        self.load(pair + 1)
        if pair < len(self.pairs):
            self.wait_load(pair)
            for unit in range(2):
                self.stage(pair, unit, 0)


TOTAL_LINKS = ("x", "y", "z1", "z2", "core")


def settle_kernel(plan, kinds, layers, *refs):
    matrices = kinds * layers
    lefts, rights = refs[:matrices], refs[matrices : 2 * matrices]
    small_ref = refs[2 * matrices]
    refs = refs[2 * matrices + 1 :]
    outs, total_ref, refs = refs[:kinds], refs[kinds], refs[kinds + 1 :]
    sums, sums_in, sums_send, sums_recv = refs[:4]
    plan.bind(
        lefts, rights, [(outs[m % kinds], m // kinds) for m in range(matrices)], refs[4:]
    )
    plan.load(0)
    greet(plan.partners)
    sums[0] = small_ref[...]
    flying = None
    for pair in range(len(plan.pairs) + SETTLE_DEPTH):
        if flying is not None:
            flying.wait()
            sums[pair] = sums[pair - 1] + sums_in[pair - 1]
            flying = None
        if pair < len(TOTAL_LINKS):
            flying = pltpu.make_async_remote_copy(
                src_ref=sums.at[pair],
                dst_ref=sums_in.at[pair],
                send_sem=sums_send.at[pair],
                recv_sem=sums_recv.at[pair],
                device_id=plan.partners[TOTAL_LINKS[pair]],
                device_id_type=MESH_IDS,
            )
            flying.start()
        plan.tick(pair)
    total_ref[...] = sums[len(TOTAL_LINKS)]


def layer_pairs(base, widths):
    feed = [((base + 2, k), (base + 3, k)) for k in range(widths[2] // 2 // COLS)]
    rest = [(base, k) for k in range(widths[0] // 2 // COLS)]
    rest.insert(1, (base + 1, 0))
    return feed + [(rest[k], rest[k + 1]) for k in range(0, len(rest), 2)]


def settle_all(layer_terms, small):
    layers, kinds = len(layer_terms), len(layer_terms[0])
    widths = [right.shape[1] // 2 for _, right in layer_terms[0]]
    pairs = []
    for layer in reversed(range(layers)):
        pairs += layer_pairs(layer * kinds, widths)
    plan = Settle(widths * layers, pairs)
    lefts = [left for terms in layer_terms for left, _ in terms]
    rights = [right for terms in layer_terms for _, right in terms]
    steps = len(TOTAL_LINKS)
    any_spec, vmem_spec = pl.BlockSpec(memory_space=pl.ANY), pl.BlockSpec(memory_space=pltpu.VMEM)
    return pl.pallas_call(
        lambda *refs: settle_kernel(plan, kinds, layers, *refs),
        out_shape=[jax.ShapeDtypeStruct((layers, 2, BLOCK, width // 2), jnp.float32) for width in widths]
        + [jax.ShapeDtypeStruct(small.shape, jnp.float32)],
        in_specs=[any_spec] * (2 * kinds * layers) + [vmem_spec],
        out_specs=[vmem_spec] * (kinds + 1),
        scratch_shapes=[
            pltpu.VMEM((steps + 1, *small.shape), jnp.float32),
            pltpu.VMEM((steps, *small.shape), jnp.float32),
            pltpu.SemaphoreType.DMA((steps,)),
            pltpu.SemaphoreType.DMA((steps,)),
            *plan.scratch().values(),
        ],
        compiler_params=pltpu.CompilerParams(
            collective_id=1, has_side_effects=True, vmem_limit_bytes=58 * 1024 * 1024
        ),
        cost_estimate=pl.CostEstimate(
            flops=24 * 4 * 1024 * 1024 * ROWS, bytes_accessed=700 * 1024 * 1024, transcendentals=0
        ),
        name="settle_all",
    )(*lefts, *rights, small)


def in_order(own, other, index, axis):
    first = jnp.where(index == 0, own, other)
    second = jnp.where(index == 0, other, own)
    return jnp.concatenate((first, second), axis=axis)


def whole_norm(stream, gain, shift):
    row_mean = jnp.mean(stream, axis=1, keepdims=True)
    square_mean = jnp.mean(stream * stream, axis=1, keepdims=True)
    inverse_std = lax.rsqrt(square_mean - row_mean * row_mean + norm_eps)
    centred = (stream - row_mean) * inverse_std
    return (centred * gain + shift).astype(LOW), centred, inverse_std


def whole_norm_backward(upstream, centred, inverse_std, gain):
    scaled = upstream * gain
    return inverse_std * (
        scaled
        - jnp.mean(scaled, axis=1, keepdims=True)
        - centred * jnp.mean(scaled * centred, axis=1, keepdims=True)
    )


def image_body(
    images,
    first_gain,
    first_shift,
    query_weight,
    key_weight,
    value_weight,
    query_bias,
    value_bias,
    out_weight,
    out_bias,
    second_gain,
    second_shift,
    up_weight,
    up_bias,
    down_weight,
    down_bias,
    cotangent,
):
    layers = query_weight.shape[0]
    half = images.shape[1]
    hidden_width = 2 * up_weight.shape[2]
    y = lax.axis_index("tensor")
    far = 1 - y

    whole = gather_weights(
        (
            jnp.concatenate((query_weight, key_weight, value_weight), axis=2),
            jnp.swapaxes(out_weight, 1, 2),
            up_weight,
            jnp.swapaxes(down_weight, 1, 2),
        )
    )

    tokens = jnp.stack((images.reshape(2, SEQ, half), cotangent.reshape(2, SEQ, half)))
    near_tokens = pick(tokens, y, 1)
    far_tokens = swap_link(pick(tokens, far, 1), "y")
    tokens = in_order(near_tokens, far_tokens, y, 2)
    tokens = jnp.pad(tokens, ((0, 0), (0, ROWS - SEQ), (0, 0)))
    biases = jnp.concatenate(
        (query_bias, jnp.zeros_like(query_bias), value_bias, out_bias, down_bias, up_bias), axis=1
    )
    both = in_order(biases[None], swap_link(biases, "y")[None], y, 0)

    def whole_bias(start, size, layer):
        return both[:, layer, start : start + size].reshape(1, -1).astype(jnp.float32)

    def row(table, layer):
        return table[layer][None].astype(jnp.float32)

    stream = tokens[0].astype(jnp.float32)
    saved = []
    for layer in range(layers):
        project_w, out_w, up_w, down_w = whole[layer]
        normed, centred, inverse = whole_norm(
            stream, row(first_gain, layer), row(first_shift, layer)
        )
        projected = (dot_rows(normed, project_w) + whole_bias(0, 3 * half, layer)).astype(LOW)
        heads = mix_heads(projected)
        middle = stream + dot_cols(heads, out_w) + whole_bias(3 * half, half, layer)
        normed_two, centred_two, inverse_two = whole_norm(
            middle, row(second_gain, layer), row(second_shift, layer)
        )
        before = dot_rows(normed_two, up_w) + whole_bias(5 * half, hidden_width // 2, layer)
        hidden = (before * (0.5 * (1.0 + lax.erf(before * 0.7071067811865476)))).astype(LOW)
        saved.append(
            (
                normed,
                centred,
                inverse,
                projected,
                heads,
                normed_two,
                centred_two,
                inverse_two,
                before,
                hidden,
            )
        )
        stream = middle + dot_cols(hidden, down_w) + whole_bias(4 * half, half, layer)
    activations = stream.astype(LOW)

    upstream = tokens[1].astype(jnp.float32)
    small = [None] * layers
    terms = [None] * layers
    for layer in reversed(range(layers)):
        project_w, out_w, up_w, down_w = whole[layer]
        (
            normed,
            centred,
            inverse,
            projected,
            heads,
            normed_two,
            centred_two,
            inverse_two,
            before,
            hidden,
        ) = saved[layer]
        down_bias_sum = jnp.sum(upstream, axis=0)
        upstream_low = upstream.astype(LOW)
        down_term = (upstream_low, hidden)
        hidden_grad = (dot_rows(upstream_low, down_w) * gelu_slope(before)).astype(LOW)
        up_bias_sum = jnp.sum(hidden_grad.astype(jnp.float32), axis=0)
        up_term = (normed_two, hidden_grad)
        normed_two_grad = dot_cols(hidden_grad, up_w)
        second_gain_sum = jnp.sum(normed_two_grad * centred_two, axis=0)
        second_shift_sum = jnp.sum(normed_two_grad, axis=0)
        upstream = upstream + whole_norm_backward(
            normed_two_grad, centred_two, inverse_two, row(second_gain, layer)
        )
        out_bias_sum = jnp.sum(upstream, axis=0)
        upstream_low = upstream.astype(LOW)
        out_term = (upstream_low, heads)
        heads_grad = dot_rows(upstream_low, out_w).astype(LOW)
        joined = mix_heads_backward(projected, heads_grad)
        joined_sums = jnp.sum(joined.astype(jnp.float32), axis=0).reshape(2, 3, half)
        project_term = (normed, joined)
        normed_grad = dot_cols(joined, project_w)
        first_gain_sum = jnp.sum(normed_grad * centred, axis=0)
        first_shift_sum = jnp.sum(normed_grad, axis=0)
        upstream = upstream + whole_norm_backward(
            normed_grad, centred, inverse, row(first_gain, layer)
        )
        small[layer] = jnp.concatenate(
            (
                joined_sums[:, 0].reshape(-1),
                joined_sums[:, 2].reshape(-1),
                out_bias_sum,
                up_bias_sum,
                down_bias_sum,
                first_gain_sum,
                first_shift_sum,
                second_gain_sum,
                second_shift_sum,
            )
        )
        terms[layer] = (project_term, out_term, up_term, down_term)

    width = 2 * half
    project_out, out_out, up_out, down_out, totals = settle_all(
        terms, jnp.stack(small).reshape(-1, width)
    )
    totals = totals.reshape(layers, -1)
    project_out, out_out, up_out, down_out = [
        jnp.swapaxes(block, 1, 2).reshape(layers, BLOCK, -1)
        for block in (project_out, out_out, up_out, down_out)
    ]
    small_outs, at = [], 0
    for size in (width, width, width, hidden_width, width, width, width, width, width):
        small_outs.append(totals[:, at : at + size])
        at += size
    def to_owner(rows):
        parts = rows[:SEQ].reshape(SEQ, 2, half)
        near = pick(parts, y, 1)
        moved = swap_link(pick(parts, far, 1).astype(LOW), "y")
        return in_order(near, moved.astype(near.dtype), y, 0)

    return (
        to_owner(activations),
        to_owner(upstream),
        project_out[:, :, :half],
        project_out[:, :, half : 2 * half],
        project_out[:, :, 2 * half :],
        jnp.swapaxes(out_out, 1, 2),
        up_out,
        jnp.swapaxes(down_out, 1, 2),
        *small_outs,
    )


def solution(mesh):
    in_specs = (
        P("wide", "tensor"),
        P(),
        P(),
        P(None, "wide", "tensor"),
        P(None, "wide", "tensor"),
        P(None, "wide", "tensor"),
        P(None, "tensor"),
        P(None, "tensor"),
        P(None, "tensor", "wide"),
        P(None, "tensor"),
        P(),
        P(),
        P(None, "wide", "tensor"),
        P(None, "tensor"),
        P(None, "tensor", "wide"),
        P(None, "tensor"),
        P("wide", "tensor"),
    )
    out_specs = (
        P("wide", "tensor"),
        P("wide", "tensor"),
        P(None, "wide", "tensor"),
        P(None, "wide", "tensor"),
        P(None, "wide", "tensor"),
        P(None, "tensor", "wide"),
        P(None, "wide", "tensor"),
        P(None, "tensor", "wide"),
        P(),
        P(),
        P(),
        P(),
        P(),
        P(),
        P(),
        P(),
        P(),
    )
    chosen = body
    if mesh.shape["wide"] == 16 and mesh.shape["tensor"] == 2:
        chosen = image_body
    return jax.shard_map(
        chosen, mesh=mesh, in_specs=in_specs, out_specs=out_specs, check_vma=False
    )
```

```python
import jax
import jax.numpy as jnp
from jax import lax
from jax.experimental import pallas as pl
from jax.experimental.pallas import tpu as pltpu
from jax.sharding import PartitionSpec as P

HEAD_DIM = 64
SEQ = 577
MICRO = 2


norm_eps = 1e-06


def row_totals(first_terms, second_terms):
    return lax.psum((first_terms, second_terms), "tensor")


def full_rows(share_low):
    return lax.all_gather(share_low, "tensor", axis=1, tiled=True)


def feature_total(partial_sums):
    return lax.psum_scatter(
        partial_sums.astype(jnp.bfloat16), "tensor", scatter_dimension=1, tiled=True
    ).astype(jnp.float32)


def fetch_weights(query_block, key_block, value_block, out_block, up_block, down_block):
    return (
        lax.all_gather(query_block, "wide", axis=0, tiled=True),
        lax.all_gather(key_block, "wide", axis=0, tiled=True),
        lax.all_gather(value_block, "wide", axis=0, tiled=True),
        lax.all_gather(out_block, "wide", axis=1, tiled=True),
        lax.all_gather(up_block, "wide", axis=0, tiled=True),
        lax.all_gather(down_block, "wide", axis=1, tiled=True),
    )


def settle_grads(query_piece, key_piece, value_piece, out_piece, up_piece, down_piece):
    return (
        lax.psum_scatter(
            query_piece.astype(jnp.bfloat16), "wide", scatter_dimension=0, tiled=True
        ).astype(jnp.float32),
        lax.psum_scatter(
            key_piece.astype(jnp.bfloat16), "wide", scatter_dimension=0, tiled=True
        ).astype(jnp.float32),
        lax.psum_scatter(
            value_piece.astype(jnp.bfloat16), "wide", scatter_dimension=0, tiled=True
        ).astype(jnp.float32),
        lax.psum_scatter(
            out_piece.astype(jnp.bfloat16), "wide", scatter_dimension=1, tiled=True
        ).astype(jnp.float32),
        lax.psum_scatter(
            up_piece.astype(jnp.bfloat16), "wide", scatter_dimension=0, tiled=True
        ).astype(jnp.float32),
        lax.psum_scatter(
            down_piece.astype(jnp.bfloat16), "wide", scatter_dimension=1, tiled=True
        ).astype(jnp.float32),
    )


def add_terms(earlier, latest):
    if earlier is None:
        return latest
    return jax.tree.map(jnp.add, earlier, latest)


def norm_forward(stream, gain, shift, full_width):
    first_terms, second_terms = row_totals(
        jnp.sum(stream, axis=1), jnp.sum(stream * stream, axis=1)
    )
    row_mean = first_terms / full_width
    inverse_std = lax.rsqrt(second_terms / full_width - row_mean * row_mean + norm_eps)
    centred = (stream - row_mean[:, None]) * inverse_std[:, None]
    return (centred * gain + shift, centred, inverse_std)


def norm_backward(upstream, centred, inverse_std, gain, full_width):
    scaled = upstream * gain
    first_terms, second_terms = row_totals(
        jnp.sum(scaled, axis=1), jnp.sum(scaled * centred, axis=1)
    )
    return inverse_std[:, None] * (
        scaled - first_terms[:, None] / full_width - centred * (second_terms[:, None] / full_width)
    )


def attention_forward(queries, keys_here, values_here, image_count, heads_here):
    score_scale = HEAD_DIM ** (-0.5)
    shape_four = (image_count, SEQ, heads_here, HEAD_DIM)
    query_four = queries.reshape(shape_four)
    key_four = keys_here.reshape(shape_four)
    value_four = values_here.reshape(shape_four)
    scores = (
        jnp.einsum("iqhd,ikhd->ihqk", query_four, key_four, preferred_element_type=jnp.float32)
        * score_scale
    )
    row_peak = jnp.max(scores, axis=-1, keepdims=True)
    exponent = jnp.exp(scores - row_peak)
    row_total = jnp.sum(exponent, axis=-1, keepdims=True)
    weights_soft = (exponent / row_total).astype(jnp.bfloat16)
    mixed_heads = jnp.einsum(
        "ihqk,ikhd->iqhd", weights_soft, value_four, preferred_element_type=jnp.float32
    )
    log_total = row_peak[..., 0] + jnp.log(row_total[..., 0])
    return (mixed_heads.reshape(queries.shape).astype(jnp.bfloat16), log_total)


def attention_backward(
    queries, keys_here, values_here, log_total, mixed_grad, image_count, heads_here
):
    score_scale = HEAD_DIM ** (-0.5)
    shape_four = (image_count, SEQ, heads_here, HEAD_DIM)
    query_four = queries.reshape(shape_four)
    key_four = keys_here.reshape(shape_four)
    value_four = values_here.reshape(shape_four)
    grad_four = mixed_grad.reshape(shape_four)
    scores = (
        jnp.einsum("iqhd,ikhd->ihqk", query_four, key_four, preferred_element_type=jnp.float32)
        * score_scale
    )
    weights_soft = jnp.exp(scores - log_total[..., None])
    weight_grad = jnp.einsum(
        "iqhd,ikhd->ihqk", grad_four, value_four, preferred_element_type=jnp.float32
    )
    row_delta = jnp.sum(weight_grad * weights_soft, axis=-1, keepdims=True)
    score_grad = (weights_soft * (weight_grad - row_delta)).astype(jnp.bfloat16)
    query_grad = (
        jnp.einsum("ihqk,ikhd->iqhd", score_grad, key_four, preferred_element_type=jnp.float32)
        * score_scale
    )
    key_grad = (
        jnp.einsum("ihqk,iqhd->ikhd", score_grad, query_four, preferred_element_type=jnp.float32)
        * score_scale
    )
    value_grad = jnp.einsum(
        "ihqk,iqhd->ikhd",
        weights_soft.astype(jnp.bfloat16),
        grad_four,
        preferred_element_type=jnp.float32,
    )
    flat_shape = queries.shape
    return (
        query_grad.reshape(flat_shape),
        key_grad.reshape(flat_shape),
        value_grad.reshape(flat_shape),
    )


def gelu_slope(values):
    normal_cdf = 0.5 * (1.0 + lax.erf(values * 0.7071067811865476))
    return normal_cdf + values * jnp.exp(-0.5 * values * values) * 0.3989422804014327


def body(
    images,
    first_gain,
    first_shift,
    query_weight,
    key_weight,
    value_weight,
    query_bias,
    value_bias,
    out_weight,
    out_bias,
    second_gain,
    second_shift,
    up_weight,
    up_bias,
    down_weight,
    down_bias,
    cotangent,
):
    layer_count = query_weight.shape[0]
    feature_block = images.shape[1]
    tensor_count = lax.axis_size("tensor")
    full_width = feature_block * tensor_count
    heads_here = feature_block // HEAD_DIM
    tensor_place = lax.axis_index("tensor")
    micro_rows = images.shape[0] // MICRO
    image_count = micro_rows // SEQ

    def gain_share(param_table, layer_idx):
        return lax.dynamic_slice_in_dim(
            param_table[layer_idx], tensor_place * feature_block, feature_block
        )

    def layer_weights(layer_idx):
        return fetch_weights(
            query_weight[layer_idx],
            key_weight[layer_idx],
            value_weight[layer_idx],
            out_weight[layer_idx],
            up_weight[layer_idx],
            down_weight[layer_idx],
        )

    weight_sums = [None] * layer_count
    small_sums = [None] * layer_count
    activation_parts = []
    gradient_parts = []
    for micro_idx in range(MICRO):
        row_start = micro_idx * micro_rows
        stream = images[row_start : row_start + micro_rows].astype(jnp.float32)
        saved_state = []
        for layer_idx in range(layer_count):
            query_full, key_full, value_full, out_full, up_full, down_full = layer_weights(
                layer_idx
            )
            normed, centred_one, inverse_one = norm_forward(
                stream,
                gain_share(first_gain, layer_idx),
                gain_share(first_shift, layer_idx),
                full_width,
            )
            normed_full = full_rows(normed.astype(jnp.bfloat16))
            joined_weight = jnp.concatenate((query_full, key_full, value_full), axis=1)
            projected = jnp.dot(normed_full, joined_weight, preferred_element_type=jnp.float32)
            queries = (projected[:, :feature_block] + query_bias[layer_idx]).astype(jnp.bfloat16)
            keys_here = projected[:, feature_block : 2 * feature_block].astype(jnp.bfloat16)
            values_here = (projected[:, 2 * feature_block :] + value_bias[layer_idx]).astype(
                jnp.bfloat16
            )
            mixed_heads, log_total = attention_forward(
                queries, keys_here, values_here, image_count, heads_here
            )
            attention_sum = feature_total(
                jnp.dot(mixed_heads, out_full, preferred_element_type=jnp.float32)
            )
            after_attention = stream + attention_sum + out_bias[layer_idx]
            normed_two, centred_two, inverse_two = norm_forward(
                after_attention,
                gain_share(second_gain, layer_idx),
                gain_share(second_shift, layer_idx),
                full_width,
            )
            normed_two_full = full_rows(normed_two.astype(jnp.bfloat16))
            hidden_pre = (
                jnp.dot(normed_two_full, up_full, preferred_element_type=jnp.float32)
                + up_bias[layer_idx]
            )
            hidden = jax.nn.gelu(hidden_pre, approximate=False).astype(jnp.bfloat16)
            feedforward_sum = feature_total(
                jnp.dot(hidden, down_full, preferred_element_type=jnp.float32)
            )
            saved_state.append(
                (
                    centred_one,
                    inverse_one,
                    normed_full,
                    queries,
                    keys_here,
                    values_here,
                    mixed_heads,
                    log_total,
                    centred_two,
                    inverse_two,
                    normed_two_full,
                    hidden_pre,
                    hidden,
                )
            )
            stream = after_attention + feedforward_sum + down_bias[layer_idx]
        activation_parts.append(stream.astype(jnp.bfloat16))
        upstream = cotangent[row_start : row_start + micro_rows].astype(jnp.float32)
        for layer_idx in reversed(range(layer_count)):
            query_full, key_full, value_full, out_full, up_full, down_full = layer_weights(
                layer_idx
            )
            (
                centred_one,
                inverse_one,
                normed_full,
                queries,
                keys_here,
                values_here,
                mixed_heads,
                log_total,
                centred_two,
                inverse_two,
                normed_two_full,
                hidden_pre,
                hidden,
            ) = saved_state[layer_idx]
            down_bias_term = jnp.sum(upstream, axis=0)
            upstream_full = full_rows(upstream.astype(jnp.bfloat16))
            down_term = jnp.einsum(
                "rc,rd->cd", hidden, upstream_full, preferred_element_type=jnp.float32
            )
            hidden_grad = jnp.einsum(
                "rd,cd->rc", upstream_full, down_full, preferred_element_type=jnp.float32
            )
            pre_grad = (hidden_grad * gelu_slope(hidden_pre)).astype(jnp.bfloat16)
            up_bias_term = jnp.sum(pre_grad.astype(jnp.float32), axis=0)
            up_term = jnp.einsum(
                "rd,rc->dc", normed_two_full, pre_grad, preferred_element_type=jnp.float32
            )
            normed_two_grad = feature_total(
                jnp.einsum("rc,dc->rd", pre_grad, up_full, preferred_element_type=jnp.float32)
            )
            second_gain_term = jnp.sum(normed_two_grad * centred_two, axis=0)
            second_shift_term = jnp.sum(normed_two_grad, axis=0)
            upstream = upstream + norm_backward(
                normed_two_grad,
                centred_two,
                inverse_two,
                gain_share(second_gain, layer_idx),
                full_width,
            )
            out_bias_term = jnp.sum(upstream, axis=0)
            upstream_full = full_rows(upstream.astype(jnp.bfloat16))
            out_term = jnp.einsum(
                "rc,rd->cd", mixed_heads, upstream_full, preferred_element_type=jnp.float32
            )
            mixed_grad = jnp.einsum(
                "rd,cd->rc", upstream_full, out_full, preferred_element_type=jnp.float32
            ).astype(jnp.bfloat16)
            query_grad, key_grad, value_grad = attention_backward(
                queries, keys_here, values_here, log_total, mixed_grad, image_count, heads_here
            )
            joined_grad = jnp.concatenate((query_grad, key_grad, value_grad), axis=1).astype(
                jnp.bfloat16
            )
            joined_float = joined_grad.astype(jnp.float32)
            query_bias_term = jnp.sum(joined_float[:, :feature_block], axis=0)
            value_bias_term = jnp.sum(joined_float[:, 2 * feature_block :], axis=0)
            joined_term = jnp.einsum(
                "rd,rc->dc", normed_full, joined_grad, preferred_element_type=jnp.float32
            )
            joined_weight = jnp.concatenate((query_full, key_full, value_full), axis=1)
            normed_grad = feature_total(
                jnp.einsum(
                    "rc,dc->rd", joined_grad, joined_weight, preferred_element_type=jnp.float32
                )
            )
            first_gain_term = jnp.sum(normed_grad * centred_one, axis=0)
            first_shift_term = jnp.sum(normed_grad, axis=0)
            upstream = upstream + norm_backward(
                normed_grad, centred_one, inverse_one, gain_share(first_gain, layer_idx), full_width
            )
            query_term = joined_term[:, :feature_block]
            key_term = joined_term[:, feature_block : 2 * feature_block]
            value_term = joined_term[:, 2 * feature_block :]
            weight_sums[layer_idx] = add_terms(
                weight_sums[layer_idx],
                settle_grads(query_term, key_term, value_term, out_term, up_term, down_term),
            )
            small_sums[layer_idx] = add_terms(
                small_sums[layer_idx],
                (
                    query_bias_term,
                    value_bias_term,
                    out_bias_term,
                    up_bias_term,
                    down_bias_term,
                    first_gain_term,
                    first_shift_term,
                    second_gain_term,
                    second_shift_term,
                ),
            )
        gradient_parts.append(upstream)
    share_sets = []
    for layer_idx in range(layer_count):
        share_sets.append(weight_sums[layer_idx])
    weight_outputs = [
        jnp.stack([share_sets[layer_idx][entry_idx] for layer_idx in range(layer_count)])
        for entry_idx in range(6)
    ]
    small_stack = [
        jnp.stack([small_sums[layer_idx][entry_idx] for layer_idx in range(layer_count)])
        for entry_idx in range(9)
    ]
    widened = [
        lax.dynamic_update_slice_in_dim(
            jnp.zeros((layer_count, share_piece.shape[1] * tensor_count), jnp.float32),
            share_piece,
            tensor_place * share_piece.shape[1],
            1,
        )
        for share_piece in small_stack
    ]
    totals = lax.psum(
        (
            widened[0],
            widened[1],
            widened[2],
            widened[3],
            widened[4],
            widened[5],
            widened[6],
            widened[7],
            widened[8],
        ),
        ("wide", "tensor"),
    )
    activations = jnp.concatenate(activation_parts, axis=0)
    input_gradient = jnp.concatenate(gradient_parts, axis=0)
    return (
        activations,
        input_gradient,
        weight_outputs[0],
        weight_outputs[1],
        weight_outputs[2],
        weight_outputs[3],
        weight_outputs[4],
        weight_outputs[5],
        totals[0],
        totals[1],
        totals[2],
        totals[3],
        totals[4],
        totals[5],
        totals[6],
        totals[7],
        totals[8],
    )


MESH_IDS = pl.DeviceIdType.MESH
LOW = jnp.bfloat16
BLOCK = 64
ROWS = -(-SEQ // 16) * 16
DEEP = -(-SEQ // 128) * 128


def place():
    wide = lax.axis_index("wide")
    return (
        lax.div(wide, 4),
        lax.rem(lax.div(wide, 2), 2),
        lax.rem(wide, 2),
        lax.axis_index("tensor"),
    )


def neighbours():
    z, x, c, y = place()

    def at(z, x, c, y):
        return (z * 4 + x * 2 + c, y)

    return {
        "core": at(z, x, 1 - c, y),
        "x": at(z, 1 - x, c, y),
        "y": at(z, x, c, 1 - y),
        "z1": at(z + 1 - 2 * lax.rem(z, 2), x, c, y),
        "z2": at(lax.rem(z + 2, 4), x, c, y),
    }


LINKS = ("core", "x", "y", "z1", "z2")


def greet(partners):
    barrier = pltpu.get_barrier_semaphore()
    for link in LINKS:
        pl.semaphore_signal(barrier, inc=1, device_id=partners[link], device_id_type=MESH_IDS)
    pl.semaphore_wait(barrier, len(LINKS))


def dot_rows(left, right):
    return lax.dot_general(
        left, right, (((1,), (0,)), ((), ())), preferred_element_type=jnp.float32
    )


def dot_cols(left, right):
    return lax.dot_general(
        left, right, (((1,), (1,)), ((), ())), preferred_element_type=jnp.float32
    )


def dot_tokens(left, right):
    return lax.dot_general(
        left, right, (((0,), (0,)), ((), ())), preferred_element_type=jnp.float32
    )


PAIR = 2 * HEAD_DIM


def turned_softmax(keys_here, queries):
    scores = dot_cols(keys_here, queries)
    exponent = jnp.exp(scores - jnp.max(scores, axis=0, keepdims=True))
    return exponent * (1.0 / jnp.sum(exponent, axis=0, keepdims=True))


def store_rows(ref, at, pieces):
    full = SEQ // 16 * 16
    ref[pl.ds(full, ROWS - full), pl.ds(at, PAIR)] = jnp.zeros((ROWS - full, PAIR), LOW)
    ref[pl.ds(0, SEQ), pl.ds(at, PAIR)] = jnp.concatenate(pieces, axis=1)


def projected_specs(blocks):
    def spec(offset):
        return pl.BlockSpec((ROWS, PAIR), lambda step: (0, offset + step))

    return [spec(t * 3 * blocks + part * blocks) for t in range(2) for part in range(3)]


def heads_backward_kernel(
    query_a, key_a, value_a, query_b, key_b, value_b, grad_a, grad_b, out_ref
):
    step = pl.program_id(0)
    scale = jnp.asarray(HEAD_DIM**-0.5, LOW)
    part_width = out_ref.shape[1] // 6
    for t, (query_ref, key_ref, value_ref, grad_ref) in enumerate(
        ((query_a, key_a, value_a, grad_a), (query_b, key_b, value_b, grad_b))
    ):
        pieces = ([], [], [])
        for head in range(2):
            cols = slice(head * HEAD_DIM, (head + 1) * HEAD_DIM)
            keys_here, values_here = key_ref[:SEQ, cols], value_ref[:SEQ, cols]
            grads = grad_ref[:SEQ, cols]
            queries = query_ref[:SEQ, cols] * scale
            soft = turned_softmax(keys_here, queries)
            soft_grad = dot_cols(values_here, grads)
            delta = jnp.sum(soft_grad * soft, axis=0, keepdims=True)
            score_grad = (soft * (soft_grad - delta)).astype(LOW)
            pieces[0].append((dot_tokens(score_grad, keys_here) * HEAD_DIM**-0.5).astype(LOW))
            pieces[1].append(dot_rows(score_grad, queries).astype(LOW))
            pieces[2].append(dot_rows(soft.astype(LOW), grads).astype(LOW))
        for part in range(3):
            at = pl.multiple_of((t * 3 + part) * part_width + step * PAIR, PAIR)
            store_rows(out_ref, at, pieces[part])


def mix_heads_backward(projected, mixed_grad):
    width = mixed_grad.shape[1]
    blocks = width // 2 // PAIR

    def grad_spec(offset):
        return pl.BlockSpec((ROWS, PAIR), lambda step: (0, offset + step))

    return pl.pallas_call(
        heads_backward_kernel,
        grid=(blocks,),
        in_specs=projected_specs(blocks) + [grad_spec(0), grad_spec(blocks)],
        out_specs=pl.BlockSpec((ROWS, 3 * width), lambda step: (0, 0)),
        out_shape=jax.ShapeDtypeStruct((ROWS, 3 * width), LOW),
        compiler_params=pltpu.CompilerParams(vmem_limit_bytes=48 * 1024 * 1024),
        cost_estimate=pl.CostEstimate(
            flops=10 * SEQ * SEQ * width, bytes_accessed=90 * 1024 * 1024, transcendentals=0
        ),
        name="mix_heads_backward",
    )(*[projected] * 6, mixed_grad, mixed_grad)


def pick(block, at, axis):
    return lax.dynamic_index_in_dim(block, at, axis, keepdims=False)


def gather_parts(width):
    last = 256 if width >= 1024 else 0
    share = (width - last) // 2
    return share, last


def gather_stages(z, x, c, y, whole, start, width):
    share, last = gather_parts(width)

    def cols(t, at, size):
        return pl.ds(pl.multiple_of(t * whole + start + at, 128), size)

    all_rows = pl.ds(0, BLOCK)
    pair = pl.ds(lax.div(z, 2) * 2, 2)
    every_z, every_x = pl.ds(0, 4), pl.ds(0, 2)
    far_x, far_y = 1 - x, 1 - y

    def part_a(t):
        return cols(t, 0, share)

    def part_b(t):
        return cols(t, share, share)

    def part_ab(t):
        return cols(t, 0, 2 * share)

    def part_c(t):
        return cols(t, 2 * share, last)

    stages = [
        [("z1", (z, x, c, all_rows, part_ab(y)))],
        [("z2", (pair, x, c, all_rows, part_ab(y)))],
        [
            ("x", (every_z, x, c, all_rows, part_a(y))),
            ("y", (every_z, x, c, all_rows, part_b(y))),
            ("core", (every_z, x, c, all_rows, part_ab(y))),
        ],
        [
            ("y", (every_z, every_x, c, all_rows, part_a(y))),
            ("x", (every_z, x, c, all_rows, part_b(0))),
            ("x", (every_z, x, c, all_rows, part_b(1))),
            ("core", (every_z, far_x, c, all_rows, part_a(y))),
            ("core", (every_z, x, c, all_rows, part_b(far_y))),
        ],
        [
            ("core", (every_z, every_x, c, all_rows, part_a(far_y))),
            ("core", (every_z, far_x, c, all_rows, part_b(0))),
            ("core", (every_z, far_x, c, all_rows, part_b(1))),
        ],
    ]
    if last:
        stages[0].append(("x", (z, x, c, all_rows, part_c(y))))
        stages[1].append(("y", (z, every_x, c, all_rows, part_c(y))))
        for t in range(2):
            stages[2].append(("z1", (z, every_x, c, all_rows, part_c(t))))
            stages[3].append(("z2", (pair, every_x, c, all_rows, part_c(t))))
            stages[4].append(("core", (every_z, every_x, c, all_rows, part_c(t))))
    return stages


GATHER_COPIES = 21
GATHER_DEPTH = 5


class Gather:
    def __init__(self, chunks):
        self.chunks = chunks

    def scratch(self):
        count = len(self.chunks)
        return dict(
            gather_send=pltpu.SemaphoreType.DMA((count, GATHER_COPIES)),
            gather_recv=pltpu.SemaphoreType.DMA((count, GATHER_COPIES)),
            gather_own=pltpu.SemaphoreType.DMA((count,)),
        )

    def bind(self, shards, wholes, refs):
        self.wholes = wholes
        self.send_sem, self.recv_sem, own_sem = refs
        z, x, c, y = place()
        self.partners = neighbours()
        self.plans, self.own, self.flying = [], [], {}
        for chunk, (matrix, start, width) in enumerate(self.chunks):
            whole = shards[matrix].shape[1]
            self.plans.append(gather_stages(z, x, c, y, whole, start, width))
            mine = pl.ds(pl.multiple_of(y * whole + start, 128), width)
            copy = pltpu.make_async_copy(
                shards[matrix].at[:, pl.ds(start, width)],
                wholes[matrix].at[z, x, c, pl.ds(0, BLOCK), mine],
                own_sem.at[chunk],
            )
            copy.start()
            self.own.append(copy)

    def tick(self, tick):
        done = None
        for stage_idx in range(GATHER_DEPTH, -1, -1):
            chunk = tick - stage_idx
            if chunk < 0 or chunk >= len(self.chunks):
                continue
            if stage_idx == 0:
                self.own[chunk].wait()
            for copy in self.flying.get((chunk, stage_idx - 1), ()):
                copy.wait_recv()
            if stage_idx == GATHER_DEPTH:
                done = chunk
                continue
            started = []
            plan = self.plans[chunk]
            base = sum(len(stage) for stage in plan[:stage_idx])
            whole = self.wholes[self.chunks[chunk][0]]
            for entry, (link, index) in enumerate(plan[stage_idx]):
                copy = pltpu.make_async_remote_copy(
                    src_ref=whole.at[index],
                    dst_ref=whole.at[index],
                    send_sem=self.send_sem.at[chunk, base + entry],
                    recv_sem=self.recv_sem.at[chunk, base + entry],
                    device_id=self.partners[link],
                    device_id_type=MESH_IDS,
                )
                copy.start()
                started.append(copy)
            self.flying[(chunk, stage_idx)] = started
        return done

    def finish(self):
        for started in self.flying.values():
            for copy in started:
                copy.wait_send()


BIAS_ROWS = 9
SAVED = ("normed", "projected", "heads", "normed_two", "hidden", "slope", "middle", "incoming")


class Forward:
    def __init__(self, layers, widths):
        self.layers, self.widths = layers, widths
        chunks = []
        for layer in range(layers):
            base = layer * len(widths)
            for kind, width in enumerate(widths):
                split = 2 if layer == layers - 1 and kind == len(widths) - 1 else 1
                part = width // split
                chunks += [(base + kind, k * part, part) for k in range(split)]
        self.gather = Gather(chunks)

    def scratch(self):
        project, out, up, down = self.widths
        low, full = (lambda cols: pltpu.VMEM((ROWS, cols), LOW)), pltpu.VMEM((ROWS, 1024), jnp.float32)
        sem = pltpu.SemaphoreType.DMA
        own = dict(
            weights_project=pltpu.VMEM((4, 2, 2, BLOCK, 2 * project), LOW),
            weights_out=pltpu.VMEM((4, 2, 2, BLOCK, 2 * out), LOW),
            weights_up=pltpu.VMEM((4, 2, 2, BLOCK, 2 * up), LOW),
            weights_down=pltpu.VMEM((4, 2, 2, BLOCK, 2 * down), LOW),
            stream=full,
            tokens_in=low(512),
            biases=pltpu.VMEM((2, 24, 512), jnp.float32),
            normed=low(1024),
            projected=low(2 * project),
            heads=low(2 * out),
            normed_two=low(1024),
            hidden=low(2 * up),
            slope=low(2 * up),
            weight_sem=sem((self.layers * 4, 1)),
            split_sem=sem((2, 2)),
            saved_sem=sem((self.layers, len(SAVED))),
            swap_send=sem((3,)),
            swap_recv=sem((3,)),
            bias_sem=sem((1,)),
        )
        return {**own, **self.gather.scratch()}

    def bind(self, inputs, outputs, refs):
        names = list(self.scratch())
        for name, ref in zip(names, refs, strict=True):
            setattr(self, name, ref)
        shards, self.near, self.far, bias_ref, self.norms = (
            inputs[:4],
            inputs[4],
            inputs[5],
            inputs[6],
            inputs[7],
        )
        count = self.layers * 4
        self.wholes, outputs = outputs[:count], outputs[count:]
        self.cotangent_in, self.activations, outputs = outputs[0], outputs[1], outputs[2:]
        self.saved_out = [outputs[k * len(SAVED) : (k + 1) * len(SAVED)] for k in range(self.layers)]
        self.saving, self.loading = {}, {}
        self.y = lax.axis_index("tensor")
        copy = pltpu.make_async_copy(bias_ref, self.biases.at[self.y], self.bias_sem.at[0])
        copy.start()
        self.gather.bind(
            [shards[m % 4].at[m // 4] for m in range(count)],
            self.wholes,
            [getattr(self, name) for name in self.gather.scratch()],
        )
        copy.wait()

    def swap(self):
        partner = self.gather.partners["y"]
        pairs = (
            (self.biases.at[self.y], self.biases.at[self.y]),
            (self.far.at[0], self.tokens_in),
            (self.far.at[1], self.cotangent_in),
        )
        self.swaps = []
        for entry, (source, target) in enumerate(pairs):
            copy = pltpu.make_async_remote_copy(
                src_ref=source,
                dst_ref=target,
                send_sem=self.swap_send.at[entry],
                recv_sem=self.swap_recv.at[entry],
                device_id=partner,
                device_id_type=MESH_IDS,
            )
            copy.start()
            self.swaps.append(copy)

    def save(self, layer, name, source):
        entry = SAVED.index(name)
        copy = pltpu.make_async_copy(
            source, self.saved_out[layer][entry], self.saved_sem.at[layer, entry]
        )
        copy.start()
        self.saving[(layer, name)] = copy

    def saved(self, layer, name):
        if (layer, name) in self.saving:
            self.saving.pop((layer, name)).wait()

    def load(self, chunk):
        matrix, start, width = self.gather.chunks[chunk]
        whole = self.gather.wholes[matrix]
        buffer = (self.weights_project, self.weights_out, self.weights_up, self.weights_down)[
            matrix % 4
        ]
        copies = []
        full = whole.shape[4] // 2
        if width == full:
            copies.append((whole, buffer))
        else:
            for t in range(2):
                at = (slice(None),) * 4 + (pl.ds(t * full + start, width),)
                copies.append((whole.at[at], buffer.at[at]))
        started = self.loading.setdefault(matrix, [])
        for entry, (source, target) in enumerate(copies):
            half = 0 if start == 0 else 1
            if len(copies) == 2:
                sem = self.split_sem.at[half, entry]
            else:
                sem = self.weight_sem.at[matrix, 0]
            copy = pltpu.make_async_copy(source, target, sem)
            copy.start()
            started.append(copy)

    def wait_weights(self, matrix):
        for copy in self.loading.pop(matrix):
            copy.wait()

    def bias_row(self, row):
        return jnp.concatenate([self.biases[t, pl.ds(row, 1), :] for t in range(2)], axis=1)

    def norm(self, target, gain_row, shift_row, bias_at):
        gain = self.norms[pl.ds(gain_row, 1), :]
        shift = self.norms[pl.ds(shift_row, 1), :]
        bias = None if bias_at is None else self.bias_row(bias_at)

        @pl.loop(0, ROWS // 16)
        def _(step):
            rows = pl.ds(pl.multiple_of(step * 16, 16), 16)
            values = self.stream[rows, :]
            if bias is not None:
                values = values + bias
                self.stream[rows, :] = values
            mean = jnp.mean(values, axis=1, keepdims=True)
            square = jnp.mean(values * values, axis=1, keepdims=True)
            inverse = lax.rsqrt(square - mean * mean + norm_eps)
            target[rows, :] = ((values - mean) * inverse * gain + shift).astype(LOW)

    def begin(self):
        for copy in self.swaps:
            copy.wait_recv()
        y = self.y
        near_at = pl.ds(pl.multiple_of(y * 512, 512), 512)
        far_at = pl.ds(pl.multiple_of((1 - y) * 512, 512), 512)
        self.stream[:, near_at] = self.near[...].astype(jnp.float32)
        self.stream[:, far_at] = self.tokens_in[...].astype(jnp.float32)

    def project(self, layer):
        self.saved(layer - 1, "normed")
        self.norm(
            self.normed,
            layer,
            self.layers + layer,
            None if layer == 0 else (layer - 1) * BIAS_ROWS + 4,
        )
        self.save(layer, "incoming", self.stream)
        self.save(layer, "normed", self.normed)
        self.saved(layer - 1, "projected")
        self.wait_weights(layer * 4)
        parts = 6

        @pl.loop(0, parts)
        def _(part):
            cols = pl.ds(pl.multiple_of(part * 512, 512), 512)
            weights = self.weights_project[:, :, :, :, cols].reshape(1024, 512)
            row = layer * BIAS_ROWS + lax.rem(part, 3)
            bias = self.biases[lax.div(part, 3), pl.ds(row, 1), :]
            self.projected[:, cols] = (dot_rows(self.normed[...], weights) + bias).astype(LOW)

        self.save(layer, "projected", self.projected)

    def mix(self, layer, first, last):
        if first == 0:
            self.saved(layer - 1, "heads")
        half = self.heads.shape[1] // 2

        @pl.loop(first, last)
        def _(step):
            for t in range(2):
                def at(part):
                    start = (t * 3 + part) * half + step * PAIR
                    return pl.ds(pl.multiple_of(start, PAIR), PAIR)

                queries = self.projected[pl.ds(0, SEQ), at(0)] * jnp.asarray(HEAD_DIM**-0.5, LOW)
                keys_here = self.projected[pl.ds(0, SEQ), at(1)]
                values_here = self.projected[pl.ds(0, SEQ), at(2)]
                pieces = []
                for head in range(2):
                    cols = slice(head * HEAD_DIM, (head + 1) * HEAD_DIM)
                    soft = turned_softmax(keys_here[:, cols], queries[:, cols])
                    pieces.append(dot_tokens(soft.astype(LOW), values_here[:, cols]).astype(LOW))
                store_rows(self.heads, pl.multiple_of(t * half + step * PAIR, PAIR), pieces)

        if last * PAIR == half:
            self.save(layer, "heads", self.heads)

    def attend(self, layer):
        self.wait_weights(layer * 4 + 1)
        self.saved(layer, "incoming")

        @pl.loop(0, 4)
        def _(row):
            cols = pl.ds(pl.multiple_of(row * 256, 256), 256)
            weights = self.weights_out[row].reshape(256, -1)
            self.stream[:, cols] = self.stream[:, cols] + dot_cols(self.heads[...], weights)

        self.saved(layer - 1, "normed_two")
        self.norm(
            self.normed_two,
            2 * self.layers + layer,
            3 * self.layers + layer,
            layer * BIAS_ROWS + 3,
        )
        self.save(layer, "normed_two", self.normed_two)
        self.save(layer, "middle", self.stream)

    def feed_up(self, layer, first, last):
        if first == 0:
            self.saved(layer - 1, "hidden")
            self.saved(layer - 1, "slope")
            self.wait_weights(layer * 4 + 2)

        @pl.loop(first, last)
        def _(part):
            cols = pl.ds(pl.multiple_of(part * 512, 512), 512)
            weights = self.weights_up[:, :, :, :, cols].reshape(1024, 512)
            row = layer * BIAS_ROWS + 5 + lax.rem(part, 4)
            bias = self.biases[lax.div(part, 4), pl.ds(row, 1), :]
            before = dot_rows(self.normed_two[...], weights) + bias
            normal = 0.5 * (1.0 + lax.erf(before * 0.7071067811865476))
            self.hidden[:, cols] = (before * normal).astype(LOW)
            density = jnp.exp(-0.5 * before * before) * 0.3989422804014327
            self.slope[:, cols] = (normal + before * density).astype(LOW)

        if last * 512 == self.hidden.shape[1]:
            self.save(layer, "hidden", self.hidden)
            self.save(layer, "slope", self.slope)

    def feed_down(self, layer, first, last):
        if first == 0:
            self.saved(layer, "middle")
            self.wait_weights(layer * 4 + 3)

        @pl.loop(first, last)
        def _(row):
            cols = pl.ds(pl.multiple_of(row * 256, 256), 256)
            weights = self.weights_down[row].reshape(256, -1)
            self.stream[:, cols] = self.stream[:, cols] + dot_cols(self.hidden[...], weights)

    def end(self):
        bias = self.bias_row((self.layers - 1) * BIAS_ROWS + 4)

        @pl.loop(0, ROWS // 16)
        def _(step):
            rows = pl.ds(pl.multiple_of(step * 16, 16), 16)
            self.activations[rows, :] = (self.stream[rows, :] + bias).astype(LOW)

    def work(self):
        steps = [(0, 1, self.begin)]
        for layer in range(self.layers):
            base = layer * 4
            steps += [
                (base, 6, lambda layer=layer: self.project(layer)),
                (base, 7, lambda layer=layer: self.mix(layer, 0, 2)),
                (base, 7, lambda layer=layer: self.mix(layer, 2, 4)),
                (base + 1, 4, lambda layer=layer: self.attend(layer)),
                (base + 2, 6, lambda layer=layer: self.feed_up(layer, 0, 4)),
                (base + 2, 6, lambda layer=layer: self.feed_up(layer, 4, 8)),
                (base + 3, 4, lambda layer=layer: self.feed_down(layer, 0, 2)),
                (base + 3, 4, lambda layer=layer: self.feed_down(layer, 2, 4)),
            ]
        return steps + [(self.layers * 4 - 1, 1, self.end)]

    def run(self):
        greet(self.gather.partners)
        self.swap()
        steps = self.work()
        ready = set()
        remaining = {}
        for matrix, _, _ in self.gather.chunks:
            remaining[matrix] = remaining.get(matrix, 0) + 1
        ticks = len(self.gather.chunks) + GATHER_DEPTH
        for tick in range(ticks):
            budget = WORK_A_TICK
            done = self.gather.tick(tick)
            while steps and steps[0][0] in ready and budget > 0:
                _, cost, step = steps.pop(0)
                budget -= cost
                step()
            if done is not None:
                self.free_buffer(done, steps)
                matrix = self.gather.chunks[done][0]
                self.load(done)
                remaining[matrix] -= 1
                if remaining[matrix] == 0:
                    ready.add(matrix)
        for _, _, step in steps:
            step()
        self.gather.finish()
        for copy in self.swaps:
            copy.wait_send()
        for copy in self.saving.values():
            copy.wait()

    def free_buffer(self, chunk, steps):
        matrix = self.gather.chunks[chunk][0]
        while steps and any(entry[0] == matrix - 4 for entry in steps):
            steps.pop(0)[2]()


WORK_A_TICK = 12


def forward(shards, near, far, biases, norms):
    layers = shards[0].shape[0]
    widths = [shard.shape[2] for shard in shards]
    plan = Forward(layers, widths)
    project, out, up, down = widths
    low = lambda cols: jax.ShapeDtypeStruct((ROWS, cols), LOW)
    full = jax.ShapeDtypeStruct((ROWS, 1024), jnp.float32)
    saved = [
        low(1024), low(2 * project), low(2 * out), low(1024), low(2 * up), low(2 * up), full, full
    ]
    wholes = [
        jax.ShapeDtypeStruct((4, 2, 2, BLOCK, 2 * width), LOW) for width in widths
    ] * layers
    outs = [*wholes, low(512), low(1024), *(saved * layers)]
    any_spec, vmem_spec = pl.BlockSpec(memory_space=pl.ANY), pl.BlockSpec(memory_space=pltpu.VMEM)
    out_specs = [any_spec] * len(outs)
    out_specs[len(wholes) + 1] = vmem_spec

    def kernel(*refs):
        outputs = refs[8 : 8 + len(outs)]
        plan.bind(refs[:8], outputs, refs[8 + len(outs) :])
        plan.run()

    results = pl.pallas_call(
        kernel,
        out_shape=outs,
        in_specs=[any_spec] * 4 + [vmem_spec, any_spec, any_spec, vmem_spec],
        out_specs=out_specs,
        scratch_shapes=list(plan.scratch().values()),
        compiler_params=pltpu.CompilerParams(
            collective_id=0, has_side_effects=True, vmem_limit_bytes=60 * 1024 * 1024
        ),
        cost_estimate=pl.CostEstimate(
            flops=60 * 1024**3, bytes_accessed=700 * 1024 * 1024, transcendentals=0
        ),
        name="forward",
    )(*shards, near, far, biases, norms)
    whole, results = results[: len(wholes)], results[len(wholes) :]
    weights = [
        [whole[layer * 4 + kind].reshape(1024, -1) for kind in range(4)] for layer in range(layers)
    ]
    cotangent_in, activations, results = results[0], results[1], results[2:]
    kept = [
        dict(zip(SAVED, results[k * len(SAVED) : (k + 1) * len(SAVED)])) for k in range(layers)
    ]
    return weights, cotangent_in, activations, kept


COLS = 256
SETTLE_DEPTH = 6
VAL_SLOTS, ARRIVAL_SLOTS = 6, 3


class Settle:
    def __init__(self, widths, pairs):
        self.widths, self.pairs = widths, pairs

    def scratch(self):
        rows = (4, 2, 2, BLOCK, COLS)
        pairs, vals, slots = len(self.pairs), VAL_SLOTS, ARRIVAL_SLOTS
        sem = pltpu.SemaphoreType.DMA
        return dict(
            left_in=pltpu.VMEM((2, ROWS, 1024), LOW),
            left_turned=pltpu.VMEM((4, 1024, DEEP), LOW),
            right_in=pltpu.VMEM((2, 2, 4, DEEP, COLS), LOW),
            core_out=pltpu.VMEM((2, 2, 2, *rows), LOW),
            core_in=pltpu.VMEM((slots, 2, 2, *rows), LOW),
            val=pltpu.VMEM((vals, 2, 2, *rows), LOW),
            first_a=pltpu.VMEM((slots, *rows), LOW),
            first_b=pltpu.VMEM((slots, 2, 4, 2, BLOCK, COLS), LOW),
            second=pltpu.VMEM((slots, 2, 4, 2, BLOCK, COLS), LOW),
            third=pltpu.VMEM((slots, 2, 2, 2, BLOCK, COLS), LOW),
            fourth=pltpu.VMEM((slots, 2, 2, BLOCK, COLS), LOW),
            fifth=pltpu.VMEM((slots, 2, BLOCK, COLS), LOW),
            send_sem=sem((pairs, 2, SETTLE_DEPTH)),
            recv_sem=sem((pairs, 2, SETTLE_DEPTH)),
            right_sem=sem((pairs, 2, 4)),
            left_sem=sem((len(self.widths),)),
        )

    def bind(self, lefts, rights, outs, refs):
        self.lefts, self.rights, self.outs = lefts, rights, outs
        for name, ref in zip(self.scratch(), refs, strict=True):
            setattr(self, name, ref)
        self.z, self.x, self.c, self.y = place()
        self.partners = neighbours()
        self.copies = {}
        self.left_copies = {}
        self.turned = {}
        self.loaded = []
        tail = ROWS // 128 * 128
        self.left_turned[:, :, pl.ds(tail, DEEP - tail)] = jnp.zeros((4, 1024, DEEP - tail), LOW)
        self.right_in[:, :, :, pl.ds(ROWS, DEEP - ROWS)] = jnp.zeros(
            (2, 2, 4, DEEP - ROWS, COLS), LOW
        )

    def load(self, pair):
        if pair >= len(self.pairs):
            return
        for unit, (matrix, step) in enumerate(self.pairs[pair]):
            if matrix not in self.left_copies:
                copy = pltpu.make_async_copy(
                    self.lefts[matrix],
                    self.left_in.at[len(self.loaded) % 2],
                    self.left_sem.at[len(self.loaded)],
                )
                copy.start()
                self.left_copies[matrix] = (copy, len(self.loaded))
                self.loaded.append(matrix)
            width = self.widths[matrix]
            for t in range(2):
                for core in range(2):
                    at = t * width + core * (width // 2) + step * COLS
                    copy = pltpu.make_async_copy(
                        self.rights[matrix].at[:, pl.ds(at, COLS)],
                        self.right_in.at[pair % 2, unit, 2 * t + core, pl.ds(0, ROWS)],
                        self.right_sem.at[pair, unit, 2 * t + core],
                    )
                    copy.start()
                    self.copies[(pair, unit, "right", 2 * t + core)] = copy

    def wait_load(self, pair):
        for unit, (matrix, _) in enumerate(self.pairs[pair]):
            if matrix not in self.turned:
                copy, at = self.left_copies[matrix]
                copy.wait()
                self.left_turned[at % 4, :, pl.ds(0, ROWS)] = self.left_in[at % 2].T
                self.turned[matrix] = at % 4
            for entry in range(4):
                self.copies.pop((pair, unit, "right", entry)).wait()

    def send(self, pair, unit, stage, source, target, link):
        copy = pltpu.make_async_remote_copy(
            src_ref=source,
            dst_ref=target,
            send_sem=self.send_sem.at[pair, unit, stage],
            recv_sem=self.recv_sem.at[pair, unit, stage],
            device_id=self.partners[link],
            device_id_type=MESH_IDS,
        )
        copy.start()
        self.copies[(pair, unit, stage)] = copy

    def product(self, pair, unit, t, core, z):
        matrix, _ = self.pairs[pair][unit]
        at = pl.multiple_of(z * 256, 256)
        left = self.left_turned[self.turned[matrix], pl.ds(at, 256), :]
        right = self.right_in[pair % 2, unit, 2 * t + core]
        total = dot_rows(left[:, :512], right[:512]) + dot_rows(left[:, 512:], right[512:])
        return total.reshape(2, 2, BLOCK, COLS)

    def stage(self, pair, unit, stage):
        if pair < 0 or pair >= len(self.pairs):
            return
        z, x, c, y = self.z, self.x, self.c, self.y
        slot, arrival = pair % VAL_SLOTS, pair % ARRIVAL_SLOTS
        high, lower = lax.div(z, 2), lax.rem(z, 2)
        near_pair, far_pair = pl.ds(2 * high, 2), pl.ds(2 * (1 - high), 2)
        far_z = z + 1 - 2 * lower
        val = self.val.at[slot, unit]
        if stage == 0:
            out = self.core_out.at[pair % 2, unit]

            @pl.loop(0, 4)
            def _(row):
                for t in range(2):
                    out[t, row] = self.product(pair, unit, t, 1 - c, row).astype(LOW)

            self.send(pair, unit, 0, out, self.core_in.at[arrival, unit], "core")
            return
        self.copies.pop((pair, unit, stage - 1)).wait()
        if stage == 1:
            other = self.core_in.at[arrival, unit]

            @pl.loop(0, 4)
            def _(row):
                for t in range(2):
                    total = self.product(pair, unit, t, c, row)
                    val[t, row] = (total + other[t, row].astype(jnp.float32)).astype(LOW)

            if unit == 0:
                self.send(pair, unit, 1, val.at[1 - y], self.first_a.at[arrival], "y")
            else:
                self.send(pair, unit, 1, val.at[:, :, 1 - x], self.first_b.at[arrival], "x")
        elif stage == 2:
            target = self.second.at[arrival, unit]
            if unit == 0:

                @pl.loop(0, 4)
                def _(row):
                    val[y, row] = val[y, row] + self.first_a[arrival, row]

                self.send(pair, unit, 2, val.at[y, :, 1 - x], target, "x")
            else:

                @pl.loop(0, 4)
                def _(row):
                    for t in range(2):
                        val[t, row, x] = val[t, row, x] + self.first_b[arrival, t, row]

                self.send(pair, unit, 2, val.at[1 - y, :, x], target, "y")
        elif stage == 3:

            @pl.loop(0, 4)
            def _(row):
                val[y, row, x] = val[y, row, x] + self.second[arrival, unit, row]

            target = self.third.at[arrival, unit]
            self.send(pair, unit, 3, val.at[y, far_pair, x], target, "z2")
        elif stage == 4:
            for row in range(2):
                at = 2 * high + row
                val[y, at, x] = val[y, at, x] + self.third[arrival, unit, row]
            target = self.fourth.at[arrival, unit]
            self.send(pair, unit, 4, val.at[y, far_z, x], target, "z1")
        elif stage == 5:
            val[y, z, x] = val[y, z, x] + self.fourth[arrival, unit]
            target = self.fifth.at[arrival, unit]
            self.send(pair, unit, 5, val.at[y, z, x, 1 - c], target, "core")
        else:
            matrix, step = self.pairs[pair][unit]
            out_ref, layer = self.outs[matrix]
            cols = pl.ds(step * COLS, COLS)
            out_ref[layer, c, :, cols] = val[y, z, x, c].astype(jnp.float32)
            out_ref[layer, 1 - c, :, cols] = self.fifth[arrival, unit].astype(jnp.float32)

    def tick(self, pair):
        for stage in range(SETTLE_DEPTH, 0, -1):
            for unit in range(2):
                self.stage(pair - stage, unit, stage)
        self.load(pair + 1)
        if pair < len(self.pairs):
            self.wait_load(pair)
            for unit in range(2):
                self.stage(pair, unit, 0)


TOTAL_LINKS = ("x", "y", "z1", "z2", "core")


def settle_kernel(plan, kinds, layers, *refs):
    matrices = kinds * layers
    lefts, rights = refs[:matrices], refs[matrices : 2 * matrices]
    small_ref, leaving_ref = refs[2 * matrices : 2 * matrices + 2]
    refs = refs[2 * matrices + 2 :]
    outs, total_ref, arriving_ref, refs = refs[:kinds], refs[kinds], refs[kinds + 1], refs[kinds + 2 :]
    sums, sums_in, sums_send, sums_recv, swap_send, swap_recv = refs[:6]
    plan.bind(
        lefts, rights, [(outs[m % kinds], m // kinds) for m in range(matrices)], refs[6:]
    )
    plan.load(0)
    greet(plan.partners)
    swap = pltpu.make_async_remote_copy(
        src_ref=leaving_ref,
        dst_ref=arriving_ref,
        send_sem=swap_send.at[0],
        recv_sem=swap_recv.at[0],
        device_id=plan.partners["y"],
        device_id_type=MESH_IDS,
    )
    swap.start()
    sums[0] = small_ref[...]
    flying = None
    for pair in range(len(plan.pairs) + SETTLE_DEPTH):
        if flying is not None:
            flying.wait()
            sums[pair] = sums[pair - 1] + sums_in[pair - 1]
            flying = None
        if pair < len(TOTAL_LINKS):
            flying = pltpu.make_async_remote_copy(
                src_ref=sums.at[pair],
                dst_ref=sums_in.at[pair],
                send_sem=sums_send.at[pair],
                recv_sem=sums_recv.at[pair],
                device_id=plan.partners[TOTAL_LINKS[pair]],
                device_id_type=MESH_IDS,
            )
            flying.start()
        plan.tick(pair)
    total_ref[...] = sums[len(TOTAL_LINKS)]
    swap.wait()


def layer_pairs(base, widths):
    feed = [((base + 2, k), (base + 3, k)) for k in range(widths[2] // 2 // COLS)]
    rest = [(base, k) for k in range(widths[0] // 2 // COLS)]
    rest.insert(1, (base + 1, 0))
    return feed + [(rest[k], rest[k + 1]) for k in range(0, len(rest), 2)]


def settle_all(layer_terms, small, leaving):
    layers, kinds = len(layer_terms), len(layer_terms[0])
    widths = [right.shape[1] // 2 for _, right in layer_terms[0]]
    pairs = []
    for layer in reversed(range(layers)):
        pairs += layer_pairs(layer * kinds, widths)
    plan = Settle(widths * layers, pairs)
    lefts = [left for terms in layer_terms for left, _ in terms]
    rights = [right for terms in layer_terms for _, right in terms]
    steps = len(TOTAL_LINKS)
    any_spec, vmem_spec = pl.BlockSpec(memory_space=pl.ANY), pl.BlockSpec(memory_space=pltpu.VMEM)
    return pl.pallas_call(
        lambda *refs: settle_kernel(plan, kinds, layers, *refs),
        out_shape=[jax.ShapeDtypeStruct((layers, 2, BLOCK, width // 2), jnp.float32) for width in widths]
        + [
            jax.ShapeDtypeStruct(small.shape, jnp.float32),
            jax.ShapeDtypeStruct(leaving.shape, leaving.dtype),
        ],
        in_specs=[any_spec] * (2 * kinds * layers) + [vmem_spec, any_spec],
        out_specs=[vmem_spec] * (kinds + 1) + [any_spec],
        scratch_shapes=[
            pltpu.VMEM((steps + 1, *small.shape), jnp.float32),
            pltpu.VMEM((steps, *small.shape), jnp.float32),
            pltpu.SemaphoreType.DMA((steps,)),
            pltpu.SemaphoreType.DMA((steps,)),
            pltpu.SemaphoreType.DMA((1,)),
            pltpu.SemaphoreType.DMA((1,)),
            *plan.scratch().values(),
        ],
        compiler_params=pltpu.CompilerParams(
            collective_id=1, has_side_effects=True, vmem_limit_bytes=58 * 1024 * 1024
        ),
        cost_estimate=pl.CostEstimate(
            flops=24 * 4 * 1024 * 1024 * ROWS, bytes_accessed=700 * 1024 * 1024, transcendentals=0
        ),
        name="settle_all",
    )(*lefts, *rights, small, leaving)


def in_order(own, other, index, axis):
    first = jnp.where(index == 0, own, other)
    second = jnp.where(index == 0, other, own)
    return jnp.concatenate((first, second), axis=axis)


def centre(stream):
    row_mean = jnp.mean(stream, axis=1, keepdims=True)
    square_mean = jnp.mean(stream * stream, axis=1, keepdims=True)
    inverse_std = lax.rsqrt(square_mean - row_mean * row_mean + norm_eps)
    return (stream - row_mean) * inverse_std, inverse_std


def whole_norm_backward(upstream, centred, inverse_std, gain):
    scaled = upstream * gain
    return inverse_std * (
        scaled
        - jnp.mean(scaled, axis=1, keepdims=True)
        - centred * jnp.mean(scaled * centred, axis=1, keepdims=True)
    )


def image_body(
    images,
    first_gain,
    first_shift,
    query_weight,
    key_weight,
    value_weight,
    query_bias,
    value_bias,
    out_weight,
    out_bias,
    second_gain,
    second_shift,
    up_weight,
    up_bias,
    down_weight,
    down_bias,
    cotangent,
):
    layers = query_weight.shape[0]
    half = images.shape[1]
    hidden_width = 2 * up_weight.shape[2]
    y = lax.axis_index("tensor")
    far = 1 - y

    def own_rows(block, image):
        rows = lax.dynamic_slice_in_dim(block, image * SEQ, SEQ)
        return jnp.pad(rows, ((0, ROWS - SEQ), (0, 0)))

    biases = jnp.concatenate(
        (query_bias, jnp.zeros_like(query_bias), value_bias, out_bias, down_bias, up_bias), axis=1
    )
    biases = biases.astype(jnp.float32).reshape(layers * BIAS_ROWS, -1)
    biases = jnp.pad(biases, ((0, 24 - layers * BIAS_ROWS), (0, 0)))
    norms = jnp.concatenate((first_gain, first_shift, second_gain, second_shift))
    weights, cotangent_in, activations, kept = forward(
        (
            jnp.concatenate((query_weight, key_weight, value_weight), axis=2),
            jnp.swapaxes(out_weight, 1, 2),
            up_weight,
            jnp.swapaxes(down_weight, 1, 2),
        ),
        own_rows(images, y),
        jnp.stack((own_rows(images, far), own_rows(cotangent, far))),
        biases,
        norms.astype(jnp.float32),
    )

    def row(table, layer):
        return table[layer][None].astype(jnp.float32)

    upstream = in_order(own_rows(cotangent, y), cotangent_in, y, 1).astype(jnp.float32)
    small = [None] * layers
    terms = [None] * layers
    for layer in reversed(range(layers)):
        project_w, out_w, up_w, down_w = weights[layer]
        values = kept[layer]
        normed, projected, heads = values["normed"], values["projected"], values["heads"]
        normed_two, hidden = values["normed_two"], values["hidden"]
        centred_two, inverse_two = centre(values["middle"])
        centred, inverse = centre(values["incoming"])
        down_bias_sum = jnp.sum(upstream, axis=0)
        upstream_low = upstream.astype(LOW)
        down_term = (upstream_low, hidden)
        hidden_grad = (dot_rows(upstream_low, down_w) * values["slope"].astype(jnp.float32)).astype(
            LOW
        )
        up_bias_sum = jnp.sum(hidden_grad.astype(jnp.float32), axis=0)
        up_term = (normed_two, hidden_grad)
        normed_two_grad = dot_cols(hidden_grad, up_w)
        second_gain_sum = jnp.sum(normed_two_grad * centred_two, axis=0)
        second_shift_sum = jnp.sum(normed_two_grad, axis=0)
        upstream = upstream + whole_norm_backward(
            normed_two_grad, centred_two, inverse_two, row(second_gain, layer)
        )
        out_bias_sum = jnp.sum(upstream, axis=0)
        upstream_low = upstream.astype(LOW)
        out_term = (upstream_low, heads)
        heads_grad = dot_rows(upstream_low, out_w).astype(LOW)
        joined = mix_heads_backward(projected, heads_grad)
        joined_sums = jnp.sum(joined.astype(jnp.float32), axis=0).reshape(2, 3, half)
        project_term = (normed, joined)
        normed_grad = dot_cols(joined, project_w)
        first_gain_sum = jnp.sum(normed_grad * centred, axis=0)
        first_shift_sum = jnp.sum(normed_grad, axis=0)
        upstream = upstream + whole_norm_backward(
            normed_grad, centred, inverse, row(first_gain, layer)
        )
        small[layer] = jnp.concatenate(
            (
                joined_sums[:, 0].reshape(-1),
                joined_sums[:, 2].reshape(-1),
                out_bias_sum,
                up_bias_sum,
                down_bias_sum,
                first_gain_sum,
                first_shift_sum,
                second_gain_sum,
                second_shift_sum,
            )
        )
        terms[layer] = (project_term, out_term, up_term, down_term)

    width = 2 * half

    def columns(rows, t):
        return lax.dynamic_slice_in_dim(rows, t * half, half, axis=1)

    leaving = jnp.stack((columns(activations, far), columns(upstream, far).astype(LOW)))
    project_out, out_out, up_out, down_out, totals, arriving = settle_all(
        terms, jnp.stack(small).reshape(-1, width), leaving
    )
    totals = totals.reshape(layers, -1)
    project_out, out_out, up_out, down_out = [
        jnp.swapaxes(block, 1, 2).reshape(layers, BLOCK, -1)
        for block in (project_out, out_out, up_out, down_out)
    ]
    small_outs, at = [], 0
    for size in (width, width, width, hidden_width, width, width, width, width, width):
        small_outs.append(totals[:, at : at + size])
        at += size
    def to_owner(rows, arrived):
        return in_order(columns(rows, y)[:SEQ], arrived[:SEQ].astype(rows.dtype), y, 0)

    return (
        to_owner(activations, arriving[0]),
        to_owner(upstream, arriving[1]),
        project_out[:, :, :half],
        project_out[:, :, half : 2 * half],
        project_out[:, :, 2 * half :],
        jnp.swapaxes(out_out, 1, 2),
        up_out,
        jnp.swapaxes(down_out, 1, 2),
        *small_outs,
    )


def solution(mesh):
    in_specs = (
        P("wide", "tensor"),
        P(),
        P(),
        P(None, "wide", "tensor"),
        P(None, "wide", "tensor"),
        P(None, "wide", "tensor"),
        P(None, "tensor"),
        P(None, "tensor"),
        P(None, "tensor", "wide"),
        P(None, "tensor"),
        P(),
        P(),
        P(None, "wide", "tensor"),
        P(None, "tensor"),
        P(None, "tensor", "wide"),
        P(None, "tensor"),
        P("wide", "tensor"),
    )
    out_specs = (
        P("wide", "tensor"),
        P("wide", "tensor"),
        P(None, "wide", "tensor"),
        P(None, "wide", "tensor"),
        P(None, "wide", "tensor"),
        P(None, "tensor", "wide"),
        P(None, "wide", "tensor"),
        P(None, "tensor", "wide"),
        P(),
        P(),
        P(),
        P(),
        P(),
        P(),
        P(),
        P(),
        P(),
    )
    chosen = body
    if mesh.shape["wide"] == 16 and mesh.shape["tensor"] == 2:
        chosen = image_body
    return jax.shard_map(
        chosen, mesh=mesh, in_specs=in_specs, out_specs=out_specs, check_vma=False
    )
```

```python
import jax
import jax.numpy as jnp
from jax import lax
from jax.experimental import pallas as pl
from jax.experimental.pallas import tpu as pltpu
from jax.sharding import PartitionSpec as P

HEAD_DIM = 64
SEQ = 577
MICRO = 2


norm_eps = 1e-06


def row_totals(first_terms, second_terms):
    return lax.psum((first_terms, second_terms), "tensor")


def full_rows(share_low):
    return lax.all_gather(share_low, "tensor", axis=1, tiled=True)


def feature_total(partial_sums):
    return lax.psum_scatter(
        partial_sums.astype(jnp.bfloat16), "tensor", scatter_dimension=1, tiled=True
    ).astype(jnp.float32)


def fetch_weights(query_block, key_block, value_block, out_block, up_block, down_block):
    return (
        lax.all_gather(query_block, "wide", axis=0, tiled=True),
        lax.all_gather(key_block, "wide", axis=0, tiled=True),
        lax.all_gather(value_block, "wide", axis=0, tiled=True),
        lax.all_gather(out_block, "wide", axis=1, tiled=True),
        lax.all_gather(up_block, "wide", axis=0, tiled=True),
        lax.all_gather(down_block, "wide", axis=1, tiled=True),
    )


def settle_grads(query_piece, key_piece, value_piece, out_piece, up_piece, down_piece):
    return (
        lax.psum_scatter(
            query_piece.astype(jnp.bfloat16), "wide", scatter_dimension=0, tiled=True
        ).astype(jnp.float32),
        lax.psum_scatter(
            key_piece.astype(jnp.bfloat16), "wide", scatter_dimension=0, tiled=True
        ).astype(jnp.float32),
        lax.psum_scatter(
            value_piece.astype(jnp.bfloat16), "wide", scatter_dimension=0, tiled=True
        ).astype(jnp.float32),
        lax.psum_scatter(
            out_piece.astype(jnp.bfloat16), "wide", scatter_dimension=1, tiled=True
        ).astype(jnp.float32),
        lax.psum_scatter(
            up_piece.astype(jnp.bfloat16), "wide", scatter_dimension=0, tiled=True
        ).astype(jnp.float32),
        lax.psum_scatter(
            down_piece.astype(jnp.bfloat16), "wide", scatter_dimension=1, tiled=True
        ).astype(jnp.float32),
    )


def add_terms(earlier, latest):
    if earlier is None:
        return latest
    return jax.tree.map(jnp.add, earlier, latest)


def norm_forward(stream, gain, shift, full_width):
    first_terms, second_terms = row_totals(
        jnp.sum(stream, axis=1), jnp.sum(stream * stream, axis=1)
    )
    row_mean = first_terms / full_width
    inverse_std = lax.rsqrt(second_terms / full_width - row_mean * row_mean + norm_eps)
    centred = (stream - row_mean[:, None]) * inverse_std[:, None]
    return (centred * gain + shift, centred, inverse_std)


def norm_backward(upstream, centred, inverse_std, gain, full_width):
    scaled = upstream * gain
    first_terms, second_terms = row_totals(
        jnp.sum(scaled, axis=1), jnp.sum(scaled * centred, axis=1)
    )
    return inverse_std[:, None] * (
        scaled - first_terms[:, None] / full_width - centred * (second_terms[:, None] / full_width)
    )


def attention_forward(queries, keys_here, values_here, image_count, heads_here):
    score_scale = HEAD_DIM ** (-0.5)
    shape_four = (image_count, SEQ, heads_here, HEAD_DIM)
    query_four = queries.reshape(shape_four)
    key_four = keys_here.reshape(shape_four)
    value_four = values_here.reshape(shape_four)
    scores = (
        jnp.einsum("iqhd,ikhd->ihqk", query_four, key_four, preferred_element_type=jnp.float32)
        * score_scale
    )
    row_peak = jnp.max(scores, axis=-1, keepdims=True)
    exponent = jnp.exp(scores - row_peak)
    row_total = jnp.sum(exponent, axis=-1, keepdims=True)
    weights_soft = (exponent / row_total).astype(jnp.bfloat16)
    mixed_heads = jnp.einsum(
        "ihqk,ikhd->iqhd", weights_soft, value_four, preferred_element_type=jnp.float32
    )
    log_total = row_peak[..., 0] + jnp.log(row_total[..., 0])
    return (mixed_heads.reshape(queries.shape).astype(jnp.bfloat16), log_total)


def attention_backward(
    queries, keys_here, values_here, log_total, mixed_grad, image_count, heads_here
):
    score_scale = HEAD_DIM ** (-0.5)
    shape_four = (image_count, SEQ, heads_here, HEAD_DIM)
    query_four = queries.reshape(shape_four)
    key_four = keys_here.reshape(shape_four)
    value_four = values_here.reshape(shape_four)
    grad_four = mixed_grad.reshape(shape_four)
    scores = (
        jnp.einsum("iqhd,ikhd->ihqk", query_four, key_four, preferred_element_type=jnp.float32)
        * score_scale
    )
    weights_soft = jnp.exp(scores - log_total[..., None])
    weight_grad = jnp.einsum(
        "iqhd,ikhd->ihqk", grad_four, value_four, preferred_element_type=jnp.float32
    )
    row_delta = jnp.sum(weight_grad * weights_soft, axis=-1, keepdims=True)
    score_grad = (weights_soft * (weight_grad - row_delta)).astype(jnp.bfloat16)
    query_grad = (
        jnp.einsum("ihqk,ikhd->iqhd", score_grad, key_four, preferred_element_type=jnp.float32)
        * score_scale
    )
    key_grad = (
        jnp.einsum("ihqk,iqhd->ikhd", score_grad, query_four, preferred_element_type=jnp.float32)
        * score_scale
    )
    value_grad = jnp.einsum(
        "ihqk,iqhd->ikhd",
        weights_soft.astype(jnp.bfloat16),
        grad_four,
        preferred_element_type=jnp.float32,
    )
    flat_shape = queries.shape
    return (
        query_grad.reshape(flat_shape),
        key_grad.reshape(flat_shape),
        value_grad.reshape(flat_shape),
    )


def gelu_slope(values):
    normal_cdf = 0.5 * (1.0 + lax.erf(values * 0.7071067811865476))
    return normal_cdf + values * jnp.exp(-0.5 * values * values) * 0.3989422804014327


def body(
    images,
    first_gain,
    first_shift,
    query_weight,
    key_weight,
    value_weight,
    query_bias,
    value_bias,
    out_weight,
    out_bias,
    second_gain,
    second_shift,
    up_weight,
    up_bias,
    down_weight,
    down_bias,
    cotangent,
):
    layer_count = query_weight.shape[0]
    feature_block = images.shape[1]
    tensor_count = lax.axis_size("tensor")
    full_width = feature_block * tensor_count
    heads_here = feature_block // HEAD_DIM
    tensor_place = lax.axis_index("tensor")
    micro_rows = images.shape[0] // MICRO
    image_count = micro_rows // SEQ

    def gain_share(param_table, layer_idx):
        return lax.dynamic_slice_in_dim(
            param_table[layer_idx], tensor_place * feature_block, feature_block
        )

    def layer_weights(layer_idx):
        return fetch_weights(
            query_weight[layer_idx],
            key_weight[layer_idx],
            value_weight[layer_idx],
            out_weight[layer_idx],
            up_weight[layer_idx],
            down_weight[layer_idx],
        )

    weight_sums = [None] * layer_count
    small_sums = [None] * layer_count
    activation_parts = []
    gradient_parts = []
    for micro_idx in range(MICRO):
        row_start = micro_idx * micro_rows
        stream = images[row_start : row_start + micro_rows].astype(jnp.float32)
        saved_state = []
        for layer_idx in range(layer_count):
            query_full, key_full, value_full, out_full, up_full, down_full = layer_weights(
                layer_idx
            )
            normed, centred_one, inverse_one = norm_forward(
                stream,
                gain_share(first_gain, layer_idx),
                gain_share(first_shift, layer_idx),
                full_width,
            )
            normed_full = full_rows(normed.astype(jnp.bfloat16))
            joined_weight = jnp.concatenate((query_full, key_full, value_full), axis=1)
            projected = jnp.dot(normed_full, joined_weight, preferred_element_type=jnp.float32)
            queries = (projected[:, :feature_block] + query_bias[layer_idx]).astype(jnp.bfloat16)
            keys_here = projected[:, feature_block : 2 * feature_block].astype(jnp.bfloat16)
            values_here = (projected[:, 2 * feature_block :] + value_bias[layer_idx]).astype(
                jnp.bfloat16
            )
            mixed_heads, log_total = attention_forward(
                queries, keys_here, values_here, image_count, heads_here
            )
            attention_sum = feature_total(
                jnp.dot(mixed_heads, out_full, preferred_element_type=jnp.float32)
            )
            after_attention = stream + attention_sum + out_bias[layer_idx]
            normed_two, centred_two, inverse_two = norm_forward(
                after_attention,
                gain_share(second_gain, layer_idx),
                gain_share(second_shift, layer_idx),
                full_width,
            )
            normed_two_full = full_rows(normed_two.astype(jnp.bfloat16))
            hidden_pre = (
                jnp.dot(normed_two_full, up_full, preferred_element_type=jnp.float32)
                + up_bias[layer_idx]
            )
            hidden = jax.nn.gelu(hidden_pre, approximate=False).astype(jnp.bfloat16)
            feedforward_sum = feature_total(
                jnp.dot(hidden, down_full, preferred_element_type=jnp.float32)
            )
            saved_state.append(
                (
                    centred_one,
                    inverse_one,
                    normed_full,
                    queries,
                    keys_here,
                    values_here,
                    mixed_heads,
                    log_total,
                    centred_two,
                    inverse_two,
                    normed_two_full,
                    hidden_pre,
                    hidden,
                )
            )
            stream = after_attention + feedforward_sum + down_bias[layer_idx]
        activation_parts.append(stream.astype(jnp.bfloat16))
        upstream = cotangent[row_start : row_start + micro_rows].astype(jnp.float32)
        for layer_idx in reversed(range(layer_count)):
            query_full, key_full, value_full, out_full, up_full, down_full = layer_weights(
                layer_idx
            )
            (
                centred_one,
                inverse_one,
                normed_full,
                queries,
                keys_here,
                values_here,
                mixed_heads,
                log_total,
                centred_two,
                inverse_two,
                normed_two_full,
                hidden_pre,
                hidden,
            ) = saved_state[layer_idx]
            down_bias_term = jnp.sum(upstream, axis=0)
            upstream_full = full_rows(upstream.astype(jnp.bfloat16))
            down_term = jnp.einsum(
                "rc,rd->cd", hidden, upstream_full, preferred_element_type=jnp.float32
            )
            hidden_grad = jnp.einsum(
                "rd,cd->rc", upstream_full, down_full, preferred_element_type=jnp.float32
            )
            pre_grad = (hidden_grad * gelu_slope(hidden_pre)).astype(jnp.bfloat16)
            up_bias_term = jnp.sum(pre_grad.astype(jnp.float32), axis=0)
            up_term = jnp.einsum(
                "rd,rc->dc", normed_two_full, pre_grad, preferred_element_type=jnp.float32
            )
            normed_two_grad = feature_total(
                jnp.einsum("rc,dc->rd", pre_grad, up_full, preferred_element_type=jnp.float32)
            )
            second_gain_term = jnp.sum(normed_two_grad * centred_two, axis=0)
            second_shift_term = jnp.sum(normed_two_grad, axis=0)
            upstream = upstream + norm_backward(
                normed_two_grad,
                centred_two,
                inverse_two,
                gain_share(second_gain, layer_idx),
                full_width,
            )
            out_bias_term = jnp.sum(upstream, axis=0)
            upstream_full = full_rows(upstream.astype(jnp.bfloat16))
            out_term = jnp.einsum(
                "rc,rd->cd", mixed_heads, upstream_full, preferred_element_type=jnp.float32
            )
            mixed_grad = jnp.einsum(
                "rd,cd->rc", upstream_full, out_full, preferred_element_type=jnp.float32
            ).astype(jnp.bfloat16)
            query_grad, key_grad, value_grad = attention_backward(
                queries, keys_here, values_here, log_total, mixed_grad, image_count, heads_here
            )
            joined_grad = jnp.concatenate((query_grad, key_grad, value_grad), axis=1).astype(
                jnp.bfloat16
            )
            joined_float = joined_grad.astype(jnp.float32)
            query_bias_term = jnp.sum(joined_float[:, :feature_block], axis=0)
            value_bias_term = jnp.sum(joined_float[:, 2 * feature_block :], axis=0)
            joined_term = jnp.einsum(
                "rd,rc->dc", normed_full, joined_grad, preferred_element_type=jnp.float32
            )
            joined_weight = jnp.concatenate((query_full, key_full, value_full), axis=1)
            normed_grad = feature_total(
                jnp.einsum(
                    "rc,dc->rd", joined_grad, joined_weight, preferred_element_type=jnp.float32
                )
            )
            first_gain_term = jnp.sum(normed_grad * centred_one, axis=0)
            first_shift_term = jnp.sum(normed_grad, axis=0)
            upstream = upstream + norm_backward(
                normed_grad, centred_one, inverse_one, gain_share(first_gain, layer_idx), full_width
            )
            query_term = joined_term[:, :feature_block]
            key_term = joined_term[:, feature_block : 2 * feature_block]
            value_term = joined_term[:, 2 * feature_block :]
            weight_sums[layer_idx] = add_terms(
                weight_sums[layer_idx],
                settle_grads(query_term, key_term, value_term, out_term, up_term, down_term),
            )
            small_sums[layer_idx] = add_terms(
                small_sums[layer_idx],
                (
                    query_bias_term,
                    value_bias_term,
                    out_bias_term,
                    up_bias_term,
                    down_bias_term,
                    first_gain_term,
                    first_shift_term,
                    second_gain_term,
                    second_shift_term,
                ),
            )
        gradient_parts.append(upstream)
    share_sets = []
    for layer_idx in range(layer_count):
        share_sets.append(weight_sums[layer_idx])
    weight_outputs = [
        jnp.stack([share_sets[layer_idx][entry_idx] for layer_idx in range(layer_count)])
        for entry_idx in range(6)
    ]
    small_stack = [
        jnp.stack([small_sums[layer_idx][entry_idx] for layer_idx in range(layer_count)])
        for entry_idx in range(9)
    ]
    widened = [
        lax.dynamic_update_slice_in_dim(
            jnp.zeros((layer_count, share_piece.shape[1] * tensor_count), jnp.float32),
            share_piece,
            tensor_place * share_piece.shape[1],
            1,
        )
        for share_piece in small_stack
    ]
    totals = lax.psum(
        (
            widened[0],
            widened[1],
            widened[2],
            widened[3],
            widened[4],
            widened[5],
            widened[6],
            widened[7],
            widened[8],
        ),
        ("wide", "tensor"),
    )
    activations = jnp.concatenate(activation_parts, axis=0)
    input_gradient = jnp.concatenate(gradient_parts, axis=0)
    return (
        activations,
        input_gradient,
        weight_outputs[0],
        weight_outputs[1],
        weight_outputs[2],
        weight_outputs[3],
        weight_outputs[4],
        weight_outputs[5],
        totals[0],
        totals[1],
        totals[2],
        totals[3],
        totals[4],
        totals[5],
        totals[6],
        totals[7],
        totals[8],
    )


MESH_IDS = pl.DeviceIdType.MESH
LOW = jnp.bfloat16
BLOCK = 64
ROWS = -(-SEQ // 16) * 16
DEEP = -(-SEQ // 128) * 128


def place():
    wide = lax.axis_index("wide")
    return (
        lax.div(wide, 4),
        lax.rem(lax.div(wide, 2), 2),
        lax.rem(wide, 2),
        lax.axis_index("tensor"),
    )


def neighbours():
    z, x, c, y = place()

    def at(z, x, c, y):
        return (z * 4 + x * 2 + c, y)

    return {
        "core": at(z, x, 1 - c, y),
        "x": at(z, 1 - x, c, y),
        "y": at(z, x, c, 1 - y),
        "z1": at(z + 1 - 2 * lax.rem(z, 2), x, c, y),
        "z2": at(lax.rem(z + 2, 4), x, c, y),
    }


LINKS = ("core", "x", "y", "z1", "z2")


def greet(partners):
    barrier = pltpu.get_barrier_semaphore()
    for link in LINKS:
        pl.semaphore_signal(barrier, inc=1, device_id=partners[link], device_id_type=MESH_IDS)
    pl.semaphore_wait(barrier, len(LINKS))


def dot_rows(left, right):
    return lax.dot_general(
        left, right, (((1,), (0,)), ((), ())), preferred_element_type=jnp.float32
    )


def dot_cols(left, right):
    return lax.dot_general(
        left, right, (((1,), (1,)), ((), ())), preferred_element_type=jnp.float32
    )


def dot_tokens(left, right):
    return lax.dot_general(
        left, right, (((0,), (0,)), ((), ())), preferred_element_type=jnp.float32
    )


PAIR = 2 * HEAD_DIM


def turned_softmax(keys_here, queries):
    scores = dot_cols(keys_here, queries)
    exponent = jnp.exp(scores - jnp.max(scores, axis=0, keepdims=True))
    return exponent * (1.0 / jnp.sum(exponent, axis=0, keepdims=True))


def store_rows(ref, at, pieces):
    full = SEQ // 16 * 16
    ref[pl.ds(full, ROWS - full), pl.ds(at, PAIR)] = jnp.zeros((ROWS - full, PAIR), LOW)
    ref[pl.ds(0, SEQ), pl.ds(at, PAIR)] = jnp.concatenate(pieces, axis=1)


def gather_parts(width):
    last = 256 if width >= 1024 else 0
    share = (width - last) // 2
    return share, last


def gather_stages(z, x, c, y, whole, start, width):
    share, last = gather_parts(width)

    def cols(t, at, size):
        return pl.ds(pl.multiple_of(t * whole + start + at, 128), size)

    all_rows = pl.ds(0, BLOCK)
    pair = pl.ds(lax.div(z, 2) * 2, 2)
    every_z, every_x = pl.ds(0, 4), pl.ds(0, 2)
    far_x, far_y = 1 - x, 1 - y

    def part_a(t):
        return cols(t, 0, share)

    def part_b(t):
        return cols(t, share, share)

    def part_ab(t):
        return cols(t, 0, 2 * share)

    def part_c(t):
        return cols(t, 2 * share, last)

    stages = [
        [("z1", (z, x, c, all_rows, part_ab(y)))],
        [("z2", (pair, x, c, all_rows, part_ab(y)))],
        [
            ("x", (every_z, x, c, all_rows, part_a(y))),
            ("y", (every_z, x, c, all_rows, part_b(y))),
            ("core", (every_z, x, c, all_rows, part_ab(y))),
        ],
        [
            ("y", (every_z, every_x, c, all_rows, part_a(y))),
            ("x", (every_z, x, c, all_rows, part_b(0))),
            ("x", (every_z, x, c, all_rows, part_b(1))),
            ("core", (every_z, far_x, c, all_rows, part_a(y))),
            ("core", (every_z, x, c, all_rows, part_b(far_y))),
        ],
        [
            ("core", (every_z, every_x, c, all_rows, part_a(far_y))),
            ("core", (every_z, far_x, c, all_rows, part_b(0))),
            ("core", (every_z, far_x, c, all_rows, part_b(1))),
        ],
    ]
    if last:
        stages[0].append(("x", (z, x, c, all_rows, part_c(y))))
        stages[1].append(("y", (z, every_x, c, all_rows, part_c(y))))
        for t in range(2):
            stages[2].append(("z1", (z, every_x, c, all_rows, part_c(t))))
            stages[3].append(("z2", (pair, every_x, c, all_rows, part_c(t))))
            stages[4].append(("core", (every_z, every_x, c, all_rows, part_c(t))))
    return stages


GATHER_COPIES = 21
GATHER_DEPTH = 5


class Gather:
    def __init__(self, chunks):
        self.chunks = chunks

    def scratch(self):
        count = len(self.chunks)
        return dict(
            gather_send=pltpu.SemaphoreType.DMA((count, GATHER_COPIES)),
            gather_recv=pltpu.SemaphoreType.DMA((count, GATHER_COPIES)),
            gather_own=pltpu.SemaphoreType.DMA((count,)),
        )

    def bind(self, shards, wholes, refs):
        self.wholes = wholes
        self.send_sem, self.recv_sem, own_sem = refs
        z, x, c, y = place()
        self.partners = neighbours()
        self.plans, self.own, self.flying = [], [], {}
        for chunk, (matrix, start, width) in enumerate(self.chunks):
            whole = shards[matrix].shape[1]
            self.plans.append(gather_stages(z, x, c, y, whole, start, width))
            mine = pl.ds(pl.multiple_of(y * whole + start, 128), width)
            copy = pltpu.make_async_copy(
                shards[matrix].at[:, pl.ds(start, width)],
                wholes[matrix].at[z, x, c, pl.ds(0, BLOCK), mine],
                own_sem.at[chunk],
            )
            copy.start()
            self.own.append(copy)

    def tick(self, tick):
        done = None
        for stage_idx in range(GATHER_DEPTH, -1, -1):
            chunk = tick - stage_idx
            if chunk < 0 or chunk >= len(self.chunks):
                continue
            if stage_idx == 0:
                self.own[chunk].wait()
            for copy in self.flying.get((chunk, stage_idx - 1), ()):
                copy.wait_recv()
            if stage_idx == GATHER_DEPTH:
                done = chunk
                continue
            started = []
            plan = self.plans[chunk]
            base = sum(len(stage) for stage in plan[:stage_idx])
            whole = self.wholes[self.chunks[chunk][0]]
            for entry, (link, index) in enumerate(plan[stage_idx]):
                copy = pltpu.make_async_remote_copy(
                    src_ref=whole.at[index],
                    dst_ref=whole.at[index],
                    send_sem=self.send_sem.at[chunk, base + entry],
                    recv_sem=self.recv_sem.at[chunk, base + entry],
                    device_id=self.partners[link],
                    device_id_type=MESH_IDS,
                )
                copy.start()
                started.append(copy)
            self.flying[(chunk, stage_idx)] = started
        return done

    def finish(self):
        for started in self.flying.values():
            for copy in started:
                copy.wait_send()


BIAS_ROWS = 9
SAVED = ("normed", "projected", "heads", "normed_two", "hidden", "slope", "middle", "incoming")


class Forward:
    def __init__(self, layers, widths):
        self.layers, self.widths = layers, widths
        chunks = []
        for layer in range(layers):
            base = layer * len(widths)
            for kind, width in enumerate(widths):
                split = 2 if layer == layers - 1 and kind == len(widths) - 1 else 1
                part = width // split
                chunks += [(base + kind, k * part, part) for k in range(split)]
        self.gather = Gather(chunks)

    def scratch(self):
        project, out, up, down = self.widths
        low, full = (lambda cols: pltpu.VMEM((ROWS, cols), LOW)), pltpu.VMEM((ROWS, 1024), jnp.float32)
        sem = pltpu.SemaphoreType.DMA
        own = dict(
            weights_project=pltpu.VMEM((4, 2, 2, BLOCK, 2 * project), LOW),
            weights_out=pltpu.VMEM((4, 2, 2, BLOCK, 2 * out), LOW),
            weights_up=pltpu.VMEM((4, 2, 2, BLOCK, 2 * up), LOW),
            weights_down=pltpu.VMEM((4, 2, 2, BLOCK, 2 * down), LOW),
            stream=full,
            tokens_in=low(512),
            biases=pltpu.VMEM((2, 24, 512), jnp.float32),
            normed=low(1024),
            projected=low(2 * project),
            heads=low(2 * out),
            normed_two=low(1024),
            hidden=low(2 * up),
            slope=low(2 * up),
            weight_sem=sem((self.layers * 4, 1)),
            split_sem=sem((2, 2)),
            saved_sem=sem((self.layers, len(SAVED))),
            swap_send=sem((3,)),
            swap_recv=sem((3,)),
            bias_sem=sem((1,)),
        )
        return {**own, **self.gather.scratch()}

    def bind(self, inputs, outputs, refs):
        names = list(self.scratch())
        for name, ref in zip(names, refs, strict=True):
            setattr(self, name, ref)
        shards, self.near, self.far, bias_ref, self.norms = (
            inputs[:4],
            inputs[4],
            inputs[5],
            inputs[6],
            inputs[7],
        )
        count = self.layers * 4
        self.wholes, outputs = outputs[:count], outputs[count:]
        self.cotangent_in, self.activations, outputs = outputs[0], outputs[1], outputs[2:]
        self.saved_out = [outputs[k * len(SAVED) : (k + 1) * len(SAVED)] for k in range(self.layers)]
        self.saving, self.loading = {}, {}
        self.y = lax.axis_index("tensor")
        copy = pltpu.make_async_copy(bias_ref, self.biases.at[self.y], self.bias_sem.at[0])
        copy.start()
        self.gather.bind(
            [shards[m % 4].at[m // 4] for m in range(count)],
            self.wholes,
            [getattr(self, name) for name in self.gather.scratch()],
        )
        copy.wait()

    def swap(self):
        partner = self.gather.partners["y"]
        pairs = (
            (self.biases.at[self.y], self.biases.at[self.y]),
            (self.far.at[0], self.tokens_in),
            (self.far.at[1], self.cotangent_in),
        )
        self.swaps = []
        for entry, (source, target) in enumerate(pairs):
            copy = pltpu.make_async_remote_copy(
                src_ref=source,
                dst_ref=target,
                send_sem=self.swap_send.at[entry],
                recv_sem=self.swap_recv.at[entry],
                device_id=partner,
                device_id_type=MESH_IDS,
            )
            copy.start()
            self.swaps.append(copy)

    def save(self, layer, name, source):
        entry = SAVED.index(name)
        copy = pltpu.make_async_copy(
            source, self.saved_out[layer][entry], self.saved_sem.at[layer, entry]
        )
        copy.start()
        self.saving[(layer, name)] = copy

    def saved(self, layer, name):
        if (layer, name) in self.saving:
            self.saving.pop((layer, name)).wait()

    def load(self, chunk):
        matrix, start, width = self.gather.chunks[chunk]
        whole = self.gather.wholes[matrix]
        buffer = (self.weights_project, self.weights_out, self.weights_up, self.weights_down)[
            matrix % 4
        ]
        copies = []
        full = whole.shape[4] // 2
        if width == full:
            copies.append((whole, buffer))
        else:
            for t in range(2):
                at = (slice(None),) * 4 + (pl.ds(t * full + start, width),)
                copies.append((whole.at[at], buffer.at[at]))
        started = self.loading.setdefault(matrix, [])
        for entry, (source, target) in enumerate(copies):
            half = 0 if start == 0 else 1
            if len(copies) == 2:
                sem = self.split_sem.at[half, entry]
            else:
                sem = self.weight_sem.at[matrix, 0]
            copy = pltpu.make_async_copy(source, target, sem)
            copy.start()
            started.append(copy)

    def wait_weights(self, matrix):
        for copy in self.loading.pop(matrix):
            copy.wait()

    def bias_row(self, row):
        return jnp.concatenate([self.biases[t, pl.ds(row, 1), :] for t in range(2)], axis=1)

    def norm(self, target, gain_row, shift_row, bias_at):
        gain = self.norms[pl.ds(gain_row, 1), :]
        shift = self.norms[pl.ds(shift_row, 1), :]
        bias = None if bias_at is None else self.bias_row(bias_at)

        @pl.loop(0, ROWS // 16)
        def _(step):
            rows = pl.ds(pl.multiple_of(step * 16, 16), 16)
            values = self.stream[rows, :]
            if bias is not None:
                values = values + bias
                self.stream[rows, :] = values
            mean = jnp.mean(values, axis=1, keepdims=True)
            square = jnp.mean(values * values, axis=1, keepdims=True)
            inverse = lax.rsqrt(square - mean * mean + norm_eps)
            target[rows, :] = ((values - mean) * inverse * gain + shift).astype(LOW)

    def begin(self):
        for copy in self.swaps:
            copy.wait_recv()
        y = self.y
        near_at = pl.ds(pl.multiple_of(y * 512, 512), 512)
        far_at = pl.ds(pl.multiple_of((1 - y) * 512, 512), 512)
        self.stream[:, near_at] = self.near[...].astype(jnp.float32)
        self.stream[:, far_at] = self.tokens_in[...].astype(jnp.float32)

    def project(self, layer):
        self.saved(layer - 1, "normed")
        self.norm(
            self.normed,
            layer,
            self.layers + layer,
            None if layer == 0 else (layer - 1) * BIAS_ROWS + 4,
        )
        self.save(layer, "incoming", self.stream)
        self.save(layer, "normed", self.normed)
        self.saved(layer - 1, "projected")
        self.wait_weights(layer * 4)
        parts = 6

        @pl.loop(0, parts)
        def _(part):
            cols = pl.ds(pl.multiple_of(part * 512, 512), 512)
            weights = self.weights_project[:, :, :, :, cols].reshape(1024, 512)
            row = layer * BIAS_ROWS + lax.rem(part, 3)
            bias = self.biases[lax.div(part, 3), pl.ds(row, 1), :]
            self.projected[:, cols] = (dot_rows(self.normed[...], weights) + bias).astype(LOW)

        self.save(layer, "projected", self.projected)

    def mix(self, layer, first, last):
        if first == 0:
            self.saved(layer - 1, "heads")
        half = self.heads.shape[1] // 2

        @pl.loop(first, last)
        def _(step):
            for t in range(2):
                def at(part):
                    start = (t * 3 + part) * half + step * PAIR
                    return pl.ds(pl.multiple_of(start, PAIR), PAIR)

                queries = self.projected[pl.ds(0, SEQ), at(0)] * jnp.asarray(HEAD_DIM**-0.5, LOW)
                keys_here = self.projected[pl.ds(0, SEQ), at(1)]
                values_here = self.projected[pl.ds(0, SEQ), at(2)]
                pieces = []
                for head in range(2):
                    cols = slice(head * HEAD_DIM, (head + 1) * HEAD_DIM)
                    soft = turned_softmax(keys_here[:, cols], queries[:, cols])
                    pieces.append(dot_tokens(soft.astype(LOW), values_here[:, cols]).astype(LOW))
                store_rows(self.heads, pl.multiple_of(t * half + step * PAIR, PAIR), pieces)

        if last * PAIR == half:
            self.save(layer, "heads", self.heads)

    def attend(self, layer):
        self.wait_weights(layer * 4 + 1)
        self.saved(layer, "incoming")

        @pl.loop(0, 4)
        def _(row):
            cols = pl.ds(pl.multiple_of(row * 256, 256), 256)
            weights = self.weights_out[row].reshape(256, -1)
            self.stream[:, cols] = self.stream[:, cols] + dot_cols(self.heads[...], weights)

        self.saved(layer - 1, "normed_two")
        self.norm(
            self.normed_two,
            2 * self.layers + layer,
            3 * self.layers + layer,
            layer * BIAS_ROWS + 3,
        )
        self.save(layer, "normed_two", self.normed_two)
        self.save(layer, "middle", self.stream)

    def feed_up(self, layer, first, last):
        if first == 0:
            self.saved(layer - 1, "hidden")
            self.saved(layer - 1, "slope")
            self.wait_weights(layer * 4 + 2)

        @pl.loop(first, last)
        def _(part):
            cols = pl.ds(pl.multiple_of(part * 512, 512), 512)
            weights = self.weights_up[:, :, :, :, cols].reshape(1024, 512)
            row = layer * BIAS_ROWS + 5 + lax.rem(part, 4)
            bias = self.biases[lax.div(part, 4), pl.ds(row, 1), :]
            before = dot_rows(self.normed_two[...], weights) + bias
            normal = 0.5 * (1.0 + lax.erf(before * 0.7071067811865476))
            self.hidden[:, cols] = (before * normal).astype(LOW)
            density = jnp.exp(-0.5 * before * before) * 0.3989422804014327
            self.slope[:, cols] = (normal + before * density).astype(LOW)

        if last * 512 == self.hidden.shape[1]:
            self.save(layer, "hidden", self.hidden)
            self.save(layer, "slope", self.slope)

    def feed_down(self, layer, first, last):
        if first == 0:
            self.saved(layer, "middle")
            self.wait_weights(layer * 4 + 3)

        @pl.loop(first, last)
        def _(row):
            cols = pl.ds(pl.multiple_of(row * 256, 256), 256)
            weights = self.weights_down[row].reshape(256, -1)
            self.stream[:, cols] = self.stream[:, cols] + dot_cols(self.hidden[...], weights)

    def end(self):
        bias = self.bias_row((self.layers - 1) * BIAS_ROWS + 4)

        @pl.loop(0, ROWS // 16)
        def _(step):
            rows = pl.ds(pl.multiple_of(step * 16, 16), 16)
            self.activations[rows, :] = (self.stream[rows, :] + bias).astype(LOW)

    def work(self):
        steps = [(0, 1, self.begin)]
        for layer in range(self.layers):
            base = layer * 4
            steps += [
                (base, 6, lambda layer=layer: self.project(layer)),
                (base, 7, lambda layer=layer: self.mix(layer, 0, 2)),
                (base, 7, lambda layer=layer: self.mix(layer, 2, 4)),
                (base + 1, 4, lambda layer=layer: self.attend(layer)),
                (base + 2, 6, lambda layer=layer: self.feed_up(layer, 0, 4)),
                (base + 2, 6, lambda layer=layer: self.feed_up(layer, 4, 8)),
                (base + 3, 4, lambda layer=layer: self.feed_down(layer, 0, 2)),
                (base + 3, 4, lambda layer=layer: self.feed_down(layer, 2, 4)),
            ]
        return steps + [(self.layers * 4 - 1, 1, self.end)]

    def run(self):
        greet(self.gather.partners)
        self.swap()
        steps = self.work()
        ready = set()
        remaining = {}
        for matrix, _, _ in self.gather.chunks:
            remaining[matrix] = remaining.get(matrix, 0) + 1
        ticks = len(self.gather.chunks) + GATHER_DEPTH
        for tick in range(ticks):
            budget = WORK_A_TICK
            done = self.gather.tick(tick)
            while steps and steps[0][0] in ready and budget > 0:
                _, cost, step = steps.pop(0)
                budget -= cost
                step()
            if done is not None:
                self.free_buffer(done, steps)
                matrix = self.gather.chunks[done][0]
                self.load(done)
                remaining[matrix] -= 1
                if remaining[matrix] == 0:
                    ready.add(matrix)
        for _, _, step in steps:
            step()
        self.gather.finish()
        for copy in self.swaps:
            copy.wait_send()
        for copy in self.saving.values():
            copy.wait()

    def free_buffer(self, chunk, steps):
        matrix = self.gather.chunks[chunk][0]
        while steps and any(entry[0] == matrix - 4 for entry in steps):
            steps.pop(0)[2]()


WORK_A_TICK = 12


def forward(shards, near, far, biases, norms):
    layers = shards[0].shape[0]
    widths = [shard.shape[2] for shard in shards]
    plan = Forward(layers, widths)
    project, out, up, down = widths
    low = lambda cols: jax.ShapeDtypeStruct((ROWS, cols), LOW)
    full = jax.ShapeDtypeStruct((ROWS, 1024), jnp.float32)
    saved = [
        low(1024), low(2 * project), low(2 * out), low(1024), low(2 * up), low(2 * up), full, full
    ]
    wholes = [
        jax.ShapeDtypeStruct((4, 2, 2, BLOCK, 2 * width), LOW) for width in widths
    ] * layers
    outs = [*wholes, low(512), low(1024), *(saved * layers)]
    any_spec, vmem_spec = pl.BlockSpec(memory_space=pl.ANY), pl.BlockSpec(memory_space=pltpu.VMEM)
    out_specs = [any_spec] * len(outs)
    out_specs[len(wholes) + 1] = vmem_spec

    def kernel(*refs):
        outputs = refs[8 : 8 + len(outs)]
        plan.bind(refs[:8], outputs, refs[8 + len(outs) :])
        plan.run()

    results = pl.pallas_call(
        kernel,
        out_shape=outs,
        in_specs=[any_spec] * 4 + [vmem_spec, any_spec, any_spec, vmem_spec],
        out_specs=out_specs,
        scratch_shapes=list(plan.scratch().values()),
        compiler_params=pltpu.CompilerParams(
            collective_id=0, has_side_effects=True, vmem_limit_bytes=60 * 1024 * 1024
        ),
        cost_estimate=pl.CostEstimate(
            flops=60 * 1024**3, bytes_accessed=700 * 1024 * 1024, transcendentals=0
        ),
        name="forward",
    )(*shards, near, far, biases, norms)
    whole, results = results[: len(wholes)], results[len(wholes) :]
    weights = [
        [whole[layer * 4 + kind] for kind in range(4)] for layer in range(layers)
    ]
    cotangent_in, activations, results = results[0], results[1], results[2:]
    kept = [
        dict(zip(SAVED, results[k * len(SAVED) : (k + 1) * len(SAVED)])) for k in range(layers)
    ]
    return weights, cotangent_in, activations, kept


COLS = 256
SETTLE_DEPTH = 6
VAL_SLOTS, ARRIVAL_SLOTS, REST_SLOTS, TURNED_SLOTS = 2, 2, 4, 3


class Settle:
    def __init__(self, widths, pairs):
        self.widths, self.pairs = widths, pairs

    def scratch(self):
        rows = (4, 2, 2, BLOCK, COLS)
        pairs, slots = len(self.pairs), ARRIVAL_SLOTS
        sem = pltpu.SemaphoreType.DMA
        return dict(
            left_in=pltpu.VMEM((ROWS, 1024), LOW),
            left_turned=pltpu.VMEM((TURNED_SLOTS, 1024, DEEP), LOW),
            right_in=pltpu.VMEM((2, 2, 4, DEEP, COLS), LOW),
            core_out=pltpu.VMEM((2, 2, *rows), LOW),
            core_in=pltpu.VMEM((slots, 2, 2, *rows), LOW),
            val=pltpu.VMEM((VAL_SLOTS, 2, 2, *rows), LOW),
            rest=pltpu.VMEM((REST_SLOTS, 2, 4, 2, BLOCK, COLS), LOW),
            first_a=pltpu.VMEM((slots, *rows), LOW),
            first_b=pltpu.VMEM((slots, 2, 4, 2, BLOCK, COLS), LOW),
            second=pltpu.VMEM((slots, 2, 4, 2, BLOCK, COLS), LOW),
            third=pltpu.VMEM((slots, 2, 2, 2, BLOCK, COLS), LOW),
            fourth=pltpu.VMEM((slots, 2, 2, BLOCK, COLS), LOW),
            fifth=pltpu.VMEM((slots, 2, BLOCK, COLS), LOW),
            result=pltpu.VMEM((2, 2, 2, BLOCK, COLS), jnp.float32),
            result_sem=sem((2, 2, 2)),
            send_sem=sem((pairs, 2, SETTLE_DEPTH)),
            recv_sem=sem((pairs, 2, SETTLE_DEPTH)),
            right_sem=sem((pairs, 2, 4)),
            left_sem=sem((1,)),
        )

    def bind(self, lefts, rights, outs, refs):
        self.lefts, self.rights, self.outs = lefts, rights, outs
        for name, ref in zip(self.scratch(), refs, strict=True):
            setattr(self, name, ref)
        self.z, self.x, self.c, self.y = place()
        self.partners = neighbours()
        self.copies, self.turned, self.results = {}, {}, {}
        tail = ROWS // 128 * 128
        self.left_turned[:, :, pl.ds(tail, DEEP - tail)] = jnp.zeros(
            (TURNED_SLOTS, 1024, DEEP - tail), LOW
        )
        self.right_in[:, :, :, pl.ds(ROWS, DEEP - ROWS)] = jnp.zeros(
            (2, 2, 4, DEEP - ROWS, COLS), LOW
        )

    def load(self, pair):
        for unit, (matrix, step) in enumerate(self.pairs[pair]):
            width = self.widths[matrix]
            for t in range(2):
                for core in range(2):
                    at = t * width + core * (width // 2) + step * COLS
                    copy = pltpu.make_async_copy(
                        self.rights[matrix].at[:, pl.ds(at, COLS)],
                        self.right_in.at[pair % 2, unit, 2 * t + core, pl.ds(0, ROWS)],
                        self.right_sem.at[pair, unit, 2 * t + core],
                    )
                    copy.start()
                    self.copies[(pair, unit, "right", 2 * t + core)] = copy

    def turn(self, matrix):
        if matrix in self.turned:
            return
        source, here = self.lefts[matrix]
        if not here:
            copy = pltpu.make_async_copy(source, self.left_in, self.left_sem.at[0])
            copy.start()
            copy.wait()
            source = self.left_in
        slot = len(self.turned) % TURNED_SLOTS
        for quarter in range(4):
            cols = pl.ds(quarter * 256, 256)
            self.left_turned[slot, cols, pl.ds(0, ROWS)] = source[:, cols].T
        self.turned[matrix] = slot

    def wait_load(self, pair):
        for unit, (matrix, _) in enumerate(self.pairs[pair]):
            self.turn(matrix)
            for entry in range(4):
                self.copies.pop((pair, unit, "right", entry)).wait()

    def send(self, pair, unit, stage, source, target, link):
        copy = pltpu.make_async_remote_copy(
            src_ref=source,
            dst_ref=target,
            send_sem=self.send_sem.at[pair, unit, stage],
            recv_sem=self.recv_sem.at[pair, unit, stage],
            device_id=self.partners[link],
            device_id_type=MESH_IDS,
        )
        copy.start()
        self.copies[(pair, unit, stage)] = copy

    def product(self, pair, unit, t, core, z):
        matrix, _ = self.pairs[pair][unit]
        at = pl.multiple_of(z * 256, 256)
        left = self.left_turned[self.turned[matrix], pl.ds(at, 256), :]
        right = self.right_in[pair % 2, unit, 2 * t + core]
        total = dot_rows(left[:, :512], right[:512]) + dot_rows(left[:, 512:], right[512:])
        return total.reshape(2, 2, BLOCK, COLS)

    def stage(self, pair, unit, stage):
        if pair < 0 or pair >= len(self.pairs):
            return
        z, x, c, y = self.z, self.x, self.c, self.y
        arrival = pair % ARRIVAL_SLOTS
        high, lower = lax.div(z, 2), lax.rem(z, 2)
        far_pair = pl.ds(2 * (1 - high), 2)
        far_z = z + 1 - 2 * lower
        val, rest = self.val.at[pair % VAL_SLOTS, unit], self.rest.at[pair % REST_SLOTS, unit]
        if stage == 0:
            out = self.core_out.at[unit]

            @pl.loop(0, 4)
            def _(row):
                for t in range(2):
                    out[t, row] = self.product(pair, unit, t, 1 - c, row).astype(LOW)

            self.send(pair, unit, 0, out, self.core_in.at[arrival, unit], "core")
            return
        self.copies.pop((pair, unit, stage - 1)).wait()
        if stage == 1:
            other = self.core_in.at[arrival, unit]

            @pl.loop(0, 4)
            def _(row):
                for t in range(2):
                    total = self.product(pair, unit, t, c, row)
                    val[t, row] = (total + other[t, row].astype(jnp.float32)).astype(LOW)

            if unit == 0:
                self.send(pair, unit, 1, val.at[1 - y], self.first_a.at[arrival], "y")
            else:
                self.send(pair, unit, 1, val.at[:, :, 1 - x], self.first_b.at[arrival], "x")
        elif stage == 2:
            target = self.second.at[arrival, unit]
            if unit == 0:

                @pl.loop(0, 4)
                def _(row):
                    val[y, row] = val[y, row] + self.first_a[arrival, row]

                self.send(pair, unit, 2, val.at[y, :, 1 - x], target, "x")
            else:

                @pl.loop(0, 4)
                def _(row):
                    for t in range(2):
                        val[t, row, x] = val[t, row, x] + self.first_b[arrival, t, row]

                self.send(pair, unit, 2, val.at[1 - y, :, x], target, "y")
        elif stage == 3:

            @pl.loop(0, 4)
            def _(row):
                rest[row] = val[y, row, x] + self.second[arrival, unit, row]

            self.send(pair, unit, 3, rest.at[far_pair], self.third.at[arrival, unit], "z2")
        elif stage == 4:
            for row in range(2):
                at = 2 * high + row
                rest[at] = rest[at] + self.third[arrival, unit, row]
            self.send(pair, unit, 4, rest.at[far_z], self.fourth.at[arrival, unit], "z1")
        elif stage == 5:
            rest[z] = rest[z] + self.fourth[arrival, unit]
            self.send(pair, unit, 5, rest.at[z, 1 - c], self.fifth.at[arrival, unit], "core")
        else:
            matrix, step = self.pairs[pair][unit]
            out_ref, layer = self.outs[matrix]
            slot = pair % 2
            for copy in self.results.pop((slot, unit), ()):
                copy.wait()
            result = self.result.at[slot, unit]
            result[c] = rest[z, c].astype(jnp.float32)
            result[1 - c] = self.fifth[arrival, unit].astype(jnp.float32)
            self.results[(slot, unit)] = []
            for core in range(2):
                copy = pltpu.make_async_copy(
                    result.at[core],
                    out_ref.at[layer, core, :, pl.ds(step * COLS, COLS)],
                    self.result_sem.at[slot, unit, core],
                )
                copy.start()
                self.results[(slot, unit)].append(copy)

    def finish(self):
        for copies in self.results.values():
            for copy in copies:
                copy.wait()

    def tick(self, pair):
        for stage in range(SETTLE_DEPTH, 0, -1):
            for unit in range(2):
                self.stage(pair - stage, unit, stage)
        if pair < len(self.pairs):
            self.wait_load(pair)
            for unit in range(2):
                self.stage(pair, unit, 0)


TOTAL_LINKS = ("x", "y", "z1", "z2", "core")
SUM_ROWS = 12
TILE = 512
KEPT = ("normed", "projected", "heads", "normed_two", "hidden", "slope", "middle", "incoming")


class Backward:
    def __init__(self, layers, widths):
        self.layers, self.widths = layers, widths
        pairs, self.needs = [], []
        for layer in reversed(range(layers)):
            base = layer * 4
            feed = widths[2] // 2 // COLS
            for kind, fact in ((3, "arrived"), (2, "fed")):
                for k in range(0, feed, 2):
                    pairs.append(((base + kind, k), (base + kind, k + 1)))
                    self.needs.append((layer, fact))
            rest = [(base + 1, k) for k in range(widths[1] // 2 // COLS)]
            rest += [(base, k) for k in range(widths[0] // 2 // COLS)]
            for k in range(0, len(rest), 2):
                pairs.append((rest[k], rest[k + 1]))
                self.needs.append((layer, "mixed"))
        self.settle = Settle(widths * layers, pairs)

    def scratch(self):
        sem = pltpu.SemaphoreType.DMA
        full = pltpu.VMEM((ROWS, 1024), jnp.float32)
        low = pltpu.VMEM((ROWS, 1024), LOW)
        steps = len(TOTAL_LINKS)
        rows = self.layers * SUM_ROWS
        own = dict(
            grad=full,
            delta=full,
            values=full,
            feed_grad=low,
            mix_grad=low,
            heads_grad=low,
            projected=pltpu.VMEM((ROWS, 2 * self.widths[0]), LOW),
            joined=pltpu.VMEM((ROWS, 2 * self.widths[0]), LOW),
            tile_a=pltpu.VMEM((2, 4, 2, 2, BLOCK, TILE), LOW),
            tile_b=pltpu.VMEM((2, 4, 2, 2, BLOCK, TILE), LOW),
            slope_in=pltpu.VMEM((2, ROWS, TILE), LOW),
            hidden_out=pltpu.VMEM((2, ROWS, TILE), LOW),
            column_sums=pltpu.VMEM((8, 1, TILE), jnp.float32),
            sums_part=pltpu.VMEM((3, 16, 1024), jnp.float32),
            sums=pltpu.VMEM((steps + 1, rows, 1024), jnp.float32),
            sums_in=pltpu.VMEM((steps, rows, 1024), jnp.float32),
            leave=pltpu.VMEM((ROWS, 512), LOW),
            tile_sem=sem((2, 3)),
            hidden_sem=sem((2,)),
            value_sem=sem((3,)),
            sums_send=sem((steps,)),
            sums_recv=sem((steps,)),
            swap_send=sem((2,)),
            swap_recv=sem((2,)),
        )
        return {**own, **self.settle.scratch()}

    def bind(self, inputs, outputs, refs):
        for name, ref in zip(self.scratch(), refs, strict=True):
            setattr(self, name, ref)
        layers = self.layers
        count = layers * 4
        self.weights, inputs = inputs[:count], inputs[count:]
        self.kept = [
            dict(zip(KEPT, inputs[k * len(KEPT) : (k + 1) * len(KEPT)])) for k in range(layers)
        ]
        self.upstream, self.gains, self.leaving = inputs[layers * len(KEPT) :]
        outs, outputs = outputs[:4], outputs[4:]
        self.total_out, self.near_out, self.arriving, outputs = (*outputs[:3], outputs[3:])
        self.hidden_grads = outputs
        self.facts = set()
        lefts, rights = [], []
        for layer in range(layers):
            kept = self.kept[layer]
            lefts += [
                (kept["normed"], False),
                (self.mix_grad, True),
                (kept["normed_two"], False),
                (self.feed_grad, True),
            ]
            rights += [self.joined, kept["heads"], self.hidden_grads[layer], kept["hidden"]]
        self.settle.bind(
            lefts,
            rights,
            [(outs[m % 4], m // 4) for m in range(count)],
            [getattr(self, name) for name in self.settle.scratch()],
        )
        self.loaded_pair = -1

    def fetch(self, entry, source, target):
        copy = pltpu.make_async_copy(source, target, self.value_sem.at[entry])
        copy.start()
        return copy

    def swap(self, entry, source):
        copy = pltpu.make_async_remote_copy(
            src_ref=source,
            dst_ref=self.arriving.at[entry],
            send_sem=self.swap_send.at[entry],
            recv_sem=self.swap_recv.at[entry],
            device_id=self.settle.partners["y"],
            device_id_type=MESH_IDS,
        )
        copy.start()
        return copy

    def row_loop(self, body):
        @pl.loop(0, ROWS // 16)
        def _(step):
            body(pl.ds(pl.multiple_of(step * 16, 16), 16))

    def put_sum(self, layer, row, values):
        self.sums[0, pl.ds(layer * SUM_ROWS + row, 1), :] = values

    def begin(self):
        self.fetch(0, self.upstream, self.feed_grad).wait()
        self.facts.add((self.layers - 1, "arrived"))

    def widen(self):
        self.sums_part[...] = jnp.zeros_like(self.sums_part)

        def body(rows):
            values = self.feed_grad[rows, :].astype(jnp.float32)
            self.grad[rows, :] = values
            self.sums_part[2] += values

        self.row_loop(body)
        self.put_sum(self.layers - 1, 7, jnp.sum(self.sums_part[2], axis=0, keepdims=True))

    def tiles(self, first, last, sources, targets, body):
        def copies(part, slot):
            cols = pl.ds(pl.multiple_of(part * TILE, TILE), TILE)
            return [
                pltpu.make_async_copy(
                    source.at[(slice(None),) * (len(source.shape) - 1) + (cols,)],
                    target.at[slot],
                    self.tile_sem.at[slot, entry],
                )
                for entry, (source, target) in enumerate(zip(sources, targets))
            ]

        for copy in copies(first, first % 2):
            copy.start()

        @pl.loop(first, last)
        def _(part):
            slot = lax.rem(part, 2)

            @pl.when(part + 1 < last)
            def _():
                for copy in copies(part + 1, 1 - slot):
                    copy.start()

            for copy in copies(part, slot):
                copy.wait()
            body(part, slot)

    def add_delta(self, is_first, grads, weights):
        for half in range(2):
            cols = slice(half * 512, (half + 1) * 512)
            product = dot_cols(grads, weights[2 * half : 2 * half + 2].reshape(512, TILE))
            before = jnp.where(is_first, 0.0, self.delta[:, cols])
            self.delta[:, cols] = before + product

    def feed(self, layer, first, last):
        out_ref = self.hidden_grads[layer]
        if first == 0:
            self.value_copy = self.fetch(1, self.kept[layer]["middle"], self.values)

        def out_copy(part, slot):
            cols = pl.ds(pl.multiple_of(part * TILE, TILE), TILE)
            return pltpu.make_async_copy(
                self.hidden_out.at[slot], out_ref.at[:, cols], self.hidden_sem.at[slot]
            )

        def body(part, slot):
            @pl.when(part >= first + 2)
            def _():
                out_copy(part - 2, slot).wait()

            down = self.tile_a[slot].reshape(1024, TILE)
            slope = self.slope_in[slot].astype(jnp.float32)
            grads = (dot_rows(self.feed_grad[...], down) * slope).astype(LOW)
            self.hidden_out[slot] = grads
            out_copy(part, slot).start()
            self.column_sums[part] = jnp.sum(grads.astype(jnp.float32), axis=0, keepdims=True)
            self.add_delta(part == 0, grads, self.tile_b.at[slot])

        self.tiles(
            first,
            last,
            (self.weights[layer * 4 + 3], self.weights[layer * 4 + 2], self.kept[layer]["slope"]),
            (self.tile_a, self.tile_b, self.slope_in),
            body,
        )
        for part in (last - 2, last - 1):
            out_copy(part, part % 2).wait()
        if last * TILE == out_ref.shape[1]:
            for row in range(4):
                pieces = [self.column_sums[2 * row], self.column_sums[2 * row + 1]]
                self.put_sum(layer, 3 + row, jnp.concatenate(pieces, axis=1))
            self.facts.add((layer, "fed"))

    def norm_back(self, layer, gain_row, sum_row, low_ref, total_at):
        self.value_copy.wait()
        gain = self.gains[pl.ds(gain_row, 1), :]
        self.sums_part[...] = jnp.zeros_like(self.sums_part)

        def body(rows):
            stream, delta = self.values[rows, :], self.delta[rows, :]
            mean = jnp.mean(stream, axis=1, keepdims=True)
            square = jnp.mean(stream * stream, axis=1, keepdims=True)
            inverse = lax.rsqrt(square - mean * mean + norm_eps)
            centred = (stream - mean) * inverse
            weighted = delta * centred
            self.sums_part[0] += weighted
            self.sums_part[1] += delta
            scaled = delta * gain
            grad = self.grad[rows, :] + inverse * (
                scaled
                - jnp.mean(scaled, axis=1, keepdims=True)
                - centred * jnp.mean(weighted * gain, axis=1, keepdims=True)
            )
            self.grad[rows, :] = grad
            self.sums_part[2] += grad
            if low_ref is not None:
                low_ref[rows, :] = grad.astype(LOW)

        self.row_loop(body)
        for entry in range(2):
            total = jnp.sum(self.sums_part[entry], axis=0, keepdims=True)
            self.put_sum(layer, sum_row + entry, total)
        if total_at is not None:
            total = jnp.sum(self.sums_part[2], axis=0, keepdims=True)
            self.put_sum(*total_at, total)

    def out_back(self, layer):
        self.norm_back(layer, self.layers + layer, 10, self.mix_grad, (layer, 2))
        self.value_copy = self.fetch(1, self.kept[layer]["incoming"], self.values)
        self.projected_copy = self.fetch(2, self.kept[layer]["projected"], self.projected)

        def body(part, slot):
            cols = pl.ds(pl.multiple_of(part * TILE, TILE), TILE)
            weights = self.tile_a[slot].reshape(1024, TILE)
            self.heads_grad[:, cols] = dot_rows(self.mix_grad[...], weights).astype(LOW)

        self.tiles(0, 2, (self.weights[layer * 4 + 1],), (self.tile_a,), body)

    def mix_back(self, layer, first, last):
        if first == 0:
            self.projected_copy.wait()
        half = self.heads_grad.shape[1] // 2

        @pl.loop(2 * first, 2 * last)
        def _(turn):
            step, t = lax.div(turn, 2), lax.rem(turn, 2)

            def at(part):
                start = (t * 3 + part) * half + step * PAIR
                return pl.ds(pl.multiple_of(start, PAIR), PAIR)

            here = pl.ds(pl.multiple_of(t * half + step * PAIR, PAIR), PAIR)
            rows = pl.ds(0, SEQ)
            all_queries = self.projected[rows, at(0)] * jnp.asarray(HEAD_DIM**-0.5, LOW)
            all_keys, all_values = self.projected[rows, at(1)], self.projected[rows, at(2)]
            all_grads = self.heads_grad[rows, here]
            pieces = ([], [], [])
            for head in range(2):
                cols = slice(head * HEAD_DIM, (head + 1) * HEAD_DIM)
                keys_here, queries = all_keys[:, cols], all_queries[:, cols]
                grads = all_grads[:, cols]
                soft = turned_softmax(keys_here, queries)
                soft_grad = dot_cols(all_values[:, cols], grads)
                delta = jnp.sum(soft_grad * soft, axis=0, keepdims=True)
                score_grad = (soft * (soft_grad - delta)).astype(LOW)
                pieces[0].append(
                    (dot_tokens(score_grad, keys_here) * HEAD_DIM**-0.5).astype(LOW)
                )
                pieces[1].append(dot_rows(score_grad, queries).astype(LOW))
                pieces[2].append(dot_rows(soft.astype(LOW), grads).astype(LOW))
            for part in range(3):
                start = (t * 3 + part) * half + step * PAIR
                store_rows(self.joined, pl.multiple_of(start, PAIR), pieces[part])

        if last * PAIR == half:
            self.facts.add((layer, "mixed"))

    def project_back(self, layer):
        def body(part, slot):
            cols = pl.ds(pl.multiple_of(part * TILE, TILE), TILE)
            grads = self.joined[:, cols]
            self.column_sums[part] = jnp.sum(grads.astype(jnp.float32), axis=0, keepdims=True)
            self.add_delta(part == 0, grads, self.tile_a.at[slot])

        self.tiles(0, 6, (self.weights[layer * 4],), (self.tile_a,), body)
        for row, part in ((0, 0), (1, 2)):
            pieces = [self.column_sums[part], self.column_sums[3 + part]]
            self.put_sum(layer, row, jnp.concatenate(pieces, axis=1))

    def first_back(self, layer):
        last = layer == 0
        low_ref = None if last else self.feed_grad
        self.norm_back(layer, layer, 8, low_ref, None if last else (layer - 1, 7))
        if not last:
            self.facts.add((layer - 1, "arrived"))

    def end(self):
        y = self.y
        near_at = pl.ds(pl.multiple_of(y * 512, 512), 512)
        far_at = pl.ds(pl.multiple_of((1 - y) * 512, 512), 512)
        self.leave[...] = self.grad[:, far_at].astype(LOW)
        self.swaps.append(self.swap(1, self.leave))
        copy = self.fetch(0, self.grad.at[:, near_at], self.near_out)
        copy.wait()
        self.facts.add("summed")

    def chain(self):
        steps = [(1, self.begin, ()), (2, self.widen, ())]
        for layer in reversed(range(self.layers)):
            steps += [
                (9, lambda layer=layer: self.feed(layer, 0, 4), ()),
                (9, lambda layer=layer: self.feed(layer, 4, 8), ()),
                (4, lambda layer=layer: self.out_back(layer), ((layer + 1, 1),)),
            ]
            for k in range(4):
                needs = ((layer + 1, 0),)
                steps.append((7, lambda layer=layer, k=k: self.mix_back(layer, k, k + 1), needs))
            steps += [
                (8, lambda layer=layer: self.project_back(layer), ()),
                (3, lambda layer=layer: self.first_back(layer), ((layer, 3),)),
            ]
        return steps + [(1, self.end, ())]

    def add_sums(self, step):
        if step > 0:
            self.sums_copy.wait()
            self.sums[step] = self.sums[step - 1] + self.sums_in[step - 1]
        if step < len(TOTAL_LINKS):
            copy = pltpu.make_async_remote_copy(
                src_ref=self.sums.at[step],
                dst_ref=self.sums_in.at[step],
                send_sem=self.sums_send.at[step],
                recv_sem=self.sums_recv.at[step],
                device_id=self.settle.partners[TOTAL_LINKS[step]],
                device_id_type=MESH_IDS,
            )
            copy.start()
            self.sums_copy = copy

    def run(self):
        self.y = lax.axis_index("tensor")
        settle = self.settle
        greet(settle.partners)
        self.swaps = [self.swap(0, self.leaving)]
        chain = self.chain()
        last_pair = {}
        for pair, units in enumerate(settle.pairs):
            for matrix, _ in units:
                last_pair[matrix] = pair
        pairs, loaded, sum_step = len(settle.pairs), set(), 0
        passed = -1

        def free(needs):
            for layer, kind in needs:
                if layer < self.layers and passed < last_pair[layer * 4 + kind]:
                    return False
            return True

        def advance():
            _, step, _ = chain.pop(0)
            step()

        pair = 0
        while pair < pairs + SETTLE_DEPTH or sum_step <= len(TOTAL_LINKS):
            if pair < pairs:
                while self.needs[pair] not in self.facts:
                    advance()
                if pair not in loaded:
                    settle.load(pair)
                    loaded.add(pair)
            settle.tick(pair)
            passed = pair
            if "summed" in self.facts and sum_step <= len(TOTAL_LINKS):
                self.add_sums(sum_step)
                sum_step += 1
            if pair + 1 < pairs and self.needs[pair + 1] in self.facts:
                settle.load(pair + 1)
                loaded.add(pair + 1)
            budget = CHAIN_A_TICK
            while chain and budget > 0 and free(chain[0][2]):
                budget -= chain[0][0]
                advance()
            pair += 1
        self.total_out[...] = self.sums[len(TOTAL_LINKS)]
        settle.finish()
        for copy in self.swaps:
            copy.wait()


CHAIN_A_TICK = 10


def backward(weights, kept, upstream, gains, leaving):
    layers = len(weights)
    widths = [block.shape[-1] // 2 for block in weights[0]]
    plan = Backward(layers, widths)
    any_spec, vmem_spec = pl.BlockSpec(memory_space=pl.ANY), pl.BlockSpec(memory_space=pltpu.VMEM)
    operands = [block for layer in weights for block in layer]
    operands += [values[name] for values in kept for name in KEPT]
    operands += [upstream, gains, leaving]
    in_specs = [any_spec] * len(operands)
    in_specs[-2] = vmem_spec
    outs = [jax.ShapeDtypeStruct((layers, 2, BLOCK, width // 2), jnp.float32) for width in widths]
    outs += [
        jax.ShapeDtypeStruct((layers * SUM_ROWS, 1024), jnp.float32),
        jax.ShapeDtypeStruct((ROWS, 512), jnp.float32),
        jax.ShapeDtypeStruct((2, ROWS, 512), LOW),
    ]
    outs += [jax.ShapeDtypeStruct((ROWS, 2 * widths[2]), LOW)] * layers
    out_specs = [any_spec] * len(outs)
    out_specs[4] = vmem_spec

    def kernel(*refs):
        ins, refs = refs[: len(operands)], refs[len(operands) :]
        plan.bind(ins, refs[: len(outs)], refs[len(outs) :])
        plan.run()

    results = pl.pallas_call(
        kernel,
        out_shape=outs,
        in_specs=in_specs,
        out_specs=out_specs,
        scratch_shapes=list(plan.scratch().values()),
        compiler_params=pltpu.CompilerParams(
            collective_id=1, has_side_effects=True, vmem_limit_bytes=60 * 1024 * 1024
        ),
        cost_estimate=pl.CostEstimate(
            flops=120 * 1024**3, bytes_accessed=700 * 1024 * 1024, transcendentals=0
        ),
        name="backward",
    )(*operands)
    return results[:4], results[4], results[5], results[6]


def in_order(own, other, index, axis):
    first = jnp.where(index == 0, own, other)
    second = jnp.where(index == 0, other, own)
    return jnp.concatenate((first, second), axis=axis)


def image_body(
    images,
    first_gain,
    first_shift,
    query_weight,
    key_weight,
    value_weight,
    query_bias,
    value_bias,
    out_weight,
    out_bias,
    second_gain,
    second_shift,
    up_weight,
    up_bias,
    down_weight,
    down_bias,
    cotangent,
):
    layers = query_weight.shape[0]
    half = images.shape[1]
    hidden_width = 2 * up_weight.shape[2]
    y = lax.axis_index("tensor")
    far = 1 - y

    def own_rows(block, image):
        rows = lax.dynamic_slice_in_dim(block, image * SEQ, SEQ)
        return jnp.pad(rows, ((0, ROWS - SEQ), (0, 0)))

    biases = jnp.concatenate(
        (query_bias, jnp.zeros_like(query_bias), value_bias, out_bias, down_bias, up_bias), axis=1
    )
    biases = biases.astype(jnp.float32).reshape(layers * BIAS_ROWS, -1)
    biases = jnp.pad(biases, ((0, 24 - layers * BIAS_ROWS), (0, 0)))
    norms = jnp.concatenate((first_gain, first_shift, second_gain, second_shift))
    weights, cotangent_in, activations, kept = forward(
        (
            jnp.concatenate((query_weight, key_weight, value_weight), axis=2),
            jnp.swapaxes(out_weight, 1, 2),
            up_weight,
            jnp.swapaxes(down_weight, 1, 2),
        ),
        own_rows(images, y),
        jnp.stack((own_rows(images, far), own_rows(cotangent, far))),
        biases,
        norms.astype(jnp.float32),
    )

    def columns(rows, t):
        return lax.dynamic_slice_in_dim(rows, t * half, half, axis=1)

    upstream = in_order(own_rows(cotangent, y), cotangent_in, y, 1)
    gains = jnp.concatenate((first_gain, second_gain)).astype(jnp.float32)
    (project_out, out_out, up_out, down_out), totals, near_gradient, arriving = backward(
        weights, kept, upstream, gains, columns(activations, far)
    )
    totals = totals.reshape(layers, -1)
    project_out, out_out, up_out, down_out = [
        jnp.swapaxes(block, 1, 2).reshape(layers, BLOCK, -1)
        for block in (project_out, out_out, up_out, down_out)
    ]
    width = 2 * half
    small_outs, at = [], 0
    for size in (width, width, width, hidden_width, width, width, width, width, width):
        small_outs.append(totals[:, at : at + size])
        at += size
    return (
        in_order(columns(activations, y)[:SEQ], arriving[0, :SEQ], y, 0),
        in_order(near_gradient[:SEQ], arriving[1, :SEQ].astype(jnp.float32), y, 0),
        project_out[:, :, :half],
        project_out[:, :, half : 2 * half],
        project_out[:, :, 2 * half :],
        jnp.swapaxes(out_out, 1, 2),
        up_out,
        jnp.swapaxes(down_out, 1, 2),
        *small_outs,
    )


def solution(mesh):
    in_specs = (
        P("wide", "tensor"),
        P(),
        P(),
        P(None, "wide", "tensor"),
        P(None, "wide", "tensor"),
        P(None, "wide", "tensor"),
        P(None, "tensor"),
        P(None, "tensor"),
        P(None, "tensor", "wide"),
        P(None, "tensor"),
        P(),
        P(),
        P(None, "wide", "tensor"),
        P(None, "tensor"),
        P(None, "tensor", "wide"),
        P(None, "tensor"),
        P("wide", "tensor"),
    )
    out_specs = (
        P("wide", "tensor"),
        P("wide", "tensor"),
        P(None, "wide", "tensor"),
        P(None, "wide", "tensor"),
        P(None, "wide", "tensor"),
        P(None, "tensor", "wide"),
        P(None, "wide", "tensor"),
        P(None, "tensor", "wide"),
        P(),
        P(),
        P(),
        P(),
        P(),
        P(),
        P(),
        P(),
        P(),
    )
    chosen = body
    if mesh.shape["wide"] == 16 and mesh.shape["tensor"] == 2:
        chosen = image_body
    return jax.shard_map(
        chosen, mesh=mesh, in_specs=in_specs, out_specs=out_specs, check_vma=False
    )
```

```python
import jax
import jax.numpy as jnp
from jax import lax
from jax.experimental import pallas as pl
from jax.experimental.pallas import tpu as pltpu
from jax.sharding import PartitionSpec as P

HEAD_DIM = 64
SEQ = 577
MICRO = 2


norm_eps = 1e-06


def row_totals(first_terms, second_terms):
    return lax.psum((first_terms, second_terms), "tensor")


def full_rows(share_low):
    return lax.all_gather(share_low, "tensor", axis=1, tiled=True)


def feature_total(partial_sums):
    return lax.psum_scatter(
        partial_sums.astype(jnp.bfloat16), "tensor", scatter_dimension=1, tiled=True
    ).astype(jnp.float32)


def fetch_weights(query_block, key_block, value_block, out_block, up_block, down_block):
    return (
        lax.all_gather(query_block, "wide", axis=0, tiled=True),
        lax.all_gather(key_block, "wide", axis=0, tiled=True),
        lax.all_gather(value_block, "wide", axis=0, tiled=True),
        lax.all_gather(out_block, "wide", axis=1, tiled=True),
        lax.all_gather(up_block, "wide", axis=0, tiled=True),
        lax.all_gather(down_block, "wide", axis=1, tiled=True),
    )


def settle_grads(query_piece, key_piece, value_piece, out_piece, up_piece, down_piece):
    return (
        lax.psum_scatter(
            query_piece.astype(jnp.bfloat16), "wide", scatter_dimension=0, tiled=True
        ).astype(jnp.float32),
        lax.psum_scatter(
            key_piece.astype(jnp.bfloat16), "wide", scatter_dimension=0, tiled=True
        ).astype(jnp.float32),
        lax.psum_scatter(
            value_piece.astype(jnp.bfloat16), "wide", scatter_dimension=0, tiled=True
        ).astype(jnp.float32),
        lax.psum_scatter(
            out_piece.astype(jnp.bfloat16), "wide", scatter_dimension=1, tiled=True
        ).astype(jnp.float32),
        lax.psum_scatter(
            up_piece.astype(jnp.bfloat16), "wide", scatter_dimension=0, tiled=True
        ).astype(jnp.float32),
        lax.psum_scatter(
            down_piece.astype(jnp.bfloat16), "wide", scatter_dimension=1, tiled=True
        ).astype(jnp.float32),
    )


def add_terms(earlier, latest):
    if earlier is None:
        return latest
    return jax.tree.map(jnp.add, earlier, latest)


def norm_forward(stream, gain, shift, full_width):
    first_terms, second_terms = row_totals(
        jnp.sum(stream, axis=1), jnp.sum(stream * stream, axis=1)
    )
    row_mean = first_terms / full_width
    inverse_std = lax.rsqrt(second_terms / full_width - row_mean * row_mean + norm_eps)
    centred = (stream - row_mean[:, None]) * inverse_std[:, None]
    return (centred * gain + shift, centred, inverse_std)


def norm_backward(upstream, centred, inverse_std, gain, full_width):
    scaled = upstream * gain
    first_terms, second_terms = row_totals(
        jnp.sum(scaled, axis=1), jnp.sum(scaled * centred, axis=1)
    )
    return inverse_std[:, None] * (
        scaled - first_terms[:, None] / full_width - centred * (second_terms[:, None] / full_width)
    )


def attention_forward(queries, keys_here, values_here, image_count, heads_here):
    score_scale = HEAD_DIM ** (-0.5)
    shape_four = (image_count, SEQ, heads_here, HEAD_DIM)
    query_four = queries.reshape(shape_four)
    key_four = keys_here.reshape(shape_four)
    value_four = values_here.reshape(shape_four)
    scores = (
        jnp.einsum("iqhd,ikhd->ihqk", query_four, key_four, preferred_element_type=jnp.float32)
        * score_scale
    )
    row_peak = jnp.max(scores, axis=-1, keepdims=True)
    exponent = jnp.exp(scores - row_peak)
    row_total = jnp.sum(exponent, axis=-1, keepdims=True)
    weights_soft = (exponent / row_total).astype(jnp.bfloat16)
    mixed_heads = jnp.einsum(
        "ihqk,ikhd->iqhd", weights_soft, value_four, preferred_element_type=jnp.float32
    )
    log_total = row_peak[..., 0] + jnp.log(row_total[..., 0])
    return (mixed_heads.reshape(queries.shape).astype(jnp.bfloat16), log_total)


def attention_backward(
    queries, keys_here, values_here, log_total, mixed_grad, image_count, heads_here
):
    score_scale = HEAD_DIM ** (-0.5)
    shape_four = (image_count, SEQ, heads_here, HEAD_DIM)
    query_four = queries.reshape(shape_four)
    key_four = keys_here.reshape(shape_four)
    value_four = values_here.reshape(shape_four)
    grad_four = mixed_grad.reshape(shape_four)
    scores = (
        jnp.einsum("iqhd,ikhd->ihqk", query_four, key_four, preferred_element_type=jnp.float32)
        * score_scale
    )
    weights_soft = jnp.exp(scores - log_total[..., None])
    weight_grad = jnp.einsum(
        "iqhd,ikhd->ihqk", grad_four, value_four, preferred_element_type=jnp.float32
    )
    row_delta = jnp.sum(weight_grad * weights_soft, axis=-1, keepdims=True)
    score_grad = (weights_soft * (weight_grad - row_delta)).astype(jnp.bfloat16)
    query_grad = (
        jnp.einsum("ihqk,ikhd->iqhd", score_grad, key_four, preferred_element_type=jnp.float32)
        * score_scale
    )
    key_grad = (
        jnp.einsum("ihqk,iqhd->ikhd", score_grad, query_four, preferred_element_type=jnp.float32)
        * score_scale
    )
    value_grad = jnp.einsum(
        "ihqk,iqhd->ikhd",
        weights_soft.astype(jnp.bfloat16),
        grad_four,
        preferred_element_type=jnp.float32,
    )
    flat_shape = queries.shape
    return (
        query_grad.reshape(flat_shape),
        key_grad.reshape(flat_shape),
        value_grad.reshape(flat_shape),
    )


def gelu_slope(values):
    normal_cdf = 0.5 * (1.0 + lax.erf(values * 0.7071067811865476))
    return normal_cdf + values * jnp.exp(-0.5 * values * values) * 0.3989422804014327


def body(
    images,
    first_gain,
    first_shift,
    query_weight,
    key_weight,
    value_weight,
    query_bias,
    value_bias,
    out_weight,
    out_bias,
    second_gain,
    second_shift,
    up_weight,
    up_bias,
    down_weight,
    down_bias,
    cotangent,
):
    layer_count = query_weight.shape[0]
    feature_block = images.shape[1]
    tensor_count = lax.axis_size("tensor")
    full_width = feature_block * tensor_count
    heads_here = feature_block // HEAD_DIM
    tensor_place = lax.axis_index("tensor")
    micro_rows = images.shape[0] // MICRO
    image_count = micro_rows // SEQ

    def gain_share(param_table, layer_idx):
        return lax.dynamic_slice_in_dim(
            param_table[layer_idx], tensor_place * feature_block, feature_block
        )

    def layer_weights(layer_idx):
        return fetch_weights(
            query_weight[layer_idx],
            key_weight[layer_idx],
            value_weight[layer_idx],
            out_weight[layer_idx],
            up_weight[layer_idx],
            down_weight[layer_idx],
        )

    weight_sums = [None] * layer_count
    small_sums = [None] * layer_count
    activation_parts = []
    gradient_parts = []
    for micro_idx in range(MICRO):
        row_start = micro_idx * micro_rows
        stream = images[row_start : row_start + micro_rows].astype(jnp.float32)
        saved_state = []
        for layer_idx in range(layer_count):
            query_full, key_full, value_full, out_full, up_full, down_full = layer_weights(
                layer_idx
            )
            normed, centred_one, inverse_one = norm_forward(
                stream,
                gain_share(first_gain, layer_idx),
                gain_share(first_shift, layer_idx),
                full_width,
            )
            normed_full = full_rows(normed.astype(jnp.bfloat16))
            joined_weight = jnp.concatenate((query_full, key_full, value_full), axis=1)
            projected = jnp.dot(normed_full, joined_weight, preferred_element_type=jnp.float32)
            queries = (projected[:, :feature_block] + query_bias[layer_idx]).astype(jnp.bfloat16)
            keys_here = projected[:, feature_block : 2 * feature_block].astype(jnp.bfloat16)
            values_here = (projected[:, 2 * feature_block :] + value_bias[layer_idx]).astype(
                jnp.bfloat16
            )
            mixed_heads, log_total = attention_forward(
                queries, keys_here, values_here, image_count, heads_here
            )
            attention_sum = feature_total(
                jnp.dot(mixed_heads, out_full, preferred_element_type=jnp.float32)
            )
            after_attention = stream + attention_sum + out_bias[layer_idx]
            normed_two, centred_two, inverse_two = norm_forward(
                after_attention,
                gain_share(second_gain, layer_idx),
                gain_share(second_shift, layer_idx),
                full_width,
            )
            normed_two_full = full_rows(normed_two.astype(jnp.bfloat16))
            hidden_pre = (
                jnp.dot(normed_two_full, up_full, preferred_element_type=jnp.float32)
                + up_bias[layer_idx]
            )
            hidden = jax.nn.gelu(hidden_pre, approximate=False).astype(jnp.bfloat16)
            feedforward_sum = feature_total(
                jnp.dot(hidden, down_full, preferred_element_type=jnp.float32)
            )
            saved_state.append(
                (
                    centred_one,
                    inverse_one,
                    normed_full,
                    queries,
                    keys_here,
                    values_here,
                    mixed_heads,
                    log_total,
                    centred_two,
                    inverse_two,
                    normed_two_full,
                    hidden_pre,
                    hidden,
                )
            )
            stream = after_attention + feedforward_sum + down_bias[layer_idx]
        activation_parts.append(stream.astype(jnp.bfloat16))
        upstream = cotangent[row_start : row_start + micro_rows].astype(jnp.float32)
        for layer_idx in reversed(range(layer_count)):
            query_full, key_full, value_full, out_full, up_full, down_full = layer_weights(
                layer_idx
            )
            (
                centred_one,
                inverse_one,
                normed_full,
                queries,
                keys_here,
                values_here,
                mixed_heads,
                log_total,
                centred_two,
                inverse_two,
                normed_two_full,
                hidden_pre,
                hidden,
            ) = saved_state[layer_idx]
            down_bias_term = jnp.sum(upstream, axis=0)
            upstream_full = full_rows(upstream.astype(jnp.bfloat16))
            down_term = jnp.einsum(
                "rc,rd->cd", hidden, upstream_full, preferred_element_type=jnp.float32
            )
            hidden_grad = jnp.einsum(
                "rd,cd->rc", upstream_full, down_full, preferred_element_type=jnp.float32
            )
            pre_grad = (hidden_grad * gelu_slope(hidden_pre)).astype(jnp.bfloat16)
            up_bias_term = jnp.sum(pre_grad.astype(jnp.float32), axis=0)
            up_term = jnp.einsum(
                "rd,rc->dc", normed_two_full, pre_grad, preferred_element_type=jnp.float32
            )
            normed_two_grad = feature_total(
                jnp.einsum("rc,dc->rd", pre_grad, up_full, preferred_element_type=jnp.float32)
            )
            second_gain_term = jnp.sum(normed_two_grad * centred_two, axis=0)
            second_shift_term = jnp.sum(normed_two_grad, axis=0)
            upstream = upstream + norm_backward(
                normed_two_grad,
                centred_two,
                inverse_two,
                gain_share(second_gain, layer_idx),
                full_width,
            )
            out_bias_term = jnp.sum(upstream, axis=0)
            upstream_full = full_rows(upstream.astype(jnp.bfloat16))
            out_term = jnp.einsum(
                "rc,rd->cd", mixed_heads, upstream_full, preferred_element_type=jnp.float32
            )
            mixed_grad = jnp.einsum(
                "rd,cd->rc", upstream_full, out_full, preferred_element_type=jnp.float32
            ).astype(jnp.bfloat16)
            query_grad, key_grad, value_grad = attention_backward(
                queries, keys_here, values_here, log_total, mixed_grad, image_count, heads_here
            )
            joined_grad = jnp.concatenate((query_grad, key_grad, value_grad), axis=1).astype(
                jnp.bfloat16
            )
            joined_float = joined_grad.astype(jnp.float32)
            query_bias_term = jnp.sum(joined_float[:, :feature_block], axis=0)
            value_bias_term = jnp.sum(joined_float[:, 2 * feature_block :], axis=0)
            joined_term = jnp.einsum(
                "rd,rc->dc", normed_full, joined_grad, preferred_element_type=jnp.float32
            )
            joined_weight = jnp.concatenate((query_full, key_full, value_full), axis=1)
            normed_grad = feature_total(
                jnp.einsum(
                    "rc,dc->rd", joined_grad, joined_weight, preferred_element_type=jnp.float32
                )
            )
            first_gain_term = jnp.sum(normed_grad * centred_one, axis=0)
            first_shift_term = jnp.sum(normed_grad, axis=0)
            upstream = upstream + norm_backward(
                normed_grad, centred_one, inverse_one, gain_share(first_gain, layer_idx), full_width
            )
            query_term = joined_term[:, :feature_block]
            key_term = joined_term[:, feature_block : 2 * feature_block]
            value_term = joined_term[:, 2 * feature_block :]
            weight_sums[layer_idx] = add_terms(
                weight_sums[layer_idx],
                settle_grads(query_term, key_term, value_term, out_term, up_term, down_term),
            )
            small_sums[layer_idx] = add_terms(
                small_sums[layer_idx],
                (
                    query_bias_term,
                    value_bias_term,
                    out_bias_term,
                    up_bias_term,
                    down_bias_term,
                    first_gain_term,
                    first_shift_term,
                    second_gain_term,
                    second_shift_term,
                ),
            )
        gradient_parts.append(upstream)
    share_sets = []
    for layer_idx in range(layer_count):
        share_sets.append(weight_sums[layer_idx])
    weight_outputs = [
        jnp.stack([share_sets[layer_idx][entry_idx] for layer_idx in range(layer_count)])
        for entry_idx in range(6)
    ]
    small_stack = [
        jnp.stack([small_sums[layer_idx][entry_idx] for layer_idx in range(layer_count)])
        for entry_idx in range(9)
    ]
    widened = [
        lax.dynamic_update_slice_in_dim(
            jnp.zeros((layer_count, share_piece.shape[1] * tensor_count), jnp.float32),
            share_piece,
            tensor_place * share_piece.shape[1],
            1,
        )
        for share_piece in small_stack
    ]
    totals = lax.psum(
        (
            widened[0],
            widened[1],
            widened[2],
            widened[3],
            widened[4],
            widened[5],
            widened[6],
            widened[7],
            widened[8],
        ),
        ("wide", "tensor"),
    )
    activations = jnp.concatenate(activation_parts, axis=0)
    input_gradient = jnp.concatenate(gradient_parts, axis=0)
    return (
        activations,
        input_gradient,
        weight_outputs[0],
        weight_outputs[1],
        weight_outputs[2],
        weight_outputs[3],
        weight_outputs[4],
        weight_outputs[5],
        totals[0],
        totals[1],
        totals[2],
        totals[3],
        totals[4],
        totals[5],
        totals[6],
        totals[7],
        totals[8],
    )


MESH_IDS = pl.DeviceIdType.MESH
LOW = jnp.bfloat16
BLOCK = 64
ROWS = -(-SEQ // 16) * 16
DEEP = -(-SEQ // 128) * 128


def place():
    wide = lax.axis_index("wide")
    return (
        lax.div(wide, 4),
        lax.rem(lax.div(wide, 2), 2),
        lax.rem(wide, 2),
        lax.axis_index("tensor"),
    )


def neighbours():
    z, x, c, y = place()

    def at(z, x, c, y):
        return (z * 4 + x * 2 + c, y)

    return {
        "core": at(z, x, 1 - c, y),
        "x": at(z, 1 - x, c, y),
        "y": at(z, x, c, 1 - y),
        "z1": at(z + 1 - 2 * lax.rem(z, 2), x, c, y),
        "z2": at(lax.rem(z + 2, 4), x, c, y),
    }


LINKS = ("core", "x", "y", "z1", "z2")


def greet(partners):
    barrier = pltpu.get_barrier_semaphore()
    for link in LINKS:
        pl.semaphore_signal(barrier, inc=1, device_id=partners[link], device_id_type=MESH_IDS)
    pl.semaphore_wait(barrier, len(LINKS))


def dot_rows(left, right):
    return lax.dot_general(
        left, right, (((1,), (0,)), ((), ())), preferred_element_type=jnp.float32
    )


def dot_cols(left, right):
    return lax.dot_general(
        left, right, (((1,), (1,)), ((), ())), preferred_element_type=jnp.float32
    )


def dot_tokens(left, right):
    return lax.dot_general(
        left, right, (((0,), (0,)), ((), ())), preferred_element_type=jnp.float32
    )


PAIR = 2 * HEAD_DIM


def turned_softmax(keys_here, queries):
    scores = dot_cols(keys_here, queries)
    exponent = jnp.exp(scores - jnp.max(scores, axis=0, keepdims=True))
    return exponent * (1.0 / jnp.sum(exponent, axis=0, keepdims=True))


def store_rows(ref, at, pieces):
    full = SEQ // 16 * 16
    ref[pl.ds(full, ROWS - full), pl.ds(at, PAIR)] = jnp.zeros((ROWS - full, PAIR), LOW)
    ref[pl.ds(0, SEQ), pl.ds(at, PAIR)] = jnp.concatenate(pieces, axis=1)


def gather_stages(z, x, c, y, whole, start, width, last):
    share = (width - last) // 2

    def cols(t, at, size):
        return pl.ds(pl.multiple_of(t * whole + start + at, 128), size)

    all_rows = pl.ds(0, BLOCK)
    pair = pl.ds(lax.div(z, 2) * 2, 2)
    every_z, every_x = pl.ds(0, 4), pl.ds(0, 2)
    far_x, far_y = 1 - x, 1 - y

    def part_a(t):
        return cols(t, 0, share)

    def part_b(t):
        return cols(t, share, share)

    def part_ab(t):
        return cols(t, 0, 2 * share)

    def part_c(t):
        return cols(t, 2 * share, last)

    stages = [
        [("z1", (z, x, c, all_rows, part_ab(y)))],
        [("z2", (pair, x, c, all_rows, part_ab(y)))],
        [
            ("x", (every_z, x, c, all_rows, part_a(y))),
            ("y", (every_z, x, c, all_rows, part_b(y))),
            ("core", (every_z, x, c, all_rows, part_ab(y))),
        ],
        [
            ("y", (every_z, every_x, c, all_rows, part_a(y))),
            ("x", (every_z, x, c, all_rows, part_b(0))),
            ("x", (every_z, x, c, all_rows, part_b(1))),
            ("core", (every_z, far_x, c, all_rows, part_a(y))),
            ("core", (every_z, x, c, all_rows, part_b(far_y))),
        ],
        [
            ("core", (every_z, every_x, c, all_rows, part_a(far_y))),
            ("core", (every_z, far_x, c, all_rows, part_b(0))),
            ("core", (every_z, far_x, c, all_rows, part_b(1))),
        ],
    ]
    if last:
        stages[0].append(("x", (z, x, c, all_rows, part_c(y))))
        stages[1].append(("y", (z, every_x, c, all_rows, part_c(y))))
        for t in range(2):
            stages[2].append(("z1", (z, every_x, c, all_rows, part_c(t))))
            stages[3].append(("z2", (pair, every_x, c, all_rows, part_c(t))))
            stages[4].append(("core", (every_z, every_x, c, all_rows, part_c(t))))
    return stages


GATHER_COPIES = 21
GATHER_DEPTH = 5
GATHER_LAG = 2
CHUNK = 512


class Gather:
    def __init__(self, chunks):
        self.chunks = chunks

    def scratch(self):
        count = len(self.chunks)
        return dict(
            gather_send=pltpu.SemaphoreType.DMA((count, GATHER_COPIES)),
            gather_recv=pltpu.SemaphoreType.DMA((count, GATHER_COPIES)),
            gather_own=pltpu.SemaphoreType.DMA((count,)),
        )

    def bind(self, shards, wholes, refs):
        self.wholes = wholes
        self.send_sem, self.recv_sem, own_sem = refs
        z, x, c, y = place()
        self.partners = neighbours()
        self.plans, self.own, self.flying = [], [], {}
        for chunk, (matrix, start, width, last) in enumerate(self.chunks):
            whole = wholes[matrix].shape[4] // 2
            self.plans.append(gather_stages(z, x, c, y, whole, start, width, last))
            mine = pl.ds(pl.multiple_of(y * whole + start, 128), width)
            size = shards[matrix][0].shape[1]
            shard = shards[matrix][start // size]
            copy = pltpu.make_async_copy(
                shard.at[:, pl.ds(start % size, width)],
                wholes[matrix].at[z, x, c, pl.ds(0, BLOCK), mine],
                own_sem.at[chunk],
            )
            copy.start()
            self.own.append(copy)

    def tick(self, tick):
        done = None
        for stage_idx in range(GATHER_DEPTH, -1, -1):
            chunk = tick - GATHER_LAG * stage_idx
            if chunk < 0 or chunk >= len(self.chunks):
                continue
            if stage_idx == 0:
                self.own[chunk].wait()
            for copy in self.flying.get((chunk, stage_idx - 1), ()):
                copy.wait_recv()
            if stage_idx == GATHER_DEPTH:
                done = chunk
                continue
            started = []
            plan = self.plans[chunk]
            base = sum(len(stage) for stage in plan[:stage_idx])
            whole = self.wholes[self.chunks[chunk][0]]
            for entry, (link, index) in enumerate(plan[stage_idx]):
                copy = pltpu.make_async_remote_copy(
                    src_ref=whole.at[index],
                    dst_ref=whole.at[index],
                    send_sem=self.send_sem.at[chunk, base + entry],
                    recv_sem=self.recv_sem.at[chunk, base + entry],
                    device_id=self.partners[link],
                    device_id_type=MESH_IDS,
                )
                copy.start()
                started.append(copy)
            self.flying[(chunk, stage_idx)] = started
        return done

    def finish(self):
        for started in self.flying.values():
            for copy in started:
                copy.wait_send()


BIAS_ROWS = 9
SAVED = ("normed", "projected", "heads", "normed_two", "hidden", "slope", "middle", "incoming")


class Forward:
    def __init__(self, layers, widths):
        self.layers, self.widths = layers, widths
        chunks = []
        for layer in range(layers):
            for kind, width in enumerate(widths):
                for start in range(0, width, CHUNK):
                    last = CHUNK // 2 if len(chunks) % 4 == 3 else 0
                    chunks.append((layer * len(widths) + kind, start, CHUNK, last))
        self.gather = Gather(chunks)

    def scratch(self):
        project, out, up, down = self.widths
        low, full = (lambda cols: pltpu.VMEM((ROWS, cols), LOW)), pltpu.VMEM((ROWS, 1024), jnp.float32)
        sem = pltpu.SemaphoreType.DMA
        own = dict(
            weights_project=pltpu.VMEM((4, 2, 2, BLOCK, 2 * project), LOW),
            weights_out=pltpu.VMEM((4, 2, 2, BLOCK, 2 * out), LOW),
            weights_up=pltpu.VMEM((4, 2, 2, BLOCK, 2 * up), LOW),
            weights_down=pltpu.VMEM((4, 2, 2, BLOCK, 2 * down), LOW),
            stream=full,
            tokens_in=low(512),
            biases=pltpu.VMEM((2, self.layers * BIAS_ROWS, 512), jnp.float32),
            normed=low(1024),
            projected=low(2 * project),
            heads=low(2 * out),
            normed_two=low(1024),
            hidden=low(2 * up),
            slope=low(2 * up),
            weight_sem=sem((len(self.gather.chunks), 2)),
            saved_sem=sem((self.layers, len(SAVED))),
            swap_send=sem((3,)),
            swap_recv=sem((3,)),
        )
        return {**own, **self.gather.scratch()}

    def bind(self, inputs, outputs, refs):
        for name, ref in zip(self.scratch(), refs, strict=True):
            setattr(self, name, ref)
        shards, inputs = inputs[:6], inputs[6:]
        self.near, self.far, self.norm_refs, bias_refs = inputs[0], inputs[1], inputs[2:6], inputs[6:]
        count = self.layers * 4
        self.wholes, outputs = outputs[:count], outputs[count:]
        self.cotangent_in, self.activations, outputs = outputs[0], outputs[1], outputs[2:]
        self.saved_out = [outputs[k * len(SAVED) : (k + 1) * len(SAVED)] for k in range(self.layers)]
        self.saving, self.loading = {}, {}
        self.y = lax.axis_index("tensor")
        kinds = (shards[:3], shards[3:4], shards[4:5], shards[5:6])
        self.gather.bind(
            [[shard.at[m // 4] for shard in kinds[m % 4]] for m in range(count)],
            self.wholes,
            [getattr(self, name) for name in self.gather.scratch()],
        )
        zeros = jnp.zeros((1, 512), jnp.float32)
        for layer in range(self.layers):
            row = layer * BIAS_ROWS
            for ref in bias_refs:
                line = ref[layer : layer + 1, :].astype(jnp.float32)
                for start in range(0, ref.shape[1], 512):
                    self.biases[self.y, row : row + 1, :] = line[:, start : start + 512]
                    row += 1
                if ref is bias_refs[0]:
                    self.biases[self.y, row : row + 1, :] = zeros
                    row += 1

    def swap(self):
        partner = self.gather.partners["y"]
        pairs = (
            (self.biases.at[self.y], self.biases.at[self.y]),
            (self.far.at[0], self.tokens_in),
            (self.far.at[1], self.cotangent_in),
        )
        self.swaps = []
        for entry, (source, target) in enumerate(pairs):
            copy = pltpu.make_async_remote_copy(
                src_ref=source,
                dst_ref=target,
                send_sem=self.swap_send.at[entry],
                recv_sem=self.swap_recv.at[entry],
                device_id=partner,
                device_id_type=MESH_IDS,
            )
            copy.start()
            self.swaps.append(copy)

    def save(self, layer, name, source):
        entry = SAVED.index(name)
        copy = pltpu.make_async_copy(
            source, self.saved_out[layer][entry], self.saved_sem.at[layer, entry]
        )
        copy.start()
        self.saving[(layer, name)] = copy

    def saved(self, layer, name):
        if (layer, name) in self.saving:
            self.saving.pop((layer, name)).wait()

    def load(self, chunk):
        matrix, start, width, _ = self.gather.chunks[chunk]
        whole = self.gather.wholes[matrix]
        buffer = (self.weights_project, self.weights_out, self.weights_up, self.weights_down)[
            matrix % 4
        ]
        for t in range(2):
            at = (slice(None),) * 4 + (pl.ds(t * (whole.shape[4] // 2) + start, width),)
            copy = pltpu.make_async_copy(whole.at[at], buffer.at[at], self.weight_sem.at[chunk, t])
            copy.start()
            self.loading.setdefault(matrix, []).append(copy)

    def wait_weights(self, matrix):
        for copy in self.loading.pop(matrix):
            copy.wait()

    def bias_row(self, row):
        return jnp.concatenate([self.biases[t, pl.ds(row, 1), :] for t in range(2)], axis=1)

    def norm(self, target, gain_ref, shift_ref, layer, bias_at):
        gain = gain_ref[layer : layer + 1, :].astype(jnp.float32)
        shift = shift_ref[layer : layer + 1, :].astype(jnp.float32)
        bias = None if bias_at is None else self.bias_row(bias_at)

        @pl.loop(0, ROWS // 16)
        def _(step):
            rows = pl.ds(pl.multiple_of(step * 16, 16), 16)
            values = self.stream[rows, :]
            if bias is not None:
                values = values + bias
                self.stream[rows, :] = values
            mean = jnp.mean(values, axis=1, keepdims=True)
            square = jnp.mean(values * values, axis=1, keepdims=True)
            inverse = lax.rsqrt(square - mean * mean + norm_eps)
            target[rows, :] = ((values - mean) * inverse * gain + shift).astype(LOW)

    def begin(self):
        for copy in self.swaps:
            copy.wait_recv()
        y = self.y
        near_at = pl.ds(pl.multiple_of(y * 512, 512), 512)
        far_at = pl.ds(pl.multiple_of((1 - y) * 512, 512), 512)
        self.stream[:, near_at] = self.near[...].astype(jnp.float32)
        self.stream[:, far_at] = self.tokens_in[...].astype(jnp.float32)

    def project(self, layer):
        self.saved(layer - 1, "normed")
        self.norm(
            self.normed,
            *self.norm_refs[:2],
            layer,
            None if layer == 0 else (layer - 1) * BIAS_ROWS + 4,
        )
        self.save(layer, "incoming", self.stream)
        self.save(layer, "normed", self.normed)
        self.saved(layer - 1, "projected")
        self.wait_weights(layer * 4)
        parts = 6

        @pl.loop(0, parts)
        def _(part):
            cols = pl.ds(pl.multiple_of(part * 512, 512), 512)
            weights = self.weights_project[:, :, :, :, cols].reshape(1024, 512)
            row = layer * BIAS_ROWS + lax.rem(part, 3)
            bias = self.biases[lax.div(part, 3), pl.ds(row, 1), :]
            self.projected[:, cols] = (dot_rows(self.normed[...], weights) + bias).astype(LOW)

        self.save(layer, "projected", self.projected)

    def mix(self, layer, first, last):
        if first == 0:
            self.saved(layer - 1, "heads")
        half = self.heads.shape[1] // 2

        @pl.loop(first, last)
        def _(step):
            for t in range(2):
                def at(part):
                    start = (t * 3 + part) * half + step * PAIR
                    return pl.ds(pl.multiple_of(start, PAIR), PAIR)

                queries = self.projected[pl.ds(0, SEQ), at(0)] * jnp.asarray(HEAD_DIM**-0.5, LOW)
                keys_here = self.projected[pl.ds(0, SEQ), at(1)]
                values_here = self.projected[pl.ds(0, SEQ), at(2)]
                pieces = []
                for head in range(2):
                    cols = slice(head * HEAD_DIM, (head + 1) * HEAD_DIM)
                    soft = turned_softmax(keys_here[:, cols], queries[:, cols])
                    pieces.append(dot_tokens(soft.astype(LOW), values_here[:, cols]).astype(LOW))
                store_rows(self.heads, pl.multiple_of(t * half + step * PAIR, PAIR), pieces)

        if last * PAIR == half:
            self.save(layer, "heads", self.heads)

    def attend(self, layer):
        self.wait_weights(layer * 4 + 1)
        self.saved(layer, "incoming")

        @pl.loop(0, 4)
        def _(row):
            cols = pl.ds(pl.multiple_of(row * 256, 256), 256)
            weights = self.weights_out[row].reshape(256, -1)
            self.stream[:, cols] = self.stream[:, cols] + dot_cols(self.heads[...], weights)

        self.saved(layer - 1, "normed_two")
        self.norm(
            self.normed_two,
            *self.norm_refs[2:],
            layer,
            layer * BIAS_ROWS + 3,
        )
        self.save(layer, "normed_two", self.normed_two)
        self.save(layer, "middle", self.stream)

    def feed_up(self, layer, first, last):
        if first == 0:
            self.saved(layer - 1, "hidden")
            self.saved(layer - 1, "slope")
            self.wait_weights(layer * 4 + 2)

        @pl.loop(first, last)
        def _(part):
            cols = pl.ds(pl.multiple_of(part * 512, 512), 512)
            weights = self.weights_up[:, :, :, :, cols].reshape(1024, 512)
            row = layer * BIAS_ROWS + 5 + lax.rem(part, 4)
            bias = self.biases[lax.div(part, 4), pl.ds(row, 1), :]
            before = dot_rows(self.normed_two[...], weights) + bias
            normal = 0.5 * (1.0 + lax.erf(before * 0.7071067811865476))
            self.hidden[:, cols] = (before * normal).astype(LOW)
            density = jnp.exp(-0.5 * before * before) * 0.3989422804014327
            self.slope[:, cols] = (normal + before * density).astype(LOW)

        if last * 512 == self.hidden.shape[1]:
            self.save(layer, "hidden", self.hidden)
            self.save(layer, "slope", self.slope)

    def feed_down(self, layer, first, last):
        if first == 0:
            self.saved(layer, "middle")
            self.wait_weights(layer * 4 + 3)

        @pl.loop(first, last)
        def _(row):
            cols = pl.ds(pl.multiple_of(row * 256, 256), 256)
            weights = self.weights_down[row].reshape(256, -1)
            self.stream[:, cols] = self.stream[:, cols] + dot_cols(self.hidden[...], weights)

    def end(self):
        bias = self.bias_row((self.layers - 1) * BIAS_ROWS + 4)

        @pl.loop(0, ROWS // 16)
        def _(step):
            rows = pl.ds(pl.multiple_of(step * 16, 16), 16)
            self.activations[rows, :] = (self.stream[rows, :] + bias).astype(LOW)

    def work(self):
        steps = [(0, 1, self.begin)]
        for layer in range(self.layers):
            base = layer * 4
            steps += [
                (base, 6, lambda layer=layer: self.project(layer)),
                (base, 7, lambda layer=layer: self.mix(layer, 0, 2)),
                (base, 7, lambda layer=layer: self.mix(layer, 2, 4)),
                (base + 1, 4, lambda layer=layer: self.attend(layer)),
                (base + 2, 6, lambda layer=layer: self.feed_up(layer, 0, 4)),
                (base + 2, 6, lambda layer=layer: self.feed_up(layer, 4, 8)),
                (base + 3, 4, lambda layer=layer: self.feed_down(layer, 0, 2)),
                (base + 3, 4, lambda layer=layer: self.feed_down(layer, 2, 4)),
            ]
        return steps + [(self.layers * 4 - 1, 1, self.end)]

    def run(self):
        greet(self.gather.partners)
        self.swap()
        steps = self.work()
        ready = set()
        remaining = {}
        for matrix, _, _, _ in self.gather.chunks:
            remaining[matrix] = remaining.get(matrix, 0) + 1
        ticks = len(self.gather.chunks) + GATHER_LAG * GATHER_DEPTH
        for tick in range(ticks):
            budget = WORK_A_TICK
            done = self.gather.tick(tick)
            while steps and steps[0][0] in ready and budget > 0:
                _, cost, step = steps.pop(0)
                budget -= cost
                step()
            if done is not None:
                self.free_buffer(done, steps)
                matrix = self.gather.chunks[done][0]
                self.load(done)
                remaining[matrix] -= 1
                if remaining[matrix] == 0:
                    ready.add(matrix)
        for _, _, step in steps:
            step()
        self.gather.finish()
        for copy in self.swaps:
            copy.wait_send()
        for copy in self.saving.values():
            copy.wait()

    def free_buffer(self, chunk, steps):
        matrix = self.gather.chunks[chunk][0]
        while steps and any(entry[0] == matrix - 4 for entry in steps):
            steps.pop(0)[2]()


WORK_A_TICK = 5


def forward(shards, near, far, norms, biases):
    layers = shards[0].shape[0]
    widths = [3 * shards[0].shape[2], *[shard.shape[2] for shard in shards[3:]]]
    plan = Forward(layers, widths)
    project, out, up, down = widths
    low = lambda cols: jax.ShapeDtypeStruct((ROWS, cols), LOW)
    full = jax.ShapeDtypeStruct((ROWS, 1024), jnp.float32)
    saved = [
        low(1024), low(2 * project), low(2 * out), low(1024), low(2 * up), low(2 * up), full, full
    ]
    wholes = [
        jax.ShapeDtypeStruct((4, 2, 2, BLOCK, 2 * width), LOW) for width in widths
    ] * layers
    outs = [*wholes, low(512), low(1024), *(saved * layers)]
    any_spec, vmem_spec = pl.BlockSpec(memory_space=pl.ANY), pl.BlockSpec(memory_space=pltpu.VMEM)
    out_specs = [any_spec] * len(outs)
    out_specs[len(wholes) + 1] = vmem_spec

    operands = [*shards, near, far, *norms, *biases]

    def kernel(*refs):
        ins, refs = refs[: len(operands)], refs[len(operands) :]
        plan.bind(ins, refs[: len(outs)], refs[len(outs) :])
        plan.run()

    results = pl.pallas_call(
        kernel,
        out_shape=outs,
        in_specs=[any_spec] * 6 + [vmem_spec, any_spec] + [vmem_spec] * 9,
        out_specs=out_specs,
        scratch_shapes=list(plan.scratch().values()),
        compiler_params=pltpu.CompilerParams(
            collective_id=0, has_side_effects=True, vmem_limit_bytes=60 * 1024 * 1024
        ),
        cost_estimate=pl.CostEstimate(
            flops=60 * 1024**3, bytes_accessed=700 * 1024 * 1024, transcendentals=0
        ),
        name="forward",
    )(*operands)
    whole, results = results[: len(wholes)], results[len(wholes) :]
    weights = [
        [whole[layer * 4 + kind] for kind in range(4)] for layer in range(layers)
    ]
    cotangent_in, activations, results = results[0], results[1], results[2:]
    kept = [
        dict(zip(SAVED, results[k * len(SAVED) : (k + 1) * len(SAVED)])) for k in range(layers)
    ]
    return weights, cotangent_in, activations, kept


COLS = 128
STAGE_AT = (0, 1, 3, 5, 6, 7, 8)
SETTLE_DEPTH = len(STAGE_AT) - 1
SLOTS = dict(core_in=2, val=5, first_a=4, first_b=4, second=4, third=2, fourth=2, fifth=2, rest=4)
TURNED_SLOTS = 3


class Settle:
    def __init__(self, widths, pairs):
        self.widths, self.pairs = widths, pairs

    def scratch(self):
        shapes = dict(
            core_in=(2, 2, 4, 2, 2, BLOCK, COLS),
            val=(2, 2, 4, 2, 2, BLOCK, COLS),
            first_a=(4, 2, 2, BLOCK, COLS),
            first_b=(2, 4, 2, BLOCK, COLS),
            second=(2, 4, 2, BLOCK, COLS),
            third=(2, 2, 2, BLOCK, COLS),
            fourth=(2, 2, BLOCK, COLS),
            fifth=(2, BLOCK, COLS),
            rest=(2, 4, 2, BLOCK, COLS),
        )
        pairs, sem = len(self.pairs), pltpu.SemaphoreType.DMA
        return dict(
            left_in=pltpu.VMEM((ROWS, 1024), LOW),
            left_turned=pltpu.VMEM((TURNED_SLOTS, 1024, DEEP), LOW),
            right_in=pltpu.VMEM((2, 2, 2, DEEP, 2 * COLS), LOW),
            core_out=pltpu.VMEM((2, 2, 4, 2, 2, BLOCK, COLS), LOW),
            **{name: pltpu.VMEM((SLOTS[name], *shape), LOW) for name, shape in shapes.items()},
            result=pltpu.VMEM((2, 2, 2, BLOCK, COLS), jnp.float32),
            result_sem=sem((2, 2, 2)),
            send_sem=sem((pairs, 2, SETTLE_DEPTH)),
            recv_sem=sem((pairs, 2, SETTLE_DEPTH)),
            right_sem=sem((pairs, 2, 4)),
            left_sem=sem((1,)),
        )

    def bind(self, lefts, rights, outs, refs):
        self.lefts, self.rights, self.outs = lefts, rights, outs
        for name, ref in zip(self.scratch(), refs, strict=True):
            setattr(self, name, ref)
        self.z, self.x, self.c, self.y = place()
        self.partners = neighbours()
        self.copies, self.turned, self.results = {}, {}, {}
        tail = ROWS // 128 * 128
        self.left_turned[:, :, pl.ds(tail, DEEP - tail)] = jnp.zeros(
            (TURNED_SLOTS, 1024, DEEP - tail), LOW
        )
        self.right_in[:, :, :, pl.ds(ROWS, DEEP - ROWS)] = jnp.zeros(
            (2, 2, 2, DEEP - ROWS, 2 * COLS), LOW
        )

    def load(self, pair):
        for unit, (matrix, step) in enumerate(self.pairs[pair]):
            width = self.widths[matrix]
            for t in range(2):
                for near in range(2):
                    core = self.c if near else 1 - self.c
                    at = pl.multiple_of(t * width + core * (width // 2) + step * COLS, COLS)
                    copy = pltpu.make_async_copy(
                        self.rights[matrix].at[:, pl.ds(at, COLS)],
                        self.right_in.at[
                            pair % 2, unit, t, pl.ds(0, ROWS), pl.ds(near * COLS, COLS)
                        ],
                        self.right_sem.at[pair, unit, 2 * t + near],
                    )
                    copy.start()
                    self.copies[(pair, unit, "right", 2 * t + near)] = copy

    def turn(self, matrix):
        if matrix in self.turned:
            return
        source, here = self.lefts[matrix]
        if not here:
            copy = pltpu.make_async_copy(source, self.left_in, self.left_sem.at[0])
            copy.start()
            copy.wait()
            source = self.left_in
        slot = len(self.turned) % TURNED_SLOTS
        for quarter in range(4):
            cols = pl.ds(quarter * 256, 256)
            self.left_turned[slot, cols, pl.ds(0, ROWS)] = source[:, cols].T
        self.turned[matrix] = slot

    def wait_load(self, pair):
        for unit, (matrix, _) in enumerate(self.pairs[pair]):
            self.turn(matrix)
            for entry in range(4):
                self.copies.pop((pair, unit, "right", entry)).wait()

    def send(self, pair, unit, stage, source, target, link):
        copy = pltpu.make_async_remote_copy(
            src_ref=source,
            dst_ref=target,
            send_sem=self.send_sem.at[pair, unit, stage],
            recv_sem=self.recv_sem.at[pair, unit, stage],
            device_id=self.partners[link],
            device_id_type=MESH_IDS,
        )
        copy.start()
        self.copies[(pair, unit, stage)] = copy

    def product(self, pair, unit, t, z):
        matrix, _ = self.pairs[pair][unit]
        at = pl.multiple_of(z * 256, 256)
        left = self.left_turned[self.turned[matrix], pl.ds(at, 256), :]
        right = self.right_in[pair % 2, unit, t]
        total = dot_rows(left[:, :512], right[:512]) + dot_rows(left[:, 512:], right[512:])
        return total.astype(LOW)

    def stage(self, pair, unit, stage):
        if pair < 0 or pair >= len(self.pairs):
            return
        z, x, c, y = self.z, self.x, self.c, self.y
        high, lower = lax.div(z, 2), lax.rem(z, 2)
        far_pair = pl.ds(2 * (1 - high), 2)
        far_z = z + 1 - 2 * lower

        def buffer(name):
            return getattr(self, name).at[pair % SLOTS[name], unit]

        val, rest = buffer("val"), buffer("rest")
        first_a = self.first_a.at[pair % SLOTS["first_a"]]
        first_b = self.first_b.at[pair % SLOTS["first_b"]]
        shape = (2, 2, BLOCK, COLS)
        if stage == 0:
            out = self.core_out.at[unit]

            @pl.loop(0, 4)
            def _(row):
                for t in range(2):
                    total = self.product(pair, unit, t, row)
                    out[t, row] = total[:, :COLS].reshape(shape)
                    val[t, row] = total[:, COLS:].reshape(shape)

            self.send(pair, unit, 0, out, buffer("core_in"), "core")
            return
        self.copies.pop((pair, unit, stage - 1)).wait()
        if stage == 1:
            other = buffer("core_in")

            @pl.loop(0, 4)
            def _(row):
                for t in range(2):
                    val[t, row] = val[t, row] + other[t, row]

            if unit == 0:
                self.send(pair, unit, 1, val.at[1 - y], first_a, "y")
            else:
                self.send(pair, unit, 1, val.at[:, :, 1 - x], first_b, "x")
        elif stage == 2:
            target = buffer("second")
            if unit == 0:

                @pl.loop(0, 4)
                def _(row):
                    val[y, row] = val[y, row] + first_a[row]

                self.send(pair, unit, 2, val.at[y, :, 1 - x], target, "x")
            else:

                @pl.loop(0, 4)
                def _(row):
                    for t in range(2):
                        val[t, row, x] = val[t, row, x] + first_b[t, row]

                self.send(pair, unit, 2, val.at[1 - y, :, x], target, "y")
        elif stage == 3:

            second = buffer("second")

            @pl.loop(0, 4)
            def _(row):
                rest[row] = val[y, row, x] + second[row]

            self.send(pair, unit, 3, rest.at[far_pair], buffer("third"), "z2")
        elif stage == 4:
            third = buffer("third")
            for row in range(2):
                at = 2 * high + row
                rest[at] = rest[at] + third[row]
            self.send(pair, unit, 4, rest.at[far_z], buffer("fourth"), "z1")
        elif stage == 5:
            rest[z] = rest[z] + buffer("fourth")[...]
            self.send(pair, unit, 5, rest.at[z, 1 - c], buffer("fifth"), "core")
        else:
            matrix, step = self.pairs[pair][unit]
            out_ref, layer = self.outs[matrix]
            slot = pair % 2
            for copy in self.results.pop((slot, unit), ()):
                copy.wait()
            result = self.result.at[slot, unit]
            result[c] = rest[z, c].astype(jnp.float32)
            result[1 - c] = buffer("fifth")[...].astype(jnp.float32)
            self.results[(slot, unit)] = []
            for core in range(2):
                copy = pltpu.make_async_copy(
                    result.at[core],
                    out_ref.at[layer, core, :, pl.ds(step * COLS, COLS)],
                    self.result_sem.at[slot, unit, core],
                )
                copy.start()
                self.results[(slot, unit)].append(copy)

    def finish(self):
        for copies in self.results.values():
            for copy in copies:
                copy.wait()

    def tick(self, pair):
        for stage in range(SETTLE_DEPTH, 0, -1):
            for unit in range(2):
                self.stage(pair - STAGE_AT[stage], unit, stage)
        if pair < len(self.pairs):
            self.wait_load(pair)
            for unit in range(2):
                self.stage(pair, unit, 0)


TOTAL_LINKS = ("x", "y", "z1", "z2", "core")
SUM_ROWS = 12
TILE = 512
KEPT = ("normed", "projected", "heads", "normed_two", "hidden", "slope", "middle", "incoming")


class Backward:
    def __init__(self, layers, widths):
        self.layers, self.widths = layers, widths
        pairs, self.needs = [], []
        for layer in reversed(range(layers)):
            base = layer * 4
            feed = widths[2] // 2 // COLS
            for kind, fact in ((3, "arrived"), (2, "fed")):
                for k in range(0, feed, 2):
                    pairs.append(((base + kind, k), (base + kind, k + 1)))
                    self.needs.append((layer, fact))
            rest = [(base + 1, k) for k in range(widths[1] // 2 // COLS)]
            rest += [(base, k) for k in range(widths[0] // 2 // COLS)]
            for k in range(0, len(rest), 2):
                pairs.append((rest[k], rest[k + 1]))
                self.needs.append((layer, "mixed"))
        self.settle = Settle(widths * layers, pairs)

    def scratch(self):
        sem = pltpu.SemaphoreType.DMA
        full = pltpu.VMEM((ROWS, 1024), jnp.float32)
        low = pltpu.VMEM((ROWS, 1024), LOW)
        steps = len(TOTAL_LINKS)
        rows = self.layers * SUM_ROWS
        own = dict(
            grad=full,
            delta=full,
            values=full,
            feed_grad=low,
            mix_grad=low,
            heads_grad=low,
            projected=pltpu.VMEM((ROWS, 2 * self.widths[0]), LOW),
            joined=pltpu.VMEM((ROWS, 2 * self.widths[0]), LOW),
            tile_a=pltpu.VMEM((2, 4, 2, 2, BLOCK, TILE), LOW),
            tile_b=pltpu.VMEM((2, 4, 2, 2, BLOCK, TILE), LOW),
            slope_in=pltpu.VMEM((2, ROWS, TILE), LOW),
            hidden_out=pltpu.VMEM((2, ROWS, TILE), LOW),
            column_sums=pltpu.VMEM((8, 1, TILE), jnp.float32),
            sums_part=pltpu.VMEM((3, 16, 1024), jnp.float32),
            sums=pltpu.VMEM((steps + 1, rows, 1024), jnp.float32),
            sums_in=pltpu.VMEM((steps, rows, 1024), jnp.float32),
            leave=pltpu.VMEM((ROWS, 512), LOW),
            tile_sem=sem((2, 3)),
            hidden_sem=sem((2,)),
            value_sem=sem((3,)),
            sums_send=sem((steps,)),
            sums_recv=sem((steps,)),
            swap_send=sem((2,)),
            swap_recv=sem((2,)),
        )
        return {**own, **self.settle.scratch()}

    def bind(self, inputs, outputs, refs):
        for name, ref in zip(self.scratch(), refs, strict=True):
            setattr(self, name, ref)
        layers = self.layers
        count = layers * 4
        self.weights, inputs = inputs[:count], inputs[count:]
        self.kept = [
            dict(zip(KEPT, inputs[k * len(KEPT) : (k + 1) * len(KEPT)])) for k in range(layers)
        ]
        self.upstream, self.leaving, *self.gains = inputs[layers * len(KEPT) :]
        outs, outputs = outputs[:4], outputs[4:]
        self.total_out, self.near_out, self.arriving, outputs = (*outputs[:3], outputs[3:])
        self.hidden_grads = outputs
        self.facts, self.hidden_copies = set(), []
        lefts, rights = [], []
        for layer in range(layers):
            kept = self.kept[layer]
            lefts += [
                (kept["normed"], False),
                (self.mix_grad, True),
                (kept["normed_two"], False),
                (self.feed_grad, True),
            ]
            rights += [self.joined, kept["heads"], self.hidden_grads[layer], kept["hidden"]]
        self.settle.bind(
            lefts,
            rights,
            [(outs[m % 4], m // 4) for m in range(count)],
            [getattr(self, name) for name in self.settle.scratch()],
        )
        self.loaded_pair = -1

    def fetch(self, entry, source, target):
        copy = pltpu.make_async_copy(source, target, self.value_sem.at[entry])
        copy.start()
        return copy

    def swap(self, entry, source):
        copy = pltpu.make_async_remote_copy(
            src_ref=source,
            dst_ref=self.arriving.at[entry],
            send_sem=self.swap_send.at[entry],
            recv_sem=self.swap_recv.at[entry],
            device_id=self.settle.partners["y"],
            device_id_type=MESH_IDS,
        )
        copy.start()
        return copy

    def row_loop(self, body):
        @pl.loop(0, ROWS // 16)
        def _(step):
            body(pl.ds(pl.multiple_of(step * 16, 16), 16))

    def put_sum(self, layer, row, values):
        self.sums[0, pl.ds(layer * SUM_ROWS + row, 1), :] = values

    def begin(self):
        self.fetch(0, self.upstream, self.feed_grad).wait()
        self.facts.add((self.layers - 1, "arrived"))

    def widen(self):
        self.sums_part[...] = jnp.zeros_like(self.sums_part)

        def body(rows):
            values = self.feed_grad[rows, :].astype(jnp.float32)
            self.grad[rows, :] = values
            self.sums_part[2] += values

        self.row_loop(body)
        self.put_sum(self.layers - 1, 7, jnp.sum(self.sums_part[2], axis=0, keepdims=True))

    def tile_copies(self, part, sources, targets):
        cols = pl.ds(part * TILE, TILE)
        slot = part % 2
        copies = []
        for entry, (source, target) in enumerate(zip(sources, targets)):
            at = (slice(None),) * (len(source.shape) - 1) + (cols,)
            copy = pltpu.make_async_copy(
                source.at[at], target.at[slot], self.tile_sem.at[slot, entry]
            )
            copy.start()
            copies.append(copy)
        return copies

    def tile(self, part, parts, sources, targets):
        if part == 0:
            self.coming = self.tile_copies(0, sources, targets)
        for copy in self.coming:
            copy.wait()
        if part + 1 < parts:
            self.coming = self.tile_copies(part + 1, sources, targets)

    def add_delta(self, is_first, grads, weights):
        for half in range(2):
            cols = slice(half * 512, (half + 1) * 512)
            product = dot_cols(grads, weights[2 * half : 2 * half + 2].reshape(512, TILE))
            self.delta[:, cols] = product if is_first else self.delta[:, cols] + product

    def feed(self, layer, part):
        out_ref = self.hidden_grads[layer]
        parts, slot = out_ref.shape[1] // TILE, part % 2
        if part == 0:
            self.value_copy = self.fetch(1, self.kept[layer]["middle"], self.values)
        sources = (self.weights[layer * 4 + 3], self.weights[layer * 4 + 2], self.kept[layer]["slope"])
        self.tile(part, parts, sources, (self.tile_a, self.tile_b, self.slope_in))
        if part >= 2:
            self.hidden_copies.pop(0).wait()
        down = self.tile_a[slot].reshape(1024, TILE)
        slope = self.slope_in[slot].astype(jnp.float32)
        grads = (dot_rows(self.feed_grad[...], down) * slope).astype(LOW)
        self.hidden_out[slot] = grads
        copy = pltpu.make_async_copy(
            self.hidden_out.at[slot],
            out_ref.at[:, pl.ds(part * TILE, TILE)],
            self.hidden_sem.at[slot],
        )
        copy.start()
        self.hidden_copies.append(copy)
        self.column_sums[part] = jnp.sum(grads.astype(jnp.float32), axis=0, keepdims=True)
        self.add_delta(part == 0, grads, self.tile_b.at[slot])
        if part == parts - 1:
            while self.hidden_copies:
                self.hidden_copies.pop(0).wait()
            for row in range(4):
                pieces = [self.column_sums[2 * row], self.column_sums[2 * row + 1]]
                self.put_sum(layer, 3 + row, jnp.concatenate(pieces, axis=1))
            self.facts.add((layer, "fed"))

    def norm_back(self, layer, gain_ref, sum_row, low_ref, total_at):
        self.value_copy.wait()
        gain = gain_ref[layer : layer + 1, :].astype(jnp.float32)
        self.sums_part[...] = jnp.zeros_like(self.sums_part)

        def body(rows):
            stream, delta = self.values[rows, :], self.delta[rows, :]
            mean = jnp.mean(stream, axis=1, keepdims=True)
            square = jnp.mean(stream * stream, axis=1, keepdims=True)
            inverse = lax.rsqrt(square - mean * mean + norm_eps)
            centred = (stream - mean) * inverse
            weighted = delta * centred
            self.sums_part[0] += weighted
            self.sums_part[1] += delta
            scaled = delta * gain
            grad = self.grad[rows, :] + inverse * (
                scaled
                - jnp.mean(scaled, axis=1, keepdims=True)
                - centred * jnp.mean(weighted * gain, axis=1, keepdims=True)
            )
            self.grad[rows, :] = grad
            self.sums_part[2] += grad
            if low_ref is not None:
                low_ref[rows, :] = grad.astype(LOW)

        self.row_loop(body)
        for entry in range(2):
            total = jnp.sum(self.sums_part[entry], axis=0, keepdims=True)
            self.put_sum(layer, sum_row + entry, total)
        if total_at is not None:
            total = jnp.sum(self.sums_part[2], axis=0, keepdims=True)
            self.put_sum(*total_at, total)

    def out_back(self, layer):
        self.norm_back(layer, self.gains[1], 10, self.mix_grad, (layer, 2))
        self.value_copy = self.fetch(1, self.kept[layer]["incoming"], self.values)
        self.projected_copy = self.fetch(2, self.kept[layer]["projected"], self.projected)

        for part in range(2):
            self.tile(part, 2, (self.weights[layer * 4 + 1],), (self.tile_a,))
            cols = pl.ds(part * TILE, TILE)
            weights = self.tile_a[part].reshape(1024, TILE)
            self.heads_grad[:, cols] = dot_rows(self.mix_grad[...], weights).astype(LOW)

    def mix_back(self, layer, first, last):
        if first == 0:
            self.projected_copy.wait()
        half = self.heads_grad.shape[1] // 2

        @pl.loop(2 * first, 2 * last)
        def _(turn):
            step, t = lax.div(turn, 2), lax.rem(turn, 2)

            def at(part):
                start = (t * 3 + part) * half + step * PAIR
                return pl.ds(pl.multiple_of(start, PAIR), PAIR)

            here = pl.ds(pl.multiple_of(t * half + step * PAIR, PAIR), PAIR)
            rows = pl.ds(0, SEQ)
            all_queries = self.projected[rows, at(0)] * jnp.asarray(HEAD_DIM**-0.5, LOW)
            all_keys, all_values = self.projected[rows, at(1)], self.projected[rows, at(2)]
            all_grads = self.heads_grad[rows, here]
            pieces = ([], [], [])
            for head in range(2):
                cols = slice(head * HEAD_DIM, (head + 1) * HEAD_DIM)
                keys_here, queries = all_keys[:, cols], all_queries[:, cols]
                grads = all_grads[:, cols]
                soft = turned_softmax(keys_here, queries)
                soft_grad = dot_cols(all_values[:, cols], grads)
                delta = jnp.sum(soft_grad * soft, axis=0, keepdims=True)
                score_grad = (soft * (soft_grad - delta)).astype(LOW)
                pieces[0].append(
                    (dot_tokens(score_grad, keys_here) * HEAD_DIM**-0.5).astype(LOW)
                )
                pieces[1].append(dot_rows(score_grad, queries).astype(LOW))
                pieces[2].append(dot_rows(soft.astype(LOW), grads).astype(LOW))
            for part in range(3):
                start = (t * 3 + part) * half + step * PAIR
                store_rows(self.joined, pl.multiple_of(start, PAIR), pieces[part])

        if last * PAIR == half:
            self.facts.add((layer, "mixed"))

    def project_back(self, layer, part):
        self.tile(part, 6, (self.weights[layer * 4],), (self.tile_a,))
        grads = self.joined[:, pl.ds(part * TILE, TILE)]
        self.column_sums[part] = jnp.sum(grads.astype(jnp.float32), axis=0, keepdims=True)
        self.add_delta(part == 0, grads, self.tile_a.at[part % 2])
        if part == 5:
            for row, at in ((0, 0), (1, 2)):
                pieces = [self.column_sums[at], self.column_sums[3 + at]]
                self.put_sum(layer, row, jnp.concatenate(pieces, axis=1))

    def first_back(self, layer):
        last = layer == 0
        low_ref = None if last else self.feed_grad
        self.norm_back(layer, self.gains[0], 8, low_ref, None if last else (layer - 1, 7))
        if not last:
            self.facts.add((layer - 1, "arrived"))

    def end(self):
        y = self.y
        near_at = pl.ds(pl.multiple_of(y * 512, 512), 512)
        far_at = pl.ds(pl.multiple_of((1 - y) * 512, 512), 512)
        self.leave[...] = self.grad[:, far_at].astype(LOW)
        self.swaps.append(self.swap(1, self.leave))
        copy = self.fetch(0, self.grad.at[:, near_at], self.near_out)
        copy.wait()
        self.facts.add("summed")

    def chain(self):
        steps = [(1, self.begin, ()), (2, self.widen, ())]
        for layer in reversed(range(self.layers)):
            for part in range(2 * self.widths[2] // TILE):
                steps.append((2.5, lambda layer=layer, part=part: self.feed(layer, part), ()))
            steps.append((4, lambda layer=layer: self.out_back(layer), ((layer + 1, 1),)))
            for k in range(4):
                needs = ((layer + 1, 0),)
                steps.append((7, lambda layer=layer, k=k: self.mix_back(layer, k, k + 1), needs))
            for part in range(6):
                steps.append(
                    (1.5, lambda layer=layer, part=part: self.project_back(layer, part), ())
                )
            steps.append((3, lambda layer=layer: self.first_back(layer), ((layer, 3),)))
        return steps + [(1, self.end, ())]

    def add_sums(self, step):
        if step > 0:
            self.sums_copy.wait()
            self.sums[step] = self.sums[step - 1] + self.sums_in[step - 1]
        if step < len(TOTAL_LINKS):
            copy = pltpu.make_async_remote_copy(
                src_ref=self.sums.at[step],
                dst_ref=self.sums_in.at[step],
                send_sem=self.sums_send.at[step],
                recv_sem=self.sums_recv.at[step],
                device_id=self.settle.partners[TOTAL_LINKS[step]],
                device_id_type=MESH_IDS,
            )
            copy.start()
            self.sums_copy = copy

    def run(self):
        self.y = lax.axis_index("tensor")
        settle = self.settle
        greet(settle.partners)
        self.swaps = [self.swap(0, self.leaving)]
        chain = self.chain()
        last_pair = {}
        for pair, units in enumerate(settle.pairs):
            for matrix, _ in units:
                last_pair[matrix] = pair
        pairs, loaded, sum_step = len(settle.pairs), set(), 0
        passed = -1

        def free(needs):
            for layer, kind in needs:
                if layer < self.layers and passed < last_pair[layer * 4 + kind]:
                    return False
            return True

        def advance():
            _, step, _ = chain.pop(0)
            step()

        pair = 0
        while pair < pairs + STAGE_AT[-1] or sum_step <= len(TOTAL_LINKS):
            if pair < pairs:
                while self.needs[pair] not in self.facts:
                    advance()
                if pair not in loaded:
                    settle.load(pair)
                    loaded.add(pair)
            settle.tick(pair)
            passed = pair
            if "summed" in self.facts and sum_step <= len(TOTAL_LINKS):
                self.add_sums(sum_step)
                sum_step += 1
            if pair + 1 < pairs and self.needs[pair + 1] in self.facts:
                settle.load(pair + 1)
                loaded.add(pair + 1)
            budget = CHAIN_A_TICK
            while chain and budget > 0 and free(chain[0][2]):
                budget -= chain[0][0]
                advance()
            pair += 1
        self.total_out[...] = self.sums[len(TOTAL_LINKS)]
        settle.finish()
        for copy in self.swaps:
            copy.wait()


CHAIN_A_TICK = 5


def backward(weights, kept, upstream, gains, leaving):
    layers = len(weights)
    widths = [block.shape[-1] // 2 for block in weights[0]]
    plan = Backward(layers, widths)
    any_spec, vmem_spec = pl.BlockSpec(memory_space=pl.ANY), pl.BlockSpec(memory_space=pltpu.VMEM)
    operands = [block for layer in weights for block in layer]
    operands += [values[name] for values in kept for name in KEPT]
    operands += [upstream, leaving]
    in_specs = [any_spec] * len(operands) + [vmem_spec] * len(gains)
    operands += gains
    outs = [jax.ShapeDtypeStruct((layers, 2, BLOCK, width // 2), jnp.float32) for width in widths]
    outs += [
        jax.ShapeDtypeStruct((layers * SUM_ROWS, 1024), jnp.float32),
        jax.ShapeDtypeStruct((ROWS, 512), jnp.float32),
        jax.ShapeDtypeStruct((2, ROWS, 512), LOW),
    ]
    outs += [jax.ShapeDtypeStruct((ROWS, 2 * widths[2]), LOW)] * layers
    out_specs = [any_spec] * len(outs)
    out_specs[4] = vmem_spec

    def kernel(*refs):
        ins, refs = refs[: len(operands)], refs[len(operands) :]
        plan.bind(ins, refs[: len(outs)], refs[len(outs) :])
        plan.run()

    results = pl.pallas_call(
        kernel,
        out_shape=outs,
        in_specs=in_specs,
        out_specs=out_specs,
        scratch_shapes=list(plan.scratch().values()),
        compiler_params=pltpu.CompilerParams(
            collective_id=1, has_side_effects=True, vmem_limit_bytes=60 * 1024 * 1024
        ),
        cost_estimate=pl.CostEstimate(
            flops=120 * 1024**3, bytes_accessed=700 * 1024 * 1024, transcendentals=0
        ),
        name="backward",
    )(*operands)
    return results[:4], results[4], results[5], results[6]


def in_order(own, other, index, axis):
    first = jnp.where(index == 0, own, other)
    second = jnp.where(index == 0, other, own)
    return jnp.concatenate((first, second), axis=axis)


def image_body(
    images,
    first_gain,
    first_shift,
    query_weight,
    key_weight,
    value_weight,
    query_bias,
    value_bias,
    out_weight,
    out_bias,
    second_gain,
    second_shift,
    up_weight,
    up_bias,
    down_weight,
    down_bias,
    cotangent,
):
    layers = query_weight.shape[0]
    half = images.shape[1]
    hidden_width = 2 * up_weight.shape[2]
    y = lax.axis_index("tensor")
    far = 1 - y

    def own_rows(block, image):
        rows = lax.dynamic_slice_in_dim(block, image * SEQ, SEQ)
        return jnp.pad(rows, ((0, ROWS - SEQ), (0, 0)))

    weights, cotangent_in, activations, kept = forward(
        (
            query_weight,
            key_weight,
            value_weight,
            jnp.swapaxes(out_weight, 1, 2),
            up_weight,
            jnp.swapaxes(down_weight, 1, 2),
        ),
        own_rows(images, y),
        jnp.stack((own_rows(images, far), own_rows(cotangent, far))),
        (first_gain, first_shift, second_gain, second_shift),
        (query_bias, value_bias, out_bias, down_bias, up_bias),
    )

    def columns(rows, t):
        return lax.dynamic_slice_in_dim(rows, t * half, half, axis=1)

    upstream = in_order(own_rows(cotangent, y), cotangent_in, y, 1)
    (project_out, out_out, up_out, down_out), totals, near_gradient, arriving = backward(
        weights, kept, upstream, (first_gain, second_gain), columns(activations, far)
    )
    totals = totals.reshape(layers, -1)
    project_out, out_out, up_out, down_out = [
        jnp.swapaxes(block, 1, 2).reshape(layers, BLOCK, -1)
        for block in (project_out, out_out, up_out, down_out)
    ]
    width = 2 * half
    small_outs, at = [], 0
    for size in (width, width, width, hidden_width, width, width, width, width, width):
        small_outs.append(totals[:, at : at + size])
        at += size
    return (
        in_order(columns(activations, y)[:SEQ], arriving[0, :SEQ], y, 0),
        in_order(near_gradient[:SEQ], arriving[1, :SEQ].astype(jnp.float32), y, 0),
        project_out[:, :, :half],
        project_out[:, :, half : 2 * half],
        project_out[:, :, 2 * half :],
        jnp.swapaxes(out_out, 1, 2),
        up_out,
        jnp.swapaxes(down_out, 1, 2),
        *small_outs,
    )


def solution(mesh):
    in_specs = (
        P("wide", "tensor"),
        P(),
        P(),
        P(None, "wide", "tensor"),
        P(None, "wide", "tensor"),
        P(None, "wide", "tensor"),
        P(None, "tensor"),
        P(None, "tensor"),
        P(None, "tensor", "wide"),
        P(None, "tensor"),
        P(),
        P(),
        P(None, "wide", "tensor"),
        P(None, "tensor"),
        P(None, "tensor", "wide"),
        P(None, "tensor"),
        P("wide", "tensor"),
    )
    out_specs = (
        P("wide", "tensor"),
        P("wide", "tensor"),
        P(None, "wide", "tensor"),
        P(None, "wide", "tensor"),
        P(None, "wide", "tensor"),
        P(None, "tensor", "wide"),
        P(None, "wide", "tensor"),
        P(None, "tensor", "wide"),
        P(),
        P(),
        P(),
        P(),
        P(),
        P(),
        P(),
        P(),
        P(),
    )
    chosen = body
    if mesh.shape["wide"] == 16 and mesh.shape["tensor"] == 2:
        chosen = image_body
    return jax.shard_map(
        chosen, mesh=mesh, in_specs=in_specs, out_specs=out_specs, check_vma=False
    )
```

```python
import jax
import jax.numpy as jnp
from jax import lax
from jax.experimental import pallas as pl
from jax.experimental.pallas import tpu as pltpu
from jax.sharding import PartitionSpec as P

HEAD_DIM = 64
SEQ = 577
MICRO = 2


norm_eps = 1e-06


def row_totals(first_terms, second_terms):
    return lax.psum((first_terms, second_terms), "tensor")


def full_rows(share_low):
    return lax.all_gather(share_low, "tensor", axis=1, tiled=True)


def feature_total(partial_sums):
    return lax.psum_scatter(
        partial_sums.astype(jnp.bfloat16), "tensor", scatter_dimension=1, tiled=True
    ).astype(jnp.float32)


def fetch_weights(query_block, key_block, value_block, out_block, up_block, down_block):
    return (
        lax.all_gather(query_block, "wide", axis=0, tiled=True),
        lax.all_gather(key_block, "wide", axis=0, tiled=True),
        lax.all_gather(value_block, "wide", axis=0, tiled=True),
        lax.all_gather(out_block, "wide", axis=1, tiled=True),
        lax.all_gather(up_block, "wide", axis=0, tiled=True),
        lax.all_gather(down_block, "wide", axis=1, tiled=True),
    )


def settle_grads(query_piece, key_piece, value_piece, out_piece, up_piece, down_piece):
    return (
        lax.psum_scatter(
            query_piece.astype(jnp.bfloat16), "wide", scatter_dimension=0, tiled=True
        ).astype(jnp.float32),
        lax.psum_scatter(
            key_piece.astype(jnp.bfloat16), "wide", scatter_dimension=0, tiled=True
        ).astype(jnp.float32),
        lax.psum_scatter(
            value_piece.astype(jnp.bfloat16), "wide", scatter_dimension=0, tiled=True
        ).astype(jnp.float32),
        lax.psum_scatter(
            out_piece.astype(jnp.bfloat16), "wide", scatter_dimension=1, tiled=True
        ).astype(jnp.float32),
        lax.psum_scatter(
            up_piece.astype(jnp.bfloat16), "wide", scatter_dimension=0, tiled=True
        ).astype(jnp.float32),
        lax.psum_scatter(
            down_piece.astype(jnp.bfloat16), "wide", scatter_dimension=1, tiled=True
        ).astype(jnp.float32),
    )


def add_terms(earlier, latest):
    if earlier is None:
        return latest
    return jax.tree.map(jnp.add, earlier, latest)


def norm_forward(stream, gain, shift, full_width):
    first_terms, second_terms = row_totals(
        jnp.sum(stream, axis=1), jnp.sum(stream * stream, axis=1)
    )
    row_mean = first_terms / full_width
    inverse_std = lax.rsqrt(second_terms / full_width - row_mean * row_mean + norm_eps)
    centred = (stream - row_mean[:, None]) * inverse_std[:, None]
    return (centred * gain + shift, centred, inverse_std)


def norm_backward(upstream, centred, inverse_std, gain, full_width):
    scaled = upstream * gain
    first_terms, second_terms = row_totals(
        jnp.sum(scaled, axis=1), jnp.sum(scaled * centred, axis=1)
    )
    return inverse_std[:, None] * (
        scaled - first_terms[:, None] / full_width - centred * (second_terms[:, None] / full_width)
    )


def attention_forward(queries, keys_here, values_here, image_count, heads_here):
    score_scale = HEAD_DIM ** (-0.5)
    shape_four = (image_count, SEQ, heads_here, HEAD_DIM)
    query_four = queries.reshape(shape_four)
    key_four = keys_here.reshape(shape_four)
    value_four = values_here.reshape(shape_four)
    scores = (
        jnp.einsum("iqhd,ikhd->ihqk", query_four, key_four, preferred_element_type=jnp.float32)
        * score_scale
    )
    row_peak = jnp.max(scores, axis=-1, keepdims=True)
    exponent = jnp.exp(scores - row_peak)
    row_total = jnp.sum(exponent, axis=-1, keepdims=True)
    weights_soft = (exponent / row_total).astype(jnp.bfloat16)
    mixed_heads = jnp.einsum(
        "ihqk,ikhd->iqhd", weights_soft, value_four, preferred_element_type=jnp.float32
    )
    log_total = row_peak[..., 0] + jnp.log(row_total[..., 0])
    return (mixed_heads.reshape(queries.shape).astype(jnp.bfloat16), log_total)


def attention_backward(
    queries, keys_here, values_here, log_total, mixed_grad, image_count, heads_here
):
    score_scale = HEAD_DIM ** (-0.5)
    shape_four = (image_count, SEQ, heads_here, HEAD_DIM)
    query_four = queries.reshape(shape_four)
    key_four = keys_here.reshape(shape_four)
    value_four = values_here.reshape(shape_four)
    grad_four = mixed_grad.reshape(shape_four)
    scores = (
        jnp.einsum("iqhd,ikhd->ihqk", query_four, key_four, preferred_element_type=jnp.float32)
        * score_scale
    )
    weights_soft = jnp.exp(scores - log_total[..., None])
    weight_grad = jnp.einsum(
        "iqhd,ikhd->ihqk", grad_four, value_four, preferred_element_type=jnp.float32
    )
    row_delta = jnp.sum(weight_grad * weights_soft, axis=-1, keepdims=True)
    score_grad = (weights_soft * (weight_grad - row_delta)).astype(jnp.bfloat16)
    query_grad = (
        jnp.einsum("ihqk,ikhd->iqhd", score_grad, key_four, preferred_element_type=jnp.float32)
        * score_scale
    )
    key_grad = (
        jnp.einsum("ihqk,iqhd->ikhd", score_grad, query_four, preferred_element_type=jnp.float32)
        * score_scale
    )
    value_grad = jnp.einsum(
        "ihqk,iqhd->ikhd",
        weights_soft.astype(jnp.bfloat16),
        grad_four,
        preferred_element_type=jnp.float32,
    )
    flat_shape = queries.shape
    return (
        query_grad.reshape(flat_shape),
        key_grad.reshape(flat_shape),
        value_grad.reshape(flat_shape),
    )


def gelu_slope(values):
    normal_cdf = 0.5 * (1.0 + lax.erf(values * 0.7071067811865476))
    return normal_cdf + values * jnp.exp(-0.5 * values * values) * 0.3989422804014327


def body(
    images,
    first_gain,
    first_shift,
    query_weight,
    key_weight,
    value_weight,
    query_bias,
    value_bias,
    out_weight,
    out_bias,
    second_gain,
    second_shift,
    up_weight,
    up_bias,
    down_weight,
    down_bias,
    cotangent,
):
    layer_count = query_weight.shape[0]
    feature_block = images.shape[1]
    tensor_count = lax.axis_size("tensor")
    full_width = feature_block * tensor_count
    heads_here = feature_block // HEAD_DIM
    tensor_place = lax.axis_index("tensor")
    micro_rows = images.shape[0] // MICRO
    image_count = micro_rows // SEQ

    def gain_share(param_table, layer_idx):
        return lax.dynamic_slice_in_dim(
            param_table[layer_idx], tensor_place * feature_block, feature_block
        )

    def layer_weights(layer_idx):
        return fetch_weights(
            query_weight[layer_idx],
            key_weight[layer_idx],
            value_weight[layer_idx],
            out_weight[layer_idx],
            up_weight[layer_idx],
            down_weight[layer_idx],
        )

    weight_sums = [None] * layer_count
    small_sums = [None] * layer_count
    activation_parts = []
    gradient_parts = []
    for micro_idx in range(MICRO):
        row_start = micro_idx * micro_rows
        stream = images[row_start : row_start + micro_rows].astype(jnp.float32)
        saved_state = []
        for layer_idx in range(layer_count):
            query_full, key_full, value_full, out_full, up_full, down_full = layer_weights(
                layer_idx
            )
            normed, centred_one, inverse_one = norm_forward(
                stream,
                gain_share(first_gain, layer_idx),
                gain_share(first_shift, layer_idx),
                full_width,
            )
            normed_full = full_rows(normed.astype(jnp.bfloat16))
            joined_weight = jnp.concatenate((query_full, key_full, value_full), axis=1)
            projected = jnp.dot(normed_full, joined_weight, preferred_element_type=jnp.float32)
            queries = (projected[:, :feature_block] + query_bias[layer_idx]).astype(jnp.bfloat16)
            keys_here = projected[:, feature_block : 2 * feature_block].astype(jnp.bfloat16)
            values_here = (projected[:, 2 * feature_block :] + value_bias[layer_idx]).astype(
                jnp.bfloat16
            )
            mixed_heads, log_total = attention_forward(
                queries, keys_here, values_here, image_count, heads_here
            )
            attention_sum = feature_total(
                jnp.dot(mixed_heads, out_full, preferred_element_type=jnp.float32)
            )
            after_attention = stream + attention_sum + out_bias[layer_idx]
            normed_two, centred_two, inverse_two = norm_forward(
                after_attention,
                gain_share(second_gain, layer_idx),
                gain_share(second_shift, layer_idx),
                full_width,
            )
            normed_two_full = full_rows(normed_two.astype(jnp.bfloat16))
            hidden_pre = (
                jnp.dot(normed_two_full, up_full, preferred_element_type=jnp.float32)
                + up_bias[layer_idx]
            )
            hidden = jax.nn.gelu(hidden_pre, approximate=False).astype(jnp.bfloat16)
            feedforward_sum = feature_total(
                jnp.dot(hidden, down_full, preferred_element_type=jnp.float32)
            )
            saved_state.append(
                (
                    centred_one,
                    inverse_one,
                    normed_full,
                    queries,
                    keys_here,
                    values_here,
                    mixed_heads,
                    log_total,
                    centred_two,
                    inverse_two,
                    normed_two_full,
                    hidden_pre,
                    hidden,
                )
            )
            stream = after_attention + feedforward_sum + down_bias[layer_idx]
        activation_parts.append(stream.astype(jnp.bfloat16))
        upstream = cotangent[row_start : row_start + micro_rows].astype(jnp.float32)
        for layer_idx in reversed(range(layer_count)):
            query_full, key_full, value_full, out_full, up_full, down_full = layer_weights(
                layer_idx
            )
            (
                centred_one,
                inverse_one,
                normed_full,
                queries,
                keys_here,
                values_here,
                mixed_heads,
                log_total,
                centred_two,
                inverse_two,
                normed_two_full,
                hidden_pre,
                hidden,
            ) = saved_state[layer_idx]
            down_bias_term = jnp.sum(upstream, axis=0)
            upstream_full = full_rows(upstream.astype(jnp.bfloat16))
            down_term = jnp.einsum(
                "rc,rd->cd", hidden, upstream_full, preferred_element_type=jnp.float32
            )
            hidden_grad = jnp.einsum(
                "rd,cd->rc", upstream_full, down_full, preferred_element_type=jnp.float32
            )
            pre_grad = (hidden_grad * gelu_slope(hidden_pre)).astype(jnp.bfloat16)
            up_bias_term = jnp.sum(pre_grad.astype(jnp.float32), axis=0)
            up_term = jnp.einsum(
                "rd,rc->dc", normed_two_full, pre_grad, preferred_element_type=jnp.float32
            )
            normed_two_grad = feature_total(
                jnp.einsum("rc,dc->rd", pre_grad, up_full, preferred_element_type=jnp.float32)
            )
            second_gain_term = jnp.sum(normed_two_grad * centred_two, axis=0)
            second_shift_term = jnp.sum(normed_two_grad, axis=0)
            upstream = upstream + norm_backward(
                normed_two_grad,
                centred_two,
                inverse_two,
                gain_share(second_gain, layer_idx),
                full_width,
            )
            out_bias_term = jnp.sum(upstream, axis=0)
            upstream_full = full_rows(upstream.astype(jnp.bfloat16))
            out_term = jnp.einsum(
                "rc,rd->cd", mixed_heads, upstream_full, preferred_element_type=jnp.float32
            )
            mixed_grad = jnp.einsum(
                "rd,cd->rc", upstream_full, out_full, preferred_element_type=jnp.float32
            ).astype(jnp.bfloat16)
            query_grad, key_grad, value_grad = attention_backward(
                queries, keys_here, values_here, log_total, mixed_grad, image_count, heads_here
            )
            joined_grad = jnp.concatenate((query_grad, key_grad, value_grad), axis=1).astype(
                jnp.bfloat16
            )
            joined_float = joined_grad.astype(jnp.float32)
            query_bias_term = jnp.sum(joined_float[:, :feature_block], axis=0)
            value_bias_term = jnp.sum(joined_float[:, 2 * feature_block :], axis=0)
            joined_term = jnp.einsum(
                "rd,rc->dc", normed_full, joined_grad, preferred_element_type=jnp.float32
            )
            joined_weight = jnp.concatenate((query_full, key_full, value_full), axis=1)
            normed_grad = feature_total(
                jnp.einsum(
                    "rc,dc->rd", joined_grad, joined_weight, preferred_element_type=jnp.float32
                )
            )
            first_gain_term = jnp.sum(normed_grad * centred_one, axis=0)
            first_shift_term = jnp.sum(normed_grad, axis=0)
            upstream = upstream + norm_backward(
                normed_grad, centred_one, inverse_one, gain_share(first_gain, layer_idx), full_width
            )
            query_term = joined_term[:, :feature_block]
            key_term = joined_term[:, feature_block : 2 * feature_block]
            value_term = joined_term[:, 2 * feature_block :]
            weight_sums[layer_idx] = add_terms(
                weight_sums[layer_idx],
                settle_grads(query_term, key_term, value_term, out_term, up_term, down_term),
            )
            small_sums[layer_idx] = add_terms(
                small_sums[layer_idx],
                (
                    query_bias_term,
                    value_bias_term,
                    out_bias_term,
                    up_bias_term,
                    down_bias_term,
                    first_gain_term,
                    first_shift_term,
                    second_gain_term,
                    second_shift_term,
                ),
            )
        gradient_parts.append(upstream)
    share_sets = []
    for layer_idx in range(layer_count):
        share_sets.append(weight_sums[layer_idx])
    weight_outputs = [
        jnp.stack([share_sets[layer_idx][entry_idx] for layer_idx in range(layer_count)])
        for entry_idx in range(6)
    ]
    small_stack = [
        jnp.stack([small_sums[layer_idx][entry_idx] for layer_idx in range(layer_count)])
        for entry_idx in range(9)
    ]
    widened = [
        lax.dynamic_update_slice_in_dim(
            jnp.zeros((layer_count, share_piece.shape[1] * tensor_count), jnp.float32),
            share_piece,
            tensor_place * share_piece.shape[1],
            1,
        )
        for share_piece in small_stack
    ]
    totals = lax.psum(
        (
            widened[0],
            widened[1],
            widened[2],
            widened[3],
            widened[4],
            widened[5],
            widened[6],
            widened[7],
            widened[8],
        ),
        ("wide", "tensor"),
    )
    activations = jnp.concatenate(activation_parts, axis=0)
    input_gradient = jnp.concatenate(gradient_parts, axis=0)
    return (
        activations,
        input_gradient,
        weight_outputs[0],
        weight_outputs[1],
        weight_outputs[2],
        weight_outputs[3],
        weight_outputs[4],
        weight_outputs[5],
        totals[0],
        totals[1],
        totals[2],
        totals[3],
        totals[4],
        totals[5],
        totals[6],
        totals[7],
        totals[8],
    )


MESH_IDS = pl.DeviceIdType.MESH
LOW = jnp.bfloat16
BLOCK = 64
ROWS = -(-SEQ // 16) * 16
DEEP = -(-SEQ // 128) * 128


def place():
    wide = lax.axis_index("wide")
    return (
        lax.div(wide, 4),
        lax.rem(lax.div(wide, 2), 2),
        lax.rem(wide, 2),
        lax.axis_index("tensor"),
    )


def neighbours():
    z, x, c, y = place()

    def at(z, x, c, y):
        return (z * 4 + x * 2 + c, y)

    return {
        "core": at(z, x, 1 - c, y),
        "x": at(z, 1 - x, c, y),
        "y": at(z, x, c, 1 - y),
        "z1": at(z + 1 - 2 * lax.rem(z, 2), x, c, y),
        "z2": at(lax.rem(z + 2, 4), x, c, y),
    }


LINKS = ("core", "x", "y", "z1", "z2")


def greet(partners):
    barrier = pltpu.get_barrier_semaphore()
    for link in LINKS:
        pl.semaphore_signal(barrier, inc=1, device_id=partners[link], device_id_type=MESH_IDS)
    pl.semaphore_wait(barrier, len(LINKS))


def dot_rows(left, right):
    return lax.dot_general(
        left, right, (((1,), (0,)), ((), ())), preferred_element_type=jnp.float32
    )


def dot_cols(left, right):
    return lax.dot_general(
        left, right, (((1,), (1,)), ((), ())), preferred_element_type=jnp.float32
    )


def dot_tokens(left, right):
    return lax.dot_general(
        left, right, (((0,), (0,)), ((), ())), preferred_element_type=jnp.float32
    )


PAIR = 2 * HEAD_DIM


def turned_softmax(keys_here, queries):
    scores = dot_cols(keys_here, queries)
    exponent = jnp.exp(scores - jnp.max(scores, axis=0, keepdims=True))
    return exponent * (1.0 / jnp.sum(exponent, axis=0, keepdims=True))


def store_rows(ref, at, pieces):
    full = SEQ // 16 * 16
    ref[pl.ds(full, ROWS - full), pl.ds(at, PAIR)] = jnp.zeros((ROWS - full, PAIR), LOW)
    ref[pl.ds(0, SEQ), pl.ds(at, PAIR)] = jnp.concatenate(pieces, axis=1)


def gather_stages(z, x, c, y, whole, start, shares):
    share_a, share_b, last = shares

    def cols(t, at, size):
        return pl.ds(pl.multiple_of(t * whole + start + at, 128), size)

    all_rows = pl.ds(0, BLOCK)
    pair = pl.ds(lax.div(z, 2) * 2, 2)
    every_z, every_x = pl.ds(0, 4), pl.ds(0, 2)
    far_x, far_y = 1 - x, 1 - y

    def part_a(t):
        return cols(t, 0, share_a)

    def part_b(t):
        return cols(t, share_a, share_b)

    def part_ab(t):
        return cols(t, 0, share_a + share_b)

    def part_c(t):
        return cols(t, share_a + share_b, last)

    stages = [
        [("z1", (z, x, c, all_rows, part_ab(y)))],
        [("z2", (pair, x, c, all_rows, part_ab(y)))],
        [
            ("x", (every_z, x, c, all_rows, part_a(y))),
            ("y", (every_z, x, c, all_rows, part_b(y))),
            ("core", (every_z, x, c, all_rows, part_ab(y))),
        ],
        [
            ("y", (every_z, every_x, c, all_rows, part_a(y))),
            ("x", (every_z, x, c, all_rows, part_b(0))),
            ("x", (every_z, x, c, all_rows, part_b(1))),
            ("core", (every_z, far_x, c, all_rows, part_a(y))),
            ("core", (every_z, x, c, all_rows, part_b(far_y))),
        ],
        [
            ("core", (every_z, every_x, c, all_rows, part_a(far_y))),
            ("core", (every_z, far_x, c, all_rows, part_b(0))),
            ("core", (every_z, far_x, c, all_rows, part_b(1))),
        ],
    ]
    if last:
        stages[0].append(("x", (z, x, c, all_rows, part_c(y))))
        stages[1].append(("y", (z, every_x, c, all_rows, part_c(y))))
        for t in range(2):
            stages[2].append(("z1", (z, every_x, c, all_rows, part_c(t))))
            stages[3].append(("z2", (pair, every_x, c, all_rows, part_c(t))))
            stages[4].append(("core", (every_z, every_x, c, all_rows, part_c(t))))
    return stages


GATHER_COPIES = 21
GATHER_DEPTH = 5
GATHER_LAG = 2
CHUNK = 512
CHUNK_SHARES = (
    (256, 256, 0),
    (128, 384, 0),
    (256, 256, 0),
    (128, 128, 256),
    (128, 384, 0),
    (256, 256, 0),
    (128, 384, 0),
    (128, 128, 256),
)


class Gather:
    def __init__(self, chunks):
        self.chunks = chunks

    def scratch(self):
        count = len(self.chunks)
        return dict(
            gather_send=pltpu.SemaphoreType.DMA((count, GATHER_COPIES)),
            gather_recv=pltpu.SemaphoreType.DMA((count, GATHER_COPIES)),
            gather_own=pltpu.SemaphoreType.DMA((count,)),
        )

    def bind(self, shards, wholes, refs):
        self.wholes = wholes
        self.send_sem, self.recv_sem, own_sem = refs
        z, x, c, y = place()
        self.partners = neighbours()
        self.plans, self.own, self.flying = [], [], {}
        for chunk, (matrix, start, shares) in enumerate(self.chunks):
            width = sum(shares)
            whole = wholes[matrix].shape[4] // 2
            self.plans.append(gather_stages(z, x, c, y, whole, start, shares))
            mine = pl.ds(pl.multiple_of(y * whole + start, 128), width)
            size = shards[matrix][0].shape[1]
            shard = shards[matrix][start // size]
            copy = pltpu.make_async_copy(
                shard.at[:, pl.ds(start % size, width)],
                wholes[matrix].at[z, x, c, pl.ds(0, BLOCK), mine],
                own_sem.at[chunk],
            )
            copy.start()
            self.own.append(copy)

    def tick(self, tick):
        done = None
        for stage_idx in range(GATHER_DEPTH, -1, -1):
            chunk = tick - GATHER_LAG * stage_idx
            if chunk < 0 or chunk >= len(self.chunks):
                continue
            if stage_idx == 0:
                self.own[chunk].wait()
            for copy in self.flying.get((chunk, stage_idx - 1), ()):
                copy.wait_recv()
            if stage_idx == GATHER_DEPTH:
                done = chunk
                continue
            started = []
            plan = self.plans[chunk]
            base = sum(len(stage) for stage in plan[:stage_idx])
            whole = self.wholes[self.chunks[chunk][0]]
            for entry, (link, index) in enumerate(plan[stage_idx]):
                copy = pltpu.make_async_remote_copy(
                    src_ref=whole.at[index],
                    dst_ref=whole.at[index],
                    send_sem=self.send_sem.at[chunk, base + entry],
                    recv_sem=self.recv_sem.at[chunk, base + entry],
                    device_id=self.partners[link],
                    device_id_type=MESH_IDS,
                )
                copy.start()
                started.append(copy)
            self.flying[(chunk, stage_idx)] = started
        return done

    def finish(self):
        for started in self.flying.values():
            for copy in started:
                copy.wait_send()


BIAS_ROWS = 9
SAVED = (
    "normed",
    "projected",
    "heads",
    "normed_two",
    "hidden",
    "slope",
    "centred",
    "inverse",
    "centred_two",
    "inverse_two",
)


def row_loop(body):
    @pl.loop(0, ROWS // 32)
    def _(step):
        body(pl.ds(pl.multiple_of(step * 32, 32), 32), 32)

    left = ROWS % 32
    if left:
        body(pl.ds(ROWS - left, left), left)


class Forward:
    def __init__(self, layers, widths):
        self.layers, self.widths = layers, widths
        chunks = []
        for layer in range(layers):
            for kind, width in enumerate(widths):
                for start in range(0, width, CHUNK):
                    shares = CHUNK_SHARES[len(chunks) % len(CHUNK_SHARES)]
                    chunks.append((layer * len(widths) + kind, start, shares))
        self.gather = Gather(chunks)

    def scratch(self):
        project, out, up, down = self.widths
        low, full = (lambda cols: pltpu.VMEM((ROWS, cols), LOW)), pltpu.VMEM((ROWS, 1024), jnp.float32)
        sem = pltpu.SemaphoreType.DMA
        own = dict(
            weights_project=pltpu.VMEM((4, 2, 2, BLOCK, 2 * project), LOW),
            weights_out=pltpu.VMEM((4, 2, 2, BLOCK, 2 * out), LOW),
            weights_up=pltpu.VMEM((4, 2, 2, BLOCK, 2 * up), LOW),
            weights_down=pltpu.VMEM((4, 2, 2, BLOCK, 2 * down), LOW),
            stream=full,
            centred=full,
            inverse=pltpu.VMEM((ROWS, 128), jnp.float32),
            tokens_in=low(512),
            biases=pltpu.VMEM((2, self.layers * BIAS_ROWS, 512), jnp.float32),
            normed=low(1024),
            projected=low(2 * project),
            heads=low(2 * out),
            normed_two=low(1024),
            hidden=low(2 * up),
            slope=low(2 * up),
            weight_sem=sem((len(self.gather.chunks), 2)),
            saved_sem=sem((self.layers, len(SAVED))),
            swap_send=sem((3,)),
            swap_recv=sem((3,)),
        )
        return {**own, **self.gather.scratch()}

    def bind(self, inputs, outputs, refs):
        for name, ref in zip(self.scratch(), refs, strict=True):
            setattr(self, name, ref)
        shards, inputs = inputs[:6], inputs[6:]
        self.near, self.far, self.norm_refs, bias_refs = inputs[0], inputs[1], inputs[2:6], inputs[6:]
        count = self.layers * 4
        self.wholes, outputs = outputs[:count], outputs[count:]
        self.cotangent_in, self.leaving, self.staying, outputs = (*outputs[:3], outputs[3:])
        self.saved_out = [outputs[k * len(SAVED) : (k + 1) * len(SAVED)] for k in range(self.layers)]
        self.saving, self.loading, self.centred_saves = {}, {}, []
        self.y = lax.axis_index("tensor")
        kinds = (shards[:3], shards[3:4], shards[4:5], shards[5:6])
        self.gather.bind(
            [[shard.at[m // 4] for shard in kinds[m % 4]] for m in range(count)],
            self.wholes,
            [getattr(self, name) for name in self.gather.scratch()],
        )
        zeros = jnp.zeros((1, 512), jnp.float32)
        for layer in range(self.layers):
            row = layer * BIAS_ROWS
            for ref in bias_refs:
                line = ref[layer : layer + 1, :].astype(jnp.float32)
                for start in range(0, ref.shape[1], 512):
                    self.biases[self.y, row : row + 1, :] = line[:, start : start + 512]
                    row += 1
                if ref is bias_refs[0]:
                    self.biases[self.y, row : row + 1, :] = zeros
                    row += 1

    def swap(self):
        partner = self.gather.partners["y"]
        pairs = (
            (self.biases.at[self.y], self.biases.at[self.y]),
            (self.far.at[0], self.tokens_in),
            (self.far.at[1], self.cotangent_in),
        )
        self.swaps = []
        for entry, (source, target) in enumerate(pairs):
            copy = pltpu.make_async_remote_copy(
                src_ref=source,
                dst_ref=target,
                send_sem=self.swap_send.at[entry],
                recv_sem=self.swap_recv.at[entry],
                device_id=partner,
                device_id_type=MESH_IDS,
            )
            copy.start()
            self.swaps.append(copy)

    def save(self, layer, name, source):
        entry = SAVED.index(name)
        copy = pltpu.make_async_copy(
            source, self.saved_out[layer][entry], self.saved_sem.at[layer, entry]
        )
        copy.start()
        self.saving[(layer, name)] = copy

    def saved(self, layer, name):
        if (layer, name) in self.saving:
            self.saving.pop((layer, name)).wait()

    def load(self, chunk):
        matrix, start, shares = self.gather.chunks[chunk]
        width = sum(shares)
        whole = self.gather.wholes[matrix]
        buffer = (self.weights_project, self.weights_out, self.weights_up, self.weights_down)[
            matrix % 4
        ]
        for t in range(2):
            at = (slice(None),) * 4 + (pl.ds(t * (whole.shape[4] // 2) + start, width),)
            copy = pltpu.make_async_copy(whole.at[at], buffer.at[at], self.weight_sem.at[chunk, t])
            copy.start()
            self.loading.setdefault(matrix, []).append(copy)

    def wait_weights(self, matrix):
        for copy in self.loading.pop(matrix):
            copy.wait()

    def bias_row(self, row):
        return jnp.concatenate([self.biases[t, pl.ds(row, 1), :] for t in range(2)], axis=1)

    def norm(self, target, gain_ref, shift_ref, layer, bias_at, names):
        gain = gain_ref[layer : layer + 1, :].astype(jnp.float32)
        shift = shift_ref[layer : layer + 1, :].astype(jnp.float32)
        bias = None if bias_at is None else self.bias_row(bias_at)
        for key in self.centred_saves:
            self.saved(*key)

        def body(rows, size):
            values = self.stream[rows, :]
            if bias is not None:
                values = values + bias
                self.stream[rows, :] = values
            mean = jnp.mean(values, axis=1, keepdims=True)
            square = jnp.mean(values * values, axis=1, keepdims=True)
            inverse = lax.rsqrt(square - mean * mean + norm_eps)
            centred = (values - mean) * inverse
            self.centred[rows, :] = centred
            self.inverse[rows, :] = jnp.broadcast_to(inverse, (size, 128))
            target[rows, :] = (centred * gain + shift).astype(LOW)

        row_loop(body)
        self.save(layer, names[0], self.centred)
        self.save(layer, names[1], self.inverse)
        self.centred_saves = [(layer, name) for name in names]

    def begin(self):
        for copy in self.swaps:
            copy.wait_recv()
        y = self.y
        near_at = pl.ds(pl.multiple_of(y * 512, 512), 512)
        far_at = pl.ds(pl.multiple_of((1 - y) * 512, 512), 512)
        self.stream[:, near_at] = self.near[...].astype(jnp.float32)
        self.stream[:, far_at] = self.tokens_in[...].astype(jnp.float32)

    def project(self, layer):
        self.saved(layer - 1, "normed")
        self.norm(
            self.normed,
            *self.norm_refs[:2],
            layer,
            None if layer == 0 else (layer - 1) * BIAS_ROWS + 4,
            ("centred", "inverse"),
        )
        self.save(layer, "normed", self.normed)
        self.saved(layer - 1, "projected")
        self.wait_weights(layer * 4)
        parts = 6

        @pl.loop(0, parts)
        def _(part):
            cols = pl.ds(pl.multiple_of(part * 512, 512), 512)
            weights = self.weights_project[:, :, :, :, cols].reshape(1024, 512)
            row = layer * BIAS_ROWS + lax.rem(part, 3)
            bias = self.biases[lax.div(part, 3), pl.ds(row, 1), :]
            self.projected[:, cols] = (dot_rows(self.normed[...], weights) + bias).astype(LOW)

        self.save(layer, "projected", self.projected)

    def mix(self, layer, first, last):
        if first == 0:
            self.saved(layer - 1, "heads")
        half = self.heads.shape[1] // 2

        @pl.loop(first, last)
        def _(step):
            for t in range(2):
                def at(part):
                    start = (t * 3 + part) * half + step * PAIR
                    return pl.ds(pl.multiple_of(start, PAIR), PAIR)

                queries = self.projected[pl.ds(0, SEQ), at(0)] * jnp.asarray(HEAD_DIM**-0.5, LOW)
                keys_here = self.projected[pl.ds(0, SEQ), at(1)]
                values_here = self.projected[pl.ds(0, SEQ), at(2)]
                pieces = []
                for head in range(2):
                    cols = slice(head * HEAD_DIM, (head + 1) * HEAD_DIM)
                    soft = turned_softmax(keys_here[:, cols], queries[:, cols])
                    pieces.append(dot_tokens(soft.astype(LOW), values_here[:, cols]).astype(LOW))
                store_rows(self.heads, pl.multiple_of(t * half + step * PAIR, PAIR), pieces)

        if last * PAIR == half:
            self.save(layer, "heads", self.heads)

    def attend(self, layer):
        self.wait_weights(layer * 4 + 1)

        @pl.loop(0, 4)
        def _(row):
            cols = pl.ds(pl.multiple_of(row * 256, 256), 256)
            weights = self.weights_out[row].reshape(256, -1)
            self.stream[:, cols] = self.stream[:, cols] + dot_cols(self.heads[...], weights)

        self.saved(layer - 1, "normed_two")
        self.norm(
            self.normed_two,
            *self.norm_refs[2:],
            layer,
            layer * BIAS_ROWS + 3,
            ("centred_two", "inverse_two"),
        )
        self.save(layer, "normed_two", self.normed_two)

    def feed_up(self, layer, first, last):
        if first == 0:
            self.saved(layer - 1, "hidden")
            self.saved(layer - 1, "slope")
            self.wait_weights(layer * 4 + 2)

        @pl.loop(first, last)
        def _(part):
            cols = pl.ds(pl.multiple_of(part * 512, 512), 512)
            weights = self.weights_up[:, :, :, :, cols].reshape(1024, 512)
            row = layer * BIAS_ROWS + 5 + lax.rem(part, 4)
            bias = self.biases[lax.div(part, 4), pl.ds(row, 1), :]
            before = dot_rows(self.normed_two[...], weights) + bias
            normal = 0.5 * (1.0 + lax.erf(before * 0.7071067811865476))
            self.hidden[:, cols] = (before * normal).astype(LOW)
            density = jnp.exp(-0.5 * before * before) * 0.3989422804014327
            self.slope[:, cols] = (normal + before * density).astype(LOW)

        if last * 512 == self.hidden.shape[1]:
            self.save(layer, "hidden", self.hidden)
            self.save(layer, "slope", self.slope)

    def feed_down(self, layer, first, last):
        if first == 0:
            self.wait_weights(layer * 4 + 3)

        @pl.loop(first, last)
        def _(row):
            cols = pl.ds(pl.multiple_of(row * 256, 256), 256)
            weights = self.weights_down[row].reshape(256, -1)
            self.stream[:, cols] = self.stream[:, cols] + dot_cols(self.hidden[...], weights)

    def end(self):
        row = (self.layers - 1) * BIAS_ROWS + 4
        for t, ref in ((self.y, self.staying), (1 - self.y, self.leaving)):
            bias = self.biases[t, pl.ds(row, 1), :]
            cols = pl.ds(pl.multiple_of(t * 512, 512), 512)

            def body(rows, _, ref=ref, bias=bias, cols=cols):
                ref[rows, :] = (self.stream[rows, cols] + bias).astype(LOW)

            row_loop(body)

    def work(self):
        steps = [(0, 1, self.begin)]
        for layer in range(self.layers):
            base = layer * 4
            steps += [
                (base, 6, lambda layer=layer: self.project(layer)),
                (base, 7, lambda layer=layer: self.mix(layer, 0, 2)),
                (base, 7, lambda layer=layer: self.mix(layer, 2, 4)),
                (base + 1, 4, lambda layer=layer: self.attend(layer)),
                (base + 2, 6, lambda layer=layer: self.feed_up(layer, 0, 4)),
                (base + 2, 6, lambda layer=layer: self.feed_up(layer, 4, 8)),
                (base + 3, 4, lambda layer=layer: self.feed_down(layer, 0, 2)),
                (base + 3, 4, lambda layer=layer: self.feed_down(layer, 2, 4)),
            ]
        return steps + [(self.layers * 4 - 1, 1, self.end)]

    def run(self):
        greet(self.gather.partners)
        self.swap()
        steps = self.work()
        ready = set()
        remaining = {}
        for matrix, _, _ in self.gather.chunks:
            remaining[matrix] = remaining.get(matrix, 0) + 1
        ticks = len(self.gather.chunks) + GATHER_LAG * GATHER_DEPTH
        for tick in range(ticks):
            budget = WORK_A_TICK
            done = self.gather.tick(tick)
            while steps and steps[0][0] in ready and budget > 0:
                _, cost, step = steps.pop(0)
                budget -= cost
                step()
            if done is not None:
                self.free_buffer(done, steps)
                matrix = self.gather.chunks[done][0]
                self.load(done)
                remaining[matrix] -= 1
                if remaining[matrix] == 0:
                    ready.add(matrix)
        for _, _, step in steps:
            step()
        self.gather.finish()
        for copy in self.swaps:
            copy.wait_send()
        for copy in self.saving.values():
            copy.wait()

    def free_buffer(self, chunk, steps):
        matrix = self.gather.chunks[chunk][0]
        while steps and any(entry[0] == matrix - 4 for entry in steps):
            steps.pop(0)[2]()


WORK_A_TICK = 5


def forward(shards, near, far, norms, biases):
    layers = shards[0].shape[0]
    widths = [3 * shards[0].shape[2], *[shard.shape[2] for shard in shards[3:]]]
    plan = Forward(layers, widths)
    project, out, up, down = widths
    low = lambda cols: jax.ShapeDtypeStruct((ROWS, cols), LOW)
    full = jax.ShapeDtypeStruct((ROWS, 1024), jnp.float32)
    lanes = jax.ShapeDtypeStruct((ROWS, 128), jnp.float32)
    saved = [
        low(1024), low(2 * project), low(2 * out), low(1024), low(2 * up), low(2 * up),
        full, lanes, full, lanes,
    ]
    wholes = [
        jax.ShapeDtypeStruct((4, 2, 2, BLOCK, 2 * width), LOW) for width in widths
    ] * layers
    outs = [*wholes, low(512), low(512), low(512), *(saved * layers)]
    any_spec, vmem_spec = pl.BlockSpec(memory_space=pl.ANY), pl.BlockSpec(memory_space=pltpu.VMEM)
    out_specs = [any_spec] * len(outs)
    out_specs[len(wholes) + 1 : len(wholes) + 3] = [vmem_spec] * 2

    operands = [*shards, near, far, *norms, *biases]

    def kernel(*refs):
        ins, refs = refs[: len(operands)], refs[len(operands) :]
        plan.bind(ins, refs[: len(outs)], refs[len(outs) :])
        plan.run()

    results = pl.pallas_call(
        kernel,
        out_shape=outs,
        in_specs=[any_spec] * 6 + [vmem_spec, any_spec] + [vmem_spec] * 9,
        out_specs=out_specs,
        scratch_shapes=list(plan.scratch().values()),
        compiler_params=pltpu.CompilerParams(
            collective_id=0, has_side_effects=True, vmem_limit_bytes=60 * 1024 * 1024
        ),
        cost_estimate=pl.CostEstimate(
            flops=60 * 1024**3, bytes_accessed=700 * 1024 * 1024, transcendentals=0
        ),
        name="forward",
    )(*operands)
    whole, results = results[: len(wholes)], results[len(wholes) :]
    weights = [
        [whole[layer * 4 + kind] for kind in range(4)] for layer in range(layers)
    ]
    swapped, results = results[:3], results[3:]
    kept = [
        dict(zip(SAVED, results[k * len(SAVED) : (k + 1) * len(SAVED)])) for k in range(layers)
    ]
    return weights, swapped, kept


COLS = 128
STAGE_AT = (0, 1, 3, 5, 6, 7, 8)
SETTLE_DEPTH = len(STAGE_AT) - 1
SLOTS = dict(core_in=2, val=5, first_a=4, first_b=4, second=4, third=2, fourth=2, fifth=2, rest=4)
TURNED_SLOTS = 3


class Settle:
    def __init__(self, widths, pairs):
        self.widths, self.pairs = widths, pairs

    def scratch(self):
        shapes = dict(
            core_in=(2, 2, 4, 2, 2, BLOCK, COLS),
            val=(2, 2, 4, 2, 2, BLOCK, COLS),
            first_a=(4, 2, 2, BLOCK, COLS),
            first_b=(2, 4, 2, BLOCK, COLS),
            second=(2, 4, 2, BLOCK, COLS),
            third=(2, 2, 2, BLOCK, COLS),
            fourth=(2, 2, BLOCK, COLS),
            fifth=(2, BLOCK, COLS),
            rest=(2, 4, 2, BLOCK, COLS),
        )
        pairs, sem = len(self.pairs), pltpu.SemaphoreType.DMA
        return dict(
            left_in=pltpu.VMEM((ROWS, 1024), LOW),
            left_turned=pltpu.VMEM((TURNED_SLOTS, 1024, DEEP), LOW),
            right_in=pltpu.VMEM((2, 2, 2, DEEP, 2 * COLS), LOW),
            core_out=pltpu.VMEM((2, 2, 4, 2, 2, BLOCK, COLS), LOW),
            **{name: pltpu.VMEM((SLOTS[name], *shape), LOW) for name, shape in shapes.items()},
            result=pltpu.VMEM((2, 2, 2, BLOCK, COLS), jnp.float32),
            result_sem=sem((2, 2, 2)),
            send_sem=sem((pairs, 2, SETTLE_DEPTH)),
            recv_sem=sem((pairs, 2, SETTLE_DEPTH)),
            right_sem=sem((pairs, 2, 4)),
            left_sem=sem((1,)),
        )

    def bind(self, lefts, rights, outs, refs):
        self.lefts, self.rights, self.outs = lefts, rights, outs
        for name, ref in zip(self.scratch(), refs, strict=True):
            setattr(self, name, ref)
        self.z, self.x, self.c, self.y = place()
        self.partners = neighbours()
        self.copies, self.turned, self.results = {}, {}, {}
        tail = ROWS // 128 * 128
        self.left_turned[:, :, pl.ds(tail, DEEP - tail)] = jnp.zeros(
            (TURNED_SLOTS, 1024, DEEP - tail), LOW
        )
        self.right_in[:, :, :, pl.ds(ROWS, DEEP - ROWS)] = jnp.zeros(
            (2, 2, 2, DEEP - ROWS, 2 * COLS), LOW
        )

    def load(self, pair):
        for unit, (matrix, step) in enumerate(self.pairs[pair]):
            width = self.widths[matrix]
            for t in range(2):
                for near in range(2):
                    core = self.c if near else 1 - self.c
                    at = pl.multiple_of(t * width + core * (width // 2) + step * COLS, COLS)
                    copy = pltpu.make_async_copy(
                        self.rights[matrix].at[:, pl.ds(at, COLS)],
                        self.right_in.at[
                            pair % 2, unit, t, pl.ds(0, ROWS), pl.ds(near * COLS, COLS)
                        ],
                        self.right_sem.at[pair, unit, 2 * t + near],
                    )
                    copy.start()
                    self.copies[(pair, unit, "right", 2 * t + near)] = copy

    def turn(self, matrix):
        if matrix in self.turned:
            return
        source, here = self.lefts[matrix]
        if not here:
            copy = pltpu.make_async_copy(source, self.left_in, self.left_sem.at[0])
            copy.start()
            copy.wait()
            source = self.left_in
        slot = len(self.turned) % TURNED_SLOTS
        for quarter in range(4):
            cols = pl.ds(quarter * 256, 256)
            self.left_turned[slot, cols, pl.ds(0, ROWS)] = source[:, cols].T
        self.turned[matrix] = slot

    def wait_load(self, pair):
        for unit, (matrix, _) in enumerate(self.pairs[pair]):
            self.turn(matrix)
            for entry in range(4):
                self.copies.pop((pair, unit, "right", entry)).wait()

    def send(self, pair, unit, stage, source, target, link):
        copy = pltpu.make_async_remote_copy(
            src_ref=source,
            dst_ref=target,
            send_sem=self.send_sem.at[pair, unit, stage],
            recv_sem=self.recv_sem.at[pair, unit, stage],
            device_id=self.partners[link],
            device_id_type=MESH_IDS,
        )
        copy.start()
        self.copies[(pair, unit, stage)] = copy

    def product(self, pair, unit, t):
        matrix, _ = self.pairs[pair][unit]
        left = self.left_turned[self.turned[matrix]]
        right = self.right_in[pair % 2, unit, t]
        total = dot_rows(left[:, :512], right[:512]) + dot_rows(left[:, 512:], right[512:])
        return total.astype(LOW)

    def stage(self, pair, unit, stage):
        if pair < 0 or pair >= len(self.pairs):
            return
        z, x, c, y = self.z, self.x, self.c, self.y
        high, lower = lax.div(z, 2), lax.rem(z, 2)
        far_pair = pl.ds(2 * (1 - high), 2)
        far_z = z + 1 - 2 * lower

        def buffer(name):
            return getattr(self, name).at[pair % SLOTS[name], unit]

        val, rest = buffer("val"), buffer("rest")
        first_a = self.first_a.at[pair % SLOTS["first_a"]]
        first_b = self.first_b.at[pair % SLOTS["first_b"]]
        shape = (4, 2, 2, BLOCK, COLS)
        if stage == 0:
            out = self.core_out.at[unit]

            @pl.loop(0, 2)
            def _(t):
                total = self.product(pair, unit, t)
                out[t] = total[:, :COLS].reshape(shape)
                val[t] = total[:, COLS:].reshape(shape)

            self.send(pair, unit, 0, out, buffer("core_in"), "core")
            return
        self.copies.pop((pair, unit, stage - 1)).wait()
        if stage == 1:
            other = buffer("core_in")

            @pl.loop(0, 4)
            def _(row):
                for t in range(2):
                    val[t, row] = val[t, row] + other[t, row]

            if unit == 0:
                self.send(pair, unit, 1, val.at[1 - y], first_a, "y")
            else:
                self.send(pair, unit, 1, val.at[:, :, 1 - x], first_b, "x")
        elif stage == 2:
            target = buffer("second")
            if unit == 0:

                @pl.loop(0, 4)
                def _(row):
                    val[y, row] = val[y, row] + first_a[row]

                self.send(pair, unit, 2, val.at[y, :, 1 - x], target, "x")
            else:

                @pl.loop(0, 4)
                def _(row):
                    for t in range(2):
                        val[t, row, x] = val[t, row, x] + first_b[t, row]

                self.send(pair, unit, 2, val.at[1 - y, :, x], target, "y")
        elif stage == 3:

            second = buffer("second")

            @pl.loop(0, 4)
            def _(row):
                rest[row] = val[y, row, x] + second[row]

            self.send(pair, unit, 3, rest.at[far_pair], buffer("third"), "z2")
        elif stage == 4:
            third = buffer("third")
            for row in range(2):
                at = 2 * high + row
                rest[at] = rest[at] + third[row]
            self.send(pair, unit, 4, rest.at[far_z], buffer("fourth"), "z1")
        elif stage == 5:
            rest[z] = rest[z] + buffer("fourth")[...]
            self.send(pair, unit, 5, rest.at[z, 1 - c], buffer("fifth"), "core")
        else:
            matrix, step = self.pairs[pair][unit]
            out_ref, layer = self.outs[matrix]
            slot = pair % 2
            for copy in self.results.pop((slot, unit), ()):
                copy.wait()
            result = self.result.at[slot, unit]
            result[c] = rest[z, c].astype(jnp.float32)
            result[1 - c] = buffer("fifth")[...].astype(jnp.float32)
            self.results[(slot, unit)] = []
            for core in range(2):
                copy = pltpu.make_async_copy(
                    result.at[core],
                    out_ref.at[layer, core, :, pl.ds(step * COLS, COLS)],
                    self.result_sem.at[slot, unit, core],
                )
                copy.start()
                self.results[(slot, unit)].append(copy)

    def finish(self):
        for copies in self.results.values():
            for copy in copies:
                copy.wait()

    def tick(self, pair):
        for stage in range(SETTLE_DEPTH, 0, -1):
            for unit in range(2):
                self.stage(pair - STAGE_AT[stage], unit, stage)
        if pair < len(self.pairs):
            self.wait_load(pair)
            for unit in range(2):
                self.stage(pair, unit, 0)


TOTAL_LINKS = ("x", "y", "z1", "z2", "core")
SUM_ROWS = 12
TILE = 512
KEPT = SAVED


class Backward:
    def __init__(self, layers, widths):
        self.layers, self.widths = layers, widths
        pairs, self.needs = [], []
        for layer in reversed(range(layers)):
            base = layer * 4
            feed = widths[2] // 2 // COLS
            for kind, fact in ((3, "arrived"), (2, "fed")):
                for k in range(0, feed, 2):
                    pairs.append(((base + kind, k), (base + kind, k + 1)))
                    self.needs.append((layer, fact))
            rest = [(base + 1, k) for k in range(widths[1] // 2 // COLS)]
            rest += [(base, k) for k in range(widths[0] // 2 // COLS)]
            for k in range(0, len(rest), 2):
                pairs.append((rest[k], rest[k + 1]))
                self.needs.append((layer, "mixed"))
        self.settle = Settle(widths * layers, pairs)

    def scratch(self):
        sem = pltpu.SemaphoreType.DMA
        full = pltpu.VMEM((ROWS, 1024), jnp.float32)
        low = pltpu.VMEM((ROWS, 1024), LOW)
        steps = len(TOTAL_LINKS)
        rows = self.layers * SUM_ROWS
        own = dict(
            grad=full,
            delta=full,
            centred=full,
            inverse=pltpu.VMEM((ROWS, 128), jnp.float32),
            feed_grad=low,
            mix_grad=low,
            heads_grad=low,
            projected=pltpu.VMEM((ROWS, 2 * self.widths[0]), LOW),
            joined=pltpu.VMEM((ROWS, 2 * self.widths[0]), LOW),
            tile_a=pltpu.VMEM((2, 4, 2, 2, BLOCK, TILE), LOW),
            tile_b=pltpu.VMEM((2, 4, 2, 2, BLOCK, TILE), LOW),
            slope_in=pltpu.VMEM((2, ROWS, TILE), LOW),
            hidden_out=pltpu.VMEM((2, ROWS, TILE), LOW),
            column_sums=pltpu.VMEM((8, 1, TILE), jnp.float32),
            sums_part=pltpu.VMEM((3, 16, 1024), jnp.float32),
            sums=pltpu.VMEM((steps + 1, rows, 1024), jnp.float32),
            sums_in=pltpu.VMEM((steps, rows, 1024), jnp.float32),
            leave=pltpu.VMEM((ROWS, 512), LOW),
            tile_sem=sem((2, 3)),
            hidden_sem=sem((2,)),
            value_sem=sem((4,)),
            sums_send=sem((steps,)),
            sums_recv=sem((steps,)),
            swap_send=sem((2,)),
            swap_recv=sem((2,)),
        )
        return {**own, **self.settle.scratch()}

    def bind(self, inputs, outputs, refs):
        for name, ref in zip(self.scratch(), refs, strict=True):
            setattr(self, name, ref)
        layers = self.layers
        count = layers * 4
        self.weights, inputs = inputs[:count], inputs[count:]
        self.kept = [
            dict(zip(KEPT, inputs[k * len(KEPT) : (k + 1) * len(KEPT)])) for k in range(layers)
        ]
        *self.upstream, self.leaving, first_gain, second_gain = inputs[layers * len(KEPT) :]
        self.gains = (first_gain, second_gain)
        outs, outputs = outputs[:4], outputs[4:]
        self.total_out, self.near_out, self.arriving, outputs = (*outputs[:3], outputs[3:])
        self.hidden_grads = outputs
        self.facts, self.hidden_copies = set(), []
        lefts, rights = [], []
        for layer in range(layers):
            kept = self.kept[layer]
            lefts += [
                (kept["normed"], False),
                (self.mix_grad, True),
                (kept["normed_two"], False),
                (self.feed_grad, True),
            ]
            rights += [self.joined, kept["heads"], self.hidden_grads[layer], kept["hidden"]]
        self.settle.bind(
            lefts,
            rights,
            [(outs[m % 4], m // 4) for m in range(count)],
            [getattr(self, name) for name in self.settle.scratch()],
        )
        self.loaded_pair = -1

    def fetch(self, entry, source, target):
        copy = pltpu.make_async_copy(source, target, self.value_sem.at[entry])
        copy.start()
        return copy

    def fetch_centred(self, layer, centred, inverse):
        self.centred_copies = [
            self.fetch(1, self.kept[layer][centred], self.centred),
            self.fetch(3, self.kept[layer][inverse], self.inverse),
        ]

    def swap(self, entry, source):
        copy = pltpu.make_async_remote_copy(
            src_ref=source,
            dst_ref=self.arriving.at[entry],
            send_sem=self.swap_send.at[entry],
            recv_sem=self.swap_recv.at[entry],
            device_id=self.settle.partners["y"],
            device_id_type=MESH_IDS,
        )
        copy.start()
        return copy

    def add_sum(self, entry, values):
        for start in range(0, values.shape[0], 16):
            self.sums_part[entry] += values[start : start + 16]

    def put_sum(self, layer, row, values):
        self.sums[0, pl.ds(layer * SUM_ROWS + row, 1), :] = values

    def begin(self):
        copies = []
        for entry, t in enumerate((self.y, 1 - self.y)):
            cols = pl.ds(pl.multiple_of(t * 512, 512), 512)
            copies.append(self.fetch(entry, self.upstream[entry], self.feed_grad.at[:, cols]))
        for copy in copies:
            copy.wait()
        self.facts.add((self.layers - 1, "arrived"))

    def widen(self):
        self.sums_part[...] = jnp.zeros_like(self.sums_part)

        def body(rows, _):
            values = self.feed_grad[rows, :].astype(jnp.float32)
            self.grad[rows, :] = values
            self.add_sum(2, values)

        row_loop(body)
        self.put_sum(self.layers - 1, 7, jnp.sum(self.sums_part[2], axis=0, keepdims=True))

    def tile_copies(self, part, sources, targets):
        cols = pl.ds(part * TILE, TILE)
        slot = part % 2
        copies = []
        for entry, (source, target) in enumerate(zip(sources, targets)):
            at = (slice(None),) * (len(source.shape) - 1) + (cols,)
            copy = pltpu.make_async_copy(
                source.at[at], target.at[slot], self.tile_sem.at[slot, entry]
            )
            copy.start()
            copies.append(copy)
        return copies

    def tile(self, part, parts, sources, targets):
        if part == 0:
            self.coming = self.tile_copies(0, sources, targets)
        for copy in self.coming:
            copy.wait()
        if part + 1 < parts:
            self.coming = self.tile_copies(part + 1, sources, targets)

    def add_delta(self, is_first, grads, weights):
        for half in range(2):
            cols = slice(half * 512, (half + 1) * 512)
            product = dot_cols(grads, weights[2 * half : 2 * half + 2].reshape(512, TILE))
            self.delta[:, cols] = product if is_first else self.delta[:, cols] + product

    def feed(self, layer, part):
        out_ref = self.hidden_grads[layer]
        parts, slot = out_ref.shape[1] // TILE, part % 2
        if part == 0:
            self.fetch_centred(layer, "centred_two", "inverse_two")
        sources = (self.weights[layer * 4 + 3], self.weights[layer * 4 + 2], self.kept[layer]["slope"])
        self.tile(part, parts, sources, (self.tile_a, self.tile_b, self.slope_in))
        if part >= 2:
            self.hidden_copies.pop(0).wait()
        down = self.tile_a[slot].reshape(1024, TILE)
        slope = self.slope_in[slot].astype(jnp.float32)
        grads = (dot_rows(self.feed_grad[...], down) * slope).astype(LOW)
        self.hidden_out[slot] = grads
        copy = pltpu.make_async_copy(
            self.hidden_out.at[slot],
            out_ref.at[:, pl.ds(part * TILE, TILE)],
            self.hidden_sem.at[slot],
        )
        copy.start()
        self.hidden_copies.append(copy)
        self.column_sums[part] = jnp.sum(grads.astype(jnp.float32), axis=0, keepdims=True)
        self.add_delta(part == 0, grads, self.tile_b.at[slot])
        if part == parts - 1:
            while self.hidden_copies:
                self.hidden_copies.pop(0).wait()
            for row in range(4):
                pieces = [self.column_sums[2 * row], self.column_sums[2 * row + 1]]
                self.put_sum(layer, 3 + row, jnp.concatenate(pieces, axis=1))
            self.facts.add((layer, "fed"))

    def norm_back(self, layer, gain_ref, sum_row, low_ref, total_at):
        for copy in self.centred_copies:
            copy.wait()
        gain = gain_ref[layer : layer + 1, :].astype(jnp.float32)
        self.sums_part[...] = jnp.zeros_like(self.sums_part)

        def body(rows, _):
            centred, delta = self.centred[rows, :], self.delta[rows, :]
            weighted = delta * centred
            self.add_sum(0, weighted)
            self.add_sum(1, delta)
            scaled = delta * gain
            grad = self.grad[rows, :] + self.inverse[rows, 0:1] * (
                scaled
                - jnp.mean(scaled, axis=1, keepdims=True)
                - centred * jnp.mean(weighted * gain, axis=1, keepdims=True)
            )
            self.grad[rows, :] = grad
            self.add_sum(2, grad)
            if low_ref is not None:
                low_ref[rows, :] = grad.astype(LOW)

        row_loop(body)
        for entry in range(2):
            total = jnp.sum(self.sums_part[entry], axis=0, keepdims=True)
            self.put_sum(layer, sum_row + entry, total)
        if total_at is not None:
            total = jnp.sum(self.sums_part[2], axis=0, keepdims=True)
            self.put_sum(*total_at, total)

    def out_back(self, layer):
        self.norm_back(layer, self.gains[1], 10, self.mix_grad, (layer, 2))
        self.fetch_centred(layer, "centred", "inverse")
        self.projected_copy = self.fetch(2, self.kept[layer]["projected"], self.projected)

        for part in range(2):
            self.tile(part, 2, (self.weights[layer * 4 + 1],), (self.tile_a,))
            cols = pl.ds(part * TILE, TILE)
            weights = self.tile_a[part].reshape(1024, TILE)
            self.heads_grad[:, cols] = dot_rows(self.mix_grad[...], weights).astype(LOW)

    def mix_back(self, layer, first, last):
        if first == 0:
            self.projected_copy.wait()
        half = self.heads_grad.shape[1] // 2

        @pl.loop(2 * first, 2 * last)
        def _(turn):
            step, t = lax.div(turn, 2), lax.rem(turn, 2)

            def at(part):
                start = (t * 3 + part) * half + step * PAIR
                return pl.ds(pl.multiple_of(start, PAIR), PAIR)

            here = pl.ds(pl.multiple_of(t * half + step * PAIR, PAIR), PAIR)
            rows = pl.ds(0, SEQ)
            all_queries = self.projected[rows, at(0)] * jnp.asarray(HEAD_DIM**-0.5, LOW)
            all_keys, all_values = self.projected[rows, at(1)], self.projected[rows, at(2)]
            all_grads = self.heads_grad[rows, here]
            pieces = ([], [], [])
            for head in range(2):
                cols = slice(head * HEAD_DIM, (head + 1) * HEAD_DIM)
                keys_here, queries = all_keys[:, cols], all_queries[:, cols]
                grads = all_grads[:, cols]
                soft = turned_softmax(keys_here, queries)
                soft_grad = dot_cols(all_values[:, cols], grads)
                delta = jnp.sum(soft_grad * soft, axis=0, keepdims=True)
                score_grad = (soft * (soft_grad - delta)).astype(LOW)
                pieces[0].append(
                    (dot_tokens(score_grad, keys_here) * HEAD_DIM**-0.5).astype(LOW)
                )
                pieces[1].append(dot_rows(score_grad, queries).astype(LOW))
                pieces[2].append(dot_rows(soft.astype(LOW), grads).astype(LOW))
            for part in range(3):
                start = (t * 3 + part) * half + step * PAIR
                store_rows(self.joined, pl.multiple_of(start, PAIR), pieces[part])

        if last * PAIR == half:
            self.facts.add((layer, "mixed"))

    def project_back(self, layer, part):
        self.tile(part, 6, (self.weights[layer * 4],), (self.tile_a,))
        grads = self.joined[:, pl.ds(part * TILE, TILE)]
        self.column_sums[part] = jnp.sum(grads.astype(jnp.float32), axis=0, keepdims=True)
        self.add_delta(part == 0, grads, self.tile_a.at[part % 2])
        if part == 5:
            for row, at in ((0, 0), (1, 2)):
                pieces = [self.column_sums[at], self.column_sums[3 + at]]
                self.put_sum(layer, row, jnp.concatenate(pieces, axis=1))

    def first_back(self, layer):
        last = layer == 0
        low_ref = None if last else self.feed_grad
        self.norm_back(layer, self.gains[0], 8, low_ref, None if last else (layer - 1, 7))
        if not last:
            self.facts.add((layer - 1, "arrived"))

    def end(self):
        y = self.y
        near_at = pl.ds(pl.multiple_of(y * 512, 512), 512)
        far_at = pl.ds(pl.multiple_of((1 - y) * 512, 512), 512)
        self.leave[...] = self.grad[:, far_at].astype(LOW)
        self.swaps.append(self.swap(1, self.leave))
        copy = self.fetch(0, self.grad.at[:, near_at], self.near_out)
        copy.wait()
        self.facts.add("summed")

    def chain(self):
        steps = [(1, self.begin, ()), (2, self.widen, ())]
        for layer in reversed(range(self.layers)):
            for part in range(2 * self.widths[2] // TILE):
                steps.append((2.5, lambda layer=layer, part=part: self.feed(layer, part), ()))
            steps.append((4, lambda layer=layer: self.out_back(layer), ((layer + 1, 1),)))
            for k in range(4):
                needs = ((layer + 1, 0),)
                steps.append((7, lambda layer=layer, k=k: self.mix_back(layer, k, k + 1), needs))
            for part in range(6):
                steps.append(
                    (1.5, lambda layer=layer, part=part: self.project_back(layer, part), ())
                )
            steps.append((3, lambda layer=layer: self.first_back(layer), ((layer, 3),)))
        return steps + [(1, self.end, ())]

    def add_sums(self, step):
        if step > 0:
            self.sums_copy.wait()
            self.sums[step] = self.sums[step - 1] + self.sums_in[step - 1]
        if step < len(TOTAL_LINKS):
            copy = pltpu.make_async_remote_copy(
                src_ref=self.sums.at[step],
                dst_ref=self.sums_in.at[step],
                send_sem=self.sums_send.at[step],
                recv_sem=self.sums_recv.at[step],
                device_id=self.settle.partners[TOTAL_LINKS[step]],
                device_id_type=MESH_IDS,
            )
            copy.start()
            self.sums_copy = copy

    def run(self):
        self.y = lax.axis_index("tensor")
        settle = self.settle
        greet(settle.partners)
        self.swaps = [self.swap(0, self.leaving)]
        chain = self.chain()
        last_pair = {}
        for pair, units in enumerate(settle.pairs):
            for matrix, _ in units:
                last_pair[matrix] = pair
        pairs, loaded, sum_step = len(settle.pairs), set(), 0
        passed = -1

        def free(needs):
            for layer, kind in needs:
                if layer < self.layers and passed < last_pair[layer * 4 + kind]:
                    return False
            return True

        def advance():
            _, step, _ = chain.pop(0)
            step()

        pair = 0
        while pair < pairs + STAGE_AT[-1] or sum_step <= len(TOTAL_LINKS):
            if pair < pairs:
                while self.needs[pair] not in self.facts:
                    advance()
                if pair not in loaded:
                    settle.load(pair)
                    loaded.add(pair)
            settle.tick(pair)
            passed = pair
            if "summed" in self.facts and sum_step <= len(TOTAL_LINKS):
                self.add_sums(sum_step)
                sum_step += 1
            if pair + 1 < pairs and self.needs[pair + 1] in self.facts:
                settle.load(pair + 1)
                loaded.add(pair + 1)
            budget = CHAIN_A_TICK
            while chain and budget > 0 and free(chain[0][2]):
                budget -= chain[0][0]
                advance()
            pair += 1
        self.total_out[...] = self.sums[len(TOTAL_LINKS)]
        settle.finish()
        for copy in self.swaps:
            copy.wait()


CHAIN_A_TICK = 5


def backward(weights, kept, upstream, gains, leaving):
    layers = len(weights)
    widths = [block.shape[-1] // 2 for block in weights[0]]
    plan = Backward(layers, widths)
    any_spec, vmem_spec = pl.BlockSpec(memory_space=pl.ANY), pl.BlockSpec(memory_space=pltpu.VMEM)
    operands = [block for layer in weights for block in layer]
    operands += [values[name] for values in kept for name in KEPT]
    operands += [*upstream, leaving]
    in_specs = [any_spec] * len(operands) + [vmem_spec] * len(gains)
    operands += gains
    outs = [jax.ShapeDtypeStruct((layers, 2, BLOCK, width // 2), jnp.float32) for width in widths]
    outs += [
        jax.ShapeDtypeStruct((layers * SUM_ROWS, 1024), jnp.float32),
        jax.ShapeDtypeStruct((ROWS, 512), jnp.float32),
        jax.ShapeDtypeStruct((2, ROWS, 512), LOW),
    ]
    outs += [jax.ShapeDtypeStruct((ROWS, 2 * widths[2]), LOW)] * layers
    out_specs = [any_spec] * len(outs)
    out_specs[4] = vmem_spec

    def kernel(*refs):
        ins, refs = refs[: len(operands)], refs[len(operands) :]
        plan.bind(ins, refs[: len(outs)], refs[len(outs) :])
        plan.run()

    results = pl.pallas_call(
        kernel,
        out_shape=outs,
        in_specs=in_specs,
        out_specs=out_specs,
        scratch_shapes=list(plan.scratch().values()),
        compiler_params=pltpu.CompilerParams(
            collective_id=1, has_side_effects=True, vmem_limit_bytes=60 * 1024 * 1024
        ),
        cost_estimate=pl.CostEstimate(
            flops=120 * 1024**3, bytes_accessed=700 * 1024 * 1024, transcendentals=0
        ),
        name="backward",
    )(*operands)
    return results[:4], results[4], results[5], results[6]


def in_order(own, other, index, axis):
    first = jnp.where(index == 0, own, other)
    second = jnp.where(index == 0, other, own)
    return jnp.concatenate((first, second), axis=axis)


def image_body(
    images,
    first_gain,
    first_shift,
    query_weight,
    key_weight,
    value_weight,
    query_bias,
    value_bias,
    out_weight,
    out_bias,
    second_gain,
    second_shift,
    up_weight,
    up_bias,
    down_weight,
    down_bias,
    cotangent,
):
    layers = query_weight.shape[0]
    half = images.shape[1]
    hidden_width = 2 * up_weight.shape[2]
    y = lax.axis_index("tensor")
    far = 1 - y

    def own_rows(block, image):
        rows = lax.dynamic_slice_in_dim(block, image * SEQ, SEQ)
        return jnp.pad(rows, ((0, ROWS - SEQ), (0, 0)))

    weights, (cotangent_in, leaving, staying), kept = forward(
        (
            query_weight,
            key_weight,
            value_weight,
            jnp.swapaxes(out_weight, 1, 2),
            up_weight,
            jnp.swapaxes(down_weight, 1, 2),
        ),
        own_rows(images, y),
        jnp.stack((own_rows(images, far), own_rows(cotangent, far))),
        (first_gain, first_shift, second_gain, second_shift),
        (query_bias, value_bias, out_bias, down_bias, up_bias),
    )

    (project_out, out_out, up_out, down_out), totals, near_gradient, arriving = backward(
        weights,
        kept,
        (own_rows(cotangent, y), cotangent_in),
        (first_gain, second_gain),
        leaving,
    )
    totals = totals.reshape(layers, -1)
    project_out, out_out, up_out, down_out = [
        jnp.swapaxes(block, 1, 2).reshape(layers, BLOCK, -1)
        for block in (project_out, out_out, up_out, down_out)
    ]
    width = 2 * half
    small_outs, at = [], 0
    for size in (width, width, width, hidden_width, width, width, width, width, width):
        small_outs.append(totals[:, at : at + size])
        at += size
    return (
        in_order(staying[:SEQ], arriving[0, :SEQ], y, 0),
        in_order(near_gradient[:SEQ], arriving[1, :SEQ].astype(jnp.float32), y, 0),
        project_out[:, :, :half],
        project_out[:, :, half : 2 * half],
        project_out[:, :, 2 * half :],
        jnp.swapaxes(out_out, 1, 2),
        up_out,
        jnp.swapaxes(down_out, 1, 2),
        *small_outs,
    )


def solution(mesh):
    in_specs = (
        P("wide", "tensor"),
        P(),
        P(),
        P(None, "wide", "tensor"),
        P(None, "wide", "tensor"),
        P(None, "wide", "tensor"),
        P(None, "tensor"),
        P(None, "tensor"),
        P(None, "tensor", "wide"),
        P(None, "tensor"),
        P(),
        P(),
        P(None, "wide", "tensor"),
        P(None, "tensor"),
        P(None, "tensor", "wide"),
        P(None, "tensor"),
        P("wide", "tensor"),
    )
    out_specs = (
        P("wide", "tensor"),
        P("wide", "tensor"),
        P(None, "wide", "tensor"),
        P(None, "wide", "tensor"),
        P(None, "wide", "tensor"),
        P(None, "tensor", "wide"),
        P(None, "wide", "tensor"),
        P(None, "tensor", "wide"),
        P(),
        P(),
        P(),
        P(),
        P(),
        P(),
        P(),
        P(),
        P(),
    )
    chosen = body
    if mesh.shape["wide"] == 16 and mesh.shape["tensor"] == 2:
        chosen = image_body
    return jax.shard_map(
        chosen, mesh=mesh, in_specs=in_specs, out_specs=out_specs, check_vma=False
    )
```

```python
import jax
import jax.numpy as jnp
from jax import lax
from jax.experimental import pallas as pl
from jax.experimental.pallas import tpu as pltpu
from jax.sharding import PartitionSpec as P

HEAD_DIM = 64
SEQ = 577
MICRO = 2


norm_eps = 1e-06


def row_totals(first_terms, second_terms):
    return lax.psum((first_terms, second_terms), "tensor")


def full_rows(share_low):
    return lax.all_gather(share_low, "tensor", axis=1, tiled=True)


def feature_total(partial_sums):
    return lax.psum_scatter(
        partial_sums.astype(jnp.bfloat16), "tensor", scatter_dimension=1, tiled=True
    ).astype(jnp.float32)


def fetch_weights(query_block, key_block, value_block, out_block, up_block, down_block):
    return (
        lax.all_gather(query_block, "wide", axis=0, tiled=True),
        lax.all_gather(key_block, "wide", axis=0, tiled=True),
        lax.all_gather(value_block, "wide", axis=0, tiled=True),
        lax.all_gather(out_block, "wide", axis=1, tiled=True),
        lax.all_gather(up_block, "wide", axis=0, tiled=True),
        lax.all_gather(down_block, "wide", axis=1, tiled=True),
    )


def settle_grads(query_piece, key_piece, value_piece, out_piece, up_piece, down_piece):
    return (
        lax.psum_scatter(
            query_piece.astype(jnp.bfloat16), "wide", scatter_dimension=0, tiled=True
        ).astype(jnp.float32),
        lax.psum_scatter(
            key_piece.astype(jnp.bfloat16), "wide", scatter_dimension=0, tiled=True
        ).astype(jnp.float32),
        lax.psum_scatter(
            value_piece.astype(jnp.bfloat16), "wide", scatter_dimension=0, tiled=True
        ).astype(jnp.float32),
        lax.psum_scatter(
            out_piece.astype(jnp.bfloat16), "wide", scatter_dimension=1, tiled=True
        ).astype(jnp.float32),
        lax.psum_scatter(
            up_piece.astype(jnp.bfloat16), "wide", scatter_dimension=0, tiled=True
        ).astype(jnp.float32),
        lax.psum_scatter(
            down_piece.astype(jnp.bfloat16), "wide", scatter_dimension=1, tiled=True
        ).astype(jnp.float32),
    )


def add_terms(earlier, latest):
    if earlier is None:
        return latest
    return jax.tree.map(jnp.add, earlier, latest)


def norm_forward(stream, gain, shift, full_width):
    first_terms, second_terms = row_totals(
        jnp.sum(stream, axis=1), jnp.sum(stream * stream, axis=1)
    )
    row_mean = first_terms / full_width
    inverse_std = lax.rsqrt(second_terms / full_width - row_mean * row_mean + norm_eps)
    centred = (stream - row_mean[:, None]) * inverse_std[:, None]
    return (centred * gain + shift, centred, inverse_std)


def norm_backward(upstream, centred, inverse_std, gain, full_width):
    scaled = upstream * gain
    first_terms, second_terms = row_totals(
        jnp.sum(scaled, axis=1), jnp.sum(scaled * centred, axis=1)
    )
    return inverse_std[:, None] * (
        scaled - first_terms[:, None] / full_width - centred * (second_terms[:, None] / full_width)
    )


def attention_forward(queries, keys_here, values_here, image_count, heads_here):
    score_scale = HEAD_DIM ** (-0.5)
    shape_four = (image_count, SEQ, heads_here, HEAD_DIM)
    query_four = queries.reshape(shape_four)
    key_four = keys_here.reshape(shape_four)
    value_four = values_here.reshape(shape_four)
    scores = (
        jnp.einsum("iqhd,ikhd->ihqk", query_four, key_four, preferred_element_type=jnp.float32)
        * score_scale
    )
    row_peak = jnp.max(scores, axis=-1, keepdims=True)
    exponent = jnp.exp(scores - row_peak)
    row_total = jnp.sum(exponent, axis=-1, keepdims=True)
    weights_soft = (exponent / row_total).astype(jnp.bfloat16)
    mixed_heads = jnp.einsum(
        "ihqk,ikhd->iqhd", weights_soft, value_four, preferred_element_type=jnp.float32
    )
    log_total = row_peak[..., 0] + jnp.log(row_total[..., 0])
    return (mixed_heads.reshape(queries.shape).astype(jnp.bfloat16), log_total)


def attention_backward(
    queries, keys_here, values_here, log_total, mixed_grad, image_count, heads_here
):
    score_scale = HEAD_DIM ** (-0.5)
    shape_four = (image_count, SEQ, heads_here, HEAD_DIM)
    query_four = queries.reshape(shape_four)
    key_four = keys_here.reshape(shape_four)
    value_four = values_here.reshape(shape_four)
    grad_four = mixed_grad.reshape(shape_four)
    scores = (
        jnp.einsum("iqhd,ikhd->ihqk", query_four, key_four, preferred_element_type=jnp.float32)
        * score_scale
    )
    weights_soft = jnp.exp(scores - log_total[..., None])
    weight_grad = jnp.einsum(
        "iqhd,ikhd->ihqk", grad_four, value_four, preferred_element_type=jnp.float32
    )
    row_delta = jnp.sum(weight_grad * weights_soft, axis=-1, keepdims=True)
    score_grad = (weights_soft * (weight_grad - row_delta)).astype(jnp.bfloat16)
    query_grad = (
        jnp.einsum("ihqk,ikhd->iqhd", score_grad, key_four, preferred_element_type=jnp.float32)
        * score_scale
    )
    key_grad = (
        jnp.einsum("ihqk,iqhd->ikhd", score_grad, query_four, preferred_element_type=jnp.float32)
        * score_scale
    )
    value_grad = jnp.einsum(
        "ihqk,iqhd->ikhd",
        weights_soft.astype(jnp.bfloat16),
        grad_four,
        preferred_element_type=jnp.float32,
    )
    flat_shape = queries.shape
    return (
        query_grad.reshape(flat_shape),
        key_grad.reshape(flat_shape),
        value_grad.reshape(flat_shape),
    )


def gelu_slope(values):
    normal_cdf = 0.5 * (1.0 + lax.erf(values * 0.7071067811865476))
    return normal_cdf + values * jnp.exp(-0.5 * values * values) * 0.3989422804014327


def body(
    images,
    first_gain,
    first_shift,
    query_weight,
    key_weight,
    value_weight,
    query_bias,
    value_bias,
    out_weight,
    out_bias,
    second_gain,
    second_shift,
    up_weight,
    up_bias,
    down_weight,
    down_bias,
    cotangent,
):
    layer_count = query_weight.shape[0]
    feature_block = images.shape[1]
    tensor_count = lax.axis_size("tensor")
    full_width = feature_block * tensor_count
    heads_here = feature_block // HEAD_DIM
    tensor_place = lax.axis_index("tensor")
    micro_rows = images.shape[0] // MICRO
    image_count = micro_rows // SEQ

    def gain_share(param_table, layer_idx):
        return lax.dynamic_slice_in_dim(
            param_table[layer_idx], tensor_place * feature_block, feature_block
        )

    def layer_weights(layer_idx):
        return fetch_weights(
            query_weight[layer_idx],
            key_weight[layer_idx],
            value_weight[layer_idx],
            out_weight[layer_idx],
            up_weight[layer_idx],
            down_weight[layer_idx],
        )

    weight_sums = [None] * layer_count
    small_sums = [None] * layer_count
    activation_parts = []
    gradient_parts = []
    for micro_idx in range(MICRO):
        row_start = micro_idx * micro_rows
        stream = images[row_start : row_start + micro_rows].astype(jnp.float32)
        saved_state = []
        for layer_idx in range(layer_count):
            query_full, key_full, value_full, out_full, up_full, down_full = layer_weights(
                layer_idx
            )
            normed, centred_one, inverse_one = norm_forward(
                stream,
                gain_share(first_gain, layer_idx),
                gain_share(first_shift, layer_idx),
                full_width,
            )
            normed_full = full_rows(normed.astype(jnp.bfloat16))
            joined_weight = jnp.concatenate((query_full, key_full, value_full), axis=1)
            projected = jnp.dot(normed_full, joined_weight, preferred_element_type=jnp.float32)
            queries = (projected[:, :feature_block] + query_bias[layer_idx]).astype(jnp.bfloat16)
            keys_here = projected[:, feature_block : 2 * feature_block].astype(jnp.bfloat16)
            values_here = (projected[:, 2 * feature_block :] + value_bias[layer_idx]).astype(
                jnp.bfloat16
            )
            mixed_heads, log_total = attention_forward(
                queries, keys_here, values_here, image_count, heads_here
            )
            attention_sum = feature_total(
                jnp.dot(mixed_heads, out_full, preferred_element_type=jnp.float32)
            )
            after_attention = stream + attention_sum + out_bias[layer_idx]
            normed_two, centred_two, inverse_two = norm_forward(
                after_attention,
                gain_share(second_gain, layer_idx),
                gain_share(second_shift, layer_idx),
                full_width,
            )
            normed_two_full = full_rows(normed_two.astype(jnp.bfloat16))
            hidden_pre = (
                jnp.dot(normed_two_full, up_full, preferred_element_type=jnp.float32)
                + up_bias[layer_idx]
            )
            hidden = jax.nn.gelu(hidden_pre, approximate=False).astype(jnp.bfloat16)
            feedforward_sum = feature_total(
                jnp.dot(hidden, down_full, preferred_element_type=jnp.float32)
            )
            saved_state.append(
                (
                    centred_one,
                    inverse_one,
                    normed_full,
                    queries,
                    keys_here,
                    values_here,
                    mixed_heads,
                    log_total,
                    centred_two,
                    inverse_two,
                    normed_two_full,
                    hidden_pre,
                    hidden,
                )
            )
            stream = after_attention + feedforward_sum + down_bias[layer_idx]
        activation_parts.append(stream.astype(jnp.bfloat16))
        upstream = cotangent[row_start : row_start + micro_rows].astype(jnp.float32)
        for layer_idx in reversed(range(layer_count)):
            query_full, key_full, value_full, out_full, up_full, down_full = layer_weights(
                layer_idx
            )
            (
                centred_one,
                inverse_one,
                normed_full,
                queries,
                keys_here,
                values_here,
                mixed_heads,
                log_total,
                centred_two,
                inverse_two,
                normed_two_full,
                hidden_pre,
                hidden,
            ) = saved_state[layer_idx]
            down_bias_term = jnp.sum(upstream, axis=0)
            upstream_full = full_rows(upstream.astype(jnp.bfloat16))
            down_term = jnp.einsum(
                "rc,rd->cd", hidden, upstream_full, preferred_element_type=jnp.float32
            )
            hidden_grad = jnp.einsum(
                "rd,cd->rc", upstream_full, down_full, preferred_element_type=jnp.float32
            )
            pre_grad = (hidden_grad * gelu_slope(hidden_pre)).astype(jnp.bfloat16)
            up_bias_term = jnp.sum(pre_grad.astype(jnp.float32), axis=0)
            up_term = jnp.einsum(
                "rd,rc->dc", normed_two_full, pre_grad, preferred_element_type=jnp.float32
            )
            normed_two_grad = feature_total(
                jnp.einsum("rc,dc->rd", pre_grad, up_full, preferred_element_type=jnp.float32)
            )
            second_gain_term = jnp.sum(normed_two_grad * centred_two, axis=0)
            second_shift_term = jnp.sum(normed_two_grad, axis=0)
            upstream = upstream + norm_backward(
                normed_two_grad,
                centred_two,
                inverse_two,
                gain_share(second_gain, layer_idx),
                full_width,
            )
            out_bias_term = jnp.sum(upstream, axis=0)
            upstream_full = full_rows(upstream.astype(jnp.bfloat16))
            out_term = jnp.einsum(
                "rc,rd->cd", mixed_heads, upstream_full, preferred_element_type=jnp.float32
            )
            mixed_grad = jnp.einsum(
                "rd,cd->rc", upstream_full, out_full, preferred_element_type=jnp.float32
            ).astype(jnp.bfloat16)
            query_grad, key_grad, value_grad = attention_backward(
                queries, keys_here, values_here, log_total, mixed_grad, image_count, heads_here
            )
            joined_grad = jnp.concatenate((query_grad, key_grad, value_grad), axis=1).astype(
                jnp.bfloat16
            )
            joined_float = joined_grad.astype(jnp.float32)
            query_bias_term = jnp.sum(joined_float[:, :feature_block], axis=0)
            value_bias_term = jnp.sum(joined_float[:, 2 * feature_block :], axis=0)
            joined_term = jnp.einsum(
                "rd,rc->dc", normed_full, joined_grad, preferred_element_type=jnp.float32
            )
            joined_weight = jnp.concatenate((query_full, key_full, value_full), axis=1)
            normed_grad = feature_total(
                jnp.einsum(
                    "rc,dc->rd", joined_grad, joined_weight, preferred_element_type=jnp.float32
                )
            )
            first_gain_term = jnp.sum(normed_grad * centred_one, axis=0)
            first_shift_term = jnp.sum(normed_grad, axis=0)
            upstream = upstream + norm_backward(
                normed_grad, centred_one, inverse_one, gain_share(first_gain, layer_idx), full_width
            )
            query_term = joined_term[:, :feature_block]
            key_term = joined_term[:, feature_block : 2 * feature_block]
            value_term = joined_term[:, 2 * feature_block :]
            weight_sums[layer_idx] = add_terms(
                weight_sums[layer_idx],
                settle_grads(query_term, key_term, value_term, out_term, up_term, down_term),
            )
            small_sums[layer_idx] = add_terms(
                small_sums[layer_idx],
                (
                    query_bias_term,
                    value_bias_term,
                    out_bias_term,
                    up_bias_term,
                    down_bias_term,
                    first_gain_term,
                    first_shift_term,
                    second_gain_term,
                    second_shift_term,
                ),
            )
        gradient_parts.append(upstream)
    share_sets = []
    for layer_idx in range(layer_count):
        share_sets.append(weight_sums[layer_idx])
    weight_outputs = [
        jnp.stack([share_sets[layer_idx][entry_idx] for layer_idx in range(layer_count)])
        for entry_idx in range(6)
    ]
    small_stack = [
        jnp.stack([small_sums[layer_idx][entry_idx] for layer_idx in range(layer_count)])
        for entry_idx in range(9)
    ]
    widened = [
        lax.dynamic_update_slice_in_dim(
            jnp.zeros((layer_count, share_piece.shape[1] * tensor_count), jnp.float32),
            share_piece,
            tensor_place * share_piece.shape[1],
            1,
        )
        for share_piece in small_stack
    ]
    totals = lax.psum(
        (
            widened[0],
            widened[1],
            widened[2],
            widened[3],
            widened[4],
            widened[5],
            widened[6],
            widened[7],
            widened[8],
        ),
        ("wide", "tensor"),
    )
    activations = jnp.concatenate(activation_parts, axis=0)
    input_gradient = jnp.concatenate(gradient_parts, axis=0)
    return (
        activations,
        input_gradient,
        weight_outputs[0],
        weight_outputs[1],
        weight_outputs[2],
        weight_outputs[3],
        weight_outputs[4],
        weight_outputs[5],
        totals[0],
        totals[1],
        totals[2],
        totals[3],
        totals[4],
        totals[5],
        totals[6],
        totals[7],
        totals[8],
    )


MESH_IDS = pl.DeviceIdType.MESH
LOW = jnp.bfloat16
BLOCK = 64
ROWS = -(-SEQ // 16) * 16
DEEP = -(-SEQ // 128) * 128


def place():
    wide = lax.axis_index("wide")
    return (
        lax.div(wide, 4),
        lax.rem(lax.div(wide, 2), 2),
        lax.rem(wide, 2),
        lax.axis_index("tensor"),
    )


def neighbours():
    z, x, c, y = place()

    def at(z, x, c, y):
        return (z * 4 + x * 2 + c, y)

    return {
        "core": at(z, x, 1 - c, y),
        "x": at(z, 1 - x, c, y),
        "y": at(z, x, c, 1 - y),
        "z1": at(z + 1 - 2 * lax.rem(z, 2), x, c, y),
        "z2": at(lax.rem(z + 2, 4), x, c, y),
    }


LINKS = ("core", "x", "y", "z1", "z2")


def greet(partners):
    barrier = pltpu.get_barrier_semaphore()
    for link in LINKS:
        pl.semaphore_signal(barrier, inc=1, device_id=partners[link], device_id_type=MESH_IDS)
    pl.semaphore_wait(barrier, len(LINKS))


def dot_rows(left, right):
    return lax.dot_general(
        left, right, (((1,), (0,)), ((), ())), preferred_element_type=jnp.float32
    )


def dot_cols(left, right):
    return lax.dot_general(
        left, right, (((1,), (1,)), ((), ())), preferred_element_type=jnp.float32
    )


def dot_tokens(left, right):
    return lax.dot_general(
        left, right, (((0,), (0,)), ((), ())), preferred_element_type=jnp.float32
    )


PAIR = 2 * HEAD_DIM


def turned_softmax(keys_here, queries):
    scores = dot_cols(keys_here, queries)
    exponent = jnp.exp(scores - jnp.max(scores, axis=0, keepdims=True))
    return exponent * (1.0 / jnp.sum(exponent, axis=0, keepdims=True))


def store_rows(ref, at, pieces):
    full = SEQ // 16 * 16
    ref[pl.ds(full, ROWS - full), pl.ds(at, PAIR)] = jnp.zeros((ROWS - full, PAIR), LOW)
    ref[pl.ds(0, SEQ), pl.ds(at, PAIR)] = jnp.concatenate(pieces, axis=1)


def gather_stages(z, x, c, y, whole, start, shares):
    share_a, share_b, last = shares

    def cols(t, at, size):
        return pl.ds(pl.multiple_of(t * whole + start + at, 128), size)

    all_rows = pl.ds(0, BLOCK)
    met = (z, lax.rem(z + 2, 4))
    every_z, every_x = pl.ds(0, 4), pl.ds(0, 2)
    far_x, far_y = 1 - x, 1 - y

    def part_a(t):
        return cols(t, 0, share_a)

    def part_b(t):
        return cols(t, share_a, share_b)

    def part_ab(t):
        return cols(t, 0, share_a + share_b)

    def part_c(t):
        return cols(t, share_a + share_b, last)

    stages = [
        [("z2", (z, x, c, all_rows, part_ab(y)))],
        [("z1", (row, x, c, all_rows, part_ab(y))) for row in met],
        [
            ("x", (every_z, x, c, all_rows, part_a(y))),
            ("y", (every_z, x, c, all_rows, part_b(y))),
            ("core", (every_z, x, c, all_rows, part_ab(y))),
        ],
        [
            ("y", (every_z, every_x, c, all_rows, part_a(y))),
            ("x", (every_z, x, c, all_rows, part_b(0))),
            ("x", (every_z, x, c, all_rows, part_b(1))),
            ("core", (every_z, far_x, c, all_rows, part_a(y))),
            ("core", (every_z, x, c, all_rows, part_b(far_y))),
        ],
        [
            ("core", (every_z, every_x, c, all_rows, part_a(far_y))),
            ("core", (every_z, far_x, c, all_rows, part_b(0))),
            ("core", (every_z, far_x, c, all_rows, part_b(1))),
        ],
    ]
    if last:
        stages[0].append(("x", (z, x, c, all_rows, part_c(y))))
        stages[1].append(("y", (z, every_x, c, all_rows, part_c(y))))
        for t in range(2):
            stages[2].append(("z2", (z, every_x, c, all_rows, part_c(t))))
            stages[3] += [("z1", (row, every_x, c, all_rows, part_c(t))) for row in met]
            stages[4].append(("core", (every_z, every_x, c, all_rows, part_c(t))))
    return stages


GATHER_COPIES = 24
GATHER_DEPTH = 5
GATHER_LAG = 2
CHUNK = 512
CHUNK_SHARES = (
    (128, 256, 128),
    (256, 128, 128),
    (256, 256, 0),
    (128, 256, 128),
    (256, 128, 128),
)


class Gather:
    def __init__(self, chunks):
        self.chunks = chunks

    def scratch(self):
        count = len(self.chunks)
        return dict(
            gather_send=pltpu.SemaphoreType.DMA((count, GATHER_COPIES)),
            gather_recv=pltpu.SemaphoreType.DMA((count, GATHER_COPIES)),
            gather_own=pltpu.SemaphoreType.DMA((count,)),
        )

    def bind(self, shards, wholes, refs):
        self.wholes = wholes
        self.send_sem, self.recv_sem, own_sem = refs
        z, x, c, y = place()
        self.partners = neighbours()
        self.plans, self.own, self.flying = [], [], {}
        for chunk, (matrix, start, shares) in enumerate(self.chunks):
            width = sum(shares)
            whole = wholes[matrix].shape[4] // 2
            self.plans.append(gather_stages(z, x, c, y, whole, start, shares))
            mine = pl.ds(pl.multiple_of(y * whole + start, 128), width)
            size = shards[matrix][0].shape[1]
            shard = shards[matrix][start // size]
            copy = pltpu.make_async_copy(
                shard.at[:, pl.ds(start % size, width)],
                wholes[matrix].at[z, x, c, pl.ds(0, BLOCK), mine],
                own_sem.at[chunk],
            )
            copy.start()
            self.own.append(copy)

    def tick(self, tick):
        done = None
        for stage_idx in range(GATHER_DEPTH, -1, -1):
            chunk = tick - GATHER_LAG * stage_idx
            if chunk < 0 or chunk >= len(self.chunks):
                continue
            if stage_idx == 0:
                self.own[chunk].wait()
            for copy in self.flying.get((chunk, stage_idx - 1), ()):
                copy.wait_recv()
            if stage_idx == GATHER_DEPTH:
                done = chunk
                continue
            started = []
            plan = self.plans[chunk]
            base = sum(len(stage) for stage in plan[:stage_idx])
            whole = self.wholes[self.chunks[chunk][0]]
            for entry, (link, index) in enumerate(plan[stage_idx]):
                copy = pltpu.make_async_remote_copy(
                    src_ref=whole.at[index],
                    dst_ref=whole.at[index],
                    send_sem=self.send_sem.at[chunk, base + entry],
                    recv_sem=self.recv_sem.at[chunk, base + entry],
                    device_id=self.partners[link],
                    device_id_type=MESH_IDS,
                )
                copy.start()
                started.append(copy)
            self.flying[(chunk, stage_idx)] = started
        return done

    def finish(self):
        for started in self.flying.values():
            for copy in started:
                copy.wait_send()


BIAS_ROWS = 9
SAVED = (
    "normed",
    "projected",
    "heads",
    "normed_two",
    "hidden",
    "slope",
    "centred",
    "inverse",
    "centred_two",
    "inverse_two",
)


def row_loop(body):
    @pl.loop(0, ROWS // 32)
    def _(step):
        body(pl.ds(pl.multiple_of(step * 32, 32), 32), 32)

    left = ROWS % 32
    if left:
        body(pl.ds(ROWS - left, left), left)


class Forward:
    def __init__(self, layers, widths):
        self.layers, self.widths = layers, widths
        chunks = []
        for layer in range(layers):
            for kind, width in enumerate(widths):
                for start in range(0, width, CHUNK):
                    shares = CHUNK_SHARES[len(chunks) % len(CHUNK_SHARES)]
                    chunks.append((layer * len(widths) + kind, start, shares))
        self.gather = Gather(chunks)

    def scratch(self):
        project, out, up, down = self.widths
        low, full = (lambda cols: pltpu.VMEM((ROWS, cols), LOW)), pltpu.VMEM((ROWS, 1024), jnp.float32)
        sem = pltpu.SemaphoreType.DMA
        own = dict(
            weights_project=pltpu.VMEM((4, 2, 2, BLOCK, 2 * project), LOW),
            weights_out=pltpu.VMEM((4, 2, 2, BLOCK, 2 * out), LOW),
            weights_up=pltpu.VMEM((4, 2, 2, BLOCK, 2 * up), LOW),
            weights_down=pltpu.VMEM((4, 2, 2, BLOCK, 2 * down), LOW),
            stream=full,
            centred=full,
            inverse=pltpu.VMEM((ROWS, 128), jnp.float32),
            tokens_in=low(512),
            biases=pltpu.VMEM((2, self.layers * BIAS_ROWS, 512), jnp.float32),
            normed=low(1024),
            projected=low(2 * project),
            heads=low(2 * out),
            normed_two=low(1024),
            hidden=low(2 * up),
            slope=low(2 * up),
            weight_sem=sem((len(self.gather.chunks), 2)),
            saved_sem=sem((self.layers, len(SAVED))),
            swap_send=sem((3,)),
            swap_recv=sem((3,)),
        )
        return {**own, **self.gather.scratch()}

    def bind(self, inputs, outputs, refs):
        for name, ref in zip(self.scratch(), refs, strict=True):
            setattr(self, name, ref)
        shards, inputs = inputs[:6], inputs[6:]
        self.near, self.far, self.norm_refs, bias_refs = inputs[0], inputs[1], inputs[2:6], inputs[6:]
        count = self.layers * 4
        self.wholes, outputs = outputs[:count], outputs[count:]
        self.cotangent_in, self.leaving, self.staying, outputs = (*outputs[:3], outputs[3:])
        self.saved_out = [outputs[k * len(SAVED) : (k + 1) * len(SAVED)] for k in range(self.layers)]
        self.saving, self.loading, self.centred_saves = {}, {}, []
        self.y = lax.axis_index("tensor")
        kinds = (shards[:3], shards[3:4], shards[4:5], shards[5:6])
        self.gather.bind(
            [[shard.at[m // 4] for shard in kinds[m % 4]] for m in range(count)],
            self.wholes,
            [getattr(self, name) for name in self.gather.scratch()],
        )
        zeros = jnp.zeros((1, 512), jnp.float32)
        for layer in range(self.layers):
            row = layer * BIAS_ROWS
            for ref in bias_refs:
                line = ref[layer : layer + 1, :].astype(jnp.float32)
                for start in range(0, ref.shape[1], 512):
                    self.biases[self.y, row : row + 1, :] = line[:, start : start + 512]
                    row += 1
                if ref is bias_refs[0]:
                    self.biases[self.y, row : row + 1, :] = zeros
                    row += 1

    def swap(self):
        partner = self.gather.partners["y"]
        pairs = (
            (self.biases.at[self.y], self.biases.at[self.y]),
            (self.far.at[0], self.tokens_in),
            (self.far.at[1], self.cotangent_in),
        )
        self.swaps = []
        for entry, (source, target) in enumerate(pairs):
            copy = pltpu.make_async_remote_copy(
                src_ref=source,
                dst_ref=target,
                send_sem=self.swap_send.at[entry],
                recv_sem=self.swap_recv.at[entry],
                device_id=partner,
                device_id_type=MESH_IDS,
            )
            copy.start()
            self.swaps.append(copy)

    def save(self, layer, name, source):
        entry = SAVED.index(name)
        copy = pltpu.make_async_copy(
            source, self.saved_out[layer][entry], self.saved_sem.at[layer, entry]
        )
        copy.start()
        self.saving[(layer, name)] = copy

    def saved(self, layer, name):
        if (layer, name) in self.saving:
            self.saving.pop((layer, name)).wait()

    def load(self, chunk):
        matrix, start, shares = self.gather.chunks[chunk]
        width = sum(shares)
        whole = self.gather.wholes[matrix]
        buffer = (self.weights_project, self.weights_out, self.weights_up, self.weights_down)[
            matrix % 4
        ]
        for t in range(2):
            at = (slice(None),) * 4 + (pl.ds(t * (whole.shape[4] // 2) + start, width),)
            copy = pltpu.make_async_copy(whole.at[at], buffer.at[at], self.weight_sem.at[chunk, t])
            copy.start()
            self.loading.setdefault(matrix, []).append(copy)

    def wait_weights(self, matrix):
        for copy in self.loading.pop(matrix):
            copy.wait()

    def bias_row(self, row):
        return jnp.concatenate([self.biases[t, pl.ds(row, 1), :] for t in range(2)], axis=1)

    def norm(self, target, gain_ref, shift_ref, layer, bias_at, names):
        gain = gain_ref[layer : layer + 1, :].astype(jnp.float32)
        shift = shift_ref[layer : layer + 1, :].astype(jnp.float32)
        bias = None if bias_at is None else self.bias_row(bias_at)
        for key in self.centred_saves:
            self.saved(*key)

        def body(rows, size):
            values = self.stream[rows, :]
            if bias is not None:
                values = values + bias
                self.stream[rows, :] = values
            mean = jnp.mean(values, axis=1, keepdims=True)
            square = jnp.mean(values * values, axis=1, keepdims=True)
            inverse = lax.rsqrt(square - mean * mean + norm_eps)
            centred = (values - mean) * inverse
            self.centred[rows, :] = centred
            self.inverse[rows, :] = jnp.broadcast_to(inverse, (size, 128))
            target[rows, :] = (centred * gain + shift).astype(LOW)

        row_loop(body)
        self.save(layer, names[0], self.centred)
        self.save(layer, names[1], self.inverse)
        self.centred_saves = [(layer, name) for name in names]

    def begin(self):
        for copy in self.swaps:
            copy.wait_recv()
        y = self.y
        near_at = pl.ds(pl.multiple_of(y * 512, 512), 512)
        far_at = pl.ds(pl.multiple_of((1 - y) * 512, 512), 512)
        self.stream[:, near_at] = self.near[...].astype(jnp.float32)
        self.stream[:, far_at] = self.tokens_in[...].astype(jnp.float32)

    def project(self, layer):
        self.saved(layer - 1, "normed")
        self.norm(
            self.normed,
            *self.norm_refs[:2],
            layer,
            None if layer == 0 else (layer - 1) * BIAS_ROWS + 4,
            ("centred", "inverse"),
        )
        self.save(layer, "normed", self.normed)
        self.saved(layer - 1, "projected")
        self.wait_weights(layer * 4)
        parts = 6

        @pl.loop(0, parts)
        def _(part):
            cols = pl.ds(pl.multiple_of(part * 512, 512), 512)
            weights = self.weights_project[:, :, :, :, cols].reshape(1024, 512)
            row = layer * BIAS_ROWS + lax.rem(part, 3)
            bias = self.biases[lax.div(part, 3), pl.ds(row, 1), :]
            self.projected[:, cols] = (dot_rows(self.normed[...], weights) + bias).astype(LOW)

        self.save(layer, "projected", self.projected)

    def mix(self, layer, first, last):
        if first == 0:
            self.saved(layer - 1, "heads")
        half = self.heads.shape[1] // 2

        @pl.loop(first, last)
        def _(step):
            for t in range(2):
                def at(part):
                    start = (t * 3 + part) * half + step * PAIR
                    return pl.ds(pl.multiple_of(start, PAIR), PAIR)

                queries = self.projected[pl.ds(0, SEQ), at(0)] * jnp.asarray(HEAD_DIM**-0.5, LOW)
                keys_here = self.projected[pl.ds(0, SEQ), at(1)]
                values_here = self.projected[pl.ds(0, SEQ), at(2)]
                pieces = []
                for head in range(2):
                    cols = slice(head * HEAD_DIM, (head + 1) * HEAD_DIM)
                    soft = turned_softmax(keys_here[:, cols], queries[:, cols])
                    pieces.append(dot_tokens(soft.astype(LOW), values_here[:, cols]).astype(LOW))
                store_rows(self.heads, pl.multiple_of(t * half + step * PAIR, PAIR), pieces)

        if last * PAIR == half:
            self.save(layer, "heads", self.heads)

    def attend(self, layer):
        self.wait_weights(layer * 4 + 1)

        @pl.loop(0, 4)
        def _(row):
            cols = pl.ds(pl.multiple_of(row * 256, 256), 256)
            weights = self.weights_out[row].reshape(256, -1)
            self.stream[:, cols] = self.stream[:, cols] + dot_cols(self.heads[...], weights)

        self.saved(layer - 1, "normed_two")
        self.norm(
            self.normed_two,
            *self.norm_refs[2:],
            layer,
            layer * BIAS_ROWS + 3,
            ("centred_two", "inverse_two"),
        )
        self.save(layer, "normed_two", self.normed_two)

    def feed_up(self, layer, first, last):
        if first == 0:
            self.saved(layer - 1, "hidden")
            self.saved(layer - 1, "slope")
            self.wait_weights(layer * 4 + 2)

        @pl.loop(first, last)
        def _(part):
            cols = pl.ds(pl.multiple_of(part * 512, 512), 512)
            weights = self.weights_up[:, :, :, :, cols].reshape(1024, 512)
            row = layer * BIAS_ROWS + 5 + lax.rem(part, 4)
            bias = self.biases[lax.div(part, 4), pl.ds(row, 1), :]
            before = dot_rows(self.normed_two[...], weights) + bias
            normal = 0.5 * (1.0 + lax.erf(before * 0.7071067811865476))
            self.hidden[:, cols] = (before * normal).astype(LOW)
            density = jnp.exp(-0.5 * before * before) * 0.3989422804014327
            self.slope[:, cols] = (normal + before * density).astype(LOW)

        if last * 512 == self.hidden.shape[1]:
            self.save(layer, "hidden", self.hidden)
            self.save(layer, "slope", self.slope)

    def feed_down(self, layer, first, last):
        if first == 0:
            self.wait_weights(layer * 4 + 3)

        @pl.loop(first, last)
        def _(row):
            cols = pl.ds(pl.multiple_of(row * 256, 256), 256)
            weights = self.weights_down[row].reshape(256, -1)
            self.stream[:, cols] = self.stream[:, cols] + dot_cols(self.hidden[...], weights)

    def end(self):
        row = (self.layers - 1) * BIAS_ROWS + 4
        for t, ref in ((self.y, self.staying), (1 - self.y, self.leaving)):
            bias = self.biases[t, pl.ds(row, 1), :]
            cols = pl.ds(pl.multiple_of(t * 512, 512), 512)

            def body(rows, _, ref=ref, bias=bias, cols=cols):
                ref[rows, :] = (self.stream[rows, cols] + bias).astype(LOW)

            row_loop(body)

    def work(self):
        steps = [(0, 1, self.begin)]
        for layer in range(self.layers):
            base = layer * 4
            steps += [
                (base, 6, lambda layer=layer: self.project(layer)),
                (base, 7, lambda layer=layer: self.mix(layer, 0, 2)),
                (base, 7, lambda layer=layer: self.mix(layer, 2, 4)),
                (base + 1, 4, lambda layer=layer: self.attend(layer)),
                (base + 2, 6, lambda layer=layer: self.feed_up(layer, 0, 4)),
                (base + 2, 6, lambda layer=layer: self.feed_up(layer, 4, 8)),
                (base + 3, 4, lambda layer=layer: self.feed_down(layer, 0, 2)),
                (base + 3, 4, lambda layer=layer: self.feed_down(layer, 2, 4)),
            ]
        return steps + [(self.layers * 4 - 1, 1, self.end)]

    def run(self):
        greet(self.gather.partners)
        self.swap()
        steps = self.work()
        ready = set()
        remaining = {}
        for matrix, _, _ in self.gather.chunks:
            remaining[matrix] = remaining.get(matrix, 0) + 1
        ticks = len(self.gather.chunks) + GATHER_LAG * GATHER_DEPTH
        for tick in range(ticks):
            budget = WORK_A_TICK
            done = self.gather.tick(tick)
            while steps and steps[0][0] in ready and budget > 0:
                _, cost, step = steps.pop(0)
                budget -= cost
                step()
            if done is not None:
                self.free_buffer(done, steps)
                matrix = self.gather.chunks[done][0]
                self.load(done)
                remaining[matrix] -= 1
                if remaining[matrix] == 0:
                    ready.add(matrix)
        for _, _, step in steps:
            step()
        self.gather.finish()
        for copy in self.swaps:
            copy.wait_send()
        for copy in self.saving.values():
            copy.wait()

    def free_buffer(self, chunk, steps):
        matrix = self.gather.chunks[chunk][0]
        while steps and any(entry[0] == matrix - 4 for entry in steps):
            steps.pop(0)[2]()


WORK_A_TICK = 5


def forward(shards, near, far, norms, biases):
    layers = shards[0].shape[0]
    widths = [3 * shards[0].shape[2], *[shard.shape[2] for shard in shards[3:]]]
    plan = Forward(layers, widths)
    project, out, up, down = widths
    low = lambda cols: jax.ShapeDtypeStruct((ROWS, cols), LOW)
    full = jax.ShapeDtypeStruct((ROWS, 1024), jnp.float32)
    lanes = jax.ShapeDtypeStruct((ROWS, 128), jnp.float32)
    saved = [
        low(1024), low(2 * project), low(2 * out), low(1024), low(2 * up), low(2 * up),
        full, lanes, full, lanes,
    ]
    wholes = [
        jax.ShapeDtypeStruct((4, 2, 2, BLOCK, 2 * width), LOW) for width in widths
    ] * layers
    outs = [*wholes, low(512), low(512), low(512), *(saved * layers)]
    any_spec, vmem_spec = pl.BlockSpec(memory_space=pl.ANY), pl.BlockSpec(memory_space=pltpu.VMEM)
    out_specs = [any_spec] * len(outs)
    out_specs[len(wholes) + 1 : len(wholes) + 3] = [vmem_spec] * 2

    operands = [*shards, near, far, *norms, *biases]

    def kernel(*refs):
        ins, refs = refs[: len(operands)], refs[len(operands) :]
        plan.bind(ins, refs[: len(outs)], refs[len(outs) :])
        plan.run()

    results = pl.pallas_call(
        kernel,
        out_shape=outs,
        in_specs=[any_spec] * 6 + [vmem_spec, any_spec] + [vmem_spec] * 9,
        out_specs=out_specs,
        scratch_shapes=list(plan.scratch().values()),
        compiler_params=pltpu.CompilerParams(
            collective_id=0, has_side_effects=True, vmem_limit_bytes=60 * 1024 * 1024
        ),
        cost_estimate=pl.CostEstimate(
            flops=60 * 1024**3, bytes_accessed=700 * 1024 * 1024, transcendentals=0
        ),
        name="forward",
    )(*operands)
    whole, results = results[: len(wholes)], results[len(wholes) :]
    weights = [
        [whole[layer * 4 + kind] for kind in range(4)] for layer in range(layers)
    ]
    swapped, results = results[:3], results[3:]
    kept = [
        dict(zip(SAVED, results[k * len(SAVED) : (k + 1) * len(SAVED)])) for k in range(layers)
    ]
    return weights, swapped, kept


COLS = 128
STAGE_AT = (0, 1, 3, 5, 6, 7, 8)
SETTLE_DEPTH = len(STAGE_AT) - 1
SLOTS = dict(core_in=2, val=5, first_a=4, first_b=4, second=4, third=2, fourth=2, fifth=2, rest=4)
TURNED_SLOTS = 3


class Settle:
    def __init__(self, widths, pairs):
        self.widths, self.pairs = widths, pairs

    def scratch(self):
        shapes = dict(
            core_in=(2, 2, 4, 2, 2, BLOCK, COLS),
            val=(2, 2, 4, 2, 2, BLOCK, COLS),
            first_a=(4, 2, 2, BLOCK, COLS),
            first_b=(2, 4, 2, BLOCK, COLS),
            second=(2, 4, 2, BLOCK, COLS),
            third=(2, 2, 2, BLOCK, COLS),
            fourth=(2, 2, BLOCK, COLS),
            fifth=(2, BLOCK, COLS),
            rest=(2, 4, 2, BLOCK, COLS),
        )
        pairs, sem = len(self.pairs), pltpu.SemaphoreType.DMA
        return dict(
            left_in=pltpu.VMEM((ROWS, 1024), LOW),
            left_turned=pltpu.VMEM((TURNED_SLOTS, 1024, DEEP), LOW),
            right_in=pltpu.VMEM((2, 2, 2, DEEP, 2 * COLS), LOW),
            core_out=pltpu.VMEM((2, 2, 4, 2, 2, BLOCK, COLS), LOW),
            **{name: pltpu.VMEM((SLOTS[name], *shape), LOW) for name, shape in shapes.items()},
            result=pltpu.VMEM((2, 2, 2, BLOCK, COLS), jnp.float32),
            result_sem=sem((2, 2, 2)),
            send_sem=sem((pairs, 2, SETTLE_DEPTH)),
            recv_sem=sem((pairs, 2, SETTLE_DEPTH)),
            right_sem=sem((pairs, 2, 4)),
            left_sem=sem((1,)),
        )

    def bind(self, lefts, rights, outs, refs):
        self.lefts, self.rights, self.outs = lefts, rights, outs
        for name, ref in zip(self.scratch(), refs, strict=True):
            setattr(self, name, ref)
        self.z, self.x, self.c, self.y = place()
        self.partners = neighbours()
        self.copies, self.turned, self.results = {}, {}, {}
        tail = ROWS // 128 * 128
        self.left_turned[:, :, pl.ds(tail, DEEP - tail)] = jnp.zeros(
            (TURNED_SLOTS, 1024, DEEP - tail), LOW
        )
        self.right_in[:, :, :, pl.ds(ROWS, DEEP - ROWS)] = jnp.zeros(
            (2, 2, 2, DEEP - ROWS, 2 * COLS), LOW
        )

    def load(self, pair):
        for unit, (matrix, step) in enumerate(self.pairs[pair]):
            width = self.widths[matrix]
            for t in range(2):
                for near in range(2):
                    core = self.c if near else 1 - self.c
                    at = pl.multiple_of(t * width + core * (width // 2) + step * COLS, COLS)
                    copy = pltpu.make_async_copy(
                        self.rights[matrix].at[:, pl.ds(at, COLS)],
                        self.right_in.at[
                            pair % 2, unit, t, pl.ds(0, ROWS), pl.ds(near * COLS, COLS)
                        ],
                        self.right_sem.at[pair, unit, 2 * t + near],
                    )
                    copy.start()
                    self.copies[(pair, unit, "right", 2 * t + near)] = copy

    def turn(self, matrix):
        if matrix in self.turned:
            return
        source, here = self.lefts[matrix]
        if not here:
            copy = pltpu.make_async_copy(source, self.left_in, self.left_sem.at[0])
            copy.start()
            copy.wait()
            source = self.left_in
        slot = len(self.turned) % TURNED_SLOTS
        for quarter in range(4):
            cols = pl.ds(quarter * 256, 256)
            self.left_turned[slot, cols, pl.ds(0, ROWS)] = source[:, cols].T
        self.turned[matrix] = slot

    def wait_load(self, pair):
        for unit, (matrix, _) in enumerate(self.pairs[pair]):
            self.turn(matrix)
            for entry in range(4):
                self.copies.pop((pair, unit, "right", entry)).wait()

    def send(self, pair, unit, stage, source, target, link):
        copy = pltpu.make_async_remote_copy(
            src_ref=source,
            dst_ref=target,
            send_sem=self.send_sem.at[pair, unit, stage],
            recv_sem=self.recv_sem.at[pair, unit, stage],
            device_id=self.partners[link],
            device_id_type=MESH_IDS,
        )
        copy.start()
        self.copies[(pair, unit, stage)] = copy

    def product(self, pair, unit, t):
        matrix, _ = self.pairs[pair][unit]
        left = self.left_turned[self.turned[matrix]]
        right = self.right_in[pair % 2, unit, t]
        total = dot_rows(left[:, :512], right[:512]) + dot_rows(left[:, 512:], right[512:])
        return total.astype(LOW)

    def stage(self, pair, unit, stage):
        if pair < 0 or pair >= len(self.pairs):
            return
        z, x, c, y = self.z, self.x, self.c, self.y
        high, lower = lax.div(z, 2), lax.rem(z, 2)
        far_pair = pl.ds(2 * (1 - high), 2)
        far_z = z + 1 - 2 * lower

        def buffer(name):
            return getattr(self, name).at[pair % SLOTS[name], unit]

        val, rest = buffer("val"), buffer("rest")
        first_a = self.first_a.at[pair % SLOTS["first_a"]]
        first_b = self.first_b.at[pair % SLOTS["first_b"]]
        shape = (4, 2, 2, BLOCK, COLS)
        if stage == 0:
            out = self.core_out.at[unit]

            @pl.loop(0, 2)
            def _(t):
                total = self.product(pair, unit, t)
                out[t] = total[:, :COLS].reshape(shape)
                val[t] = total[:, COLS:].reshape(shape)

            self.send(pair, unit, 0, out, buffer("core_in"), "core")
            return
        self.copies.pop((pair, unit, stage - 1)).wait()
        if stage == 1:
            other = buffer("core_in")

            @pl.loop(0, 4)
            def _(row):
                for t in range(2):
                    val[t, row] = val[t, row] + other[t, row]

            if unit == 0:
                self.send(pair, unit, 1, val.at[1 - y], first_a, "y")
            else:
                self.send(pair, unit, 1, val.at[:, :, 1 - x], first_b, "x")
        elif stage == 2:
            target = buffer("second")
            if unit == 0:

                @pl.loop(0, 4)
                def _(row):
                    val[y, row] = val[y, row] + first_a[row]

                self.send(pair, unit, 2, val.at[y, :, 1 - x], target, "x")
            else:

                @pl.loop(0, 4)
                def _(row):
                    for t in range(2):
                        val[t, row, x] = val[t, row, x] + first_b[t, row]

                self.send(pair, unit, 2, val.at[1 - y, :, x], target, "y")
        elif stage == 3:

            second = buffer("second")

            @pl.loop(0, 4)
            def _(row):
                rest[row] = val[y, row, x] + second[row]

            self.send(pair, unit, 3, rest.at[far_pair], buffer("third"), "z2")
        elif stage == 4:
            third = buffer("third")
            for row in range(2):
                at = 2 * high + row
                rest[at] = rest[at] + third[row]
            self.send(pair, unit, 4, rest.at[far_z], buffer("fourth"), "z1")
        elif stage == 5:
            rest[z] = rest[z] + buffer("fourth")[...]
            self.send(pair, unit, 5, rest.at[z, 1 - c], buffer("fifth"), "core")
        else:
            matrix, step = self.pairs[pair][unit]
            out_ref, layer = self.outs[matrix]
            slot = pair % 2
            for copy in self.results.pop((slot, unit), ()):
                copy.wait()
            result = self.result.at[slot, unit]
            result[c] = rest[z, c].astype(jnp.float32)
            result[1 - c] = buffer("fifth")[...].astype(jnp.float32)
            self.results[(slot, unit)] = []
            for core in range(2):
                copy = pltpu.make_async_copy(
                    result.at[core],
                    out_ref.at[layer, core, :, pl.ds(step * COLS, COLS)],
                    self.result_sem.at[slot, unit, core],
                )
                copy.start()
                self.results[(slot, unit)].append(copy)

    def finish(self):
        for copies in self.results.values():
            for copy in copies:
                copy.wait()

    def tick(self, pair):
        for stage in range(SETTLE_DEPTH, 0, -1):
            for unit in range(2):
                self.stage(pair - STAGE_AT[stage], unit, stage)
        if pair < len(self.pairs):
            self.wait_load(pair)
            for unit in range(2):
                self.stage(pair, unit, 0)


TOTAL_LINKS = ("x", "y", "z1", "z2", "core")
SUM_ROWS = 12
TILE = 512
KEPT = SAVED


class Backward:
    def __init__(self, layers, widths):
        self.layers, self.widths = layers, widths
        pairs, self.needs = [], []
        for layer in reversed(range(layers)):
            base = layer * 4
            feed = widths[2] // 2 // COLS
            for kind, fact in ((3, "arrived"), (2, "fed")):
                for k in range(0, feed, 2):
                    pairs.append(((base + kind, k), (base + kind, k + 1)))
                    self.needs.append((layer, fact))
            rest = [(base + 1, k) for k in range(widths[1] // 2 // COLS)]
            rest += [(base, k) for k in range(widths[0] // 2 // COLS)]
            for k in range(0, len(rest), 2):
                pairs.append((rest[k], rest[k + 1]))
                self.needs.append((layer, "mixed"))
        self.settle = Settle(widths * layers, pairs)

    def scratch(self):
        sem = pltpu.SemaphoreType.DMA
        full = pltpu.VMEM((ROWS, 1024), jnp.float32)
        low = pltpu.VMEM((ROWS, 1024), LOW)
        steps = len(TOTAL_LINKS)
        rows = self.layers * SUM_ROWS
        own = dict(
            grad=full,
            delta=full,
            centred=full,
            inverse=pltpu.VMEM((ROWS, 128), jnp.float32),
            feed_grad=low,
            mix_grad=low,
            heads_grad=low,
            projected=pltpu.VMEM((ROWS, 2 * self.widths[0]), LOW),
            joined=pltpu.VMEM((ROWS, 2 * self.widths[0]), LOW),
            tile_a=pltpu.VMEM((2, 4, 2, 2, BLOCK, TILE), LOW),
            tile_b=pltpu.VMEM((2, 4, 2, 2, BLOCK, TILE), LOW),
            slope_in=pltpu.VMEM((2, ROWS, TILE), LOW),
            hidden_out=pltpu.VMEM((2, ROWS, TILE), LOW),
            column_sums=pltpu.VMEM((8, 1, TILE), jnp.float32),
            sums_part=pltpu.VMEM((3, 16, 1024), jnp.float32),
            sums=pltpu.VMEM((steps + 1, rows, 1024), jnp.float32),
            sums_in=pltpu.VMEM((steps, rows, 1024), jnp.float32),
            leave=pltpu.VMEM((ROWS, 512), LOW),
            tile_sem=sem((2, 3)),
            hidden_sem=sem((2,)),
            value_sem=sem((4,)),
            sums_send=sem((steps,)),
            sums_recv=sem((steps,)),
            swap_send=sem((2,)),
            swap_recv=sem((2,)),
        )
        return {**own, **self.settle.scratch()}

    def bind(self, inputs, outputs, refs):
        for name, ref in zip(self.scratch(), refs, strict=True):
            setattr(self, name, ref)
        layers = self.layers
        count = layers * 4
        self.weights, inputs = inputs[:count], inputs[count:]
        self.kept = [
            dict(zip(KEPT, inputs[k * len(KEPT) : (k + 1) * len(KEPT)])) for k in range(layers)
        ]
        *self.upstream, self.leaving, first_gain, second_gain = inputs[layers * len(KEPT) :]
        self.gains = (first_gain, second_gain)
        outs, outputs = outputs[:4], outputs[4:]
        self.total_out, self.near_out, self.arriving, outputs = (*outputs[:3], outputs[3:])
        self.hidden_grads = outputs
        self.facts, self.hidden_copies = set(), []
        lefts, rights = [], []
        for layer in range(layers):
            kept = self.kept[layer]
            lefts += [
                (kept["normed"], False),
                (self.mix_grad, True),
                (kept["normed_two"], False),
                (self.feed_grad, True),
            ]
            rights += [self.joined, kept["heads"], self.hidden_grads[layer], kept["hidden"]]
        self.settle.bind(
            lefts,
            rights,
            [(outs[m % 4], m // 4) for m in range(count)],
            [getattr(self, name) for name in self.settle.scratch()],
        )
        self.loaded_pair = -1

    def fetch(self, entry, source, target):
        copy = pltpu.make_async_copy(source, target, self.value_sem.at[entry])
        copy.start()
        return copy

    def fetch_centred(self, layer, centred, inverse):
        self.centred_copies = [
            self.fetch(1, self.kept[layer][centred], self.centred),
            self.fetch(3, self.kept[layer][inverse], self.inverse),
        ]

    def swap(self, entry, source):
        copy = pltpu.make_async_remote_copy(
            src_ref=source,
            dst_ref=self.arriving.at[entry],
            send_sem=self.swap_send.at[entry],
            recv_sem=self.swap_recv.at[entry],
            device_id=self.settle.partners["y"],
            device_id_type=MESH_IDS,
        )
        copy.start()
        return copy

    def add_sum(self, entry, values):
        for start in range(0, values.shape[0], 16):
            self.sums_part[entry] += values[start : start + 16]

    def put_sum(self, layer, row, values):
        self.sums[0, pl.ds(layer * SUM_ROWS + row, 1), :] = values

    def begin(self):
        copies = []
        for entry, t in enumerate((self.y, 1 - self.y)):
            cols = pl.ds(pl.multiple_of(t * 512, 512), 512)
            copies.append(self.fetch(entry, self.upstream[entry], self.feed_grad.at[:, cols]))
        for copy in copies:
            copy.wait()
        self.facts.add((self.layers - 1, "arrived"))

    def widen(self):
        self.sums_part[...] = jnp.zeros_like(self.sums_part)

        def body(rows, _):
            values = self.feed_grad[rows, :].astype(jnp.float32)
            self.grad[rows, :] = values
            self.add_sum(2, values)

        row_loop(body)
        self.put_sum(self.layers - 1, 7, jnp.sum(self.sums_part[2], axis=0, keepdims=True))

    def tile_copies(self, part, sources, targets):
        cols = pl.ds(part * TILE, TILE)
        slot = part % 2
        copies = []
        for entry, (source, target) in enumerate(zip(sources, targets)):
            at = (slice(None),) * (len(source.shape) - 1) + (cols,)
            copy = pltpu.make_async_copy(
                source.at[at], target.at[slot], self.tile_sem.at[slot, entry]
            )
            copy.start()
            copies.append(copy)
        return copies

    def tile(self, part, parts, sources, targets):
        if part == 0:
            self.coming = self.tile_copies(0, sources, targets)
        for copy in self.coming:
            copy.wait()
        if part + 1 < parts:
            self.coming = self.tile_copies(part + 1, sources, targets)

    def add_delta(self, is_first, grads, weights):
        for half in range(2):
            cols = slice(half * 512, (half + 1) * 512)
            product = dot_cols(grads, weights[2 * half : 2 * half + 2].reshape(512, TILE))
            self.delta[:, cols] = product if is_first else self.delta[:, cols] + product

    def feed(self, layer, part):
        out_ref = self.hidden_grads[layer]
        parts, slot = out_ref.shape[1] // TILE, part % 2
        if part == 0:
            self.fetch_centred(layer, "centred_two", "inverse_two")
        sources = (self.weights[layer * 4 + 3], self.weights[layer * 4 + 2], self.kept[layer]["slope"])
        self.tile(part, parts, sources, (self.tile_a, self.tile_b, self.slope_in))
        if part >= 2:
            self.hidden_copies.pop(0).wait()
        down = self.tile_a[slot].reshape(1024, TILE)
        slope = self.slope_in[slot].astype(jnp.float32)
        grads = (dot_rows(self.feed_grad[...], down) * slope).astype(LOW)
        self.hidden_out[slot] = grads
        copy = pltpu.make_async_copy(
            self.hidden_out.at[slot],
            out_ref.at[:, pl.ds(part * TILE, TILE)],
            self.hidden_sem.at[slot],
        )
        copy.start()
        self.hidden_copies.append(copy)
        self.column_sums[part] = jnp.sum(grads.astype(jnp.float32), axis=0, keepdims=True)
        self.add_delta(part == 0, grads, self.tile_b.at[slot])
        if part == parts - 1:
            while self.hidden_copies:
                self.hidden_copies.pop(0).wait()
            for row in range(4):
                pieces = [self.column_sums[2 * row], self.column_sums[2 * row + 1]]
                self.put_sum(layer, 3 + row, jnp.concatenate(pieces, axis=1))
            self.facts.add((layer, "fed"))

    def norm_back(self, layer, gain_ref, sum_row, low_ref, total_at):
        for copy in self.centred_copies:
            copy.wait()
        gain = gain_ref[layer : layer + 1, :].astype(jnp.float32)
        self.sums_part[...] = jnp.zeros_like(self.sums_part)

        def body(rows, _):
            centred, delta = self.centred[rows, :], self.delta[rows, :]
            weighted = delta * centred
            self.add_sum(0, weighted)
            self.add_sum(1, delta)
            scaled = delta * gain
            grad = self.grad[rows, :] + self.inverse[rows, 0:1] * (
                scaled
                - jnp.mean(scaled, axis=1, keepdims=True)
                - centred * jnp.mean(weighted * gain, axis=1, keepdims=True)
            )
            self.grad[rows, :] = grad
            self.add_sum(2, grad)
            if low_ref is not None:
                low_ref[rows, :] = grad.astype(LOW)

        row_loop(body)
        for entry in range(2):
            total = jnp.sum(self.sums_part[entry], axis=0, keepdims=True)
            self.put_sum(layer, sum_row + entry, total)
        if total_at is not None:
            total = jnp.sum(self.sums_part[2], axis=0, keepdims=True)
            self.put_sum(*total_at, total)

    def out_back(self, layer):
        self.norm_back(layer, self.gains[1], 10, self.mix_grad, (layer, 2))
        self.fetch_centred(layer, "centred", "inverse")
        self.projected_copy = self.fetch(2, self.kept[layer]["projected"], self.projected)

        for part in range(2):
            self.tile(part, 2, (self.weights[layer * 4 + 1],), (self.tile_a,))
            cols = pl.ds(part * TILE, TILE)
            weights = self.tile_a[part].reshape(1024, TILE)
            self.heads_grad[:, cols] = dot_rows(self.mix_grad[...], weights).astype(LOW)

    def mix_back(self, layer, first, last):
        if first == 0:
            self.projected_copy.wait()
        half = self.heads_grad.shape[1] // 2

        @pl.loop(2 * first, 2 * last)
        def _(turn):
            step, t = lax.div(turn, 2), lax.rem(turn, 2)

            def at(part):
                start = (t * 3 + part) * half + step * PAIR
                return pl.ds(pl.multiple_of(start, PAIR), PAIR)

            here = pl.ds(pl.multiple_of(t * half + step * PAIR, PAIR), PAIR)
            rows = pl.ds(0, SEQ)
            all_queries = self.projected[rows, at(0)] * jnp.asarray(HEAD_DIM**-0.5, LOW)
            all_keys, all_values = self.projected[rows, at(1)], self.projected[rows, at(2)]
            all_grads = self.heads_grad[rows, here]
            pieces = ([], [], [])
            for head in range(2):
                cols = slice(head * HEAD_DIM, (head + 1) * HEAD_DIM)
                keys_here, queries = all_keys[:, cols], all_queries[:, cols]
                grads = all_grads[:, cols]
                soft = turned_softmax(keys_here, queries)
                soft_grad = dot_cols(all_values[:, cols], grads)
                delta = jnp.sum(soft_grad * soft, axis=0, keepdims=True)
                score_grad = (soft * (soft_grad - delta)).astype(LOW)
                pieces[0].append(
                    (dot_tokens(score_grad, keys_here) * HEAD_DIM**-0.5).astype(LOW)
                )
                pieces[1].append(dot_rows(score_grad, queries).astype(LOW))
                pieces[2].append(dot_rows(soft.astype(LOW), grads).astype(LOW))
            for part in range(3):
                start = (t * 3 + part) * half + step * PAIR
                store_rows(self.joined, pl.multiple_of(start, PAIR), pieces[part])

        if last * PAIR == half:
            self.facts.add((layer, "mixed"))

    def project_back(self, layer, part):
        self.tile(part, 6, (self.weights[layer * 4],), (self.tile_a,))
        grads = self.joined[:, pl.ds(part * TILE, TILE)]
        self.column_sums[part] = jnp.sum(grads.astype(jnp.float32), axis=0, keepdims=True)
        self.add_delta(part == 0, grads, self.tile_a.at[part % 2])
        if part == 5:
            for row, at in ((0, 0), (1, 2)):
                pieces = [self.column_sums[at], self.column_sums[3 + at]]
                self.put_sum(layer, row, jnp.concatenate(pieces, axis=1))

    def first_back(self, layer):
        last = layer == 0
        low_ref = None if last else self.feed_grad
        self.norm_back(layer, self.gains[0], 8, low_ref, None if last else (layer - 1, 7))
        if not last:
            self.facts.add((layer - 1, "arrived"))

    def end(self):
        y = self.y
        near_at = pl.ds(pl.multiple_of(y * 512, 512), 512)
        far_at = pl.ds(pl.multiple_of((1 - y) * 512, 512), 512)
        self.leave[...] = self.grad[:, far_at].astype(LOW)
        self.swaps.append(self.swap(1, self.leave))
        copy = self.fetch(0, self.grad.at[:, near_at], self.near_out)
        copy.wait()
        self.facts.add("summed")

    def chain(self):
        steps = [(1, self.begin, ()), (2, self.widen, ())]
        for layer in reversed(range(self.layers)):
            for part in range(2 * self.widths[2] // TILE):
                steps.append((2.5, lambda layer=layer, part=part: self.feed(layer, part), ()))
            steps.append((4, lambda layer=layer: self.out_back(layer), ((layer + 1, 1),)))
            for k in range(4):
                needs = ((layer + 1, 0),)
                steps.append((7, lambda layer=layer, k=k: self.mix_back(layer, k, k + 1), needs))
            for part in range(6):
                steps.append(
                    (1.5, lambda layer=layer, part=part: self.project_back(layer, part), ())
                )
            steps.append((3, lambda layer=layer: self.first_back(layer), ((layer, 3),)))
        return steps + [(1, self.end, ())]

    def add_sums(self, step):
        if step > 0:
            self.sums_copy.wait()
            self.sums[step] = self.sums[step - 1] + self.sums_in[step - 1]
        if step < len(TOTAL_LINKS):
            copy = pltpu.make_async_remote_copy(
                src_ref=self.sums.at[step],
                dst_ref=self.sums_in.at[step],
                send_sem=self.sums_send.at[step],
                recv_sem=self.sums_recv.at[step],
                device_id=self.settle.partners[TOTAL_LINKS[step]],
                device_id_type=MESH_IDS,
            )
            copy.start()
            self.sums_copy = copy

    def run(self):
        self.y = lax.axis_index("tensor")
        settle = self.settle
        greet(settle.partners)
        self.swaps = [self.swap(0, self.leaving)]
        chain = self.chain()
        last_pair = {}
        for pair, units in enumerate(settle.pairs):
            for matrix, _ in units:
                last_pair[matrix] = pair
        pairs, loaded, sum_step = len(settle.pairs), set(), 0
        passed = -1

        def free(needs):
            for layer, kind in needs:
                if layer < self.layers and passed < last_pair[layer * 4 + kind]:
                    return False
            return True

        def advance():
            _, step, _ = chain.pop(0)
            step()

        pair = 0
        while pair < pairs + STAGE_AT[-1] or sum_step <= len(TOTAL_LINKS):
            if pair < pairs:
                while self.needs[pair] not in self.facts:
                    advance()
                if pair not in loaded:
                    settle.load(pair)
                    loaded.add(pair)
            settle.tick(pair)
            passed = pair
            if "summed" in self.facts and sum_step <= len(TOTAL_LINKS):
                self.add_sums(sum_step)
                sum_step += 1
            if pair + 1 < pairs and self.needs[pair + 1] in self.facts:
                settle.load(pair + 1)
                loaded.add(pair + 1)
            budget = CHAIN_A_TICK
            while chain and budget > 0 and free(chain[0][2]):
                budget -= chain[0][0]
                advance()
            pair += 1
        self.total_out[...] = self.sums[len(TOTAL_LINKS)]
        settle.finish()
        for copy in self.swaps:
            copy.wait()


CHAIN_A_TICK = 5


def backward(weights, kept, upstream, gains, leaving):
    layers = len(weights)
    widths = [block.shape[-1] // 2 for block in weights[0]]
    plan = Backward(layers, widths)
    any_spec, vmem_spec = pl.BlockSpec(memory_space=pl.ANY), pl.BlockSpec(memory_space=pltpu.VMEM)
    operands = [block for layer in weights for block in layer]
    operands += [values[name] for values in kept for name in KEPT]
    operands += [*upstream, leaving]
    in_specs = [any_spec] * len(operands) + [vmem_spec] * len(gains)
    operands += gains
    outs = [jax.ShapeDtypeStruct((layers, 2, BLOCK, width // 2), jnp.float32) for width in widths]
    outs += [
        jax.ShapeDtypeStruct((layers * SUM_ROWS, 1024), jnp.float32),
        jax.ShapeDtypeStruct((ROWS, 512), jnp.float32),
        jax.ShapeDtypeStruct((2, ROWS, 512), LOW),
    ]
    outs += [jax.ShapeDtypeStruct((ROWS, 2 * widths[2]), LOW)] * layers
    out_specs = [any_spec] * len(outs)
    out_specs[4] = vmem_spec

    def kernel(*refs):
        ins, refs = refs[: len(operands)], refs[len(operands) :]
        plan.bind(ins, refs[: len(outs)], refs[len(outs) :])
        plan.run()

    results = pl.pallas_call(
        kernel,
        out_shape=outs,
        in_specs=in_specs,
        out_specs=out_specs,
        scratch_shapes=list(plan.scratch().values()),
        compiler_params=pltpu.CompilerParams(
            collective_id=1, has_side_effects=True, vmem_limit_bytes=60 * 1024 * 1024
        ),
        cost_estimate=pl.CostEstimate(
            flops=120 * 1024**3, bytes_accessed=700 * 1024 * 1024, transcendentals=0
        ),
        name="backward",
    )(*operands)
    return results[:4], results[4], results[5], results[6]


def in_order(own, other, index, axis):
    first = jnp.where(index == 0, own, other)
    second = jnp.where(index == 0, other, own)
    return jnp.concatenate((first, second), axis=axis)


def image_body(
    images,
    first_gain,
    first_shift,
    query_weight,
    key_weight,
    value_weight,
    query_bias,
    value_bias,
    out_weight,
    out_bias,
    second_gain,
    second_shift,
    up_weight,
    up_bias,
    down_weight,
    down_bias,
    cotangent,
):
    layers = query_weight.shape[0]
    half = images.shape[1]
    hidden_width = 2 * up_weight.shape[2]
    y = lax.axis_index("tensor")
    far = 1 - y

    def own_rows(block, image):
        rows = lax.dynamic_slice_in_dim(block, image * SEQ, SEQ)
        return jnp.pad(rows, ((0, ROWS - SEQ), (0, 0)))

    weights, (cotangent_in, leaving, staying), kept = forward(
        (
            query_weight,
            key_weight,
            value_weight,
            jnp.swapaxes(out_weight, 1, 2),
            up_weight,
            jnp.swapaxes(down_weight, 1, 2),
        ),
        own_rows(images, y),
        jnp.stack((own_rows(images, far), own_rows(cotangent, far))),
        (first_gain, first_shift, second_gain, second_shift),
        (query_bias, value_bias, out_bias, down_bias, up_bias),
    )

    (project_out, out_out, up_out, down_out), totals, near_gradient, arriving = backward(
        weights,
        kept,
        (own_rows(cotangent, y), cotangent_in),
        (first_gain, second_gain),
        leaving,
    )
    totals = totals.reshape(layers, -1)
    project_out, out_out, up_out, down_out = [
        jnp.swapaxes(block, 1, 2).reshape(layers, BLOCK, -1)
        for block in (project_out, out_out, up_out, down_out)
    ]
    width = 2 * half
    small_outs, at = [], 0
    for size in (width, width, width, hidden_width, width, width, width, width, width):
        small_outs.append(totals[:, at : at + size])
        at += size
    return (
        in_order(staying[:SEQ], arriving[0, :SEQ], y, 0),
        in_order(near_gradient[:SEQ], arriving[1, :SEQ].astype(jnp.float32), y, 0),
        project_out[:, :, :half],
        project_out[:, :, half : 2 * half],
        project_out[:, :, 2 * half :],
        jnp.swapaxes(out_out, 1, 2),
        up_out,
        jnp.swapaxes(down_out, 1, 2),
        *small_outs,
    )


def solution(mesh):
    in_specs = (
        P("wide", "tensor"),
        P(),
        P(),
        P(None, "wide", "tensor"),
        P(None, "wide", "tensor"),
        P(None, "wide", "tensor"),
        P(None, "tensor"),
        P(None, "tensor"),
        P(None, "tensor", "wide"),
        P(None, "tensor"),
        P(),
        P(),
        P(None, "wide", "tensor"),
        P(None, "tensor"),
        P(None, "tensor", "wide"),
        P(None, "tensor"),
        P("wide", "tensor"),
    )
    out_specs = (
        P("wide", "tensor"),
        P("wide", "tensor"),
        P(None, "wide", "tensor"),
        P(None, "wide", "tensor"),
        P(None, "wide", "tensor"),
        P(None, "tensor", "wide"),
        P(None, "wide", "tensor"),
        P(None, "tensor", "wide"),
        P(),
        P(),
        P(),
        P(),
        P(),
        P(),
        P(),
        P(),
        P(),
    )
    chosen = body
    if mesh.shape["wide"] == 16 and mesh.shape["tensor"] == 2:
        chosen = image_body
    return jax.shard_map(
        chosen, mesh=mesh, in_specs=in_specs, out_specs=out_specs, check_vma=False
    )
```
